32 devices in a mesh: shots: 2 (over x), xline: 8 (over z, y), inline: 2 (over core).
Axes of the slice: x: 2, y: 2, z: 4, core: 2. Of those that a mesh axis runs over, the one named last changes fastest.
Arguments:
- fwd_now: float32 [128, 64, 256], P(('shots', 'inline'), 'xline'), parts along dimension 0, may hold values from -6 to 6
- fwd_before: float32 [128, 64, 256], P(('shots', 'inline'), 'xline'), parts along dimension 0, may hold values from -6 to 6
- adj_now: float32 [128, 64, 256], P(('shots', 'inline'), 'xline'), parts along dimension 0, may hold values from -6 to 6
- adj_before: float32 [128, 64, 256], P(('shots', 'inline'), 'xline'), parts along dimension 0, may hold values from -6 to 6
- velocity: float32 [64, 64, 256], P('inline', 'xline'), may hold values from 0.2 to 0.4
- log_density: float32 [64, 64, 256], P('inline', 'xline'), may hold values from -0.3 to 0.3
- observed: float32 [16, 2048], P('shots', ('xline', 'inline')), parts along dimension 0, may hold values from -48 to 48
- rec_cells: int32 [16, 128], P(('xline', 'inline')), may hold values from 0 to 65535
- rec_counts: int32 [16, 16], P(('xline', 'inline')), may hold values from 0 to 8, as said below
- src_cell: int32 [32], P('shots'), parts along dimension 0, may hold values from 0 to 1048575
- wavelet: float32 [16, 16], P('shots'), parts along dimension 0, may hold values from -144 to 144
Outputs:
- gradient: float32 [512, 64, 64], P(('shots', 'xline'), 'inline'), parts along dimension 0
- adjoint_state: float32 [128, 64, 256], P(('shots', 'inline'), 'xline'), parts along dimension 0
- adjoint_previous: float32 [128, 64, 256], P(('shots', 'inline'), 'xline'), parts along dimension 0
The draws below stay inside these ranges and needn't reach their ends.
There are 2 independent parts, one for each index of `shots`. The reference program is written for one: setup_inputs(seed, part) draws one part's arguments, and reference() takes and returns one part's arrays. A program takes and returns all parts, laid end to end along the dimension named above; an argument that names none is the same for every part. Nothing has to cross between parts.
Inputs may be any that keep to these rules, and one draw needn't show every extreme that they name: rec_counts[o, s] live slots of the 8 that device s sends to subdomain o; in every draw one subdomain receives 8 live slots from every device.
All inputs are finite; a program needn't handle non-finite values.
Results may differ from the reference program's by a relative error of at most 0.04.
Values sent between devices are 32-bit elements; how exact they have to be, the bound alone decides.
No kernel may reach another device: no remote copies, remote signals or barrier semaphores. Data moves between devices by JAX's collectives and lax.ppermute only.
A program may use at most 64 MiB of HBM per device.

```python
import jax
import jax.numpy as jnp
from jax import lax

CI = 32
CX = 8
NZ = 256
NT = 8
NSRC = 16
CAP = 8
NI = 64
NX = 64
SUBS = 16
SMOOTH = 16
N_INLINE = 2


def draw_rec_counts(key, part):
    key_top, key_raw, key_full = jax.random.split(key, 3)
    ceiling = jax.random.randint(key_top, (SUBS, 1), 1, CAP + 1)
    spread = jax.random.randint(key_raw, (SUBS, SUBS), 0, 1 << 20) % (ceiling + 1)
    counts = (ceiling + spread) // 2
    owner = jax.random.randint(key_full, (), 0, SUBS)
    return jnp.where(jnp.arange(SUBS)[:, None] == owner, CAP, counts).astype(jnp.int32)


def plant(entries, own_key, least, largest):
    dims = entries.shape
    index_at = [jax.random.randint(jax.random.fold_in(own_key, axis), (), 0, dims[axis]) for axis in range(len(dims))]
    entries = entries.at[tuple(index_at)].set(least)
    longest = dims.index(max(dims))
    index_at[longest] = (index_at[longest] + 1) % dims[longest]
    return entries.at[tuple(index_at)].set(largest)


def shard_levels(rng, shape, pieces, smallest, top_value):
    level, own = 1.0, jax.random.fold_in(rng, 6)
    for axis_at, shards_of in pieces:
        steps = jnp.exp(jax.random.uniform(jax.random.fold_in(own, axis_at), (shards_of,), jnp.float32, smallest / len(pieces), top_value / len(pieces)))
        level = level * jnp.repeat(steps, shape[axis_at] // shards_of).reshape([-1 if axis == axis_at else 1 for axis in range(len(shape))])
    return level


def noise(stream_key, shape, scale, bound, shards=(), dtype=jnp.bfloat16):
    array = scale * jax.random.normal(stream_key, shape, jnp.float32)
    if shards:
        array = array * shard_levels(stream_key, shape, shards, -0.22, 0.18)
    return jnp.clip(array, -bound, bound).astype(dtype)


def setup_inputs(seed: int = 0, part: int = 0) -> dict:
    key_list = jax.random.split(jax.random.key(seed), 12)
    part_splits = jax.random.split(jax.random.fold_in(key_list[11], part), 12)
    return {
        "fwd_now": noise(part_splits[0], (NI, NX, NZ), 1.0, 6.0, ((0, 2), (1, 8)), jnp.float32),
        "fwd_before": noise(part_splits[1], (NI, NX, NZ), 1.0, 6.0, ((0, 2), (1, 8)), jnp.float32),
        "adj_now": noise(part_splits[2], (NI, NX, NZ), 1.0, 6.0, ((0, 2), (1, 8)), jnp.float32),
        "adj_before": noise(part_splits[3], (NI, NX, NZ), 1.0, 6.0, ((0, 2), (1, 8)), jnp.float32),
        "velocity": jnp.clip(0.2 + 0.2 * jax.random.uniform(key_list[4], (NI, NX, NZ), jnp.float32) ** shard_levels(key_list[4], (NI, NX, NZ), ((0, 2), (1, 8)), -0.2, 0.2), 0.2, 0.4),
        "log_density": jnp.clip(jax.random.uniform(key_list[5], (NI, NX, NZ), jnp.float32, -0.3, 0.3) * shard_levels(key_list[5], (NI, NX, NZ), ((0, 2), (1, 8)), -0.4, 0.0), -0.3, 0.3),
        "observed": noise(part_splits[6], (NT, SUBS * SUBS * CAP), 8.0, 48.0, ((1, 16),), jnp.float32),
        "rec_cells": plant(jax.random.randint(key_list[7], (SUBS, SUBS * CAP), 0, CI * CX * NZ), jax.random.fold_in(key_list[7], 1), 0, (CI * CX * NZ) - 1).astype(jnp.int32),
        "rec_counts": draw_rec_counts(jax.random.fold_in(key_list[11], 71), part),
        "src_cell": plant(jax.random.randint(part_splits[9], (NSRC,), 0, NI * NX * NZ), jax.random.fold_in(part_splits[9], 1), 0, (NI * NX * NZ) - 1).astype(jnp.int32),
        "wavelet": noise(part_splits[10], (NT, NSRC), 24.0, 144.0, (), jnp.float32),
    }


SECOND_COEFFS = (-205.0 / 72.0, 8.0 / 5.0, -1.0 / 5.0, 8.0 / 315.0, -1.0 / 560.0)
FIRST_COEFFS = (4.0 / 5.0, -1.0 / 5.0, 4.0 / 105.0, -1.0 / 280.0)


def differences(padded):
    inner_a = padded.shape[0] - 8
    inner_b = padded.shape[1] - 8
    center = padded[4:4 + inner_a, 4:4 + inner_b]
    extent = center.shape[2]
    deep_pad = jnp.pad(center, ((0, 0), (0, 0), (4, 4)))
    laplace = (3.0 * SECOND_COEFFS[0]) * center
    slope_i = jnp.zeros_like(center)
    slope_x = jnp.zeros_like(center)
    slope_z = jnp.zeros_like(center)
    for offset in range(1, 5):
        plus_i = padded[4 + offset:4 + offset + inner_a, 4:4 + inner_b]
        minus_i = padded[4 - offset:4 - offset + inner_a, 4:4 + inner_b]
        plus_x = padded[4:4 + inner_a, 4 + offset:4 + offset + inner_b]
        minus_x = padded[4:4 + inner_a, 4 - offset:4 - offset + inner_b]
        plus_z = deep_pad[:, :, 4 + offset:4 + offset + extent]
        minus_z = deep_pad[:, :, 4 - offset:4 - offset + extent]
        weight_first = FIRST_COEFFS[offset - 1]
        slope_i = slope_i + weight_first * (plus_i - minus_i)
        slope_x = slope_x + weight_first * (plus_x - minus_x)
        slope_z = slope_z + weight_first * (plus_z - minus_z)
        laplace = laplace + SECOND_COEFFS[offset] * (plus_i + minus_i + plus_x + minus_x + plus_z + minus_z)
    return laplace, (slope_i, slope_x, slope_z)


def wave_operator(padded, density_slopes, speed_sq):
    laplace, slopes = differences(padded)
    coupling = density_slopes[0] * slopes[0] + density_slopes[1] * slopes[1] + density_slopes[2] * slopes[2]
    return speed_sq * (laplace - coupling)


def pad_four(values):
    return jnp.pad(values, ((4, 4), (4, 4), (0, 0)))


def reference(fwd_now, fwd_before, adj_now, adj_before, velocity, log_density, observed, rec_cells, rec_counts, src_cell, wavelet):
    cell_total = NI * NX * NZ
    spare_term, density_slopes = differences(pad_four(log_density))
    speed_sq = velocity * velocity
    history = [fwd_before, fwd_now]
    for moment in range(NT):
        current = history[-1]
        source_field = jnp.zeros((cell_total,), jnp.float32).at[src_cell].add(wavelet[moment]).reshape(NI, NX, NZ)
        history.append(2.0 * current - history[-2] + wave_operator(pad_four(current), density_slopes, speed_sq) + source_field)
    owner_ids = jnp.arange(SUBS).astype(jnp.int32)
    owner_x = owner_ids // N_INLINE
    owner_i = owner_ids % N_INLINE
    local_i = rec_cells // (CX * NZ)
    local_x = (rec_cells // NZ) % CX
    local_z = rec_cells % NZ
    global_cell = ((owner_i[:, None] * CI + local_i) * NX + owner_x[:, None] * CX + local_x) * NZ + local_z
    live_mask = (jnp.arange(CAP).astype(jnp.int32)[None, None, :] < rec_counts[:, :, None]).astype(jnp.float32).reshape(SUBS, SUBS * CAP)
    routed = observed.reshape(NT, SUBS, SUBS, CAP).transpose(0, 2, 1, 3).reshape(NT, SUBS, SUBS * CAP)
    predicted = jnp.stack([history[moment + 2].reshape(-1)[global_cell] for moment in range(NT)])
    residual = live_mask[None] * (predicted - routed)
    flat_cells = global_cell.reshape(-1)
    adjoint = [adj_before, adj_now]
    image_sum = jnp.zeros_like(fwd_now)
    for back_step in range(NT):
        moment = NT - 1 - back_step
        current = adjoint[-1]
        injected = jnp.zeros((cell_total,), jnp.float32).at[flat_cells].add(residual[moment].reshape(-1)).reshape(NI, NX, NZ)
        fresh_state = 2.0 * current - adjoint[-2] + wave_operator(pad_four(current), density_slopes, speed_sq) + injected
        adjoint.append(fresh_state)
        image_sum = image_sum + fresh_state * (history[moment + 2] - 2.0 * history[moment + 1] + history[moment])
    raw_gradient = image_sum * (2.0 / NT) / velocity
    positions = jnp.arange(NX).astype(jnp.float32)
    kernel = jnp.exp(-jnp.abs(positions[:, None] - positions[None, :]) / SMOOTH)
    kernel = kernel / jnp.sum(kernel, axis=1, keepdims=True)
    gradient = jnp.einsum("ixz,yx->ziy", raw_gradient, kernel, precision=lax.Precision.HIGHEST)
    return gradient, adjoint[-1], adjoint[-2]
```

```python
import functools

import jax
import jax.numpy as jnp
import numpy as np
from jax import lax
from jax.experimental import pallas as pl
from jax.experimental.pallas import tpu as pltpu
from jax.sharding import PartitionSpec as P

CAP = 8
SMOOTH = 16
SECOND = (-205.0 / 72.0, 8.0 / 5.0, -1.0 / 5.0, 8.0 / 315.0, -1.0 / 560.0)
FIRST = (4.0 / 5.0, -1.0 / 5.0, 4.0 / 105.0, -1.0 / 280.0)
ALL = ("shots", "xline", "inline")
F32 = jnp.float32
BF16 = jnp.bfloat16


class Plan:
    def __init__(self, mesh):
        self.shots = mesh.shape["shots"]
        self.nx = mesh.shape["xline"]
        self.nq = self.nx // 2

    def index(self, s, q, y, c):
        return (s * self.nx + 2 * q + y) * 2 + c

    def perm(self, partner):
        pairs = []
        for s in range(self.shots):
            for q in range(self.nq):
                for y in range(2):
                    for c in range(2):
                        t = partner(q, y, c)
                        dst = self.index(s ^ 1, q, y, c) if t is None else self.index(s, *t)
                        pairs.append((self.index(s, q, y, c), dst))
        return pairs

    def swap(self):
        return self.perm(lambda q, y, c: None if y == c else (q, c, y))

    def z(self):
        def partner(q, y, c):
            other = q + 1 if c == 1 else q - 1
            return (other, y, 1 - c) if 0 <= other < self.nq else None

        return self.perm(partner)

    def core(self):
        return self.perm(lambda q, y, c: (q, y, 1 - c))

    def y(self):
        return self.perm(lambda q, y, c: (q, 1 - y, c))

    def spread(self, shift):
        return self.perm(lambda q, y, c: ((q + shift) % self.nq, c, y))


def send(value, pairs):
    return lax.ppermute(value, ALL, pairs)


def depth_matrix(n):
    m = np.zeros((n, 2 * n), np.float32)
    for k in range(1, 5):
        for j in range(n):
            for i, sign in ((j + k, 1.0), (j - k, -1.0)):
                if 0 <= i < n:
                    m[i, j] = round(SECOND[k] * 5040)
                    m[i, n + j] = sign * round(FIRST[k - 1] * 840)
    return m


def split(value):
    high = value.astype(BF16)
    return high, (value - high.astype(F32)).astype(BF16)


def mm(a, b):
    return jnp.dot(a, b, preferred_element_type=F32)


def fill(flags, cur, zm, cm, ym, g):
    rows, cols, depth = cur.shape
    c, y, inside = flags[0], flags[1], flags[2]
    from_z = jnp.where(inside == 1, zm[...], 0.0)
    from_c = cm[...]
    low = jnp.where(c == 0, from_z, from_c)
    high = jnp.where(c == 0, from_c, from_z)
    edge = ym[...]
    top = jnp.where(y == 1, edge, 0.0)
    bottom = jnp.where(y == 0, edge, 0.0)
    own = cur[...]
    for h in range(depth // 128):
        lanes = slice(h * 128, h * 128 + 128)
        g[h, 4 : 4 + rows, 0:4, :] = low[:, :, lanes]
        g[h, 4 : 4 + rows, 4 : 4 + cols, :] = own[:, :, lanes]
        g[h, 4 : 4 + rows, 4 + cols : 8 + cols, :] = high[:, :, lanes]
        g[h, 0:4, 4 : 4 + cols, :] = top[:, :, lanes]
        g[h, 4 + rows : 8 + rows, 4 : 4 + cols, :] = bottom[:, :, lanes]


def depth_part(cur, mat, zz):
    rows, cols, depth = cur.shape
    high, low = split(cur[...].reshape(rows * cols, depth))
    zz[...] = mm(high, mat[...]) + mm(low, mat[...])


def stencil(g, zz, depth, cols, h, r):
    def at(di, dx):
        return g[h, r + 4 + di, 4 + dx : 4 + dx + cols, :]

    row = pl.ds(pl.multiple_of(r * cols, cols), cols)
    center = at(0, 0)
    lap = 3.0 * SECOND[0] * center + zz[row, h * 128 : h * 128 + 128] * (1.0 / 5040)
    slope_z = zz[row, depth + h * 128 : depth + h * 128 + 128] * (1.0 / 840)
    slope_i = slope_x = None
    for k in range(1, 5):
        pi, mi, px, mx = at(k, 0), at(-k, 0), at(0, k), at(0, -k)
        lap = lap + SECOND[k] * ((pi + mi) + (px + mx))
        si, sx = FIRST[k - 1] * (pi - mi), FIRST[k - 1] * (px - mx)
        slope_i = si if slope_i is None else slope_i + si
        slope_x = sx if slope_x is None else slope_x + sx
    return center, lap, slope_i, slope_x, slope_z


def rims(flags, new, zo, co, yo):
    rows, cols, depth = new.shape
    c, y = flags[0], flags[1]
    first, last = new[:, 0:4, :], new[:, cols - 4 : cols, :]
    zo[...] = jnp.where(c == 0, first, last)
    co[...] = jnp.where(c == 0, last, first)
    yo[...] = jnp.where(y == 0, new[rows - 4 : rows], new[0:4])


def settle_kernel(flags, a, b, recv, a_out, b_out, zo, co, yo):
    keep = flags[0] == flags[1]
    for n, (own, out) in enumerate(((a, a_out), (b, b_out))):
        out[...] = jnp.where(keep, own[...], recv[n])
        rims(flags, out, zo.at[n], co.at[n], yo.at[n])


def slope_kernel(flags, lr, zm, cm, ym, mat, gi, gx, gz, g, zz):
    rows, cols, depth = lr.shape
    fill(flags, lr, zm.at[0], cm.at[0], ym.at[0], g)
    depth_part(lr, mat, zz)

    def body(r, carry):
        for h in range(depth // 128):
            lanes = slice(h * 128, h * 128 + 128)
            spare, lap, si, sx, sz = stencil(g, zz, depth, cols, h, r)
            gi[r, :, lanes] = si
            gx[r, :, lanes] = sx
            gz[r, :, lanes] = sz
        return carry

    lax.fori_loop(0, rows, body, 0, unroll=2)


def advance(cur, prev, vel, gi, gx, gz, g, zz, inj, finish):
    rows, cols, depth = cur.shape

    def body(r, carry):
        row = pl.ds(pl.multiple_of(r * cols, cols), cols)
        for h in range(depth // 128):
            lanes = slice(h * 128, h * 128 + 128)
            center, lap, si, sx, sz = stencil(g, zz, depth, cols, h, r)
            coupling = gi[r, :, lanes] * si + gx[r, :, lanes] * sx + gz[r, :, lanes] * sz
            v = vel[r, :, lanes]
            change = (v * v) * (lap - coupling) + inj[row, lanes]
            finish(r, lanes, 2.0 * center - prev[r, :, lanes] + change, change, v)
        return carry

    lax.fori_loop(0, rows, body, 0, unroll=2)


def forward_kernel(step, flags, cur, prev, vel, gi, gx, gz, zm, cm, ym, mat, srow, sz, wave,
                   new, change_out, zo, co, yo, g, zz, inj):
    rows, cols, depth = cur.shape
    fill(flags, cur, zm, cm, ym, g)
    depth_part(cur, mat, zz)
    n = srow.shape[1]
    spot = lax.broadcasted_iota(jnp.int32, (rows * cols, n), 0) == srow[...]
    spot = spot.astype(F32).astype(BF16)
    high, low = split(jnp.where(
        lax.broadcasted_iota(jnp.int32, (n, depth), 1) == sz[...], wave[:, step : step + 1], 0.0))
    inj[...] = mm(spot, high) + mm(spot, low)

    def finish(r, lanes, value, change, v):
        new[r, :, lanes] = value
        change_out[r, :, lanes] = change

    advance(cur, prev, vel, gi, gx, gz, g, zz, inj, finish)
    rims(flags, new, zo, co, yo)


def adjoint_kernel(t, last, flags, cur, prev, vel, gi, gx, gz, zm, cm, ym, mat, pnext, change_in,
                   image, rrow, rrow_c, rz, obs, new, image_out, *rest):
    rows, cols, depth = cur.shape
    g, zz, inj = rest[-3:]
    fill(flags, cur, zm, cm, ym, g)
    depth_part(cur, mat, zz)
    n = rrow.shape[1]
    spot = lax.broadcasted_iota(jnp.int32, (rows * cols, n), 0) == rrow[...]
    spot = spot.astype(F32).astype(BF16)
    pick = lax.broadcasted_iota(jnp.int32, (n, rows * cols), 1) == rrow_c[...]
    pick = pick.astype(F32).astype(BF16)
    high, low = split(pnext[...].reshape(rows * cols, depth))
    deep = lax.broadcasted_iota(jnp.int32, (n, depth), 1) == rz[...]
    seen = jnp.where(deep, mm(pick, high) + mm(pick, low), 0.0)
    residual = jnp.sum(seen, axis=1, keepdims=True) - obs[:, t : t + 1]
    high, low = split(jnp.where(deep, residual, 0.0))
    inj[...] = mm(spot, high) + mm(spot, low)
    scale = 2.0 / obs.shape[1]

    def finish(r, lanes, value, change, v):
        new[r, :, lanes] = value
        total = value * change_in[r, :, lanes]
        if image is not None:
            total = total + image[r, :, lanes]
        if last:
            total = total * scale / v
        image_out[r, :, lanes] = total

    advance(cur, prev, vel, gi, gx, gz, g, zz, inj, finish)
    if not last:
        rims(flags, new, *rest[:3])


def first_adjoint_kernel(t, last, *refs):
    adjoint_kernel(t, last, *refs[:13], None, *refs[13:])


def shaped(*shape):
    return jax.ShapeDtypeStruct(shape, F32)


def call(kernel, name, outs, scratch, *args):
    specs = [pl.BlockSpec(memory_space=pltpu.SMEM)]
    specs += [pl.BlockSpec(memory_space=pltpu.VMEM)] * (len(args) - 1)
    return pl.pallas_call(
        kernel,
        name=name,
        out_shape=outs,
        in_specs=specs,
        out_specs=[pl.BlockSpec(memory_space=pltpu.VMEM)] * len(outs),
        scratch_shapes=scratch,
        compiler_params=pltpu.CompilerParams(vmem_limit_bytes=16 * 1024 * 1024),
        cost_estimate=pl.CostEstimate(flops=5_000_000, bytes_accessed=2_000_000, transcendentals=0),
    )(*args)


def per_device(plan, fwd_now, fwd_before, adj_now, adj_before, velocity, log_density, observed,
               rec_cells, rec_counts, src_cell, wavelet):
    block = fwd_now.shape
    rows, cols, depth = block
    steps = wavelet.shape[0]
    nx, nq = plan.nx, plan.nq
    subs = 2 * nx
    xline, c = lax.axis_index("xline"), lax.axis_index("inline")
    q, y = xline // 2, xline % 2
    z_perm, c_perm, y_perm, swap_perm = plan.z(), plan.core(), plan.y(), plan.swap()
    inside = jnp.where(c == 0, q > 0, q < nq - 1).astype(jnp.int32)
    flags = jnp.stack([c, y, inside]).astype(jnp.int32)
    mat = jnp.asarray(depth_matrix(depth), BF16)
    rims_of = [shaped(rows, 4, depth), shaped(rows, 4, depth), shaped(4, cols, depth)]
    pair_rims = [shaped(2, rows, 4, depth), shaped(2, rows, 4, depth), shaped(2, 4, cols, depth)]
    scratch = [
        pltpu.VMEM((depth // 128, rows + 8, cols + 8, 128), F32),
        pltpu.VMEM((rows * cols, 2 * depth), F32),
    ]
    full_scratch = scratch + [pltpu.VMEM((rows * cols, depth), F32)]

    def halo(zo, co, yo):
        return send(zo, z_perm), send(co, c_perm), send(yo, y_perm)

    live = jnp.arange(CAP)[None, :] < rec_counts[0][:, None]
    cells = jnp.where(live.reshape(-1), rec_cells[0], -1)
    packed = jnp.concatenate([observed, cells[None, :].astype(F32)], axis=0)
    gathered = lax.all_gather(packed, ("xline", "inline"))

    first = send(jnp.stack([log_density, fwd_now]), swap_perm)
    second = send(jnp.stack([velocity, fwd_before]), swap_perm)
    third = send(jnp.stack([adj_now, adj_before]), swap_perm)
    settle = functools.partial(call, settle_kernel, "settle", [shaped(*block)] * 2 + pair_rims, [])
    density, p_now, zo, co, yo = settle(flags, log_density, fwd_now, first)
    zm, cm, ym = halo(zo, co, yo)
    keep = y == c
    vel = jnp.where(keep, velocity, second[0])
    p_before = jnp.where(keep, fwd_before, second[1])
    u_now, u_before, zo, co, yo = settle(flags, adj_now, adj_before, third)
    u_halo = halo(zo[0], co[0], yo[0])

    gi, gx, gz = call(slope_kernel, "slopes", [shaped(*block)] * 3, scratch,
                      flags, density, zm, cm, ym, mat)

    plane = nx * cols * depth
    src_i = src_cell // plane - y * rows
    src_x = src_cell // depth % (nx * cols) - (2 * q + c) * cols
    ok = (src_i >= 0) & (src_i < rows) & (src_x >= 0) & (src_x < cols)
    srow = jnp.where(ok, src_i * cols + src_x, -1)[None, :]
    sz = (src_cell % depth)[:, None]
    wave = wavelet.T

    model = (vel, gi, gx, gz)
    halos = (zm[1], cm[1], ym[1])
    states, changes = [], []
    for t in range(steps):
        p_next, change, zo, co, yo = call(
            functools.partial(forward_kernel, t), "forward",
            [shaped(*block)] * 2 + rims_of, full_scratch,
            flags, p_now, p_before, *model, *halos, mat, srow, sz, wave)
        if t < steps - 1:
            halos = halo(zo, co, yo)
        p_before, p_now = p_now, p_next
        states.append(p_next)
        changes.append(change)

    sub = (2 * q + c) * 2 + y
    mine = lax.dynamic_index_in_dim(gathered, sub, 0, keepdims=False)[steps].astype(jnp.int32)
    traces = gathered[:, :steps].reshape(subs, steps, subs, CAP)
    traces = lax.dynamic_index_in_dim(traces, sub, 2, keepdims=False)
    obs = traces.transpose(0, 2, 1).reshape(subs * CAP, steps)
    rrow = jnp.where(mine < 0, -1, mine // depth)
    rz = (mine % depth)[:, None]

    halos = u_halo
    image = []
    for j in range(steps):
        t = steps - 1 - j
        last = j == steps - 1
        kernel = functools.partial(adjoint_kernel if image else first_adjoint_kernel, t, last)
        outs = call(
            kernel, "adjoint",
            [shaped(*block)] * 2 + ([] if last else rims_of), full_scratch,
            flags, u_now, u_before, *model, *halos, mat, states[t], changes[t], *image,
            rrow[None, :], rrow[:, None], rz, obs)
        u_before, u_now = u_now, outs[0]
        image = [outs[1]]
        if not last:
            halos = halo(*outs[2:])

    chunk = depth // nx
    raw = image[0].reshape(rows * cols, depth).T.reshape(nq, 2, chunk, rows * cols)
    own = lax.dynamic_index_in_dim(raw, c, 1, keepdims=False)
    other = send(lax.dynamic_index_in_dim(raw, 1 - c, 1, keepdims=False), c_perm)
    both = jnp.where(c == 0, jnp.stack([own, other], 1), jnp.stack([other, own], 1))
    pieces = [
        send(lax.dynamic_index_in_dim(both, (q + s) % nq, 0, keepdims=False), plan.spread(s))
        for s in range(nq)
    ]
    adj_out = send(u_now, swap_perm)
    adj_prev = send(u_before, swap_perm)
    adj_out = jnp.where(keep, u_now, adj_out)
    adj_prev = jnp.where(keep, u_before, adj_prev)

    pieces = jnp.stack(pieces).reshape(2 * nq, chunk, rows, cols)
    lines = jnp.arange(nx * cols)
    from_q = (q - jnp.arange(nq)) % nq
    places = (from_q[:, None] * (2 * cols) + jnp.arange(2 * cols)[None, :]).reshape(-1)
    weights = jnp.exp(-jnp.abs(lines[:, None] - places[None, :]).astype(F32) / SMOOTH)
    weights = weights / jnp.sum(weights, axis=1, keepdims=True)
    gradient = jnp.einsum("jzix,yjx->ziy", pieces, weights.reshape(-1, 2 * nq, cols),
                          precision=lax.Precision.HIGHEST)
    return gradient, adj_out, adj_prev


def solution(mesh):
    field = P(("shots", "inline"), "xline", None)
    model = P("inline", "xline", None)
    lists = P(("xline", "inline"), None)
    return jax.shard_map(
        functools.partial(per_device, Plan(mesh)),
        mesh=mesh,
        in_specs=(field, field, field, field, model, model, P("shots", ("xline", "inline")),
                  lists, lists, P("shots"), P("shots", None)),
        out_specs=(P(("shots", "xline"), "inline", None), field, field),
        check_vma=False,
    )
```

```python
import functools

import jax
import jax.numpy as jnp
import numpy as np
from jax import lax
from jax.experimental import pallas as pl
from jax.experimental.pallas import tpu as pltpu
from jax.sharding import PartitionSpec as P

CAP = 8
SMOOTH = 16
SECOND = (-205.0 / 72.0, 8.0 / 5.0, -1.0 / 5.0, 8.0 / 315.0, -1.0 / 560.0)
FIRST = (4.0 / 5.0, -1.0 / 5.0, 4.0 / 105.0, -1.0 / 280.0)
ALL = ("shots", "xline", "inline")
COLS = 8
GROUP = 8
VMEM_BYTES = 8 * 1024 * 1024
F32 = jnp.float32
BF16 = jnp.bfloat16


class Plan:
    def __init__(self, mesh):
        self.shots = mesh.shape["shots"]
        self.nx = mesh.shape["xline"]
        self.nq = self.nx // 2

    def index(self, s, q, y, c):
        return (s * self.nx + 2 * q + y) * 2 + c

    def perm(self, partner):
        pairs = []
        for s in range(self.shots):
            for q in range(self.nq):
                for y in range(2):
                    for c in range(2):
                        t = partner(q, y, c)
                        dst = self.index(s ^ 1, q, y, c) if t is None else self.index(s, *t)
                        pairs.append((self.index(s, q, y, c), dst))
        return pairs

    def swap(self):
        return self.perm(lambda q, y, c: None if y == c else (q, c, y))

    def z(self):
        def partner(q, y, c):
            other = q + 1 if c == 1 else q - 1
            return (other, y, 1 - c) if 0 <= other < self.nq else None

        return self.perm(partner)

    def core(self):
        return self.perm(lambda q, y, c: (q, y, 1 - c))

    def y(self):
        return self.perm(lambda q, y, c: (q, 1 - y, c))

    def flip(self, bit):
        return self.perm(lambda q, y, c: (q ^ bit, y, c) if (q ^ bit) < self.nq else None)

    def spread(self, shift):
        return self.perm(lambda q, y, c: ((q + shift) % self.nq, c, y))


def send(value, pairs):
    return lax.ppermute(value, ALL, pairs)


def depth_matrix(n):
    m = np.zeros((n, 2 * n), np.float32)
    for k in range(1, 5):
        for j in range(n):
            for i, sign in ((j + k, 1.0), (j - k, -1.0)):
                if 0 <= i < n:
                    m[i, j] = round(SECOND[k] * 5040)
                    m[i, n + j] = sign * round(FIRST[k - 1] * 840)
    return m


def stencil_matrix(rows, cols):
    own = (rows + 8) * cols
    m = np.zeros((3, rows, cols, own + rows * 8), np.float32)
    for i in range(rows):
        for x in range(cols):
            for k in range(1, 5):
                total = round(SECOND[k] * 5040)
                slope = round(FIRST[k - 1] * 840)
                for sign in (1, -1):
                    at = (i + 4 + sign * k) * cols + x
                    m[0, i, x, at] += total
                    m[1, i, x, at] += sign * slope
                    to = x + sign * k
                    if to < 0:
                        at = own + i * 4 + to + 4
                    elif to >= cols:
                        at = own + rows * 4 + i * 4 + to - cols
                    else:
                        at = (i + 4) * cols + to
                    m[0, i, x, at] += total
                    m[2, i, x, at] += sign * slope
    return m.reshape(3 * rows * cols, own + rows * 8)


def split(value):
    high = value.astype(BF16)
    return high, (value - high.astype(F32)).astype(BF16)


def mm(a, b):
    return jnp.dot(a, b, preferred_element_type=F32)


def differences(flags, cur, zm, cm, ym, near, deep):
    depth = cur.shape[1]
    size = GROUP * COLS
    own = split(cur[...])
    along = mm(jnp.concatenate(own, axis=1), deep[...])
    edge = ym[...]
    top = split(jnp.where(flags[1] == 1, edge, 0.0))
    bottom = split(jnp.where(flags[1] == 0, edge, 0.0))
    from_z, from_c = split(zm[...]), split(cm[...])
    ext = [jnp.concatenate(parts, axis=0) for parts in zip(top, own, bottom)]
    for n in range(cur.shape[0] // size):
        here = slice(n * size, n * size + size)
        sides = slice(n * GROUP * 4, n * GROUP * 4 + GROUP * 4)
        rhs = []
        for p in range(2):
            rhs += [ext[p][n * size : n * size + size + 8 * COLS], from_z[p][sides], from_c[p][sides]]
        out = mm(near[...], jnp.concatenate(rhs, axis=0))
        yield (here, out[0:size], along[here, 0:depth], out[size : 2 * size], out[2 * size :],
               along[here, depth:])


def halves(value):
    rows, depth = value.shape
    pairs = value.reshape(rows // (2 * COLS), 2, COLS, depth)
    a, b = pairs[:, 0], pairs[:, 1]
    low = lax.broadcasted_iota(jnp.int32, a.shape, 1) < 4
    first = jnp.where(low, a, pltpu.roll(b, 4, axis=1))
    last = jnp.where(low, pltpu.roll(a, 4, axis=1), b)
    return first.reshape(rows // 2, depth), last.reshape(rows // 2, depth)


def rims(flags, new, zo, co, yo):
    first, last = halves(new[...])
    zo[...] = jnp.where(flags[0] == 0, first, last)
    co[...] = jnp.where(flags[0] == 0, last, first)
    size = new.shape[0]
    yo[...] = jnp.where(flags[1] == 0, new[size - 4 * COLS :], new[0 : 4 * COLS])


def settle_kernel(rim_count, flags, a, b, recv, a_out, b_out, *outs):
    keep = flags[0] == flags[1]
    for n, (own, out) in enumerate(((a, a_out), (b, b_out))):
        out[...] = jnp.where(keep, own[...], recv[n])
        if n < rim_count:
            rims(flags, out, *(ref.at[n] for ref in outs))


def settle_one(with_rims, flags, own, recv, out, *outs):
    out[...] = jnp.where(flags[0] == flags[1], own[...], recv[...])
    if with_rims:
        rims(flags, out, *outs)


def model_kernel(flags, lr, zm, cm, ym, near, deep, vel, k0, ki, kx, kz):
    for here, spare, spare_z, di, dx, dz in differences(flags, lr, zm.at[0], cm.at[0], ym.at[0], near, deep):
        v = vel[here]
        square = v * v
        k0[here] = square * (1.0 / 5040)
        scaled = square * (1.0 / (840 * 840))
        ki[here] = scaled * di
        kx[here] = scaled * dx
        kz[here] = scaled * dz


def advance(flags, cur, prev, k0, ki, kx, kz, zm, cm, ym, near, deep, inj, finish):
    for here, sums, sums_z, di, dx, dz in differences(flags, cur, zm, cm, ym, near, deep):
        center = cur[here]
        change = k0[here] * ((sums + sums_z) + (3.0 * SECOND[0] * 5040) * center)
        change = change - (ki[here] * di + kx[here] * dx + kz[here] * dz) + inj[here]
        finish(here, (center - prev[here]) + (center + change), change)


def forward_kernel(step, flags, cur, prev, k0, ki, kx, kz, zm, cm, ym, near, deep, srow, sz, wave,
                   new, change_out, zo, co, yo):
    size, depth = cur.shape
    n = srow.shape[1]
    spot = lax.broadcasted_iota(jnp.int32, (size, n), 0) == srow[...]
    spot = spot.astype(F32).astype(BF16)
    high, low = split(jnp.where(
        lax.broadcasted_iota(jnp.int32, (n, depth), 1) == sz[...], wave[:, step : step + 1], 0.0))
    inj = mm(spot, high) + mm(spot, low)

    def finish(here, value, change):
        new[here] = value
        change_out[here] = change

    advance(flags, cur, prev, k0, ki, kx, kz, zm, cm, ym, near, deep, inj, finish)
    rims(flags, new, zo, co, yo)


def adjoint_kernel(t, last, flags, cur, prev, k0, ki, kx, kz, zm, cm, ym, near, deep, pnext,
                   change_in, image, rrow, rrow_c, rz, obs, extra, new, image_out, *outs):
    size, depth = cur.shape
    n = rrow.shape[1]
    spot = lax.broadcasted_iota(jnp.int32, (size, n), 0) == rrow[...]
    spot = spot.astype(F32).astype(BF16)
    pick = lax.broadcasted_iota(jnp.int32, (n, size), 1) == rrow_c[...]
    pick = pick.astype(F32).astype(BF16)
    high, low = split(pnext[...])
    at = lax.broadcasted_iota(jnp.int32, (n, depth), 1) == rz[...]
    seen = jnp.where(at, mm(pick, high) + mm(pick, low), 0.0)
    residual = jnp.sum(seen, axis=1, keepdims=True) - obs[:, t : t + 1]
    high, low = split(jnp.where(at, residual, 0.0))
    inj = mm(spot, high) + mm(spot, low)
    scale = 2.0 / obs.shape[1]

    def finish(here, value, change):
        new[here] = value
        total = value * change_in[here]
        if image is not None:
            total = total + image[here]
        if last:
            total = total * scale / extra[here]
        image_out[here] = total

    advance(flags, cur, prev, k0, ki, kx, kz, zm, cm, ym, near, deep, inj, finish)
    if not last:
        rims(flags, new, *outs)


def first_adjoint_kernel(t, last, *refs):
    adjoint_kernel(t, last, *refs[:14], None, *refs[14:])


def middle(kernel):
    def run(t, last, *refs):
        n = 18 if kernel is first_adjoint_kernel else 19
        kernel(t, last, *refs[:n], None, *refs[n:])

    return run


def shaped(*shape):
    return jax.ShapeDtypeStruct(shape, F32)


def call(kernel, name, outs, *args):
    specs = [pl.BlockSpec(memory_space=pltpu.SMEM)]
    specs += [pl.BlockSpec(memory_space=pltpu.VMEM)] * (len(args) - 1)
    return pl.pallas_call(
        kernel,
        name=name,
        out_shape=outs,
        in_specs=specs,
        out_specs=[pl.BlockSpec(memory_space=pltpu.VMEM)] * len(outs),
        compiler_params=pltpu.CompilerParams(vmem_limit_bytes=VMEM_BYTES),
        cost_estimate=pl.CostEstimate(flops=5_000_000, bytes_accessed=2_000_000, transcendentals=0),
    )(*args)


def per_device(plan, fwd_now, fwd_before, adj_now, adj_before, velocity, log_density, observed,
               rec_cells, rec_counts, src_cell, wavelet):
    rows, cols, depth = fwd_now.shape
    size = rows * cols
    steps = wavelet.shape[0]
    nx, nq = plan.nx, plan.nq
    subs = 2 * nx
    xline, c = lax.axis_index("xline"), lax.axis_index("inline")
    q, y = xline // 2, xline % 2
    keep = y == c
    z_perm, c_perm, y_perm, swap_perm = plan.z(), plan.core(), plan.y(), plan.swap()
    flags = jnp.stack([c, y]).astype(jnp.int32)
    field = shaped(size, depth)
    side, edge = (size // 2, depth), (4 * cols, depth)
    rim = [shaped(*side), shaped(*side), shaped(*edge)]

    deep = depth_matrix(depth)
    deep = jnp.asarray(np.concatenate([deep, deep]), BF16)
    near = stencil_matrix(GROUP, cols)
    own, half = near.shape[1] - GROUP * 8, GROUP * 4
    from_z = np.where(np.arange(near.shape[1]) // half == own // half, 0.0, 1.0)
    other = np.concatenate([near[:, :own], near[:, own + half :], near[:, own : own + half]], axis=1)
    inside = jnp.where(c == 0, q > 0, q < nq - 1)
    near = jnp.where(c == 0, jnp.asarray(near, F32), jnp.asarray(other, F32))
    near = jnp.where(inside, near, near * jnp.asarray(from_z, F32)[None, :]).astype(BF16)
    near = jnp.concatenate([near, near], axis=1)

    def halo(zo, co, yo):
        return send(zo, z_perm), send(co, c_perm), send(yo, y_perm)

    def after(value, *deps):
        return lax.optimization_barrier((value,) + deps)[0]

    def flat(value):
        return value.reshape(size, depth)

    log_density, fwd_now, velocity = flat(log_density), flat(fwd_now), flat(velocity)
    fwd_before, adj_now, adj_before = flat(fwd_before), flat(adj_now), flat(adj_before)
    first = send(jnp.stack([log_density, fwd_now]), swap_perm)
    second = send(jnp.stack([velocity, fwd_before]), swap_perm)
    density, p_now, *out = call(
        functools.partial(settle_kernel, 2), "settle",
        [field, field] + [shaped(2, *r.shape) for r in rim], flags, log_density, fwd_now, first)
    zm, cm, ym = halo(*out)
    vel, p_before = call(functools.partial(settle_kernel, 0), "settle_model", [field, field],
                         flags, velocity, fwd_before, second)
    model = call(model_kernel, "model", [field] * 4, flags, density, zm, cm, ym, near, deep, vel)
    halos = (zm[1], cm[1], ym[1])

    plane = nx * cols * depth
    src_i = src_cell // plane - y * rows
    src_x = src_cell // depth % (nx * cols) - (2 * q + c) * cols
    ok = (src_i >= 0) & (src_i < rows) & (src_x >= 0) & (src_x < cols)
    srow = jnp.where(ok, src_i * cols + src_x, -1)[None, :]
    sz = (src_cell % depth)[:, None]
    wave = wavelet.T

    live = jnp.arange(CAP)[None, :] < rec_counts[0][:, None]
    cells = jnp.where(live.reshape(-1), rec_cells[0], -1)
    lists = jnp.concatenate([observed, cells[None, :].astype(F32)], axis=0)[None]
    stages = [(c_perm, c), (y_perm, y)]
    stages += [(plan.flip(1 << b), (q >> b) & 1) for b in range((nq - 1).bit_length())]

    states, changes = [], []
    for t in range(steps):
        p_next, change, *out = call(
            functools.partial(forward_kernel, t), "forward", [field, field] + rim,
            flags, p_now, p_before, *model, *halos, near, deep, srow, sz, wave)
        if t < steps - 1:
            halos = halo(*out)
        share = -(-len(stages) // (steps - 2))
        for pairs, bit in stages[t * share : t * share + share]:
            got = send(after(lists, out[0]), pairs)
            lists = jnp.where(bit == 0, jnp.concatenate([lists, got]), jnp.concatenate([got, lists]))
        if t == 1:
            got_now = send(after(adj_now, out[0]), swap_perm)
        if t == 3:
            got_before = send(after(adj_before, out[0]), swap_perm)
            u_now, *out = call(functools.partial(settle_one, True), "settle_adjoint", [field] + rim,
                               flags, adj_now, after(got_now, out[0]))
            u_rim = out
        if t == 4:
            u_halos = halo(*(after(r, out[0]) for r in u_rim))
        if t == 5:
            u_before, = call(functools.partial(settle_one, False), "settle_before", [field],
                             flags, adj_before, after(got_before, out[0]))
        p_before, p_now = p_now, p_next
        states.append(p_next)
        changes.append(change)

    sub = (2 * q + c) * 2 + y
    mine = lax.dynamic_index_in_dim(lists, sub, 0, keepdims=False)[steps].astype(jnp.int32)
    traces = lax.dynamic_slice(lists, (0, 0, sub * CAP), (subs, steps, CAP))
    obs = traces.transpose(0, 2, 1).reshape(subs * CAP, steps)
    rrow = jnp.where(mine < 0, -1, mine // depth)
    rz = (mine % depth)[:, None]

    halos = u_halos
    image = None
    for j in range(steps):
        t = steps - 1 - j
        last = j == steps - 1
        args = [flags, u_now, u_before, *model, *halos, near, deep, states[t], changes[t]]
        kernel = adjoint_kernel
        if j == 0:
            kernel = first_adjoint_kernel
        else:
            args.append(image)
        args += [rrow[None, :], rrow[:, None], rz, obs]
        if last:
            args.append(vel)
        else:
            kernel = middle(kernel)
        outs = call(functools.partial(kernel, t, last), "adjoint",
                    [field, field] + ([] if last else rim), *args)
        u_before, u_now = u_now, outs[0]
        image = outs[1]
        if not last:
            halos = halo(*outs[2:])

    chunk = depth // nx
    raw = image.T.reshape(nq, 2, chunk, size)
    own = lax.dynamic_index_in_dim(raw, c, 1, keepdims=False)
    other = send(lax.dynamic_index_in_dim(raw, 1 - c, 1, keepdims=False), c_perm)
    both = jnp.where(c == 0, jnp.stack([own, other], 1), jnp.stack([other, own], 1))
    pieces = [
        send(lax.dynamic_index_in_dim(both, (q + s) % nq, 0, keepdims=False), plan.spread(s))
        for s in range(nq)
    ]
    block = (rows, cols, depth)
    adj_out = jnp.where(keep, u_now, send(u_now, swap_perm)).reshape(block)
    adj_prev = jnp.where(keep, u_before, send(u_before, swap_perm)).reshape(block)

    pieces = jnp.stack(pieces).reshape(2 * nq, chunk, rows, cols)
    lines = jnp.arange(nx * cols)
    from_q = (q - jnp.arange(nq)) % nq
    places = (from_q[:, None] * (2 * cols) + jnp.arange(2 * cols)[None, :]).reshape(-1)
    weights = jnp.exp(-jnp.abs(lines[:, None] - places[None, :]).astype(F32) / SMOOTH)
    weights = weights / jnp.sum(weights, axis=1, keepdims=True)
    gradient = jnp.einsum("jzix,yjx->ziy", pieces, weights.reshape(-1, 2 * nq, cols),
                          precision=lax.Precision.HIGHEST)
    return gradient, adj_out, adj_prev


def solution(mesh):
    field = P(("shots", "inline"), "xline", None)
    model = P("inline", "xline", None)
    lists = P(("xline", "inline"), None)
    return jax.shard_map(
        functools.partial(per_device, Plan(mesh)),
        mesh=mesh,
        in_specs=(field, field, field, field, model, model, P("shots", ("xline", "inline")),
                  lists, lists, P("shots"), P("shots", None)),
        out_specs=(P(("shots", "xline"), "inline", None), field, field),
        check_vma=False,
    )
```

```python
import functools

import jax
import jax.numpy as jnp
import numpy as np
from jax import lax
from jax.experimental import pallas as pl
from jax.experimental.pallas import tpu as pltpu
from jax.sharding import PartitionSpec as P

CAP = 8
SMOOTH = 16
SECOND = (-205.0 / 72.0, 8.0 / 5.0, -1.0 / 5.0, 8.0 / 315.0, -1.0 / 560.0)
FIRST = (4.0 / 5.0, -1.0 / 5.0, 4.0 / 105.0, -1.0 / 280.0)
ALL = ("shots", "xline", "inline")
COLS = 8
GROUP = 8
VMEM_BYTES = 8 * 1024 * 1024
F32 = jnp.float32
BF16 = jnp.bfloat16


class Plan:
    def __init__(self, mesh):
        self.shots = mesh.shape["shots"]
        self.nx = mesh.shape["xline"]
        self.nq = self.nx // 2

    def index(self, s, q, y, c):
        return (s * self.nx + 2 * q + y) * 2 + c

    def perm(self, partner):
        pairs = []
        for s in range(self.shots):
            for q in range(self.nq):
                for y in range(2):
                    for c in range(2):
                        t = partner(q, y, c)
                        dst = self.index(s ^ 1, q, y, c) if t is None else self.index(s, *t)
                        pairs.append((self.index(s, q, y, c), dst))
        return pairs

    def swap(self):
        return self.perm(lambda q, y, c: None if y == c else (q, c, y))

    def z(self):
        def partner(q, y, c):
            other = q + 1 if c == 1 else q - 1
            return (other, y, 1 - c) if 0 <= other < self.nq else None

        return self.perm(partner)

    def core(self):
        return self.perm(lambda q, y, c: (q, y, 1 - c))

    def y(self):
        return self.perm(lambda q, y, c: (q, 1 - y, c))

    def flip(self, bit):
        return self.perm(lambda q, y, c: (q ^ bit, y, c) if (q ^ bit) < self.nq else None)

    def spread(self, shift):
        return self.perm(lambda q, y, c: ((q + shift) % self.nq, c, y))


def send(value, pairs):
    return lax.ppermute(value, ALL, pairs)


def depth_matrix(n):
    m = np.zeros((n, 2 * n), np.float32)
    for k in range(1, 5):
        for j in range(n):
            for i, sign in ((j + k, 1.0), (j - k, -1.0)):
                if 0 <= i < n:
                    m[i, j] = round(SECOND[k] * 5040)
                    m[i, n + j] = sign * round(FIRST[k - 1] * 840)
    return m


def stencil_matrix(rows, cols):
    own = (rows + 8) * cols
    m = np.zeros((3, rows, cols, own + rows * 8), np.float32)
    for i in range(rows):
        for x in range(cols):
            for k in range(1, 5):
                total = round(SECOND[k] * 5040)
                slope = round(FIRST[k - 1] * 840)
                for sign in (1, -1):
                    at = (i + 4 + sign * k) * cols + x
                    m[0, i, x, at] += total
                    m[1, i, x, at] += sign * slope
                    to = x + sign * k
                    if to < 0:
                        at = own + i * 4 + to + 4
                    elif to >= cols:
                        at = own + rows * 4 + i * 4 + to - cols
                    else:
                        at = (i + 4) * cols + to
                    m[0, i, x, at] += total
                    m[2, i, x, at] += sign * slope
    return m.reshape(3 * rows * cols, own + rows * 8)


def split(value):
    high = value.astype(BF16)
    return high, (value - high.astype(F32)).astype(BF16)


def mm(a, b):
    return jnp.dot(a, b, preferred_element_type=F32)


def differences(flags, cur, zm, cm, ym, near, deep):
    depth = cur.shape[1]
    size = GROUP * COLS
    own = split(cur[...])
    along = mm(jnp.concatenate(own, axis=1), deep[...])
    edge = ym[...]
    top = split(jnp.where(flags[1] == 1, edge, 0.0))
    bottom = split(jnp.where(flags[1] == 0, edge, 0.0))
    from_z, from_c = split(zm[...]), split(cm[...])
    ext = [jnp.concatenate(parts, axis=0) for parts in zip(top, own, bottom)]
    for n in range(cur.shape[0] // size):
        here = slice(n * size, n * size + size)
        sides = slice(n * GROUP * 4, n * GROUP * 4 + GROUP * 4)
        rhs = []
        for p in range(2):
            rhs += [ext[p][n * size : n * size + size + 8 * COLS], from_z[p][sides], from_c[p][sides]]
        out = mm(near[...], jnp.concatenate(rhs, axis=0))
        yield (here, out[0:size], along[here, 0:depth], out[size : 2 * size], out[2 * size :],
               along[here, depth:])


def halves(value):
    rows, depth = value.shape
    pairs = value.reshape(rows // (2 * COLS), 2, COLS, depth)
    a, b = pairs[:, 0], pairs[:, 1]
    low = lax.broadcasted_iota(jnp.int32, a.shape, 1) < 4
    first = jnp.where(low, a, pltpu.roll(b, 4, axis=1))
    last = jnp.where(low, pltpu.roll(a, 4, axis=1), b)
    return first.reshape(rows // 2, depth), last.reshape(rows // 2, depth)


def rims(flags, new, zo, co, yo):
    first, last = halves(new[...])
    zo[...] = jnp.where(flags[0] == 0, first, last)
    co[...] = jnp.where(flags[0] == 0, last, first)
    size = new.shape[0]
    yo[...] = jnp.where(flags[1] == 0, new[size - 4 * COLS :], new[0 : 4 * COLS])


def settle_kernel(rim_count, flags, a, b, recv_a, recv_b, a_out, b_out, *outs):
    keep = flags[0] == flags[1]
    for n, (own, recv, out) in enumerate(((a, recv_a, a_out), (b, recv_b, b_out))):
        out[...] = jnp.where(keep, own[...], recv[...])
        if n < rim_count:
            rims(flags, out, *(ref.at[n] for ref in outs))


def settle_one(with_rims, flags, own, recv, out, *outs):
    out[...] = jnp.where(flags[0] == flags[1], own[...], recv[...])
    if with_rims:
        rims(flags, out, *outs)


def model_kernel(flags, lr, zm, cm, ym, near, deep, vel, k0, ki, kx, kz):
    for here, spare, spare_z, di, dx, dz in differences(flags, lr, zm.at[0], cm.at[0], ym.at[0], near, deep):
        v = vel[here]
        square = v * v
        k0[here] = square * (1.0 / 5040)
        scaled = square * (1.0 / (840 * 840))
        ki[here] = scaled * di
        kx[here] = scaled * dx
        kz[here] = scaled * dz


def advance(flags, cur, prev, k0, ki, kx, kz, zm, cm, ym, near, deep, inj, finish):
    for here, sums, sums_z, di, dx, dz in differences(flags, cur, zm, cm, ym, near, deep):
        center = cur[here]
        change = k0[here] * ((sums + sums_z) + (3.0 * SECOND[0] * 5040) * center)
        change = change - (ki[here] * di + kx[here] * dx + kz[here] * dz) + inj[here]
        finish(here, (center - prev[here]) + (center + change), change)


def forward_kernel(step, flags, cur, prev, k0, ki, kx, kz, zm, cm, ym, near, deep, srow, sz, wave,
                   new, change_out, zo, co, yo):
    size, depth = cur.shape
    n = srow.shape[1]
    spot = lax.broadcasted_iota(jnp.int32, (size, n), 0) == srow[...]
    spot = spot.astype(F32).astype(BF16)
    high, low = split(jnp.where(
        lax.broadcasted_iota(jnp.int32, (n, depth), 1) == sz[...], wave[:, step : step + 1], 0.0))
    inj = mm(spot, high) + mm(spot, low)

    def finish(here, value, change):
        new[here] = value
        change_out[here] = change

    advance(flags, cur, prev, k0, ki, kx, kz, zm, cm, ym, near, deep, inj, finish)
    rims(flags, new, zo, co, yo)


def merge_kernel(stage, flags, mine, got, out):
    n = mine.shape[0]
    bit = flags[4 + stage]
    out[pl.ds(bit * n, n)] = mine[...]
    out[pl.ds((1 - bit) * n, n)] = got[...]


def lists_kernel(flags, lists, spot, pick, at, obs):
    size, n = spot.shape
    depth = at.shape[1]
    steps = obs.shape[1]
    sub = flags[2]
    cell = lists[sub, steps : steps + 1, :]
    along = jnp.floor((cell + 0.5) * (1.0 / depth))
    same = lax.broadcasted_iota(jnp.int32, (n, n), 0) == lax.broadcasted_iota(jnp.int32, (n, n), 1)

    def column(row):
        return jnp.sum(jnp.where(same, row, 0.0), axis=1, keepdims=True).astype(jnp.int32)

    hot = lax.broadcasted_iota(jnp.int32, (size, n), 0) == along.astype(jnp.int32)
    spot[...] = hot.astype(F32).astype(BF16)
    hot = lax.broadcasted_iota(jnp.int32, (n, size), 1) == column(along)
    pick[...] = hot.astype(F32).astype(BF16)
    hot = lax.broadcasted_iota(jnp.int32, (n, depth), 1) == column(cell - along * depth)
    at[...] = hot.astype(F32)
    subs = lists.shape[0]
    chosen = lax.broadcasted_iota(jnp.int32, (CAP, n), 1) == (
        sub * CAP + lax.broadcasted_iota(jnp.int32, (CAP, n), 0))
    chosen = chosen.astype(F32).astype(BF16)
    traces = lists[:, 0:steps, :].reshape(subs * steps, n)
    high, mid = split(traces)
    low = (traces - high.astype(F32) - mid.astype(F32)).astype(BF16)
    sent = sum(
        lax.dot_general(chosen, part, (((1,), (1,)), ((), ())), preferred_element_type=F32)
        for part in (low, mid, high))
    for s in range(subs):
        obs[s * CAP : s * CAP + CAP, :] = sent[:, s * steps : s * steps + steps]


def adjoint_kernel(t, first, last, flags, cur, prev, k0, ki, kx, kz, zm, cm, ym, near, deep, pnext,
                   change_in, spot, pick, at, obs, *rest):
    rest = list(rest)
    image = None if first else rest.pop(0)
    vel, recv = (rest.pop(0), rest.pop(0)) if last else (None, None)
    new, image_out, *outs = rest
    high, low = split(pnext[...])
    seen = at[...] * (mm(pick[...], high) + mm(pick[...], low))
    residual = jnp.sum(seen, axis=1, keepdims=True) - obs[:, t : t + 1]
    high, low = split(at[...] * residual)
    inj = mm(spot[...], high) + mm(spot[...], low)
    scale = 2.0 / obs.shape[1]
    raw = []

    def finish(here, value, change):
        new[here] = value
        total = value * change_in[here]
        if not first:
            total = total + image[here]
        if last:
            raw.append(total * scale / vel[here])
        else:
            image_out[here] = total

    advance(flags, cur, prev, k0, ki, kx, kz, zm, cm, ym, near, deep, inj, finish)
    if not last:
        rims(flags, new, *outs)
        return
    raw = jnp.concatenate(raw, axis=0)
    parts, height, lanes = image_out.shape
    chunk = cur.shape[1] // parts
    for n in range(parts):
        image_out[n] = jnp.concatenate(
            [raw[g * height : g * height + height, n * chunk : n * chunk + chunk]
             for g in range(lanes // chunk)], axis=1)
    outs[0][...] = jnp.where(flags[0] == flags[1], cur[...], recv[...])


def pair_kernel(flags, parts, mine, other):
    for n in range(mine.shape[0]):
        mine[n] = parts[2 * n + flags[0]]
        other[n] = parts[2 * n + 1 - flags[0]]


def join_kernel(flags, mine, got, *outs):
    count = len(outs)
    for s, out in enumerate(outs):
        to = flags[3] + s
        to = jnp.where(to >= count, to - count, to)
        a, b = mine[to], got[to]
        out[0] = jnp.where(flags[0] == 0, a, b)
        out[1] = jnp.where(flags[0] == 0, b, a)


def filter_kernel(flags, *refs):
    pieces, out = refs[:-1], refs[-1]
    height, lanes = pieces[0].shape[1:]
    chunk, rows, full = out.shape
    groups = lanes // chunk
    q = flags[3]
    shape = (full, full)
    y = lax.broadcasted_iota(jnp.int32, shape, 1)
    at = lax.broadcasted_iota(jnp.int32, shape, 0)
    within = jnp.bitwise_and(at, 2 * COLS - 1)
    place = q * (2 * COLS) - (at - within)
    place = jnp.where(place < 0, place + full, place) + within
    weights = jnp.exp(jnp.abs(y - place).astype(F32) * (-1.0 / SMOOTH))
    weights = split(weights / jnp.sum(weights, axis=0, keepdims=True))
    for n in range(height // COLS):
        here = slice(n * COLS, n * COLS + COLS)
        lines = jnp.concatenate([piece[b, here, :] for piece in pieces for b in range(2)], axis=0)
        high, low = split(lines.T)
        done = mm(high, weights[0]) + mm(low, weights[0]) + mm(high, weights[1])
        for g in range(groups):
            out[:, g * (rows // groups) + n, :] = done[g * chunk : g * chunk + chunk]


def shaped(*shape):
    return jax.ShapeDtypeStruct(shape, F32)


def call(kernel, name, outs, *args):
    specs = [pl.BlockSpec(memory_space=pltpu.SMEM)]
    specs += [pl.BlockSpec(memory_space=pltpu.VMEM)] * (len(args) - 1)
    return pl.pallas_call(
        kernel,
        name=name,
        out_shape=outs,
        in_specs=specs,
        out_specs=[pl.BlockSpec(memory_space=pltpu.VMEM)] * len(outs),
        compiler_params=pltpu.CompilerParams(vmem_limit_bytes=VMEM_BYTES),
        cost_estimate=pl.CostEstimate(flops=5_000_000, bytes_accessed=2_000_000, transcendentals=0),
    )(*args)


def per_device(plan, fwd_now, fwd_before, adj_now, adj_before, velocity, log_density, observed,
               rec_cells, rec_counts, src_cell, wavelet):
    rows, cols, depth = fwd_now.shape
    size = rows * cols
    steps = wavelet.shape[0]
    nx, nq = plan.nx, plan.nq
    subs = 2 * nx
    xline, c = lax.axis_index("xline"), lax.axis_index("inline")
    q, y = xline // 2, xline % 2
    keep = y == c
    z_perm, c_perm, y_perm, swap_perm = plan.z(), plan.core(), plan.y(), plan.swap()
    stages = [(c_perm, c), (y_perm, y)]
    stages += [(plan.flip(1 << b), (q >> b) & 1) for b in range((nq - 1).bit_length())]
    sub = (2 * q + c) * 2 + y
    flags = jnp.stack([c, y, sub, q] + [bit for pairs, bit in stages]).astype(jnp.int32)
    field = shaped(size, depth)
    side, edge = (size // 2, depth), (4 * cols, depth)
    rim = [shaped(*side), shaped(*side), shaped(*edge)]

    deep = depth_matrix(depth)
    deep = jnp.asarray(np.concatenate([deep, deep]), BF16)
    near = stencil_matrix(GROUP, cols)
    own, half = near.shape[1] - GROUP * 8, GROUP * 4
    from_z = np.where(np.arange(near.shape[1]) // half == own // half, 0.0, 1.0)
    other = np.concatenate([near[:, :own], near[:, own + half :], near[:, own : own + half]], axis=1)
    inside = jnp.where(c == 0, q > 0, q < nq - 1)
    near = jnp.where(c == 0, jnp.asarray(near, F32), jnp.asarray(other, F32))
    near = jnp.where(inside, near, near * jnp.asarray(from_z, F32)[None, :]).astype(BF16)
    near = jnp.concatenate([near, near], axis=1)

    def halo(zo, co, yo):
        return send(zo, z_perm), send(co, c_perm), send(yo, y_perm)

    def after(value, *deps):
        return lax.optimization_barrier((value,) + deps)[0]

    def flat(value):
        return value.reshape(size, depth)

    log_density, fwd_now, velocity = flat(log_density), flat(fwd_now), flat(velocity)
    fwd_before, adj_now, adj_before = flat(fwd_before), flat(adj_now), flat(adj_before)
    got = [send(v, swap_perm) for v in (log_density, fwd_now, velocity, fwd_before)]
    density, p_now, *out = call(
        functools.partial(settle_kernel, 2), "settle",
        [field, field] + [shaped(2, *r.shape) for r in rim], flags, log_density, fwd_now, *got[:2])
    zm, cm, ym = halo(*out)
    vel, p_before = call(functools.partial(settle_kernel, 0), "settle_model", [field, field],
                         flags, velocity, fwd_before, *got[2:])
    model = call(model_kernel, "model", [field] * 4, flags, density, zm, cm, ym, near, deep, vel)
    halos = (zm[1], cm[1], ym[1])

    plane = nx * cols * depth
    src_i = src_cell // plane - y * rows
    src_x = src_cell // depth % (nx * cols) - (2 * q + c) * cols
    ok = (src_i >= 0) & (src_i < rows) & (src_x >= 0) & (src_x < cols)
    srow = jnp.where(ok, src_i * cols + src_x, -1)[None, :]
    sz = (src_cell % depth)[:, None]
    wave = wavelet.T

    live = jnp.arange(CAP)[None, :] < rec_counts[0][:, None]
    cells = jnp.where(live.reshape(-1), rec_cells[0], -1)
    lists = jnp.concatenate([observed, cells[None, :].astype(F32)], axis=0)[None]
    share = -(-len(stages) // (steps - 2))

    states, changes = [], []
    for t in range(steps):
        p_next, change, *out = call(
            functools.partial(forward_kernel, t), "forward", [field, field] + rim,
            flags, p_now, p_before, *model, *halos, near, deep, srow, sz, wave)
        if t < steps - 1:
            halos = halo(*out)
        for n in range(t * share, min(t * share + share, len(stages))):
            moved = send(after(lists, out[0]) if n else lists, stages[n][0])
            lists, = call(functools.partial(merge_kernel, n), "merge",
                          [shaped(2 * lists.shape[0], *lists.shape[1:])], flags, lists, moved)
        if t == 1:
            got_now = send(after(adj_now, out[0]), swap_perm)
        if t == 3:
            got_before = send(after(adj_before, out[0]), swap_perm)
            u_now, *out = call(functools.partial(settle_one, True), "settle_adjoint", [field] + rim,
                               flags, adj_now, after(got_now, out[0]))
            u_rim = out
        if t == 4:
            u_halos = halo(*(after(r, out[0]) for r in u_rim))
        if t == 5:
            u_before, = call(functools.partial(settle_one, False), "settle_before", [field],
                             flags, adj_before, after(got_before, out[0]))
        p_before, p_now = p_now, p_next
        states.append(p_next)
        changes.append(change)

    slots = subs * CAP
    receivers = call(
        lists_kernel, "lists",
        [jax.ShapeDtypeStruct((size, slots), BF16), jax.ShapeDtypeStruct((slots, size), BF16),
         shaped(slots, depth), shaped(slots, steps)], flags, lists)

    halos = u_halos
    image = ()
    chunk = depth // nx
    packed = shaped(nx, size * chunk // 128, 128)
    for j in range(steps):
        t = steps - 1 - j
        last = j == steps - 1
        args = [flags, u_now, u_before, *model, *halos, near, deep, states[t], changes[t],
                *receivers, *image]
        outs = [field, field] + rim
        if last:
            args += [vel, send(u_now, swap_perm)]
            outs = [field, packed, field]
        u_before = u_now
        u_now, *outs = call(functools.partial(adjoint_kernel, t, j == 0, last), "adjoint", outs, *args)
        image = outs[:1]
        if not last:
            halos = halo(*outs[1:])
    raw, adj_prev = outs

    half = shaped(nq, *packed.shape[1:])
    mine, other = call(pair_kernel, "pair", [half, half], flags, raw)
    piece = shaped(2, *packed.shape[1:])
    pieces = call(join_kernel, "join", [piece] * nq, flags, mine, send(other, c_perm))
    got = send(after(u_now, pieces[0]), swap_perm)
    pieces = [send(value, plan.spread(s)) for s, value in enumerate(pieces)]
    gradient, = call(filter_kernel, "filter", [shaped(chunk, rows, nx * cols)], flags, *pieces)
    adj_out = jnp.where(keep, u_now, got)
    block = (rows, cols, depth)
    return gradient, adj_out.reshape(block), adj_prev.reshape(block)


def solution(mesh):
    field = P(("shots", "inline"), "xline", None)
    model = P("inline", "xline", None)
    lists = P(("xline", "inline"), None)
    return jax.shard_map(
        functools.partial(per_device, Plan(mesh)),
        mesh=mesh,
        in_specs=(field, field, field, field, model, model, P("shots", ("xline", "inline")),
                  lists, lists, P("shots"), P("shots", None)),
        out_specs=(P(("shots", "xline"), "inline", None), field, field),
        check_vma=False,
    )
```

```python
import functools

import jax
import jax.numpy as jnp
import numpy as np
from jax import lax
from jax.experimental import pallas as pl
from jax.experimental.pallas import tpu as pltpu
from jax.sharding import PartitionSpec as P

CAP = 8
SMOOTH = 16
SECOND = (-205.0 / 72.0, 8.0 / 5.0, -1.0 / 5.0, 8.0 / 315.0, -1.0 / 560.0)
FIRST = (4.0 / 5.0, -1.0 / 5.0, 4.0 / 105.0, -1.0 / 280.0)
ALL = ("shots", "xline", "inline")
COLS = 8
GROUP = 8
VMEM_BYTES = 8 * 1024 * 1024
F32 = jnp.float32
BF16 = jnp.bfloat16


class Plan:
    def __init__(self, mesh):
        self.shots = mesh.shape["shots"]
        self.nx = mesh.shape["xline"]
        self.nq = self.nx // 2

    def index(self, s, q, y, c):
        return (s * self.nx + 2 * q + y) * 2 + c

    def perm(self, partner):
        pairs = []
        for s in range(self.shots):
            for q in range(self.nq):
                for y in range(2):
                    for c in range(2):
                        t = partner(q, y, c)
                        dst = self.index(s ^ 1, q, y, c) if t is None else self.index(s, *t)
                        pairs.append((self.index(s, q, y, c), dst))
        return pairs

    def swap(self):
        return self.perm(lambda q, y, c: None if y == c else (q, c, y))

    def z(self):
        def partner(q, y, c):
            other = q + 1 if c == 1 else q - 1
            return (other, y, 1 - c) if 0 <= other < self.nq else None

        return self.perm(partner)

    def core(self):
        return self.perm(lambda q, y, c: (q, y, 1 - c))

    def y(self):
        return self.perm(lambda q, y, c: (q, 1 - y, c))

    def flip(self, bit):
        return self.perm(lambda q, y, c: (q ^ bit, y, c) if (q ^ bit) < self.nq else None)

    def spread(self, shift):
        return self.perm(lambda q, y, c: ((q + shift) % self.nq, c, y))


def send(value, pairs):
    return lax.ppermute(value, ALL, pairs)


def depth_matrix(n):
    m = np.zeros((n, 2 * n), np.float32)
    for k in range(1, 5):
        for j in range(n):
            for i, sign in ((j + k, 1.0), (j - k, -1.0)):
                if 0 <= i < n:
                    m[i, j] = round(SECOND[k] * 5040)
                    m[i, n + j] = sign * round(FIRST[k - 1] * 840)
    return m


def stencil_matrix(rows, cols):
    own = (rows + 8) * cols
    m = np.zeros((3, rows, cols, own + rows * 8), np.float32)
    for i in range(rows):
        for x in range(cols):
            for k in range(1, 5):
                total = round(SECOND[k] * 5040)
                slope = round(FIRST[k - 1] * 840)
                for sign in (1, -1):
                    at = (i + 4 + sign * k) * cols + x
                    m[0, i, x, at] += total
                    m[1, i, x, at] += sign * slope
                    to = x + sign * k
                    if to < 0:
                        at = own + i * 4 + to + 4
                    elif to >= cols:
                        at = own + rows * 4 + i * 4 + to - cols
                    else:
                        at = (i + 4) * cols + to
                    m[0, i, x, at] += total
                    m[2, i, x, at] += sign * slope
    return m.reshape(3 * rows * cols, own + rows * 8)


def split(value):
    high = value.astype(BF16)
    return high, (value - high.astype(F32)).astype(BF16)


def mm(a, b):
    return jnp.dot(a, b, preferred_element_type=F32)


def inner_differences(cur, near, deep):
    depth = cur.shape[1]
    size = GROUP * COLS
    own = split(cur[...])
    along = mm(jnp.concatenate(own, axis=1), deep[...])
    blank = jnp.zeros((4 * COLS, depth), BF16)
    ext = [jnp.concatenate([blank, part, blank], axis=0) for part in own]
    for n in range(cur.shape[0] // size):
        here = slice(n * size, n * size + size)
        rhs = [part[n * size : n * size + size + 8 * COLS] for part in ext]
        out = mm(near[...], jnp.concatenate(rhs, axis=0))
        yield (here, out[0:size], along[here, 0:depth], out[size : 2 * size], out[2 * size :],
               along[here, depth:])


def side_differences(rows, zm, cm, side):
    size = GROUP * COLS
    from_z, from_c = split(zm[...]), split(cm[...])
    for n in range(rows // size):
        sides = slice(n * GROUP * 4, n * GROUP * 4 + GROUP * 4)
        rhs = [part[p][sides] for p in range(2) for part in (from_z, from_c)]
        out = mm(side[...], jnp.concatenate(rhs, axis=0))
        yield slice(n * size, n * size + size), out[0:size], out[size:]


def edge_differences(flags, rows, ym, edge):
    size = GROUP * COLS
    out = mm(edge[...], jnp.concatenate(split(ym[...]), axis=0))
    start = jnp.where(flags[1] == 1, 0, rows - size)
    return pl.ds(pl.multiple_of(start, size), size), out[0:size], out[size:]


def halves(value):
    rows, depth = value.shape
    pairs = value.reshape(rows // (2 * COLS), 2, COLS, depth)
    a, b = pairs[:, 0], pairs[:, 1]
    low = lax.broadcasted_iota(jnp.int32, a.shape, 1) < 4
    first = jnp.where(low, a, pltpu.roll(b, 4, axis=1))
    last = jnp.where(low, pltpu.roll(a, 4, axis=1), b)
    return first.reshape(rows // 2, depth), last.reshape(rows // 2, depth)


def rims(flags, new, zo, co, yo):
    first, last = halves(new[...])
    zo[...] = jnp.where(flags[0] == 0, first, last)
    co[...] = jnp.where(flags[0] == 0, last, first)
    size = new.shape[0]
    yo[...] = jnp.where(flags[1] == 0, new[size - 4 * COLS :], new[0 : 4 * COLS])


def settle_kernel(rim_count, flags, a, b, recv_a, recv_b, a_out, b_out, *outs):
    keep = flags[0] == flags[1]
    for n, (own, recv, out) in enumerate(((a, recv_a, a_out), (b, recv_b, b_out))):
        out[...] = jnp.where(keep, own[...], recv[...])
        if n < rim_count:
            rims(flags, out, *(ref.at[n] for ref in outs))


def settle_one(with_rims, flags, own, recv, out, *outs):
    out[...] = jnp.where(flags[0] == flags[1], own[...], recv[...])
    if with_rims:
        rims(flags, out, *outs)


def model_kernel(flags, lr, zm, cm, ym, near, deep, side, edge, vel, k0, ki, kx, kz):
    for here, spare, spare_z, di, dx, dz in inner_differences(lr, near, deep):
        ki[here], kx[here], kz[here] = di, dx, dz
    for here, spare, dx in side_differences(lr.shape[0], zm.at[0], cm.at[0], side):
        kx[here] += dx
    here, spare, di = edge_differences(flags, lr.shape[0], ym.at[0], edge)
    ki[here] += di
    square = vel[...] * vel[...]
    k0[...] = square * (1.0 / 5040)
    scaled = square * (1.0 / (840 * 840))
    for factor in (ki, kx, kz):
        factor[...] = scaled * factor[...]


def inner(cur, prev, k0, ki, kx, kz, near, deep, inj, out):
    for here, sums, sums_z, di, dx, dz in inner_differences(cur, near, deep):
        center = cur[here]
        change = k0[here] * ((sums + sums_z) + (3.0 * SECOND[0] * 5040) * center)
        change = change - (ki[here] * di + kx[here] * dx + kz[here] * dz) + inj[here]
        out[here] = (center - prev[here]) + (center + change)


def outer(flags, part, k0, ki, kx, zm, cm, ym, side, edge, new):
    rows = part.shape[0]
    for here, sums, dx in side_differences(rows, zm, cm, side):
        new[here] = part[here] + (k0[here] * sums - kx[here] * dx)
    here, sums, di = edge_differences(flags, rows, ym, edge)
    new[here] += k0[here] * sums - ki[here] * di


def forward_inner_kernel(step, flags, cur, prev, k0, ki, kx, kz, near, deep, srow, sz, wave,
                         *rest):
    size, depth = cur.shape
    n = srow.shape[1]
    spot = lax.broadcasted_iota(jnp.int32, (size, n), 0) == srow[...]
    spot = spot.astype(F32).astype(BF16)
    high, low = split(jnp.where(
        lax.broadcasted_iota(jnp.int32, (n, depth), 1) == sz[...], wave[:, step : step + 1], 0.0))
    inj = mm(spot, high) + mm(spot, low)
    if step > 0:
        before, part, change = rest
        change[...] = (cur[...] - prev[...]) - (prev[...] - before[...])
    else:
        part, = rest
    inner(cur, prev, k0, ki, kx, kz, near, deep, inj, part)


def outer_kernel(stage, flags, part, k0, ki, kx, zm, cm, ym, side, edge, *rest):
    if stage is None:
        new, zo, co, yo = rest
    else:
        mine, got, new, zo, co, yo, lists = rest
        n = mine.shape[0]
        bit = flags[4 + stage]
        lists[pl.ds(bit * n, n)] = mine[...]
        lists[pl.ds((1 - bit) * n, n)] = got[...]
    outer(flags, part, k0, ki, kx, zm, cm, ym, side, edge, new)
    rims(flags, new, zo, co, yo)


def lists_kernel(flags, lists, spot, pick, at, obs):
    size, n = spot.shape
    depth = at.shape[1]
    steps = obs.shape[1]
    sub = flags[2]
    cell = lists[sub, steps : steps + 1, :]
    along = jnp.floor((cell + 0.5) * (1.0 / depth))
    same = lax.broadcasted_iota(jnp.int32, (n, n), 0) == lax.broadcasted_iota(jnp.int32, (n, n), 1)

    def column(row):
        return jnp.sum(jnp.where(same, row, 0.0), axis=1, keepdims=True).astype(jnp.int32)

    hot = lax.broadcasted_iota(jnp.int32, (size, n), 0) == along.astype(jnp.int32)
    spot[...] = hot.astype(F32).astype(BF16)
    hot = lax.broadcasted_iota(jnp.int32, (n, size), 1) == column(along)
    pick[...] = hot.astype(F32).astype(BF16)
    hot = lax.broadcasted_iota(jnp.int32, (n, depth), 1) == column(cell - along * depth)
    at[...] = hot.astype(F32)
    subs = lists.shape[0]
    chosen = lax.broadcasted_iota(jnp.int32, (CAP, n), 1) == (
        sub * CAP + lax.broadcasted_iota(jnp.int32, (CAP, n), 0))
    chosen = chosen.astype(F32).astype(BF16)
    traces = lists[:, 0:steps, :].reshape(subs * steps, n)
    high, mid = split(traces)
    low = (traces - high.astype(F32) - mid.astype(F32)).astype(BF16)
    sent = sum(
        lax.dot_general(chosen, part, (((1,), (1,)), ((), ())), preferred_element_type=F32)
        for part in (low, mid, high))
    for s in range(subs):
        obs[s * CAP : s * CAP + CAP, :] = sent[:, s * steps : s * steps + steps]


def adjoint_inner_kernel(t, flags, cur, prev, k0, ki, kx, kz, near, deep, seen_state, spot, pick,
                         at, obs, *rest):
    if len(rest) == 1:
        part, = rest
    elif len(rest) == 4:
        change, image, part, image_out = rest
        image_out[...] = cur[...] * change[...] + image[...]
    else:
        now, mid, before, part, image_out = rest
        image_out[...] = cur[...] * ((now[...] - mid[...]) - (mid[...] - before[...]))
    high, low = split(seen_state[...])
    seen = at[...] * (mm(pick[...], high) + mm(pick[...], low))
    residual = jnp.sum(seen, axis=1, keepdims=True) - obs[:, t : t + 1]
    high, low = split(at[...] * residual)
    inj = mm(spot[...], high) + mm(spot[...], low)
    inner(cur, prev, k0, ki, kx, kz, near, deep, inj, part)


def last_kernel(scale, flags, part, k0, ki, kx, zm, cm, ym, side, edge, image, change, vel, prev,
                got, new, mine, other, prev_out):
    outer(flags, part, k0, ki, kx, zm, cm, ym, side, edge, new)
    raw = (image[...] + new[...] * change[...]) * scale / vel[...]
    count, height, lanes = mine.shape
    chunk = raw.shape[1] // (2 * count)
    for n in range(count):
        even, odd = (
            jnp.concatenate(
                [raw[g * height : g * height + height, m * chunk : m * chunk + chunk]
                 for g in range(lanes // chunk)], axis=1)
            for m in (2 * n, 2 * n + 1))
        mine[n] = jnp.where(flags[0] == 0, even, odd)
        other[n] = jnp.where(flags[0] == 0, odd, even)
    prev_out[...] = jnp.where(flags[0] == flags[1], prev[...], got[...])


def join_kernel(flags, mine, got, *outs):
    count = len(outs)
    for s, out in enumerate(outs):
        to = flags[3] + s
        to = jnp.where(to >= count, to - count, to)
        a, b = mine[to], got[to]
        out[0] = jnp.where(flags[0] == 0, a, b)
        out[1] = jnp.where(flags[0] == 0, b, a)


def filter_kernel(flags, *refs):
    *pieces, own, got, out, state = refs
    state[...] = jnp.where(flags[0] == flags[1], own[...], got[...])
    height, lanes = pieces[0].shape[1:]
    chunk, rows, full = out.shape
    groups = lanes // chunk
    q = flags[3]
    shape = (full, full)
    y = lax.broadcasted_iota(jnp.int32, shape, 1)
    at = lax.broadcasted_iota(jnp.int32, shape, 0)
    within = jnp.bitwise_and(at, 2 * COLS - 1)
    place = q * (2 * COLS) - (at - within)
    place = jnp.where(place < 0, place + full, place) + within
    weights = jnp.exp(jnp.abs(y - place).astype(F32) * (-1.0 / SMOOTH))
    weights = split(weights / jnp.sum(weights, axis=0, keepdims=True))
    for n in range(height // COLS):
        here = slice(n * COLS, n * COLS + COLS)
        lines = jnp.concatenate([piece[b, here, :] for piece in pieces for b in range(2)], axis=0)
        high, low = split(lines.T)
        done = mm(high, weights[0]) + mm(low, weights[0]) + mm(high, weights[1])
        for g in range(groups):
            out[:, g * (rows // groups) + n, :] = done[g * chunk : g * chunk + chunk]


def shaped(*shape):
    return jax.ShapeDtypeStruct(shape, F32)


def call(kernel, name, outs, *args):
    specs = [pl.BlockSpec(memory_space=pltpu.SMEM)]
    specs += [pl.BlockSpec(memory_space=pltpu.VMEM)] * (len(args) - 1)
    return pl.pallas_call(
        kernel,
        name=name,
        out_shape=outs,
        in_specs=specs,
        out_specs=[pl.BlockSpec(memory_space=pltpu.VMEM)] * len(outs),
        compiler_params=pltpu.CompilerParams(vmem_limit_bytes=VMEM_BYTES),
        cost_estimate=pl.CostEstimate(flops=5_000_000, bytes_accessed=2_000_000, transcendentals=0),
    )(*args)


def per_device(plan, fwd_now, fwd_before, adj_now, adj_before, velocity, log_density, observed,
               rec_cells, rec_counts, src_cell, wavelet):
    rows, cols, depth = fwd_now.shape
    size = rows * cols
    steps = wavelet.shape[0]
    nx, nq = plan.nx, plan.nq
    subs = 2 * nx
    xline, c = lax.axis_index("xline"), lax.axis_index("inline")
    q, y = xline // 2, xline % 2
    keep = y == c
    z_perm, c_perm, y_perm, swap_perm = plan.z(), plan.core(), plan.y(), plan.swap()
    stages = [(c_perm, c), (y_perm, y)]
    stages += [(plan.flip(1 << b), (q >> b) & 1) for b in range((nq - 1).bit_length())]
    sub = (2 * q + c) * 2 + y
    flags = jnp.stack([c, y, sub, q] + [bit for pairs, bit in stages]).astype(jnp.int32)
    field = shaped(size, depth)
    side, edge = (size // 2, depth), (4 * cols, depth)
    rim = [shaped(*side), shaped(*side), shaped(*edge)]

    deep = depth_matrix(depth)
    deep = jnp.asarray(np.concatenate([deep, deep]), BF16)
    near = stencil_matrix(GROUP, cols)
    group, own, half = GROUP * cols, near.shape[1] - GROUP * 8, GROUP * 4
    side = np.concatenate([near[:group, own:], near[2 * group :, own:]])
    other = np.concatenate([side[:, half:], side[:, :half]], axis=1)
    from_z = np.arange(2 * half) < half
    inside = jnp.where(c == 0, q > 0, q < nq - 1)
    side = jnp.where(c == 0, jnp.asarray(side, F32), jnp.asarray(other, F32))
    side = jnp.where(from_z[None, :] & ~inside, 0.0, side).astype(BF16)
    side = jnp.concatenate([side, side], axis=1)
    edge = jnp.where(y == 1, jnp.asarray(near[: 2 * group, : 4 * cols], F32),
                     jnp.asarray(near[: 2 * group, own - 4 * cols : own], F32)).astype(BF16)
    edge = jnp.concatenate([edge, edge], axis=1)
    near = jnp.asarray(np.concatenate([near[:, :own], near[:, :own]], axis=1), BF16)

    def halo(zo, co, yo):
        return send(zo, z_perm), send(co, c_perm), send(yo, y_perm)

    def after(value, *deps):
        return lax.optimization_barrier((value,) + deps)[0]

    def flat(value):
        return value.reshape(size, depth)

    log_density, fwd_now, velocity = flat(log_density), flat(fwd_now), flat(velocity)
    fwd_before, adj_now, adj_before = flat(fwd_before), flat(adj_now), flat(adj_before)
    got = [send(v, swap_perm) for v in (log_density, fwd_now)]
    density, p_now, *out = call(
        functools.partial(settle_kernel, 2), "settle",
        [field, field] + [shaped(2, *r.shape) for r in rim], flags, log_density, fwd_now, *got)
    zm, cm, ym = halo(*out)
    got = [send(after(v, out[0]), swap_perm) for v in (velocity, fwd_before)]
    vel, p_before = call(functools.partial(settle_kernel, 0), "settle_model", [field, field],
                         flags, velocity, fwd_before, *got)
    k0, ki, kx, kz = call(model_kernel, "model", [field] * 4, flags, density, zm, cm, ym, near,
                          deep, side, edge, vel)
    halos = (zm[1], cm[1], ym[1])

    plane = nx * cols * depth
    src_i = src_cell // plane - y * rows
    src_x = src_cell // depth % (nx * cols) - (2 * q + c) * cols
    ok = (src_i >= 0) & (src_i < rows) & (src_x >= 0) & (src_x < cols)
    srow = jnp.where(ok, src_i * cols + src_x, -1)[None, :]
    sz = (src_cell % depth)[:, None]
    wave = wavelet.T

    live = jnp.arange(CAP)[None, :] < rec_counts[0][:, None]
    cells = jnp.where(live.reshape(-1), rec_cells[0], -1)
    lists = jnp.concatenate([observed, cells[None, :].astype(F32)], axis=0)[None]

    states = [p_before, p_now]
    changes = []
    for t in range(steps):
        args = states[:-3:-1] + [k0, ki, kx, kz, near, deep, srow, sz, wave]
        outs = [field]
        if t > 0:
            args.append(states[-3])
            outs = [field, field]
        part, *change = call(functools.partial(forward_inner_kernel, t), "forward_inner", outs,
                             flags, *args)
        changes += change
        if t == 1:
            u_now, *u_rim = call(functools.partial(settle_one, True), "settle_adjoint", [field] + rim,
                                 flags, adj_now, got_now)
            part = after(part, u_now)
        if t == 3:
            u_before, = call(functools.partial(settle_one, False), "settle_before", [field],
                             flags, adj_before, got_before)
            part = after(part, u_before)
        if t == 6:
            part = after(part, *u_halos)
        args = [part, k0, ki, kx, *halos, side, edge]
        outs = [field] + rim
        stage = t if t < len(stages) else None
        if stage is not None:
            args += [lists, send(after(lists, out[0]) if t else lists, stages[t][0])]
            outs = outs + [shaped(2 * lists.shape[0], *lists.shape[1:])]
        new, zo, co, yo, *merged = call(functools.partial(outer_kernel, stage), "forward_outer", outs,
                                        flags, *args)
        out = (zo, co, yo)
        lists = merged[0] if merged else lists
        states.append(new)
        if t < steps - 1:
            halos = halo(*out)
        if t == 0:
            got_now = send(after(adj_now, zo), swap_perm)
        if t == 2:
            got_before = send(after(adj_before, zo), swap_perm)
        if t == 4:
            u_halos = halo(*(after(r, zo) for r in u_rim))

    slots = subs * CAP
    receivers = call(
        lists_kernel, "lists",
        [jax.ShapeDtypeStruct((size, slots), BF16), jax.ShapeDtypeStruct((slots, size), BF16),
         shaped(slots, depth), shaped(slots, steps)], flags, lists)

    halos = u_halos
    image = []
    chunk = depth // nx
    half = shaped(nq, size * chunk // 128, 128)
    for j in range(steps):
        t = steps - 1 - j
        args = [u_now, u_before, k0, ki, kx, kz, near, deep, states[t + 2], *receivers]
        outs = [field]
        if j > 0:
            args += [changes[t + 1], *image] if image else states[:-4:-1]
            outs = [field, field]
        part, *image = call(functools.partial(adjoint_inner_kernel, t), "adjoint_inner", outs,
                            flags, *args)
        args = [part, k0, ki, kx, *halos, side, edge]
        if j == steps - 1:
            args += [*image, changes[0], vel, u_now, send(u_now, swap_perm)]
            u_last, mine, other, adj_prev = call(
                functools.partial(last_kernel, 2.0 / steps), "last", [field, half, half, field],
                flags, *args)
            break
        u_before = u_now
        u_now, *out = call(functools.partial(outer_kernel, None), "adjoint_outer", [field] + rim,
                           flags, *args)
        halos = halo(*out)

    got = send(u_last, swap_perm)
    pieces = call(join_kernel, "join", [shaped(2, *half.shape[1:])] * nq, flags, mine,
                  send(other, c_perm))
    pieces = [send(value, plan.spread(s)) for s, value in enumerate(pieces)]
    gradient, adj_out = call(filter_kernel, "filter", [shaped(chunk, rows, nx * cols), field], flags,
                             *pieces, u_last, got)
    block = (rows, cols, depth)
    return gradient, adj_out.reshape(block), adj_prev.reshape(block)


def solution(mesh):
    field = P(("shots", "inline"), "xline", None)
    model = P("inline", "xline", None)
    lists = P(("xline", "inline"), None)
    return jax.shard_map(
        functools.partial(per_device, Plan(mesh)),
        mesh=mesh,
        in_specs=(field, field, field, field, model, model, P("shots", ("xline", "inline")),
                  lists, lists, P("shots"), P("shots", None)),
        out_specs=(P(("shots", "xline"), "inline", None), field, field),
        check_vma=False,
    )
```

```python
import functools

import jax
import jax.numpy as jnp
import numpy as np
from jax import lax
from jax.experimental import pallas as pl
from jax.experimental.pallas import tpu as pltpu
from jax.sharding import PartitionSpec as P

CAP = 8
SMOOTH = 16
SECOND = (-205.0 / 72.0, 8.0 / 5.0, -1.0 / 5.0, 8.0 / 315.0, -1.0 / 560.0)
FIRST = (4.0 / 5.0, -1.0 / 5.0, 4.0 / 105.0, -1.0 / 280.0)
ALL = ("shots", "xline", "inline")
COLS = 8
GROUP = 8
VMEM_BYTES = 8 * 1024 * 1024
F32 = jnp.float32
BF16 = jnp.bfloat16


class Plan:
    def __init__(self, mesh):
        self.shots = mesh.shape["shots"]
        self.nx = mesh.shape["xline"]
        self.nq = self.nx // 2

    def index(self, s, q, y, c):
        return (s * self.nx + 2 * q + y) * 2 + c

    def perm(self, partner):
        pairs = []
        for s in range(self.shots):
            for q in range(self.nq):
                for y in range(2):
                    for c in range(2):
                        t = partner(q, y, c)
                        dst = self.index(s ^ 1, q, y, c) if t is None else self.index(s, *t)
                        pairs.append((self.index(s, q, y, c), dst))
        return pairs

    def swap(self):
        return self.perm(lambda q, y, c: None if y == c else (q, c, y))

    def z(self):
        def partner(q, y, c):
            other = q + 1 if c == 1 else q - 1
            return (other, y, 1 - c) if 0 <= other < self.nq else None

        return self.perm(partner)

    def core(self):
        return self.perm(lambda q, y, c: (q, y, 1 - c))

    def y(self):
        return self.perm(lambda q, y, c: (q, 1 - y, c))

    def flip(self, bit):
        return self.perm(lambda q, y, c: (q ^ bit, y, c) if (q ^ bit) < self.nq else None)

    def spread(self, shift):
        return self.perm(lambda q, y, c: (q ^ shift, c, y))


def send(value, pairs):
    return lax.ppermute(value, ALL, pairs)


def depth_matrix(n):
    m = np.zeros((n, 2 * n), np.float32)
    for k in range(1, 5):
        for j in range(n):
            for i, sign in ((j + k, 1.0), (j - k, -1.0)):
                if 0 <= i < n:
                    m[i, j] = round(SECOND[k] * 5040)
                    m[i, n + j] = sign * round(FIRST[k - 1] * 840)
    return m


def stencil_matrix(rows, cols):
    own = (rows + 8) * cols
    m = np.zeros((3, rows, cols, own + rows * 8), np.float32)
    for i in range(rows):
        for x in range(cols):
            for k in range(1, 5):
                total = round(SECOND[k] * 5040)
                slope = round(FIRST[k - 1] * 840)
                for sign in (1, -1):
                    at = (i + 4 + sign * k) * cols + x
                    m[0, i, x, at] += total
                    m[1, i, x, at] += sign * slope
                    to = x + sign * k
                    if to < 0:
                        at = own + i * 4 + to + 4
                    elif to >= cols:
                        at = own + rows * 4 + i * 4 + to - cols
                    else:
                        at = (i + 4) * cols + to
                    m[0, i, x, at] += total
                    m[2, i, x, at] += sign * slope
    return m.reshape(3 * rows * cols, own + rows * 8)


def split(value):
    high = value.astype(BF16)
    return high, (value - high.astype(F32)).astype(BF16)


def mm(a, b):
    return jnp.dot(a, b, preferred_element_type=F32)


def inner_differences(cur, near, deep):
    depth = cur.shape[1]
    size = GROUP * COLS
    own = split(cur[...])
    along = mm(jnp.concatenate(own, axis=1), deep[...])
    blank = jnp.zeros((4 * COLS, depth), BF16)
    ext = [jnp.concatenate([blank, part, blank], axis=0) for part in own]
    for n in range(cur.shape[0] // size):
        here = slice(n * size, n * size + size)
        rhs = [part[n * size : n * size + size + 8 * COLS] for part in ext]
        out = mm(near[...], jnp.concatenate(rhs, axis=0))
        yield (here, out[0:size], along[here, 0:depth], out[size : 2 * size], out[2 * size :],
               along[here, depth:])


def side_differences(rows, zm, cm, side):
    size = GROUP * COLS
    from_z, from_c = split(zm[...]), split(cm[...])
    for n in range(rows // size):
        sides = slice(n * GROUP * 4, n * GROUP * 4 + GROUP * 4)
        rhs = [part[p][sides] for p in range(2) for part in (from_z, from_c)]
        out = mm(side[...], jnp.concatenate(rhs, axis=0))
        yield slice(n * size, n * size + size), out[0:size], out[size:]


def edge_differences(flags, rows, ym, edge):
    size = GROUP * COLS
    out = mm(edge[...], jnp.concatenate(split(ym[...]), axis=0))
    start = jnp.where(flags[1] == 1, 0, rows - size)
    return pl.ds(pl.multiple_of(start, size), size), out[0:size], out[size:]


def halves(value):
    rows, depth = value.shape
    pairs = value.reshape(rows // (2 * COLS), 2, COLS, depth)
    a, b = pairs[:, 0], pairs[:, 1]
    low = lax.broadcasted_iota(jnp.int32, a.shape, 1) < 4
    first = jnp.where(low, a, pltpu.roll(b, 4, axis=1))
    last = jnp.where(low, pltpu.roll(a, 4, axis=1), b)
    return first.reshape(rows // 2, depth), last.reshape(rows // 2, depth)


def rims(flags, new, zo, co, yo):
    first, last = halves(new[...])
    zo[...] = jnp.where(flags[0] == 0, first, last)
    co[...] = jnp.where(flags[0] == 0, last, first)
    size = new.shape[0]
    yo[...] = jnp.where(flags[1] == 0, new[size - 4 * COLS :], new[0 : 4 * COLS])


def load_kernel(flags, *refs):
    half = len(refs) // 2
    for source, out in zip(refs[:half], refs[half:]):
        out[...] = source[...]


def settle_kernel(flags, a, b, recv_a, recv_b, a_out, b_out, *outs):
    keep = flags[0] == flags[1]
    for n, (own, recv, out) in enumerate(((a, recv_a, a_out), (b, recv_b, b_out))):
        out[...] = jnp.where(keep, own[...], recv[...])
        rims(flags, out, *(ref.at[n] for ref in outs))


def settle_model_kernel(flags, a, b, recv, a_out, b_out):
    keep = flags[0] == flags[1]
    a_out[...] = jnp.where(keep, a[...], recv[0])
    b_out[...] = jnp.where(keep, b[...], recv[1])


def settle_one(with_rims, flags, own, recv, out, *outs):
    out[...] = jnp.where(flags[0] == flags[1], own[...], recv[...])
    if with_rims:
        rims(flags, out, *outs)


def model_kernel(flags, lr, zm, cm, ym, near, deep, side, edge, vel, k0, ki, kx, kz):
    for here, spare, spare_z, di, dx, dz in inner_differences(lr, near, deep):
        ki[here], kx[here], kz[here] = di, dx, dz
    for here, spare, dx in side_differences(lr.shape[0], zm.at[0], cm.at[0], side):
        kx[here] += dx
    here, spare, di = edge_differences(flags, lr.shape[0], ym.at[0], edge)
    ki[here] += di
    square = vel[...] * vel[...]
    k0[...] = square * (1.0 / 5040)
    scaled = square * (1.0 / (840 * 840))
    for factor in (ki, kx, kz):
        factor[...] = scaled * factor[...]


def inner(cur, prev, k0, ki, kx, kz, near, deep, inj, out):
    for here, sums, sums_z, di, dx, dz in inner_differences(cur, near, deep):
        center = cur[here]
        change = k0[here] * ((sums + sums_z) + (3.0 * SECOND[0] * 5040) * center)
        change = change - (ki[here] * di + kx[here] * dx + kz[here] * dz)
        if inj is not None:
            change = change + inj[here]
        out[here] = (center - prev[here]) + (center + change)


def outer(flags, part, k0, ki, kx, zm, cm, ym, side, edge, new):
    rows = part.shape[0]
    for here, sums, dx in side_differences(rows, zm, cm, side):
        new[here] = part[here] + (k0[here] * sums - kx[here] * dx)
    here, sums, di = edge_differences(flags, rows, ym, edge)
    new[here] += k0[here] * sums - ki[here] * di


def forward_inner_kernel(step, flags, cur, prev, k0, ki, kx, kz, near, deep, srow, sz, wave,
                         *rest):
    size, depth = cur.shape
    n = srow.shape[1]
    spot = lax.broadcasted_iota(jnp.int32, (size, n), 0) == srow[...]
    spot = spot.astype(F32).astype(BF16)
    high, low = split(jnp.where(
        lax.broadcasted_iota(jnp.int32, (n, depth), 1) == sz[...], wave[:, step : step + 1], 0.0))
    inj = mm(spot, high) + mm(spot, low)
    if step > 0:
        before, part, change = rest
        change[...] = (cur[...] - prev[...]) - (prev[...] - before[...])
    else:
        part, = rest
    inner(cur, prev, k0, ki, kx, kz, near, deep, inj, part)


def outer_kernel(stage, flags, part, k0, ki, kx, zm, cm, ym, side, edge, *rest):
    if stage is None:
        new, zo, co, yo = rest
    else:
        mine, got, new, zo, co, yo, lists = rest
        n = mine.shape[0]
        bit = flags[4 + stage]
        lists[pl.ds(bit * n, n)] = mine[...]
        lists[pl.ds((1 - bit) * n, n)] = got[...]
    outer(flags, part, k0, ki, kx, zm, cm, ym, side, edge, new)
    rims(flags, new, zo, co, yo)


def lists_kernel(flags, lists, spot, pick, at, obs):
    size, n = spot.shape
    depth = at.shape[1]
    steps = obs.shape[1]
    sub = flags[2]
    cell = lists[sub, steps : steps + 1, :]
    along = jnp.floor((cell + 0.5) * (1.0 / depth))
    same = lax.broadcasted_iota(jnp.int32, (n, n), 0) == lax.broadcasted_iota(jnp.int32, (n, n), 1)

    def column(row):
        return jnp.sum(jnp.where(same, row, 0.0), axis=1, keepdims=True).astype(jnp.int32)

    hot = lax.broadcasted_iota(jnp.int32, (size, n), 0) == along.astype(jnp.int32)
    spot[...] = hot.astype(F32).astype(BF16)
    hot = lax.broadcasted_iota(jnp.int32, (n, size), 1) == column(along)
    pick[...] = hot.astype(F32).astype(BF16)
    hot = lax.broadcasted_iota(jnp.int32, (n, depth), 1) == column(cell - along * depth)
    at[...] = hot.astype(F32)
    subs = lists.shape[0]
    chosen = lax.broadcasted_iota(jnp.int32, (CAP, n), 1) == (
        sub * CAP + lax.broadcasted_iota(jnp.int32, (CAP, n), 0))
    chosen = chosen.astype(F32).astype(BF16)
    traces = lists[:, 0:steps, :].reshape(subs * steps, n)
    high, mid = split(traces)
    low = (traces - high.astype(F32) - mid.astype(F32)).astype(BF16)
    sent = sum(
        lax.dot_general(chosen, part, (((1,), (1,)), ((), ())), preferred_element_type=F32)
        for part in (low, mid, high))
    for s in range(subs):
        obs[s * CAP : s * CAP + CAP, :] = sent[:, s * steps : s * steps + steps]


def injection(t, state, spot, pick, at, obs):
    high, low = split(state[...])
    seen = at[...] * (mm(pick[...], high) + mm(pick[...], low))
    residual = jnp.sum(seen, axis=1, keepdims=True) - obs[:, t : t + 1]
    high, low = split(at[...] * residual)
    return mm(spot[...], high) + mm(spot[...], low)


def adjoint_inner_kernel(t, flags, cur, prev, k0, ki, kx, kz, near, deep, state, spot, pick,
                         at, obs, *rest):
    if len(rest) == 4:
        change, image, part, image_out = rest
        image_out[...] = cur[...] * change[...] + image[...]
    else:
        now, mid, before, part, image_out = rest
        image_out[...] = cur[...] * ((now[...] - mid[...]) - (mid[...] - before[...]))
    inner(cur, prev, k0, ki, kx, kz, near, deep, injection(t, state, spot, pick, at, obs), part)


def first_inner_kernel(flags, cur, prev, k0, ki, kx, kz, near, deep, part):
    inner(cur, prev, k0, ki, kx, kz, near, deep, None, part)


def turn_kernel(t, flags, part, k0, ki, kx, zm, cm, ym, side, edge, u_part, u_zm, u_cm, u_ym,
                spot, pick, at, obs, new, u_new, zo, co, yo):
    outer(flags, part, k0, ki, kx, zm, cm, ym, side, edge, new)
    outer(flags, u_part, k0, ki, kx, u_zm, u_cm, u_ym, side, edge, u_new)
    u_new[...] += injection(t, new, spot, pick, at, obs)
    rims(flags, u_new, zo, co, yo)


def last_kernel(scale, flags, part, k0, ki, kx, zm, cm, ym, side, edge, image, change, vel,
                new, mine, other):
    outer(flags, part, k0, ki, kx, zm, cm, ym, side, edge, new)
    raw = (image[...] + new[...] * change[...]) * scale / vel[...]
    count, height, lanes = mine.shape
    chunk = raw.shape[1] // (2 * count)
    for n in range(count):
        even, odd = (
            jnp.concatenate(
                [raw[g * height : g * height + height, m * chunk : m * chunk + chunk]
                 for g in range(lanes // chunk)], axis=1)
            for m in (2 * n, 2 * n + 1))
        mine[n] = jnp.where(flags[0] == 0, even, odd)
        other[n] = jnp.where(flags[0] == 0, odd, even)


def join_kernel(flags, mine, got, *outs):
    for s, out in enumerate(outs):
        to = jnp.bitwise_xor(flags[3], s)
        a, b = mine[to], got[to]
        out[0] = jnp.where(flags[0] == 0, a, b)
        out[1] = jnp.where(flags[0] == 0, b, a)


def filter_kernel(flags, *refs):
    *pieces, own, got, prev, prev_got, out, state, prev_state = refs
    keep = flags[0] == flags[1]
    state[...] = jnp.where(keep, own[...], got[...])
    prev_state[...] = jnp.where(keep, prev[...], prev_got[...])
    height, lanes = pieces[0].shape[1:]
    chunk, rows, full = out.shape
    groups = lanes // chunk
    q = flags[3]
    shape = (full, full)
    y = lax.broadcasted_iota(jnp.int32, shape, 1)
    at = lax.broadcasted_iota(jnp.int32, shape, 0)
    within = jnp.bitwise_and(at, 2 * COLS - 1)
    place = jnp.bitwise_xor(q * (2 * COLS), at - within) + within
    weights = jnp.exp(jnp.abs(y - place).astype(F32) * (-1.0 / SMOOTH))
    weights = split(weights / jnp.sum(weights, axis=0, keepdims=True))
    for n in range(height // COLS):
        here = slice(n * COLS, n * COLS + COLS)
        lines = jnp.concatenate([piece[b, here, :] for piece in pieces for b in range(2)], axis=0)
        high, low = split(lines.T)
        done = mm(high, weights[0]) + mm(low, weights[0]) + mm(high, weights[1])
        for g in range(groups):
            out[:, g * (rows // groups) + n, :] = done[g * chunk : g * chunk + chunk]


def shaped(*shape):
    return jax.ShapeDtypeStruct(shape, F32)


def call(kernel, name, outs, *args):
    specs = [pl.BlockSpec(memory_space=pltpu.SMEM)]
    specs += [pl.BlockSpec(memory_space=pltpu.VMEM)] * (len(args) - 1)
    return pl.pallas_call(
        kernel,
        name=name,
        out_shape=outs,
        in_specs=specs,
        out_specs=[pl.BlockSpec(memory_space=pltpu.VMEM)] * len(outs),
        compiler_params=pltpu.CompilerParams(vmem_limit_bytes=VMEM_BYTES),
        cost_estimate=pl.CostEstimate(flops=5_000_000, bytes_accessed=2_000_000, transcendentals=0),
    )(*args)


def per_device(plan, fwd_now, fwd_before, adj_now, adj_before, velocity, log_density, observed,
               rec_cells, rec_counts, src_cell, wavelet):
    rows, cols, depth = fwd_now.shape
    size = rows * cols
    steps = wavelet.shape[0]
    nx, nq = plan.nx, plan.nq
    subs = 2 * nx
    xline, c = lax.axis_index("xline"), lax.axis_index("inline")
    q, y = xline // 2, xline % 2
    keep = y == c
    z_perm, c_perm, y_perm, swap_perm = plan.z(), plan.core(), plan.y(), plan.swap()
    stages = [(c_perm, c), (y_perm, y)]
    stages += [(plan.flip(1 << b), (q >> b) & 1) for b in range((nq - 1).bit_length())]
    sub = (2 * q + c) * 2 + y
    flags = jnp.stack([c, y, sub, q] + [bit for pairs, bit in stages]).astype(jnp.int32)
    field = shaped(size, depth)
    side, edge = (size // 2, depth), (4 * cols, depth)
    rim = [shaped(*side), shaped(*side), shaped(*edge)]

    deep = depth_matrix(depth)
    deep = jnp.asarray(np.concatenate([deep, deep]), BF16)
    near = stencil_matrix(GROUP, cols)
    group, own, half = GROUP * cols, near.shape[1] - GROUP * 8, GROUP * 4
    side = np.concatenate([near[:group, own:], near[2 * group :, own:]])
    other = np.concatenate([side[:, half:], side[:, :half]], axis=1)
    from_z = np.arange(2 * half) < half
    inside = jnp.where(c == 0, q > 0, q < nq - 1)
    side = jnp.where(c == 0, jnp.asarray(side, F32), jnp.asarray(other, F32))
    side = jnp.where(from_z[None, :] & ~inside, 0.0, side).astype(BF16)
    side = jnp.concatenate([side, side], axis=1)
    edge = jnp.where(y == 1, jnp.asarray(near[: 2 * group, : 4 * cols], F32),
                     jnp.asarray(near[: 2 * group, own - 4 * cols : own], F32)).astype(BF16)
    edge = jnp.concatenate([edge, edge], axis=1)
    near = jnp.asarray(np.concatenate([near[:, :own], near[:, :own]], axis=1), BF16)

    def halo(zo, co, yo):
        return send(zo, z_perm), send(co, c_perm), send(yo, y_perm)

    def after(value, *deps):
        return lax.optimization_barrier((value,) + deps)[0]

    def flat(value):
        return value.reshape(size, depth)

    log_density, fwd_now, velocity = flat(log_density), flat(fwd_now), flat(velocity)
    fwd_before, adj_now, adj_before = flat(fwd_before), flat(adj_now), flat(adj_before)
    got = [send(v, swap_perm) for v in (log_density, fwd_now)]
    got_model = send(jnp.stack([velocity, fwd_before]), swap_perm)
    log_density, fwd_now, velocity, fwd_before, adj_now, adj_before = call(
        load_kernel, "load", [field] * 6, flags, log_density, fwd_now, velocity, fwd_before,
        adj_now, adj_before)
    density, p_now, *out = call(settle_kernel, "settle",
                                [field, field] + [shaped(2, *r.shape) for r in rim],
                                flags, log_density, fwd_now, *got)
    zm, cm, ym = halo(*out)
    vel, p_before = call(settle_model_kernel, "settle_model", [field, field],
                         flags, velocity, fwd_before, got_model)
    k0, ki, kx, kz = call(model_kernel, "model", [field] * 4, flags, density, zm, cm, ym, near,
                          deep, side, edge, vel)
    halos = (zm[1], cm[1], ym[1])

    plane = nx * cols * depth
    src_i = src_cell // plane - y * rows
    src_x = src_cell // depth % (nx * cols) - (2 * q + c) * cols
    ok = (src_i >= 0) & (src_i < rows) & (src_x >= 0) & (src_x < cols)
    srow = jnp.where(ok, src_i * cols + src_x, -1)[None, :]
    sz = (src_cell % depth)[:, None]
    wave = wavelet.T

    live = jnp.arange(CAP)[None, :] < rec_counts[0][:, None]
    cells = jnp.where(live.reshape(-1), rec_cells[0], -1)
    lists = jnp.concatenate([observed, cells[None, :].astype(F32)], axis=0)[None]

    lag = 2 if 2 * (len(stages) - 1) < steps - 1 else 1
    moved = send(lists, stages[0][0])

    states = [p_before, p_now]
    changes = []
    for t in range(steps):
        args = states[:-3:-1] + [k0, ki, kx, kz, near, deep, srow, sz, wave]
        outs = [field]
        if t > 0:
            args.append(states[-3])
            outs = [field, field]
        part, *change = call(functools.partial(forward_inner_kernel, t), "forward_inner", outs,
                             flags, *args)
        changes += change
        if t == 1:
            got_now = send(after(adj_now, part), swap_perm)
        if t == 2:
            u_now, *u_rim = call(functools.partial(settle_one, True), "settle_adjoint",
                                 [field] + rim, flags, adj_now, after(got_now, part))
            part = after(part, u_now)
            got_before = send(after(adj_before, part), swap_perm)
        if t == 3:
            u_before, = call(functools.partial(settle_one, False), "settle_before", [field],
                             flags, adj_before, after(got_before, part))
            part = after(part, u_before)
            u_halos = halo(*(after(r, part) for r in u_rim))
        if t == steps - 1:
            u_part, = call(first_inner_kernel, "adjoint_inner", [field], flags, u_now, u_before,
                           k0, ki, kx, kz, near, deep)
            slots = subs * CAP
            receivers = call(
                lists_kernel, "lists",
                [jax.ShapeDtypeStruct((size, slots), BF16),
                 jax.ShapeDtypeStruct((slots, size), BF16), shaped(slots, depth),
                 shaped(slots, steps)], flags, lists)
            new, u_new, *out = call(
                functools.partial(turn_kernel, t), "turn", [field, field] + rim, flags, part,
                k0, ki, kx, *halos, side, edge, u_part, *u_halos, *receivers)
            states.append(new)
            break
        args = [part, k0, ki, kx, *halos, side, edge]
        outs = [field] + rim
        stage = t // lag if t % lag == 0 and t // lag < len(stages) else None
        if stage is not None:
            args += [lists, moved]
            outs = outs + [shaped(2 * lists.shape[0], *lists.shape[1:])]
        elif t % lag == 1 and t // lag + 1 < len(stages):
            moved = send(after(lists, part), stages[t // lag + 1][0])
        new, *out = call(functools.partial(outer_kernel, stage), "forward_outer", outs, flags, *args)
        if stage is not None:
            lists = out.pop()
            if lag == 1 and stage + 1 < len(stages):
                moved = send(lists, stages[stage + 1][0])
        states.append(new)
        halos = halo(*out)

    halos = halo(*out)
    u_before, u_now = u_now, u_new
    image = []
    chunk = depth // nx
    half = shaped(nq, size * chunk // 128, 128)
    for j in range(1, steps):
        t = steps - 1 - j
        terms = [changes[t + 1], *image] if image else states[:-4:-1]
        part, *image = call(
            functools.partial(adjoint_inner_kernel, t), "adjoint_inner", [field, field], flags,
            u_now, u_before, k0, ki, kx, kz, near, deep, states[t + 2], *receivers, *terms)
        args = [part, k0, ki, kx, *halos, side, edge]
        if j == steps - 1:
            got_prev = send(after(u_now, part), swap_perm)
            u_last, mine, other = call(
                functools.partial(last_kernel, 2.0 / steps), "last", [field, half, half],
                flags, *args, *image, changes[0], vel)
            break
        u_before = u_now
        u_now, *out = call(functools.partial(outer_kernel, None), "adjoint_outer", [field] + rim,
                           flags, *args)
        halos = halo(*out)

    pieces = call(join_kernel, "join", [shaped(2, *half.shape[1:])] * nq, flags, mine,
                  send(other, c_perm))
    got = send(after(u_last, pieces[0]), swap_perm)
    pieces = [send(value, plan.spread(s)) for s, value in enumerate(pieces)]
    gradient, adj_out, adj_prev = call(
        filter_kernel, "filter", [shaped(chunk, rows, nx * cols), field, field], flags, *pieces,
        u_last, got, u_now, got_prev)
    block = (rows, cols, depth)
    return gradient, adj_out.reshape(block), adj_prev.reshape(block)


def solution(mesh):
    field = P(("shots", "inline"), "xline", None)
    model = P("inline", "xline", None)
    lists = P(("xline", "inline"), None)
    return jax.shard_map(
        functools.partial(per_device, Plan(mesh)),
        mesh=mesh,
        in_specs=(field, field, field, field, model, model, P("shots", ("xline", "inline")),
                  lists, lists, P("shots"), P("shots", None)),
        out_specs=(P(("shots", "xline"), "inline", None), field, field),
        check_vma=False,
    )
```

```python
import functools

import jax
import jax.numpy as jnp
import numpy as np
from jax import lax
from jax.experimental import pallas as pl
from jax.experimental.pallas import tpu as pltpu
from jax.sharding import PartitionSpec as P

CAP = 8
SMOOTH = 16
SECOND = (-205.0 / 72.0, 8.0 / 5.0, -1.0 / 5.0, 8.0 / 315.0, -1.0 / 560.0)
FIRST = (4.0 / 5.0, -1.0 / 5.0, 4.0 / 105.0, -1.0 / 280.0)
ALL = ("shots", "xline", "inline")
COLS = 8
GROUP = 8
VMEM_BYTES = 8 * 1024 * 1024
F32 = jnp.float32
BF16 = jnp.bfloat16


class Plan:
    def __init__(self, mesh):
        self.shots = mesh.shape["shots"]
        self.nx = mesh.shape["xline"]
        self.nq = self.nx // 2

    def index(self, s, q, y, c):
        return (s * self.nx + 2 * q + y) * 2 + c

    def perm(self, partner):
        pairs = []
        for s in range(self.shots):
            for q in range(self.nq):
                for y in range(2):
                    for c in range(2):
                        t = partner(q, y, c)
                        dst = self.index(s ^ 1, q, y, c) if t is None else self.index(s, *t)
                        pairs.append((self.index(s, q, y, c), dst))
        return pairs

    def swap(self):
        return self.perm(lambda q, y, c: None if y == c else (q, c, y))

    def z(self):
        def partner(q, y, c):
            other = q + 1 if c == 1 else q - 1
            return (other, y, 1 - c) if 0 <= other < self.nq else None

        return self.perm(partner)

    def core(self):
        return self.perm(lambda q, y, c: (q, y, 1 - c))

    def y(self):
        return self.perm(lambda q, y, c: (q, 1 - y, c))

    def flip(self, bit):
        return self.perm(lambda q, y, c: (q ^ bit, y, c) if (q ^ bit) < self.nq else None)

    def spread(self, shift):
        return self.perm(lambda q, y, c: (q ^ shift, c, y))


def send(value, pairs):
    return lax.ppermute(value, ALL, pairs)


def depth_matrix(n):
    m = np.zeros((n, 2 * n), np.float32)
    for k in range(1, 5):
        for j in range(n):
            for i, sign in ((j + k, 1.0), (j - k, -1.0)):
                if 0 <= i < n:
                    m[i, j] = round(SECOND[k] * 5040)
                    m[i, n + j] = sign * round(FIRST[k - 1] * 840)
    return m


def stencil_matrix(rows, cols):
    own = (rows + 8) * cols
    m = np.zeros((3, rows, cols, own + rows * 8), np.float32)
    for i in range(rows):
        for x in range(cols):
            for k in range(1, 5):
                total = round(SECOND[k] * 5040)
                slope = round(FIRST[k - 1] * 840)
                for sign in (1, -1):
                    at = (i + 4 + sign * k) * cols + x
                    m[0, i, x, at] += total
                    m[1, i, x, at] += sign * slope
                    to = x + sign * k
                    if to < 0:
                        at = own + i * 4 + to + 4
                    elif to >= cols:
                        at = own + rows * 4 + i * 4 + to - cols
                    else:
                        at = (i + 4) * cols + to
                    m[0, i, x, at] += total
                    m[2, i, x, at] += sign * slope
    return m.reshape(3 * rows * cols, own + rows * 8)


def split(value):
    high = value.astype(BF16)
    return high, (value - high.astype(F32)).astype(BF16)


def mm(a, b):
    return jnp.dot(a, b, preferred_element_type=F32)


def inner_differences(cur, cm, near, deep):
    depth = cur.shape[1]
    size = GROUP * COLS
    own = split(cur[...])
    along = mm(jnp.concatenate(own, axis=1), deep[...])
    blank = jnp.zeros((4 * COLS, depth), BF16)
    ext = [jnp.concatenate([blank, part, blank], axis=0) for part in own]
    from_c = split(cm[...])
    for n in range(cur.shape[0] // size):
        here = slice(n * size, n * size + size)
        sides = slice(n * GROUP * 4, n * GROUP * 4 + GROUP * 4)
        rhs = [part[n * size : n * size + size + 8 * COLS] for part in ext]
        rhs += [part[sides] for part in from_c]
        out = mm(near[...], jnp.concatenate(rhs, axis=0))
        yield (here, out[0:size], along[here, 0:depth], out[size : 2 * size], out[2 * size :],
               along[here, depth:])


def side_differences(rows, zm, side):
    size = GROUP * COLS
    from_z = split(zm[...])
    for n in range(rows // size):
        sides = slice(n * GROUP * 4, n * GROUP * 4 + GROUP * 4)
        out = mm(side[...], jnp.concatenate([part[sides] for part in from_z], axis=0))
        yield slice(n * size, n * size + size), out[0:size], out[size:]


def edge_differences(flags, rows, ym, edge):
    size = GROUP * COLS
    out = mm(edge[...], jnp.concatenate(split(ym[...]), axis=0))
    start = jnp.where(flags[1] == 1, 0, rows - size)
    return pl.ds(pl.multiple_of(start, size), size), out[0:size], out[size:]


def halves(value):
    rows, depth = value.shape
    pairs = value.reshape(rows // (2 * COLS), 2, COLS, depth)
    a, b = pairs[:, 0], pairs[:, 1]
    low = lax.broadcasted_iota(jnp.int32, a.shape, 1) < 4
    first = jnp.where(low, a, pltpu.roll(b, 4, axis=1))
    last = jnp.where(low, pltpu.roll(a, 4, axis=1), b)
    return first.reshape(rows // 2, depth), last.reshape(rows // 2, depth)


def rims(flags, new, zo, co, yo):
    first, last = halves(new[...])
    zo[...] = jnp.where(flags[0] == 0, first, last)
    co[...] = jnp.where(flags[0] == 0, last, first)
    size = new.shape[0]
    yo[...] = jnp.where(flags[1] == 0, new[size - 4 * COLS :], new[0 : 4 * COLS])


def load_kernel(flags, *refs):
    half = len(refs) // 2
    for source, out in zip(refs[:half], refs[half:]):
        out[...] = source[...]


def settle_kernel(flags, a, b, recv_a, recv_b, a_out, b_out, *outs):
    keep = flags[0] == flags[1]
    for n, (own, recv, out) in enumerate(((a, recv_a, a_out), (b, recv_b, b_out))):
        out[...] = jnp.where(keep, own[...], recv[...])
        rims(flags, out, *(ref.at[n] for ref in outs))


def settle_model_kernel(flags, a, b, recv, a_out, b_out):
    keep = flags[0] == flags[1]
    a_out[...] = jnp.where(keep, a[...], recv[0])
    b_out[...] = jnp.where(keep, b[...], recv[1])


def settle_one(with_rims, flags, own, recv, out, *outs):
    out[...] = jnp.where(flags[0] == flags[1], own[...], recv[...])
    if with_rims:
        rims(flags, out, *outs)


def first_inner_kernel(flags, lr, cur, lr_cm, cm, near, deep, *outs):
    ri, rx, rz, sums_out, di_out, dx_out, dz_out = outs
    for here, spare, spare_z, di, dx, dz in inner_differences(lr, lr_cm, near, deep):
        ri[here], rx[here], rz[here] = di, dx, dz
    for here, sums, sums_z, di, dx, dz in inner_differences(cur, cm, near, deep):
        sums_out[here] = sums + sums_z + (3.0 * SECOND[0] * 5040) * cur[here]
        di_out[here], dx_out[here], dz_out[here] = di, dx, dz


def first_outer_kernel(flags, cur, prev, vel, ri, rx, rz, sums, di, dx, dz, inj, lr_zm, lr_ym, zm,
                       ym, side, edge, mine, got, new, zo, co, yo, lists, k0, ki, kx, kz):
    rows = cur.shape[0]
    merge(0, flags, mine, got, lists)
    kz[...] = sums[...]
    ki[...] = di[...]
    here, more, more_i = edge_differences(flags, rows, ym, edge)
    kz[here] += more
    ki[here] += more_i
    lr_here, spare, lr_more_i = edge_differences(flags, rows, lr_ym, edge)
    k0[...] = ri[...]
    k0[lr_here] += lr_more_i
    first = side_differences(rows, lr_zm, side)
    second = side_differences(rows, zm, side)
    for (here, spare, more_r), (spare_here, more, more_x) in zip(first, second):
        square = vel[here] * vel[here]
        scaled = square * (1.0 / (840 * 840))
        factor = square * (1.0 / 5040)
        along_i, along_x, along_z = scaled * k0[here], scaled * (rx[here] + more_r), scaled * rz[here]
        change = factor * (kz[here] + more) - (
            along_i * ki[here] + along_x * (dx[here] + more_x) + along_z * dz[here])
        k0[here], ki[here], kx[here], kz[here] = factor, along_i, along_x, along_z
        center = cur[here]
        new[here] = (center - prev[here]) + (center + (change + inj[here]))
    rims(flags, new, zo, co, yo)


def inner(cur, prev, k0, ki, kx, kz, cm, near, deep, inj, out):
    for here, sums, sums_z, di, dx, dz in inner_differences(cur, cm, near, deep):
        center = cur[here]
        change = k0[here] * ((sums + sums_z) + (3.0 * SECOND[0] * 5040) * center)
        change = change - (ki[here] * di + kx[here] * dx + kz[here] * dz)
        if inj is not None:
            change = change + inj[here]
        out[here] = (center - prev[here]) + (center + change)


def outer(flags, part, k0, ki, kx, zm, ym, side, edge, new):
    rows = part.shape[0]
    for here, sums, dx in side_differences(rows, zm, side):
        new[here] = part[here] + (k0[here] * sums - kx[here] * dx)
    here, sums, di = edge_differences(flags, rows, ym, edge)
    new[here] += k0[here] * sums - ki[here] * di


def merge(stage, flags, mine, got, out):
    n = mine.shape[0]
    bit = flags[4 + stage]
    out[pl.ds(bit * n, n)] = mine[...]
    out[pl.ds((1 - bit) * n, n)] = got[...]


def source_kernel(step, flags, srow, sz, wave, out):
    size, depth = out.shape
    n = srow.shape[1]
    spot = lax.broadcasted_iota(jnp.int32, (size, n), 0) == srow[...]
    spot = spot.astype(F32).astype(BF16)
    high, low = split(jnp.where(
        lax.broadcasted_iota(jnp.int32, (n, depth), 1) == sz[...], wave[:, step : step + 1], 0.0))
    out[...] = mm(spot, high) + mm(spot, low)


def forward_inner_kernel(step, flags, cur, prev, k0, ki, kx, kz, cm, near, deep, srow, sz, wave,
                         before, part, change):
    source_kernel(step, flags, srow, sz, wave, change)
    inner(cur, prev, k0, ki, kx, kz, cm, near, deep, change, part)
    change[...] = (cur[...] - prev[...]) - (prev[...] - before[...])


def outer_kernel(stage, flags, part, k0, ki, kx, zm, ym, side, edge, *rest):
    if stage is None:
        new, zo, co, yo = rest
    else:
        mine, got, new, zo, co, yo, lists = rest
        merge(stage, flags, mine, got, lists)
    outer(flags, part, k0, ki, kx, zm, ym, side, edge, new)
    rims(flags, new, zo, co, yo)


def lists_kernel(flags, lists, spot, pick, at, obs):
    size, n = spot.shape
    depth = at.shape[1]
    steps = obs.shape[1]
    sub = flags[2]
    cell = lists[sub, steps : steps + 1, :]
    along = jnp.floor((cell + 0.5) * (1.0 / depth))
    same = lax.broadcasted_iota(jnp.int32, (n, n), 0) == lax.broadcasted_iota(jnp.int32, (n, n), 1)

    def column(row):
        return jnp.sum(jnp.where(same, row, 0.0), axis=1, keepdims=True).astype(jnp.int32)

    hot = lax.broadcasted_iota(jnp.int32, (size, n), 0) == along.astype(jnp.int32)
    spot[...] = hot.astype(F32).astype(BF16)
    hot = lax.broadcasted_iota(jnp.int32, (n, size), 1) == column(along)
    pick[...] = hot.astype(F32).astype(BF16)
    hot = lax.broadcasted_iota(jnp.int32, (n, depth), 1) == column(cell - along * depth)
    at[...] = hot.astype(F32)
    subs = lists.shape[0]
    chosen = lax.broadcasted_iota(jnp.int32, (CAP, n), 1) == (
        sub * CAP + lax.broadcasted_iota(jnp.int32, (CAP, n), 0))
    chosen = chosen.astype(F32).astype(BF16)
    traces = lists[:, 0:steps, :].reshape(subs * steps, n)
    high, mid = split(traces)
    low = (traces - high.astype(F32) - mid.astype(F32)).astype(BF16)
    sent = sum(
        lax.dot_general(chosen, part, (((1,), (1,)), ((), ())), preferred_element_type=F32)
        for part in (low, mid, high))
    for s in range(subs):
        obs[s * CAP : s * CAP + CAP, :] = sent[:, s * steps : s * steps + steps]


def injection(t, state, spot, pick, at, obs):
    high, low = split(state[...])
    seen = at[...] * (mm(pick[...], high) + mm(pick[...], low))
    residual = jnp.sum(seen, axis=1, keepdims=True) - obs[:, t : t + 1]
    high, low = split(at[...] * residual)
    return mm(spot[...], high) + mm(spot[...], low)


def adjoint_inner_kernel(t, flags, cur, prev, k0, ki, kx, kz, cm, near, deep, state, spot, pick,
                         at, obs, *rest):
    if len(rest) == 4:
        change, image, part, image_out = rest
        image_out[...] = cur[...] * change[...] + image[...]
    else:
        now, mid, before, part, image_out = rest
        image_out[...] = cur[...] * ((now[...] - mid[...]) - (mid[...] - before[...]))
    inj = injection(t, state, spot, pick, at, obs)
    inner(cur, prev, k0, ki, kx, kz, cm, near, deep, inj, part)


def adjoint_first_kernel(flags, cur, prev, k0, ki, kx, kz, cm, near, deep, part):
    inner(cur, prev, k0, ki, kx, kz, cm, near, deep, None, part)


def turn_kernel(t, flags, part, k0, ki, kx, zm, ym, side, edge, u_part, u_zm, u_ym, spot, pick, at, obs, new, u_new, zo, co, yo):
    outer(flags, part, k0, ki, kx, zm, ym, side, edge, new)
    outer(flags, u_part, k0, ki, kx, u_zm, u_ym, side, edge, u_new)
    u_new[...] += injection(t, new, spot, pick, at, obs)
    rims(flags, u_new, zo, co, yo)


def last_kernel(scale, flags, part, k0, ki, kx, zm, ym, side, edge, image, change, vel,
                new, mine, other):
    outer(flags, part, k0, ki, kx, zm, ym, side, edge, new)
    raw = (image[...] + new[...] * change[...]) * scale / vel[...]
    count, height, lanes = mine.shape
    chunk = raw.shape[1] // (2 * count)
    for n in range(count):
        even, odd = (
            jnp.concatenate(
                [raw[g * height : g * height + height, m * chunk : m * chunk + chunk]
                 for g in range(lanes // chunk)], axis=1)
            for m in (2 * n, 2 * n + 1))
        mine[n] = jnp.where(flags[0] == 0, even, odd)
        other[n] = jnp.where(flags[0] == 0, odd, even)


def join_kernel(flags, mine, got, *outs):
    for s, out in enumerate(outs):
        to = jnp.bitwise_xor(flags[3], s)
        a, b = mine[to], got[to]
        out[0] = jnp.where(flags[0] == 0, a, b)
        out[1] = jnp.where(flags[0] == 0, b, a)


def filter_kernel(flags, *refs):
    *pieces, own, got, prev, prev_got, out, state, prev_state = refs
    keep = flags[0] == flags[1]
    state[...] = jnp.where(keep, own[...], got[...])
    prev_state[...] = jnp.where(keep, prev[...], prev_got[...])
    height, lanes = pieces[0].shape[1:]
    chunk, rows, full = out.shape
    groups = lanes // chunk
    q = flags[3]
    shape = (full, full)
    y = lax.broadcasted_iota(jnp.int32, shape, 1)
    at = lax.broadcasted_iota(jnp.int32, shape, 0)
    within = jnp.bitwise_and(at, 2 * COLS - 1)
    place = jnp.bitwise_xor(q * (2 * COLS), at - within) + within
    weights = jnp.exp(jnp.abs(y - place).astype(F32) * (-1.0 / SMOOTH))
    weights = split(weights / jnp.sum(weights, axis=0, keepdims=True))
    for n in range(height // COLS):
        here = slice(n * COLS, n * COLS + COLS)
        lines = jnp.concatenate([piece[b, here, :] for piece in pieces for b in range(2)], axis=0)
        high, low = split(lines.T)
        done = mm(high, weights[0]) + mm(low, weights[0]) + mm(high, weights[1])
        for g in range(groups):
            out[:, g * (rows // groups) + n, :] = done[g * chunk : g * chunk + chunk]


def shaped(*shape):
    return jax.ShapeDtypeStruct(shape, F32)


def call(kernel, name, outs, *args):
    specs = [pl.BlockSpec(memory_space=pltpu.SMEM)]
    specs += [pl.BlockSpec(memory_space=pltpu.VMEM)] * (len(args) - 1)
    return pl.pallas_call(
        kernel,
        name=name,
        out_shape=outs,
        in_specs=specs,
        out_specs=[pl.BlockSpec(memory_space=pltpu.VMEM)] * len(outs),
        compiler_params=pltpu.CompilerParams(vmem_limit_bytes=VMEM_BYTES),
        cost_estimate=pl.CostEstimate(flops=1000, bytes_accessed=1000, transcendentals=0),
    )(*args)


def per_device(plan, fwd_now, fwd_before, adj_now, adj_before, velocity, log_density, observed,
               rec_cells, rec_counts, src_cell, wavelet):
    rows, cols, depth = fwd_now.shape
    size = rows * cols
    steps = wavelet.shape[0]
    nx, nq = plan.nx, plan.nq
    subs = 2 * nx
    xline, c = lax.axis_index("xline"), lax.axis_index("inline")
    q, y = xline // 2, xline % 2
    keep = y == c
    z_perm, c_perm, y_perm, swap_perm = plan.z(), plan.core(), plan.y(), plan.swap()
    stages = [(c_perm, c), (y_perm, y)]
    stages += [(plan.flip(1 << b), (q >> b) & 1) for b in range((nq - 1).bit_length())]
    sub = (2 * q + c) * 2 + y
    flags = jnp.stack([c, y, sub, q] + [bit for pairs, bit in stages]).astype(jnp.int32)
    field = shaped(size, depth)
    side, edge = (size // 2, depth), (4 * cols, depth)
    rim = [shaped(*side), shaped(*side), shaped(*edge)]

    deep = depth_matrix(depth)
    deep = jnp.asarray(np.concatenate([deep, deep]), BF16)
    near = stencil_matrix(GROUP, cols)
    group, own, half = GROUP * cols, near.shape[1] - GROUP * 8, GROUP * 4
    both = [near[:, own : own + half], near[:, own + half :]]
    from_z = [np.concatenate([part[:group], part[2 * group :]]) for part in both]
    inside = jnp.where(c == 0, q > 0, q < nq - 1)
    side = jnp.where(c == 0, jnp.asarray(from_z[0], F32), jnp.asarray(from_z[1], F32))
    side = jnp.where(inside, side, 0.0).astype(BF16)
    side = jnp.concatenate([side, side], axis=1)
    core = jnp.where(c == 0, jnp.asarray(both[1], F32), jnp.asarray(both[0], F32)).astype(BF16)
    edge = jnp.where(y == 1, jnp.asarray(near[: 2 * group, : 4 * cols], F32),
                     jnp.asarray(near[: 2 * group, own - 4 * cols : own], F32)).astype(BF16)
    edge = jnp.concatenate([edge, edge], axis=1)
    near = jnp.asarray(np.concatenate([near[:, :own], near[:, :own]], axis=1), BF16)
    near = jnp.concatenate([near, core, core], axis=1)

    def halo(zo, co, yo):
        return send(zo, z_perm), send(co, c_perm), send(yo, y_perm)

    def after(value, *deps):
        return lax.optimization_barrier((value,) + deps)[0]

    def flat(value):
        return value.reshape(size, depth)

    log_density, fwd_now, velocity = flat(log_density), flat(fwd_now), flat(velocity)
    fwd_before, adj_now, adj_before = flat(fwd_before), flat(adj_now), flat(adj_before)
    got = [send(v, swap_perm) for v in (log_density, fwd_now)]
    got_model = send(jnp.stack([velocity, fwd_before]), swap_perm)
    log_density, fwd_now, velocity, fwd_before, adj_now, adj_before = call(
        load_kernel, "load", [field] * 6, flags, log_density, fwd_now, velocity, fwd_before,
        adj_now, adj_before)
    density, p_now, *out = call(settle_kernel, "settle",
                                [field, field] + [shaped(2, *r.shape) for r in rim],
                                flags, log_density, fwd_now, *got)
    zm, cm, ym = halo(*out)
    parts = call(first_inner_kernel, "first_inner", [field] * 7, flags, density, p_now, cm[0], cm[1],
                 near, deep)
    vel, p_before = call(settle_model_kernel, "settle_model", [field, field],
                         flags, velocity, fwd_before, got_model)

    plane = nx * cols * depth
    src_i = src_cell // plane - y * rows
    src_x = src_cell // depth % (nx * cols) - (2 * q + c) * cols
    ok = (src_i >= 0) & (src_i < rows) & (src_x >= 0) & (src_x < cols)
    srow = jnp.where(ok, src_i * cols + src_x, -1)[None, :]
    sz = (src_cell % depth)[:, None]
    wave = wavelet.T

    rec_counts, rec_cells, observed = lax.optimization_barrier(
        (rec_counts, rec_cells, observed, density))[:3]
    live = jnp.arange(CAP)[None, :] < rec_counts[0][:, None]
    cells = jnp.where(live.reshape(-1), rec_cells[0], -1)
    lists = jnp.concatenate([observed, cells[None, :].astype(F32)], axis=0)[None]

    lag = 2 if 2 * (len(stages) - 1) < steps - 1 else 1
    moved = send(lists, stages[0][0])

    inj, = call(functools.partial(source_kernel, 0), "source", [field], flags, srow, sz, wave)
    grown = shaped(2, *lists.shape[1:])
    new, zo, co, yo, lists, *model = call(
        first_outer_kernel, "first_outer", [field] + rim + [grown] + [field] * 4, flags, p_now,
        p_before, vel, *parts, inj, zm[0], ym[0], zm[1], ym[1], side, edge, lists, moved)
    k0, ki, kx, kz = model
    states = [p_before, p_now, new]
    changes = []
    zm, cm, ym = halo(zo, co, yo)
    if lag == 1:
        moved = send(lists, stages[1][0])
    for t in range(1, steps):
        cur, prev, before = states[:-4:-1]
        part, change = call(
            functools.partial(forward_inner_kernel, t), "forward_inner", [field, field], flags, cur,
            prev, *model, cm, near, deep, srow, sz, wave, before)
        changes.append(change)
        if t == 1:
            got_now = send(after(adj_now, part), swap_perm)
        if t == 2:
            u_now, *u_rim = call(functools.partial(settle_one, True), "settle_adjoint",
                                 [field] + rim, flags, adj_now, after(got_now, part))
            part = after(part, u_now)
            got_before = send(after(adj_before, part), swap_perm)
        if t == 3:
            u_before, = call(functools.partial(settle_one, False), "settle_before", [field],
                             flags, adj_before, after(got_before, part))
            part = after(part, u_before)
            u_zm, u_cm, u_ym = halo(*(after(r, part) for r in u_rim))
        if t == 4:
            u_part, = call(adjoint_first_kernel, "adjoint_inner", [field], flags, u_now, u_before,
                           *model, u_cm, near, deep)
            part = after(part, u_part)
        if t == 5:
            part = after(part, u_zm, u_ym)
        if t == steps - 1:
            slots = subs * CAP
            receivers = call(
                lists_kernel, "lists",
                [jax.ShapeDtypeStruct((size, slots), BF16),
                 jax.ShapeDtypeStruct((slots, size), BF16), shaped(slots, depth),
                 shaped(slots, steps)], flags, lists)
            new, u_new, *out = call(
                functools.partial(turn_kernel, t), "turn", [field, field] + rim, flags, part,
                k0, ki, kx, zm, ym, side, edge, u_part, u_zm, u_ym, *receivers)
            states.append(new)
            break
        args = [part, k0, ki, kx, zm, ym, side, edge]
        outs = [field] + rim
        stage = t // lag if t % lag == 0 and t // lag < len(stages) else None
        if stage is not None:
            args += [lists, moved]
            outs = outs + [shaped(2 * lists.shape[0], *lists.shape[1:])]
        elif t % lag == 1 and t // lag + 1 < len(stages):
            moved = send(after(lists, part), stages[t // lag + 1][0])
        new, *out = call(functools.partial(outer_kernel, stage), "forward_outer", outs, flags, *args)
        if stage is not None:
            lists = out.pop()
            if lag == 1 and stage + 1 < len(stages):
                moved = send(lists, stages[stage + 1][0])
        states.append(new)
        zm, cm, ym = halo(*out)

    zm, cm, ym = halo(*out)
    u_before, u_now = u_now, u_new
    image = []
    chunk = depth // nx
    half = shaped(nq, size * chunk // 128, 128)
    for j in range(1, steps):
        t = steps - 1 - j
        terms = [changes[t + 1], *image] if image else states[:-4:-1]
        part, *image = call(
            functools.partial(adjoint_inner_kernel, t), "adjoint_inner", [field, field], flags,
            u_now, u_before, *model, cm, near, deep, states[t + 2], *receivers, *terms)
        args = [part, k0, ki, kx, zm, ym, side, edge]
        if j == steps - 1:
            got_prev = send(after(u_now, part), swap_perm)
            u_last, mine, other = call(
                functools.partial(last_kernel, 2.0 / steps), "last", [field, half, half],
                flags, *args, *image, changes[0], vel)
            break
        u_before = u_now
        u_now, *out = call(functools.partial(outer_kernel, None), "adjoint_outer", [field] + rim,
                           flags, *args)
        zm, cm, ym = halo(*out)

    pieces = call(join_kernel, "join", [shaped(2, *half.shape[1:])] * nq, flags, mine,
                  send(other, c_perm))
    got = send(u_last, swap_perm)
    pieces = [send(value, plan.spread(s)) for s, value in enumerate(pieces)]
    gradient, adj_out, adj_prev = call(
        filter_kernel, "filter", [shaped(chunk, rows, nx * cols), field, field], flags, *pieces,
        u_last, got, u_now, got_prev)
    block = (rows, cols, depth)
    return gradient, adj_out.reshape(block), adj_prev.reshape(block)


def solution(mesh):
    field = P(("shots", "inline"), "xline", None)
    model = P("inline", "xline", None)
    lists = P(("xline", "inline"), None)
    return jax.shard_map(
        functools.partial(per_device, Plan(mesh)),
        mesh=mesh,
        in_specs=(field, field, field, field, model, model, P("shots", ("xline", "inline")),
                  lists, lists, P("shots"), P("shots", None)),
        out_specs=(P(("shots", "xline"), "inline", None), field, field),
        check_vma=False,
    )
```

```python
import functools

import jax
import jax.numpy as jnp
import numpy as np
from jax import lax
from jax.experimental import pallas as pl
from jax.experimental.pallas import tpu as pltpu
from jax.sharding import PartitionSpec as P

CAP = 8
SMOOTH = 16
SECOND = (-205.0 / 72.0, 8.0 / 5.0, -1.0 / 5.0, 8.0 / 315.0, -1.0 / 560.0)
FIRST = (4.0 / 5.0, -1.0 / 5.0, 4.0 / 105.0, -1.0 / 280.0)
ALL = ("shots", "xline", "inline")
COLS = 8
GROUP = 8
VMEM_BYTES = 8 * 1024 * 1024
F32 = jnp.float32
BF16 = jnp.bfloat16


class Plan:
    def __init__(self, mesh):
        self.shots = mesh.shape["shots"]
        self.nx = mesh.shape["xline"]
        self.nq = self.nx // 2

    def index(self, s, q, y, c):
        return (s * self.nx + 2 * q + y) * 2 + c

    def perm(self, partner):
        pairs = []
        for s in range(self.shots):
            for q in range(self.nq):
                for y in range(2):
                    for c in range(2):
                        t = partner(q, y, c)
                        dst = self.index(s ^ 1, q, y, c) if t is None else self.index(s, *t)
                        pairs.append((self.index(s, q, y, c), dst))
        return pairs

    def swap(self):
        return self.perm(lambda q, y, c: None if y == c else (q, c, y))

    def z(self):
        def partner(q, y, c):
            other = q + 1 if c == 1 else q - 1
            return (other, y, 1 - c) if 0 <= other < self.nq else None

        return self.perm(partner)

    def core(self):
        return self.perm(lambda q, y, c: (q, y, 1 - c))

    def y(self):
        return self.perm(lambda q, y, c: (q, 1 - y, c))

    def flip(self, bit):
        return self.perm(lambda q, y, c: (q ^ bit, y, c) if (q ^ bit) < self.nq else None)

    def spread(self, shift):
        return self.perm(lambda q, y, c: (q ^ shift, c, y))


def send(value, pairs):
    return lax.ppermute(value, ALL, pairs)


def depth_matrix(n):
    m = np.zeros((n, 2 * n), np.float32)
    for k in range(1, 5):
        for j in range(n):
            for i, sign in ((j + k, 1.0), (j - k, -1.0)):
                if 0 <= i < n:
                    m[i, j] = round(SECOND[k] * 5040)
                    m[i, n + j] = sign * round(FIRST[k - 1] * 840)
    return m


def stencil_matrix(rows, cols):
    own = (rows + 8) * cols
    m = np.zeros((3, rows, cols, own + rows * 8), np.float32)
    for i in range(rows):
        for x in range(cols):
            for k in range(1, 5):
                total = round(SECOND[k] * 5040)
                slope = round(FIRST[k - 1] * 840)
                for sign in (1, -1):
                    at = (i + 4 + sign * k) * cols + x
                    m[0, i, x, at] += total
                    m[1, i, x, at] += sign * slope
                    to = x + sign * k
                    if to < 0:
                        at = own + i * 4 + to + 4
                    elif to >= cols:
                        at = own + rows * 4 + i * 4 + to - cols
                    else:
                        at = (i + 4) * cols + to
                    m[0, i, x, at] += total
                    m[2, i, x, at] += sign * slope
    return m.reshape(3 * rows * cols, own + rows * 8)


def split(value):
    high = value.astype(BF16)
    return high, (value - high.astype(F32)).astype(BF16)


def mm(a, b):
    return jnp.dot(a, b, preferred_element_type=F32)


def inner_differences(cur, cm, near, deep):
    depth = cur.shape[1]
    size = GROUP * COLS
    cm = cm.at[0] if len(cm.shape) == 3 else cm
    own = split(cur[...])
    along = mm(jnp.concatenate(own, axis=1), deep[...])
    blank = jnp.zeros((4 * COLS, depth), BF16)
    ext = [jnp.concatenate([blank, part, blank], axis=0) for part in own]
    from_c = split(cm[...])
    for n in range(cur.shape[0] // size):
        here = slice(n * size, n * size + size)
        sides = slice(n * GROUP * 4, n * GROUP * 4 + GROUP * 4)
        rhs = [part[n * size : n * size + size + 8 * COLS] for part in ext]
        rhs += [part[sides] for part in from_c]
        out = mm(near[...], jnp.concatenate(rhs, axis=0))
        yield (here, out[0:size], along[here, 0:depth], out[size : 2 * size], out[2 * size :],
               along[here, depth:])


def side_differences(rows, zm, side):
    size = GROUP * COLS
    zm = zm.at[0] if len(zm.shape) == 3 else zm
    from_z = split(zm[...])
    for n in range(rows // size):
        sides = slice(n * GROUP * 4, n * GROUP * 4 + GROUP * 4)
        out = mm(side[...], jnp.concatenate([part[sides] for part in from_z], axis=0))
        yield slice(n * size, n * size + size), out[0:size], out[size:]


def edge_differences(flags, rows, ym, edge):
    size = GROUP * COLS
    ym = ym.at[0] if len(ym.shape) == 3 else ym
    out = mm(edge[...], jnp.concatenate(split(ym[...]), axis=0))
    start = jnp.where(flags[1] == 1, 0, rows - size)
    return pl.ds(pl.multiple_of(start, size), size), out[0:size], out[size:]


def halves(value):
    rows, depth = value.shape
    pairs = value.reshape(rows // (2 * COLS), 2, COLS, depth)
    a, b = pairs[:, 0], pairs[:, 1]
    low = lax.broadcasted_iota(jnp.int32, a.shape, 1) < 4
    first = jnp.where(low, a, pltpu.roll(b, 4, axis=1))
    last = jnp.where(low, pltpu.roll(a, 4, axis=1), b)
    return first.reshape(rows // 2, depth), last.reshape(rows // 2, depth)


def rims(flags, new, zo, co, yo):
    first, last = halves(new[...])
    zo[...] = jnp.where(flags[0] == 0, first, last)
    co[...] = jnp.where(flags[0] == 0, last, first)
    size = new.shape[0]
    yo[...] = jnp.where(flags[1] == 0, new[size - 4 * COLS :], new[0 : 4 * COLS])


def choose(flags, pairs, sems):
    keep = flags[0] == flags[1]

    @pl.when(keep)
    def _():
        copies = [pltpu.make_async_copy(own, out, sems.at[n])
                  for n, (own, recv, out) in enumerate(pairs)]
        for copy in copies:
            copy.start()
        for copy in copies:
            copy.wait()

    @pl.when(jnp.logical_not(keep))
    def _():
        for own, recv, out in pairs:
            out[...] = recv[...]


def settle_kernel(flags, a, b, recv_a, recv_b, a_out, b_out, zo, co, yo, sems):
    choose(flags, [(a, recv_a, a_out), (b, recv_b, b_out)], sems)
    for n, out in enumerate((a_out, b_out)):
        rims(flags, out, zo.at[n], co.at[n], yo.at[n])


def settle_model_kernel(flags, a, b, recv, a_out, b_out, sems):
    choose(flags, [(a, recv.at[0], a_out), (b, recv.at[1], b_out)], sems)


def settle_adjoint_kernel(flags, a, b, recv_a, recv_b, a_out, b_out, sems):
    choose(flags, [(a, recv_a, a_out), (b, recv_b, b_out)], sems)


def select_kernel(flags, own, recv, out):
    out[...] = jnp.where(flags[0] == flags[1], own[...], recv[...])


def first_inner_kernel(flags, lr, cur, cm, near, deep, *outs):
    ri, rx, rz, sums_out, di_out, dx_out, dz_out = outs
    for here, spare, spare_z, di, dx, dz in inner_differences(lr, cm.at[0], near, deep):
        ri[here], rx[here], rz[here] = di, dx, dz
    for here, sums, sums_z, di, dx, dz in inner_differences(cur, cm.at[1], near, deep):
        sums_out[here] = sums + sums_z + (3.0 * SECOND[0] * 5040) * cur[here]
        di_out[here], dx_out[here], dz_out[here] = di, dx, dz


def first_outer_kernel(flags, cur, prev, vel, ri, rx, rz, sums, di, dx, dz, inj, zm, ym, side, edge, mine, got, new, zo, co, yo, lists, k0, ki, kx, kz):
    rows = cur.shape[0]
    merge(0, flags, mine, got, lists)
    kz[...] = sums[...]
    ki[...] = di[...]
    here, more, more_i = edge_differences(flags, rows, ym.at[1], edge)
    kz[here] += more
    ki[here] += more_i
    lr_here, spare, lr_more_i = edge_differences(flags, rows, ym.at[0], edge)
    k0[...] = ri[...]
    k0[lr_here] += lr_more_i
    first = side_differences(rows, zm.at[0], side)
    second = side_differences(rows, zm.at[1], side)
    for (here, spare, more_r), (spare_here, more, more_x) in zip(first, second):
        square = vel[here] * vel[here]
        scaled = square * (1.0 / (840 * 840))
        factor = square * (1.0 / 5040)
        along_i, along_x, along_z = scaled * k0[here], scaled * (rx[here] + more_r), scaled * rz[here]
        change = factor * (kz[here] + more) - (
            along_i * ki[here] + along_x * (dx[here] + more_x) + along_z * dz[here])
        k0[here], ki[here], kx[here], kz[here] = factor, along_i, along_x, along_z
        center = cur[here]
        new[here] = (center - prev[here]) + (center + (change + inj[here]))
    rims(flags, new, zo, co, yo)


def inner(cur, prev, k0, ki, kx, kz, cm, near, deep, inj, out):
    for here, sums, sums_z, di, dx, dz in inner_differences(cur, cm, near, deep):
        center = cur[here]
        change = k0[here] * ((sums + sums_z) + (3.0 * SECOND[0] * 5040) * center)
        change = change - (ki[here] * di + kx[here] * dx + kz[here] * dz)
        if inj is not None:
            change = change + inj[here]
        out[here] = (center - prev[here]) + (center + change)


def outer(flags, part, k0, ki, kx, zm, ym, side, edge, new):
    rows = part.shape[0]
    for here, sums, dx in side_differences(rows, zm, side):
        new[here] = part[here] + (k0[here] * sums - kx[here] * dx)
    here, sums, di = edge_differences(flags, rows, ym, edge)
    new[here] += k0[here] * sums - ki[here] * di


def merge(stage, flags, mine, got, out):
    n = mine.shape[0]
    bit = flags[4 + stage]
    out[pl.ds(bit * n, n)] = mine[...]
    out[pl.ds((1 - bit) * n, n)] = got[...]


def source_kernel(step, flags, srow, sz, wave, out):
    size, depth = out.shape
    n = srow.shape[1]
    spot = lax.broadcasted_iota(jnp.int32, (size, n), 0) == srow[...]
    spot = spot.astype(F32).astype(BF16)
    high, low = split(jnp.where(
        lax.broadcasted_iota(jnp.int32, (n, depth), 1) == sz[...], wave[:, step : step + 1], 0.0))
    out[...] = mm(spot, high) + mm(spot, low)


def forward_inner_kernel(step, flags, cur, prev, k0, ki, kx, kz, cm, near, deep, srow, sz, wave,
                         before, part, change):
    source_kernel(step, flags, srow, sz, wave, change)
    inner(cur, prev, k0, ki, kx, kz, cm, near, deep, change, part)
    change[...] = (cur[...] - prev[...]) - (prev[...] - before[...])


def outer_kernel(stage, double, flags, part, k0, ki, kx, zm, ym, side, edge, *rest):
    rest = list(rest)
    other = rest.pop(0) if double else None
    if stage is not None:
        merge(stage, flags, rest.pop(0), rest.pop(0), rest.pop())
    new, zo, co, yo = rest
    outer(flags, part, k0, ki, kx, zm, ym, side, edge, new)
    if double:
        for n, field in enumerate((new, other)):
            rims(flags, field, zo.at[n], co.at[n], yo.at[n])
    else:
        rims(flags, new, zo, co, yo)


def lists_kernel(flags, lists, spot, pick, at, obs):
    size, n = spot.shape
    depth = at.shape[1]
    steps = obs.shape[1]
    sub = flags[2]
    cell = lists[sub, steps : steps + 1, :]
    along = jnp.floor((cell + 0.5) * (1.0 / depth))
    same = lax.broadcasted_iota(jnp.int32, (n, n), 0) == lax.broadcasted_iota(jnp.int32, (n, n), 1)

    def column(row):
        return jnp.sum(jnp.where(same, row, 0.0), axis=1, keepdims=True).astype(jnp.int32)

    hot = lax.broadcasted_iota(jnp.int32, (size, n), 0) == along.astype(jnp.int32)
    spot[...] = hot.astype(F32).astype(BF16)
    hot = lax.broadcasted_iota(jnp.int32, (n, size), 1) == column(along)
    pick[...] = hot.astype(F32).astype(BF16)
    hot = lax.broadcasted_iota(jnp.int32, (n, depth), 1) == column(cell - along * depth)
    at[...] = hot.astype(F32)
    subs = lists.shape[0]
    chosen = lax.broadcasted_iota(jnp.int32, (CAP, n), 1) == (
        sub * CAP + lax.broadcasted_iota(jnp.int32, (CAP, n), 0))
    chosen = chosen.astype(F32).astype(BF16)
    traces = lists[:, 0:steps, :].reshape(subs * steps, n)
    high, mid = split(traces)
    low = (traces - high.astype(F32) - mid.astype(F32)).astype(BF16)
    sent = sum(
        lax.dot_general(chosen, part, (((1,), (1,)), ((), ())), preferred_element_type=F32)
        for part in (low, mid, high))
    for s in range(subs):
        obs[s * CAP : s * CAP + CAP, :] = sent[:, s * steps : s * steps + steps]


def injection(t, state, spot, pick, at, obs):
    high, low = split(state[...])
    seen = at[...] * (mm(pick[...], high) + mm(pick[...], low))
    residual = jnp.sum(seen, axis=1, keepdims=True) - obs[:, t : t + 1]
    high, low = split(at[...] * residual)
    return mm(spot[...], high) + mm(spot[...], low)


def adjoint_inner_kernel(t, flags, cur, prev, k0, ki, kx, kz, cm, near, deep, state, spot, pick,
                         at, obs, *rest):
    if len(rest) == 4:
        change, image, part, image_out = rest
        image_out[...] = cur[...] * change[...] + image[...]
    else:
        now, mid, before, part, image_out = rest
        image_out[...] = cur[...] * ((now[...] - mid[...]) - (mid[...] - before[...]))
    inj = injection(t, state, spot, pick, at, obs)
    inner(cur, prev, k0, ki, kx, kz, cm, near, deep, inj, part)


def adjoint_first_kernel(flags, cur, prev, k0, ki, kx, kz, cm, near, deep, part):
    inner(cur, prev, k0, ki, kx, kz, cm.at[1], near, deep, None, part)


def turn_kernel(t, flags, part, k0, ki, kx, zm, ym, side, edge, u_part, u_zm, u_ym, spot, pick, at, obs, new, u_new, zo, co, yo):
    outer(flags, part, k0, ki, kx, zm, ym, side, edge, new)
    outer(flags, u_part, k0, ki, kx, u_zm.at[1], u_ym.at[1], side, edge, u_new)
    u_new[...] += injection(t, new, spot, pick, at, obs)
    rims(flags, u_new, zo, co, yo)


def last_kernel(scale, flags, part, k0, ki, kx, zm, ym, side, edge, image, change, vel,
                new, mine, other):
    outer(flags, part, k0, ki, kx, zm, ym, side, edge, new)
    raw = (image[...] + new[...] * change[...]) * scale / vel[...]
    count, height, lanes = mine.shape
    chunk = raw.shape[1] // (2 * count)
    for n in range(count):
        even, odd = (
            jnp.concatenate(
                [raw[g * height : g * height + height, m * chunk : m * chunk + chunk]
                 for g in range(lanes // chunk)], axis=1)
            for m in (2 * n, 2 * n + 1))
        mine[n] = jnp.where(flags[0] == 0, even, odd)
        other[n] = jnp.where(flags[0] == 0, odd, even)


def join_kernel(flags, mine, got, *outs):
    for s, out in enumerate(outs):
        to = jnp.bitwise_xor(flags[3], s)
        a, b = mine[to], got[to]
        out[0] = jnp.where(flags[0] == 0, a, b)
        out[1] = jnp.where(flags[0] == 0, b, a)


def filter_kernel(flags, *refs):
    *pieces, out = refs
    height, lanes = pieces[0].shape[1:]
    chunk, rows, full = out.shape
    groups = lanes // chunk
    q = flags[3]
    shape = (full, full)
    y = lax.broadcasted_iota(jnp.int32, shape, 1)
    at = lax.broadcasted_iota(jnp.int32, shape, 0)
    within = jnp.bitwise_and(at, 2 * COLS - 1)
    place = jnp.bitwise_xor(q * (2 * COLS), at - within) + within
    weights = jnp.exp(jnp.abs(y - place).astype(F32) * (-1.0 / SMOOTH))
    weights = split(weights / jnp.sum(weights, axis=0, keepdims=True))
    for n in range(height // COLS):
        here = slice(n * COLS, n * COLS + COLS)
        lines = jnp.concatenate([piece[b, here, :] for piece in pieces for b in range(2)], axis=0)
        high, low = split(lines.T)
        done = mm(high, weights[0]) + mm(low, weights[0]) + mm(high, weights[1])
        for g in range(groups):
            out[:, g * (rows // groups) + n, :] = done[g * chunk : g * chunk + chunk]


def shaped(*shape):
    return jax.ShapeDtypeStruct(shape, F32)


def call(kernel, name, outs, *args, weight=0, far=0):
    specs = [pl.BlockSpec(memory_space=pltpu.SMEM)]
    specs += [pl.BlockSpec(memory_space=pl.ANY)] * far
    specs += [pl.BlockSpec(memory_space=pltpu.VMEM)] * (len(args) - 1 - far)
    return pl.pallas_call(
        kernel,
        name=name,
        out_shape=outs,
        in_specs=specs,
        out_specs=[pl.BlockSpec(memory_space=pltpu.VMEM)] * len(outs),
        scratch_shapes=[pltpu.SemaphoreType.DMA((far,))] if far else [],
        compiler_params=pltpu.CompilerParams(vmem_limit_bytes=VMEM_BYTES),
        cost_estimate=pl.CostEstimate(
            flops=1000, bytes_accessed=1000 + int(weight * 3_600_000), transcendentals=0),
    )(*args)


def per_device(plan, fwd_now, fwd_before, adj_now, adj_before, velocity, log_density, observed,
               rec_cells, rec_counts, src_cell, wavelet):
    rows, cols, depth = fwd_now.shape
    size = rows * cols
    steps = wavelet.shape[0]
    nx, nq = plan.nx, plan.nq
    subs = 2 * nx
    xline, c = lax.axis_index("xline"), lax.axis_index("inline")
    q, y = xline // 2, xline % 2
    keep = y == c
    z_perm, c_perm, y_perm, swap_perm = plan.z(), plan.core(), plan.y(), plan.swap()
    stages = [(c_perm, c), (y_perm, y)]
    stages += [(plan.flip(1 << b), (q >> b) & 1) for b in range((nq - 1).bit_length())]
    sub = (2 * q + c) * 2 + y
    flags = jnp.stack([c, y, sub, q] + [bit for pairs, bit in stages]).astype(jnp.int32)
    field = shaped(size, depth)
    side, edge = (size // 2, depth), (4 * cols, depth)
    rim = [shaped(*side), shaped(*side), shaped(*edge)]

    deep = depth_matrix(depth)
    deep = jnp.asarray(np.concatenate([deep, deep]), BF16)
    near = stencil_matrix(GROUP, cols)
    group, own, half = GROUP * cols, near.shape[1] - GROUP * 8, GROUP * 4
    both = [near[:, own : own + half], near[:, own + half :]]
    from_z = [np.concatenate([part[:group], part[2 * group :]]) for part in both]
    inside = jnp.where(c == 0, q > 0, q < nq - 1)
    side = jnp.where(c == 0, jnp.asarray(from_z[0], F32), jnp.asarray(from_z[1], F32))
    side = jnp.where(inside, side, 0.0).astype(BF16)
    side = jnp.concatenate([side, side], axis=1)
    core = jnp.where(c == 0, jnp.asarray(both[1], F32), jnp.asarray(both[0], F32)).astype(BF16)
    edge = jnp.where(y == 1, jnp.asarray(near[: 2 * group, : 4 * cols], F32),
                     jnp.asarray(near[: 2 * group, own - 4 * cols : own], F32)).astype(BF16)
    edge = jnp.concatenate([edge, edge], axis=1)
    near = jnp.asarray(np.concatenate([near[:, :own], near[:, :own]], axis=1), BF16)
    near = jnp.concatenate([near, core, core], axis=1)

    def halo(zo, co, yo):
        return send(zo, z_perm), send(co, c_perm), send(yo, y_perm)

    def after(value, *deps):
        return lax.optimization_barrier((value,) + deps)[0]

    def flat(value):
        return value.reshape(size, depth)

    log_density, fwd_now, velocity = flat(log_density), flat(fwd_now), flat(velocity)
    fwd_before, adj_now, adj_before = flat(fwd_before), flat(adj_now), flat(adj_before)
    got = [send(v, swap_perm) for v in (log_density, fwd_now)]
    got_model = send(jnp.stack([velocity, fwd_before]), swap_perm)
    density, p_now, *out = call(settle_kernel, "settle",
                                [field, field] + [shaped(2, *r.shape) for r in rim],
                                flags, log_density, fwd_now, *got, far=2)
    zm, cm, ym = halo(*out)
    got_adjoint = [send(after(v, density), swap_perm) for v in (adj_now, adj_before)]
    vel, p_before = call(settle_model_kernel, "settle_model", [field, field],
                         flags, velocity, fwd_before, got_model, weight=0.6, far=2)
    parts = call(first_inner_kernel, "first_inner", [field] * 7, flags, density, p_now, cm,
                 near, deep, weight=1.3)

    plane = nx * cols * depth
    src_i = src_cell // plane - y * rows
    src_x = src_cell // depth % (nx * cols) - (2 * q + c) * cols
    ok = (src_i >= 0) & (src_i < rows) & (src_x >= 0) & (src_x < cols)
    srow = jnp.where(ok, src_i * cols + src_x, -1)[None, :]
    sz = (src_cell % depth)[:, None]
    wave = wavelet.T

    rec_counts, rec_cells, observed = lax.optimization_barrier(
        (rec_counts, rec_cells, observed, density))[:3]
    live = jnp.arange(CAP)[None, :] < rec_counts[0][:, None]
    cells = jnp.where(live.reshape(-1), rec_cells[0], -1)
    lists = jnp.concatenate([observed, cells[None, :].astype(F32)], axis=0)[None]

    moved = send(lists, stages[0][0])

    inj, = call(functools.partial(source_kernel, 0), "source", [field], flags, srow, sz, wave,
                weight=0.6)
    grown = shaped(2, *lists.shape[1:])
    new, zo, co, yo, lists, *model = call(
        first_outer_kernel, "first_outer", [field] + rim + [grown] + [field] * 4, flags, p_now,
        p_before, vel, *parts, inj, zm, ym, side, edge, lists, moved)
    k0, ki, kx, kz = model
    states = [p_before, p_now, new]
    changes = []
    zm, cm, ym = halo(zo, co, yo)
    u_now, u_before = call(settle_adjoint_kernel, "settle_adjoint", [field, field], flags, adj_now,
                           adj_before, *got_adjoint, weight=0.6, far=2)
    double = 2
    for t in range(1, steps):
        cur, prev, before = states[:-4:-1]
        stage = t if t < len(stages) else None
        extra = [lists, send(lists, stages[t][0])] if stage is not None else []
        part, change = call(
            functools.partial(forward_inner_kernel, t), "forward_inner", [field, field], flags, cur,
            prev, *model, cm, near, deep, srow, sz, wave, before, weight=1.2)
        changes.append(change)
        args = [flags, part, k0, ki, kx, zm, ym, side, edge]
        if t == steps - 1:
            u_part, = call(adjoint_first_kernel, "adjoint_first", [field], flags, u_now, u_before,
                           *model, u_cm, near, deep, weight=1.1)
            slots = subs * CAP
            receivers = call(
                lists_kernel, "lists",
                [jax.ShapeDtypeStruct((size, slots), BF16),
                 jax.ShapeDtypeStruct((slots, size), BF16), shaped(slots, depth),
                 shaped(slots, steps)], flags, lists, weight=0.8)
            new, u_new, *out = call(
                functools.partial(turn_kernel, t), "turn", [field, field] + rim, *args, u_part,
                u_zm, u_ym, *receivers)
            states.append(new)
            break
        if t == double:
            args.append(u_now)
        outs = [field] + ([shaped(2, *r.shape) for r in rim] if t == double else rim)
        if extra:
            outs = outs + [shaped(2 * lists.shape[0], *lists.shape[1:])]
        new, *out = call(functools.partial(outer_kernel, stage, t == double), "forward_outer", outs,
                         *args, *extra)
        if extra:
            lists = out.pop()
        states.append(new)
        zm, cm, ym = halo(*out)
        if t == double:
            u_zm, u_cm, u_ym = zm, cm, ym

    zm, cm, ym = halo(*out)
    u_before, u_now = u_now, u_new
    image = []
    chunk = depth // nx
    half = shaped(nq, size * chunk // 128, 128)
    for j in range(1, steps):
        t = steps - 1 - j
        terms = [changes[t + 1], *image] if image else states[:-4:-1]
        part, *image = call(
            functools.partial(adjoint_inner_kernel, t), "adjoint_inner", [field, field], flags,
            u_now, u_before, *model, cm, near, deep, states[t + 2], *receivers, *terms, weight=1.5)
        args = [part, k0, ki, kx, zm, ym, side, edge]
        if j == steps - 1:
            got_prev = send(after(u_now, part), swap_perm)
            u_last, mine, other = call(
                functools.partial(last_kernel, 2.0 / steps), "last", [field, half, half],
                flags, *args, *image, changes[0], vel)
            break
        u_before = u_now
        u_now, *out = call(functools.partial(outer_kernel, None, False), "adjoint_outer", [field] + rim,
                           flags, *args)
        zm, cm, ym = halo(*out)

    got = send(u_last, swap_perm)
    pieces = call(join_kernel, "join", [shaped(2, *half.shape[1:])] * nq, flags,
                  after(mine, got_prev), send(other, c_perm))
    pieces = [send(value, plan.spread(s)) for s, value in enumerate(pieces)]
    adj_prev, = call(select_kernel, "select_previous", [field], flags, u_now, got_prev, weight=0.6)
    adj_out, = call(select_kernel, "select_state", [field], flags, u_last, got, weight=0.6)
    gradient, = call(filter_kernel, "filter", [shaped(chunk, rows, nx * cols)], flags, *pieces)
    block = (rows, cols, depth)
    return gradient, adj_out.reshape(block), adj_prev.reshape(block)


def solution(mesh):
    field = P(("shots", "inline"), "xline", None)
    model = P("inline", "xline", None)
    lists = P(("xline", "inline"), None)
    return jax.shard_map(
        functools.partial(per_device, Plan(mesh)),
        mesh=mesh,
        in_specs=(field, field, field, field, model, model, P("shots", ("xline", "inline")),
                  lists, lists, P("shots"), P("shots", None)),
        out_specs=(P(("shots", "xline"), "inline", None), field, field),
        check_vma=False,
    )
```

```python
import functools

import jax
import jax.numpy as jnp
import numpy as np
from jax import lax
from jax.experimental import pallas as pl
from jax.experimental.pallas import tpu as pltpu
from jax.sharding import PartitionSpec as P

CAP = 8
SMOOTH = 16
SECOND = (-205.0 / 72.0, 8.0 / 5.0, -1.0 / 5.0, 8.0 / 315.0, -1.0 / 560.0)
FIRST = (4.0 / 5.0, -1.0 / 5.0, 4.0 / 105.0, -1.0 / 280.0)
ALL = ("shots", "xline", "inline")
COLS = 8
GROUP = 8
VMEM_BYTES = 8 * 1024 * 1024
F32 = jnp.float32
BF16 = jnp.bfloat16


class Plan:
    def __init__(self, mesh):
        self.shots = mesh.shape["shots"]
        self.nx = mesh.shape["xline"]
        self.nq = self.nx // 2

    def index(self, s, q, y, c):
        return (s * self.nx + 2 * q + y) * 2 + c

    def perm(self, partner):
        pairs = []
        for s in range(self.shots):
            for q in range(self.nq):
                for y in range(2):
                    for c in range(2):
                        t = partner(q, y, c)
                        dst = self.index(s ^ 1, q, y, c) if t is None else self.index(s, *t)
                        pairs.append((self.index(s, q, y, c), dst))
        return pairs

    def swap(self):
        return self.perm(lambda q, y, c: None if y == c else (q, c, y))

    def z(self):
        def partner(q, y, c):
            other = q + 1 if c == 1 else q - 1
            return (other, y, 1 - c) if 0 <= other < self.nq else None

        return self.perm(partner)

    def core(self):
        return self.perm(lambda q, y, c: (q, y, 1 - c))

    def y(self):
        return self.perm(lambda q, y, c: (q, 1 - y, c))

    def flip(self, bit):
        return self.perm(lambda q, y, c: (q ^ bit, y, c) if (q ^ bit) < self.nq else None)

    def spread(self, shift):
        return self.perm(lambda q, y, c: (q ^ shift, c, y))


def send(value, pairs):
    return lax.ppermute(value, ALL, pairs)


def depth_matrix(n):
    m = np.zeros((n, 2 * n), np.float32)
    for k in range(1, 5):
        for j in range(n):
            for i, sign in ((j + k, 1.0), (j - k, -1.0)):
                if 0 <= i < n:
                    m[i, j] = round(SECOND[k] * 5040)
                    m[i, n + j] = sign * round(FIRST[k - 1] * 840)
    return m


def stencil_matrix(rows, cols):
    own = (rows + 8) * cols
    m = np.zeros((3, rows, cols, own + rows * 8), np.float32)
    for i in range(rows):
        for x in range(cols):
            for k in range(1, 5):
                total = round(SECOND[k] * 5040)
                slope = round(FIRST[k - 1] * 840)
                for sign in (1, -1):
                    at = (i + 4 + sign * k) * cols + x
                    m[0, i, x, at] += total
                    m[1, i, x, at] += sign * slope
                    to = x + sign * k
                    if to < 0:
                        at = own + i * 4 + to + 4
                    elif to >= cols:
                        at = own + rows * 4 + i * 4 + to - cols
                    else:
                        at = (i + 4) * cols + to
                    m[0, i, x, at] += total
                    m[2, i, x, at] += sign * slope
    return m.reshape(3 * rows * cols, own + rows * 8)


def split(value):
    high = value.astype(BF16)
    return high, (value - high.astype(F32)).astype(BF16)


def mm(a, b):
    return jnp.dot(a, b, preferred_element_type=F32)


def inner_differences(cur, cm, near, deep):
    depth = cur.shape[1]
    size = GROUP * COLS
    cm = cm.at[0] if len(cm.shape) == 3 else cm
    own = split(cur[...])
    along = mm(jnp.concatenate(own, axis=1), deep[...])
    blank = jnp.zeros((4 * COLS, depth), BF16)
    ext = [jnp.concatenate([blank, part, blank], axis=0) for part in own]
    from_c = split(cm[...])
    for n in range(cur.shape[0] // size):
        here = slice(n * size, n * size + size)
        sides = slice(n * GROUP * 4, n * GROUP * 4 + GROUP * 4)
        rhs = [part[n * size : n * size + size + 8 * COLS] for part in ext]
        rhs += [part[sides] for part in from_c]
        out = mm(near[...], jnp.concatenate(rhs, axis=0))
        yield (here, out[0:size], along[here, 0:depth], out[size : 2 * size], out[2 * size :],
               along[here, depth:])


def side_differences(rows, zm, side):
    size = GROUP * COLS
    zm = zm.at[0] if len(zm.shape) == 3 else zm
    from_z = split(zm[...])
    for n in range(rows // size):
        sides = slice(n * GROUP * 4, n * GROUP * 4 + GROUP * 4)
        out = mm(side[...], jnp.concatenate([part[sides] for part in from_z], axis=0))
        yield slice(n * size, n * size + size), out[0:size], out[size:]


def edge_differences(flags, rows, ym, edge):
    size = GROUP * COLS
    ym = ym.at[0] if len(ym.shape) == 3 else ym
    out = mm(edge[...], jnp.concatenate(split(ym[...]), axis=0))
    start = jnp.where(flags[1] == 1, 0, rows - size)
    return pl.ds(pl.multiple_of(start, size), size), out[0:size], out[size:]


def halves(value):
    rows, depth = value.shape
    pairs = value.reshape(rows // (2 * COLS), 2, COLS, depth)
    a, b = pairs[:, 0], pairs[:, 1]
    low = lax.broadcasted_iota(jnp.int32, a.shape, 1) < 4
    first = jnp.where(low, a, pltpu.roll(b, 4, axis=1))
    last = jnp.where(low, pltpu.roll(a, 4, axis=1), b)
    return first.reshape(rows // 2, depth), last.reshape(rows // 2, depth)


def rims(flags, new, zo, co, yo):
    first, last = halves(new[...])
    zo[...] = jnp.where(flags[0] == 0, first, last)
    co[...] = jnp.where(flags[0] == 0, last, first)
    size = new.shape[0]
    yo[...] = jnp.where(flags[1] == 0, new[size - 4 * COLS :], new[0 : 4 * COLS])


def choose(flags, pairs, sems):
    keep = flags[0] == flags[1]

    @pl.when(keep)
    def _():
        copies = [pltpu.make_async_copy(own, out, sems.at[n])
                  for n, (own, recv, out) in enumerate(pairs)]
        for copy in copies:
            copy.start()
        for copy in copies:
            copy.wait()

    @pl.when(jnp.logical_not(keep))
    def _():
        for own, recv, out in pairs:
            out[...] = recv[...]


def settle_kernel(flags, a, b, recv_a, recv_b, a_out, b_out, zo, co, yo, sems):
    choose(flags, [(a, recv_a, a_out), (b, recv_b, b_out)], sems)
    for n, out in enumerate((a_out, b_out)):
        rims(flags, out, zo.at[n], co.at[n], yo.at[n])


def settle_model_kernel(flags, a, b, recv, a_out, b_out, sems):
    choose(flags, [(a, recv.at[0], a_out), (b, recv.at[1], b_out)], sems)


def settle_adjoint_kernel(flags, a, recv, out, sems):
    choose(flags, [(a, recv, out)], sems)


def select_kernel(flags, own, recv, out):
    out[...] = jnp.where(flags[0] == flags[1], own[...], recv[...])


def first_inner_kernel(flags, lr, cur, cm, near, deep, *outs):
    ri, rx, rz, sums_out, di_out, dx_out, dz_out = outs
    for here, spare, spare_z, di, dx, dz in inner_differences(lr, cm.at[0], near, deep):
        ri[here], rx[here], rz[here] = di, dx, dz
    for here, sums, sums_z, di, dx, dz in inner_differences(cur, cm.at[1], near, deep):
        sums_out[here] = sums + sums_z + (3.0 * SECOND[0] * 5040) * cur[here]
        di_out[here], dx_out[here], dz_out[here] = di, dx, dz


def first_outer_kernel(flags, cur, prev, vel, ri, rx, rz, sums, di, dx, dz, inj, zm, ym, side,
                       edge, mine, got, new, zo, co, yo, k0, ki, kx, kz, *lists):
    rows = cur.shape[0]
    trade(0, flags, mine, got, *lists)
    kz[...] = sums[...]
    ki[...] = di[...]
    here, more, more_i = edge_differences(flags, rows, ym.at[1], edge)
    kz[here] += more
    ki[here] += more_i
    lr_here, spare, lr_more_i = edge_differences(flags, rows, ym.at[0], edge)
    k0[...] = ri[...]
    k0[lr_here] += lr_more_i
    first = side_differences(rows, zm.at[0], side)
    second = side_differences(rows, zm.at[1], side)
    for (here, spare, more_r), (spare_here, more, more_x) in zip(first, second):
        square = vel[here] * vel[here]
        scaled = square * (1.0 / (840 * 840))
        factor = square * (1.0 / 5040)
        along_i, along_x, along_z = scaled * k0[here], scaled * (rx[here] + more_r), scaled * rz[here]
        change = factor * (kz[here] + more) - (
            along_i * ki[here] + along_x * (dx[here] + more_x) + along_z * dz[here])
        k0[here], ki[here], kx[here], kz[here] = factor, along_i, along_x, along_z
        center = cur[here]
        new[here] = (center - prev[here]) + (center + (change + inj[here]))
    rims(flags, new, zo, co, yo)


def inner(cur, prev, k0, ki, kx, kz, cm, near, deep, inj, out):
    for here, sums, sums_z, di, dx, dz in inner_differences(cur, cm, near, deep):
        center = cur[here]
        change = k0[here] * ((sums + sums_z) + (3.0 * SECOND[0] * 5040) * center)
        change = change - (ki[here] * di + kx[here] * dx + kz[here] * dz)
        if inj is not None:
            change = change + inj[here]
        out[here] = (center - prev[here]) + (center + change)


def outer(flags, part, k0, ki, kx, zm, ym, side, edge, new):
    rows = part.shape[0]
    for here, sums, dx in side_differences(rows, zm, side):
        new[here] = part[here] + (k0[here] * sums - kx[here] * dx)
    here, sums, di = edge_differences(flags, rows, ym, edge)
    new[here] += k0[here] * sums - ki[here] * di


def other_half(stage, flags, count):
    other = 1 - flags[4 + stage]
    for n in range(count // 2):
        high, low = n >> stage, n & ((1 << stage) - 1)
        yield n, (high << (stage + 1)) + (other << stage) + low


def trade(stage, flags, mine, got, out, give=None):
    out[...] = mine[...]
    for n, at in other_half(stage, flags, out.shape[0]):
        out[at] = got[n]
    if give is not None:
        for n, at in other_half(stage + 1, flags, out.shape[0]):
            give[n] = out[at]


def source_kernel(step, flags, srow, sz, wave, out):
    size, depth = out.shape
    n = srow.shape[1]
    spot = lax.broadcasted_iota(jnp.int32, (size, n), 0) == srow[...]
    spot = spot.astype(F32).astype(BF16)
    high, low = split(jnp.where(
        lax.broadcasted_iota(jnp.int32, (n, depth), 1) == sz[...], wave[:, step : step + 1], 0.0))
    out[...] = mm(spot, high) + mm(spot, low)


def forward_inner_kernel(step, flags, cur, prev, k0, ki, kx, kz, cm, near, deep, srow, sz, wave,
                         before, part, change):
    source_kernel(step, flags, srow, sz, wave, change)
    inner(cur, prev, k0, ki, kx, kz, cm, near, deep, change, part)
    change[...] = (cur[...] - prev[...]) - (prev[...] - before[...])


def outer_kernel(stage, double, flags, part, k0, ki, kx, zm, ym, side, edge, *rest):
    rest = list(rest)
    other = rest.pop(0) if double else None
    if stage is not None:
        mine, got, new, zo, co, yo, *lists = rest
        trade(stage, flags, mine, got, *lists)
    else:
        new, zo, co, yo = rest
    outer(flags, part, k0, ki, kx, zm, ym, side, edge, new)
    if double:
        for n, field in enumerate((new, other)):
            rims(flags, field, zo.at[n], co.at[n], yo.at[n])
    else:
        rims(flags, new, zo, co, yo)


def lists_kernel(flags, lists, spot, pick, at, obs):
    size, n = spot.shape
    depth = at.shape[1]
    subs, steps = lists.shape[0], obs.shape[1]
    whole = n // 128
    cell = jnp.concatenate(
        [jnp.sum(lists[:, m, :], axis=0, keepdims=True) for m in range(whole)], axis=1)
    along = jnp.floor((cell + 0.5) * (1.0 / depth))
    same = lax.broadcasted_iota(jnp.int32, (n, n), 0) == lax.broadcasted_iota(jnp.int32, (n, n), 1)

    def column(row):
        return jnp.sum(jnp.where(same, row, 0.0), axis=1, keepdims=True).astype(jnp.int32)

    hot = lax.broadcasted_iota(jnp.int32, (size, n), 0) == along.astype(jnp.int32)
    spot[...] = hot.astype(F32).astype(BF16)
    hot = lax.broadcasted_iota(jnp.int32, (n, size), 1) == column(along)
    pick[...] = hot.astype(F32).astype(BF16)
    hot = lax.broadcasted_iota(jnp.int32, (n, depth), 1) == column(cell - along * depth)
    at[...] = hot.astype(F32)
    traces = lists[:, whole, :]
    for k in range(CAP):
        obs[k * subs : k * subs + subs, :] = traces[:, k * steps : k * steps + steps]


def injection(t, state, spot, pick, at, obs):
    high, low = split(state[...])
    seen = at[...] * (mm(pick[...], high) + mm(pick[...], low))
    residual = jnp.sum(seen, axis=1, keepdims=True) - obs[:, t : t + 1]
    high, low = split(at[...] * residual)
    return mm(spot[...], high) + mm(spot[...], low)


def adjoint_inner_kernel(t, flags, cur, prev, k0, ki, kx, kz, cm, near, deep, state, spot, pick,
                         at, obs, *rest):
    if len(rest) == 4:
        change, image, part, image_out = rest
        image_out[...] = cur[...] * change[...] + image[...]
    else:
        now, mid, before, part, image_out = rest
        image_out[...] = cur[...] * ((now[...] - mid[...]) - (mid[...] - before[...]))
    inj = injection(t, state, spot, pick, at, obs)
    inner(cur, prev, k0, ki, kx, kz, cm, near, deep, inj, part)


def adjoint_first_kernel(flags, cur, prev, k0, ki, kx, kz, cm, near, deep, part):
    inner(cur, prev, k0, ki, kx, kz, cm.at[1], near, deep, None, part)


def turn_kernel(t, flags, part, k0, ki, kx, zm, ym, side, edge, u_part, u_zm, u_ym, spot, pick, at, obs, new, u_new, zo, co, yo):
    outer(flags, part, k0, ki, kx, zm, ym, side, edge, new)
    outer(flags, u_part, k0, ki, kx, u_zm.at[1], u_ym.at[1], side, edge, u_new)
    u_new[...] += injection(t, new, spot, pick, at, obs)
    rims(flags, u_new, zo, co, yo)


def last_kernel(scale, flags, part, k0, ki, kx, zm, ym, side, edge, image, change, vel,
                new, mine, other):
    outer(flags, part, k0, ki, kx, zm, ym, side, edge, new)
    raw = (image[...] + new[...] * change[...]) * scale / vel[...]
    count, height, lanes = mine.shape
    chunk = raw.shape[1] // (2 * count)
    for n in range(count):
        even, odd = (
            jnp.concatenate(
                [raw[g * height : g * height + height, m * chunk : m * chunk + chunk]
                 for g in range(lanes // chunk)], axis=1)
            for m in (2 * n, 2 * n + 1))
        mine[n] = jnp.where(flags[0] == 0, even, odd)
        other[n] = jnp.where(flags[0] == 0, odd, even)


def join_kernel(flags, mine, got, *outs):
    for s, out in enumerate(outs):
        to = jnp.bitwise_xor(flags[3], s)
        a, b = mine[to], got[to]
        out[0] = jnp.where(flags[0] == 0, a, b)
        out[1] = jnp.where(flags[0] == 0, b, a)


def filter_kernel(flags, *refs):
    *pieces, out = refs
    height, lanes = pieces[0].shape[1:]
    chunk, rows, full = out.shape
    groups = lanes // chunk
    q = flags[3]
    shape = (full, full)
    y = lax.broadcasted_iota(jnp.int32, shape, 1)
    at = lax.broadcasted_iota(jnp.int32, shape, 0)
    within = jnp.bitwise_and(at, 2 * COLS - 1)
    place = jnp.bitwise_xor(q * (2 * COLS), at - within) + within
    weights = jnp.exp(jnp.abs(y - place).astype(F32) * (-1.0 / SMOOTH))
    weights = split(weights / jnp.sum(weights, axis=0, keepdims=True))
    ready = []
    for n in range(height // COLS):
        here = slice(n * COLS, n * COLS + COLS)
        lines = jnp.concatenate([piece[b, here, :] for piece in pieces for b in range(2)], axis=0)
        high, low = split(lines.T)
        done = mm(high, weights[0]) + mm(low, weights[0]) + mm(high, weights[1])
        ready.append(done)
    for g in range(groups):
        lines = jnp.stack([done[g * chunk : g * chunk + chunk] for done in ready], axis=0)
        out[:, g * (rows // groups) : (g + 1) * (rows // groups), :] = jnp.swapaxes(lines, 0, 1)


def shaped(*shape):
    return jax.ShapeDtypeStruct(shape, F32)


def call(kernel, name, outs, *args, weight=0, far=0):
    specs = [pl.BlockSpec(memory_space=pltpu.SMEM)]
    specs += [pl.BlockSpec(memory_space=pl.ANY)] * far
    specs += [pl.BlockSpec(memory_space=pltpu.VMEM)] * (len(args) - 1 - far)
    return pl.pallas_call(
        kernel,
        name=name,
        out_shape=outs,
        in_specs=specs,
        out_specs=[pl.BlockSpec(memory_space=pltpu.VMEM)] * len(outs),
        scratch_shapes=[pltpu.SemaphoreType.DMA((far,))] if far else [],
        compiler_params=pltpu.CompilerParams(vmem_limit_bytes=VMEM_BYTES),
        cost_estimate=pl.CostEstimate(
            flops=1000, bytes_accessed=1000 + int(weight * 3_600_000), transcendentals=0),
    )(*args)


def per_device(plan, fwd_now, fwd_before, adj_now, adj_before, velocity, log_density, observed,
               rec_cells, rec_counts, src_cell, wavelet):
    rows, cols, depth = fwd_now.shape
    size = rows * cols
    steps = wavelet.shape[0]
    nx, nq = plan.nx, plan.nq
    subs = 2 * nx
    xline, c = lax.axis_index("xline"), lax.axis_index("inline")
    q, y = xline // 2, xline % 2
    keep = y == c
    z_perm, c_perm, y_perm, swap_perm = plan.z(), plan.core(), plan.y(), plan.swap()
    stages = [(c_perm, c), (y_perm, y)]
    stages += [(plan.flip(1 << b), (q >> b) & 1) for b in range((nq - 1).bit_length())]
    sub = (2 * q + c) * 2 + y
    flags = jnp.stack([c, y, sub, q] + [bit for pairs, bit in stages]).astype(jnp.int32)
    field = shaped(size, depth)
    side, edge = (size // 2, depth), (4 * cols, depth)
    rim = [shaped(*side), shaped(*side), shaped(*edge)]

    deep = depth_matrix(depth)
    deep = jnp.asarray(np.concatenate([deep, deep]), BF16)
    near = stencil_matrix(GROUP, cols)
    group, own, half = GROUP * cols, near.shape[1] - GROUP * 8, GROUP * 4
    both = [near[:, own : own + half], near[:, own + half :]]
    from_z = [np.concatenate([part[:group], part[2 * group :]]) for part in both]
    inside = jnp.where(c == 0, q > 0, q < nq - 1)
    side = jnp.where(c == 0, jnp.asarray(from_z[0], F32), jnp.asarray(from_z[1], F32))
    side = jnp.where(inside, side, 0.0).astype(BF16)
    side = jnp.concatenate([side, side], axis=1)
    core = jnp.where(c == 0, jnp.asarray(both[1], F32), jnp.asarray(both[0], F32)).astype(BF16)
    edge = jnp.where(y == 1, jnp.asarray(near[: 2 * group, : 4 * cols], F32),
                     jnp.asarray(near[: 2 * group, own - 4 * cols : own], F32)).astype(BF16)
    edge = jnp.concatenate([edge, edge], axis=1)
    near = jnp.asarray(np.concatenate([near[:, :own], near[:, :own]], axis=1), BF16)
    near = jnp.concatenate([near, core, core], axis=1)

    def halo(zo, co, yo):
        return send(zo, z_perm), send(co, c_perm), send(yo, y_perm)

    def after(value, *deps):
        return lax.optimization_barrier((value,) + deps)[0]

    def flat(value):
        return value.reshape(size, depth)

    log_density, fwd_now, velocity = flat(log_density), flat(fwd_now), flat(velocity)
    fwd_before, adj_now, adj_before = flat(fwd_before), flat(adj_now), flat(adj_before)
    got = [send(v, swap_perm) for v in (log_density, fwd_now)]
    stacked = jnp.stack([velocity, fwd_before])
    got_model = send(stacked, swap_perm)
    plane = nx * cols * depth
    src_i = src_cell // plane - y * rows
    src_x = src_cell // depth % (nx * cols) - (2 * q + c) * cols
    ok = (src_i >= 0) & (src_i < rows) & (src_x >= 0) & (src_x < cols)
    srow = jnp.where(ok, src_i * cols + src_x, -1)[None, :]
    sz = (src_cell % depth)[:, None]
    wave = wavelet.T

    inj, = call(functools.partial(source_kernel, 0), "source", [field], flags, srow, sz, wave,
                weight=0.6)

    slots = subs * CAP
    live = jnp.arange(CAP)[None, :] < rec_counts[0][:, None]
    cells = jnp.where(live, rec_cells[0].reshape(subs, CAP), -1).T.reshape(1, slots).astype(F32)
    worker = (2 * q + c) * 2 + y
    cells = jnp.where(jnp.arange(subs)[:, None] == worker, cells, 0.0)
    traces = observed.reshape(steps, nq, 2, 2, CAP).transpose(1, 3, 2, 4, 0).reshape(subs, CAP * steps)
    spare = jnp.zeros((subs, 128 - CAP * steps), F32)
    lists = jnp.concatenate([cells, traces, spare], axis=1).reshape(subs, -1, 128)
    give = lax.dynamic_index_in_dim(lists.reshape(subs // 2, 2, -1, 128), 1 - c, 1, keepdims=False)
    give, flags, inj = lax.optimization_barrier((give, flags, inj))
    got_list = send(give, stages[0][0])

    density, p_now, *out = call(settle_kernel, "settle",
                                [field, field] + [shaped(2, *r.shape) for r in rim],
                                flags, log_density, fwd_now, *got, far=2)
    zm, cm, ym = halo(*out)
    vel, p_before = call(settle_model_kernel, "settle_model", [field, field],
                         flags, velocity, fwd_before, got_model, weight=0.6, far=2)
    parts = call(first_inner_kernel, "first_inner", [field] * 7, flags, density, p_now, cm,
                 near, deep, weight=1.3)

    entries, half_entries = shaped(*lists.shape), shaped(*give.shape)
    new, zo, co, yo, k0, ki, kx, kz, lists, give = call(
        first_outer_kernel, "first_outer", [field] + rim + [field] * 4 + [entries, half_entries],
        flags, p_now, p_before, vel, *parts, inj, zm, ym, side, edge, lists, got_list)
    model = (k0, ki, kx, kz)
    states = [p_before, p_now, new]
    changes = []
    zm, cm, ym = halo(zo, co, yo)
    double = 3
    for t in range(1, steps):
        cur, prev, before = states[:-4:-1]
        stage = t if t < len(stages) else None
        extra = [lists, send(give, stages[t][0])] if stage is not None else []
        part, change = call(
            functools.partial(forward_inner_kernel, t), "forward_inner", [field, field], flags, cur,
            prev, *model, cm, near, deep, srow, sz, wave, before, weight=1.2)
        changes.append(change)
        args = [flags, part, k0, ki, kx, zm, ym, side, edge]
        if t == steps - 1:
            u_before, = call(settle_adjoint_kernel, "settle_before", [field], flags, adj_before,
                             got_before, weight=0.6, far=1)
            u_part, = call(adjoint_first_kernel, "adjoint_first", [field], flags, u_now, u_before,
                           *model, u_cm, near, deep, weight=1.1)
            receivers = call(
                lists_kernel, "lists",
                [jax.ShapeDtypeStruct((size, slots), BF16),
                 jax.ShapeDtypeStruct((slots, size), BF16), shaped(slots, depth),
                 shaped(slots, steps)], flags, lists, weight=0.8)
            new, u_new, *out = call(
                functools.partial(turn_kernel, t), "turn", [field, field] + rim, *args, u_part,
                u_zm, u_ym, *receivers)
            states.append(new)
            break
        if t == 1:
            got_now = send(after(adj_now, ym), swap_perm)
        if t == 4:
            got_before = send(after(adj_before, ym), swap_perm)
        if t == double:
            u_now, = call(settle_adjoint_kernel, "settle_adjoint", [field], flags, adj_now, got_now,
                          weight=0.6, far=1)
            args.append(u_now)
        outs = [field] + ([shaped(2, *r.shape) for r in rim] if t == double else rim)
        if extra:
            outs = outs + [entries] + ([half_entries] if t + 1 < len(stages) else [])
        new, *out = call(functools.partial(outer_kernel, stage, t == double), "forward_outer", outs,
                         *args, *extra)
        if extra:
            out, (lists, *give) = out[:3], out[3:]
            give = give[0] if give else None
        states.append(new)
        zm, cm, ym = halo(*out)
        if t == double:
            u_zm, u_cm, u_ym = zm, cm, ym

    zm, cm, ym = halo(*out)
    u_before, u_now = u_now, u_new
    image = []
    chunk = depth // nx
    half = shaped(nq, size * chunk // 128, 128)
    for j in range(1, steps):
        t = steps - 1 - j
        terms = [changes[t + 1], *image] if image else states[:-4:-1]
        part, *image = call(
            functools.partial(adjoint_inner_kernel, t), "adjoint_inner", [field, field], flags,
            u_now, u_before, *model, cm, near, deep, states[t + 2], *receivers, *terms, weight=1.5)
        args = [part, k0, ki, kx, zm, ym, side, edge]
        if j == steps - 1:
            got_prev = send(after(u_now, ym), swap_perm)
            u_last, mine, other = call(
                functools.partial(last_kernel, 2.0 / steps), "last", [field, half, half],
                flags, *args, *image, changes[0], vel)
            break
        u_before = u_now
        u_now, *out = call(functools.partial(outer_kernel, None, False), "adjoint_outer", [field] + rim,
                           flags, *args)
        zm, cm, ym = halo(*out)

    got = send(u_last, swap_perm)
    pieces = call(join_kernel, "join", [shaped(2, *half.shape[1:])] * nq, flags,
                  after(mine, got_prev), send(other, c_perm))
    pieces = [send(pieces[s], plan.spread(s)) for s in reversed(range(nq))][::-1]
    adj_prev, = call(select_kernel, "select_previous", [field], flags, u_now, got_prev, weight=0.6)
    adj_out, = call(select_kernel, "select_state", [field], flags, u_last, got, weight=0.6)
    gradient, = call(filter_kernel, "filter", [shaped(chunk, rows, nx * cols)], flags, *pieces)
    block = (rows, cols, depth)
    return gradient, adj_out.reshape(block), adj_prev.reshape(block)


def solution(mesh):
    field = P(("shots", "inline"), "xline", None)
    model = P("inline", "xline", None)
    lists = P(("xline", "inline"), None)
    return jax.shard_map(
        functools.partial(per_device, Plan(mesh)),
        mesh=mesh,
        in_specs=(field, field, field, field, model, model, P("shots", ("xline", "inline")),
                  lists, lists, P("shots"), P("shots", None)),
        out_specs=(P(("shots", "xline"), "inline", None), field, field),
        check_vma=False,
    )
```

```python
import functools

import jax
import jax.numpy as jnp
import numpy as np
from jax import lax
from jax.experimental import pallas as pl
from jax.experimental.pallas import tpu as pltpu
from jax.sharding import PartitionSpec as P

CAP = 8
SMOOTH = 16
SECOND = (-205.0 / 72.0, 8.0 / 5.0, -1.0 / 5.0, 8.0 / 315.0, -1.0 / 560.0)
FIRST = (4.0 / 5.0, -1.0 / 5.0, 4.0 / 105.0, -1.0 / 280.0)
ALL = ("shots", "xline", "inline")
COLS = 8
GROUP = 8
VMEM_BYTES = 8 * 1024 * 1024
F32 = jnp.float32
BF16 = jnp.bfloat16


class Plan:
    def __init__(self, mesh):
        self.shots = mesh.shape["shots"]
        self.nx = mesh.shape["xline"]
        self.nq = self.nx // 2

    def index(self, s, q, y, c):
        return (s * self.nx + 2 * q + y) * 2 + c

    def perm(self, partner):
        pairs = []
        for s in range(self.shots):
            for q in range(self.nq):
                for y in range(2):
                    for c in range(2):
                        t = partner(q, y, c)
                        dst = self.index(s ^ 1, q, y, c) if t is None else self.index(s, *t)
                        pairs.append((self.index(s, q, y, c), dst))
        return pairs

    def swap(self):
        return self.perm(lambda q, y, c: None if y == c else (q, c, y))

    def z(self):
        def partner(q, y, c):
            other = q + 1 if c == 1 else q - 1
            return (other, y, 1 - c) if 0 <= other < self.nq else None

        return self.perm(partner)

    def core(self):
        return self.perm(lambda q, y, c: (q, y, 1 - c))

    def y(self):
        return self.perm(lambda q, y, c: (q, 1 - y, c))

    def flip(self, bit):
        return self.perm(lambda q, y, c: (q ^ bit, y, c) if (q ^ bit) < self.nq else None)

    def spread(self, shift):
        return self.perm(lambda q, y, c: (q ^ shift, c, y))


def send(value, pairs):
    return lax.ppermute(value, ALL, pairs)


def depth_matrix(n):
    m = np.zeros((n, 2 * n), np.float32)
    for k in range(1, 5):
        for j in range(n):
            for i, sign in ((j + k, 1.0), (j - k, -1.0)):
                if 0 <= i < n:
                    m[i, j] = round(SECOND[k] * 5040)
                    m[i, n + j] = sign * round(FIRST[k - 1] * 840)
    return m


def stencil_matrix(rows, cols):
    own = (rows + 8) * cols
    m = np.zeros((3, rows, cols, own + rows * 8), np.float32)
    for i in range(rows):
        for x in range(cols):
            for k in range(1, 5):
                total = round(SECOND[k] * 5040)
                slope = round(FIRST[k - 1] * 840)
                for sign in (1, -1):
                    at = (i + 4 + sign * k) * cols + x
                    m[0, i, x, at] += total
                    m[1, i, x, at] += sign * slope
                    to = x + sign * k
                    if to < 0:
                        at = own + i * 4 + to + 4
                    elif to >= cols:
                        at = own + rows * 4 + i * 4 + to - cols
                    else:
                        at = (i + 4) * cols + to
                    m[0, i, x, at] += total
                    m[2, i, x, at] += sign * slope
    return m.reshape(3 * rows * cols, own + rows * 8)


def split(value):
    high = value.astype(BF16)
    return high, (value - high.astype(F32)).astype(BF16)


def mm(a, b):
    return jnp.dot(a, b, preferred_element_type=F32)


def inner_differences(cur, cm, near, deep):
    depth = cur.shape[1]
    size = GROUP * COLS
    cm = cm.at[0] if len(cm.shape) == 3 else cm
    own = split(cur[...])
    along = mm(jnp.concatenate(own, axis=1), deep[...])
    blank = jnp.zeros((4 * COLS, depth), BF16)
    ext = [jnp.concatenate([blank, part, blank], axis=0) for part in own]
    from_c = split(cm[...])
    for n in range(cur.shape[0] // size):
        here = slice(n * size, n * size + size)
        sides = slice(n * GROUP * 4, n * GROUP * 4 + GROUP * 4)
        rhs = [part[n * size : n * size + size + 8 * COLS] for part in ext]
        rhs += [part[sides] for part in from_c]
        out = mm(near[...], jnp.concatenate(rhs, axis=0))
        yield (here, out[0:size], along[here, 0:depth], out[size : 2 * size], out[2 * size :],
               along[here, depth:])


def side_differences(rows, zm, side):
    size = GROUP * COLS
    zm = zm.at[0] if len(zm.shape) == 3 else zm
    from_z = split(zm[...])
    for n in range(rows // size):
        sides = slice(n * GROUP * 4, n * GROUP * 4 + GROUP * 4)
        out = mm(side[...], jnp.concatenate([part[sides] for part in from_z], axis=0))
        yield slice(n * size, n * size + size), out[0:size], out[size:]


def edge_differences(flags, rows, ym, edge):
    size = GROUP * COLS
    ym = ym.at[0] if len(ym.shape) == 3 else ym
    out = mm(edge[...], jnp.concatenate(split(ym[...]), axis=0))
    start = jnp.where(flags[1] == 1, 0, rows - size)
    return pl.ds(pl.multiple_of(start, size), size), out[0:size], out[size:]


def halves(value):
    rows, depth = value.shape
    pairs = value.reshape(rows // (2 * COLS), 2, COLS, depth)
    a, b = pairs[:, 0], pairs[:, 1]
    low = lax.broadcasted_iota(jnp.int32, a.shape, 1) < 4
    first = jnp.where(low, a, pltpu.roll(b, 4, axis=1))
    last = jnp.where(low, pltpu.roll(a, 4, axis=1), b)
    return first.reshape(rows // 2, depth), last.reshape(rows // 2, depth)


def rims(flags, new, zo, co, yo):
    first, last = halves(new[...])
    zo[...] = jnp.where(flags[0] == 0, first, last)
    co[...] = jnp.where(flags[0] == 0, last, first)
    size = new.shape[0]
    yo[...] = jnp.where(flags[1] == 0, new[size - 4 * COLS :], new[0 : 4 * COLS])


def choose(flags, pairs, sems):
    keep = flags[0] == flags[1]

    @pl.when(keep)
    def _():
        copies = [pltpu.make_async_copy(own, out, sems.at[n])
                  for n, (own, recv, out) in enumerate(pairs)]
        for copy in copies:
            copy.start()
        for copy in copies:
            copy.wait()

    @pl.when(jnp.logical_not(keep))
    def _():
        for own, recv, out in pairs:
            out[...] = recv[...]


def settle_kernel(flags, a, b, recv_a, recv_b, a_out, b_out, zo, co, yo, sems):
    choose(flags, [(a, recv_a, a_out), (b, recv_b, b_out)], sems)
    for n, out in enumerate((a_out, b_out)):
        rims(flags, out, zo.at[n], co.at[n], yo.at[n])


def settle_pair_kernel(flags, a, b, recv, a_out, b_out, sems):
    choose(flags, [(a, recv.at[0], a_out), (b, recv.at[1], b_out)], sems)


def select_kernel(flags, own, recv, *outs):
    keep = flags[0] == flags[1]
    for n, out in enumerate(outs):
        out[...] = jnp.where(keep, own[n], recv[n])


def first_inner_kernel(flags, lr, cur, cm, near, deep, *outs):
    ri, rx, rz, sums_out, di_out, dx_out, dz_out = outs
    for here, spare, spare_z, di, dx, dz in inner_differences(lr, cm.at[0], near, deep):
        ri[here], rx[here], rz[here] = di, dx, dz
    for here, sums, sums_z, di, dx, dz in inner_differences(cur, cm.at[1], near, deep):
        sums_out[here] = sums + sums_z + (3.0 * SECOND[0] * 5040) * cur[here]
        di_out[here], dx_out[here], dz_out[here] = di, dx, dz


def first_outer_kernel(flags, cur, prev, vel, ri, rx, rz, sums, di, dx, dz, inj, zm, ym, side,
                       edge, mine, got, new, zo, co, yo, k0, ki, kx, kz, *lists):
    rows = cur.shape[0]
    trade(0, flags, mine, got, *lists)
    kz[...] = sums[...]
    ki[...] = di[...]
    here, more, more_i = edge_differences(flags, rows, ym.at[1], edge)
    kz[here] += more
    ki[here] += more_i
    lr_here, spare, lr_more_i = edge_differences(flags, rows, ym.at[0], edge)
    k0[...] = ri[...]
    k0[lr_here] += lr_more_i
    first = side_differences(rows, zm.at[0], side)
    second = side_differences(rows, zm.at[1], side)
    for (here, spare, more_r), (spare_here, more, more_x) in zip(first, second):
        square = vel[here] * vel[here]
        scaled = square * (1.0 / (840 * 840))
        factor = square * (1.0 / 5040)
        along_i, along_x, along_z = scaled * k0[here], scaled * (rx[here] + more_r), scaled * rz[here]
        change = factor * (kz[here] + more) - (
            along_i * ki[here] + along_x * (dx[here] + more_x) + along_z * dz[here])
        k0[here], ki[here], kx[here], kz[here] = factor, along_i, along_x, along_z
        center = cur[here]
        new[here] = (center - prev[here]) + (center + (change + inj[here]))
    rims(flags, new, zo, co, yo)


def inner(cur, prev, k0, ki, kx, kz, cm, near, deep, inj, out):
    for here, sums, sums_z, di, dx, dz in inner_differences(cur, cm, near, deep):
        center = cur[here]
        change = k0[here] * ((sums + sums_z) + (3.0 * SECOND[0] * 5040) * center)
        change = change - (ki[here] * di + kx[here] * dx + kz[here] * dz)
        if inj is not None:
            change = change + inj[here]
        out[here] = (center - prev[here]) + (center + change)


def outer(flags, part, k0, ki, kx, zm, ym, side, edge, new):
    rows = part.shape[0]
    for here, sums, dx in side_differences(rows, zm, side):
        new[here] = part[here] + (k0[here] * sums - kx[here] * dx)
    here, sums, di = edge_differences(flags, rows, ym, edge)
    new[here] += k0[here] * sums - ki[here] * di


def other_half(stage, flags, count):
    other = 1 - flags[4 + stage]
    for n in range(count // 2):
        high, low = n >> stage, n & ((1 << stage) - 1)
        yield n, (high << (stage + 1)) + (other << stage) + low


def trade(stage, flags, mine, got, out, give=None):
    out[...] = mine[...]
    for n, at in other_half(stage, flags, out.shape[0]):
        out[at] = got[n]
    if give is not None:
        for n, at in other_half(stage + 1, flags, out.shape[0]):
            give[n] = out[at]


def source_kernel(step, flags, srow, sz, wave, out):
    size, depth = out.shape
    n = srow.shape[1]
    spot = lax.broadcasted_iota(jnp.int32, (size, n), 0) == srow[...]
    spot = spot.astype(F32).astype(BF16)
    high, low = split(jnp.where(
        lax.broadcasted_iota(jnp.int32, (n, depth), 1) == sz[...], wave[:, step : step + 1], 0.0))
    out[...] = mm(spot, high) + mm(spot, low)


def forward_inner_kernel(step, flags, cur, prev, k0, ki, kx, kz, cm, near, deep, srow, sz, wave,
                         before, part, change):
    source_kernel(step, flags, srow, sz, wave, change)
    inner(cur, prev, k0, ki, kx, kz, cm, near, deep, change, part)
    change[...] = (cur[...] - prev[...]) - (prev[...] - before[...])


def outer_kernel(stage, double, flags, part, k0, ki, kx, zm, ym, side, edge, *rest):
    rest = list(rest)
    other = rest.pop(0) if double else None
    if stage is not None:
        mine, got, new, zo, co, yo, *lists = rest
        trade(stage, flags, mine, got, *lists)
    else:
        new, zo, co, yo = rest
    outer(flags, part, k0, ki, kx, zm, ym, side, edge, new)
    if double:
        for n, field in enumerate((new, other)):
            rims(flags, field, zo.at[n], co.at[n], yo.at[n])
    else:
        rims(flags, new, zo, co, yo)


def lists_kernel(flags, lists, spot, pick, at, obs):
    size, n = spot.shape
    depth = at.shape[1]
    subs, steps = lists.shape[0], obs.shape[1]
    whole = n // 128
    cell = jnp.concatenate(
        [jnp.sum(lists[:, m, :], axis=0, keepdims=True) for m in range(whole)], axis=1)
    along = jnp.floor((cell + 0.5) * (1.0 / depth))
    same = lax.broadcasted_iota(jnp.int32, (n, n), 0) == lax.broadcasted_iota(jnp.int32, (n, n), 1)

    def column(row):
        return jnp.sum(jnp.where(same, row, 0.0), axis=1, keepdims=True).astype(jnp.int32)

    hot = lax.broadcasted_iota(jnp.int32, (size, n), 0) == along.astype(jnp.int32)
    spot[...] = hot.astype(F32).astype(BF16)
    hot = lax.broadcasted_iota(jnp.int32, (n, size), 1) == column(along)
    pick[...] = hot.astype(F32).astype(BF16)
    hot = lax.broadcasted_iota(jnp.int32, (n, depth), 1) == column(cell - along * depth)
    at[...] = hot.astype(F32)
    traces = lists[:, whole, :]
    for k in range(CAP):
        obs[k * subs : k * subs + subs, :] = traces[:, k * steps : k * steps + steps]


def injection(t, state, spot, pick, at, obs):
    high, low = split(state[...])
    seen = at[...] * (mm(pick[...], high) + mm(pick[...], low))
    residual = jnp.sum(seen, axis=1, keepdims=True) - obs[:, t : t + 1]
    high, low = split(at[...] * residual)
    return mm(spot[...], high) + mm(spot[...], low)


def adjoint_inner_kernel(t, flags, cur, prev, k0, ki, kx, kz, cm, near, deep, state, spot, pick,
                         at, obs, *rest):
    if len(rest) == 4:
        change, image, part, image_out = rest
        image_out[...] = cur[...] * change[...] + image[...]
    else:
        now, mid, before, part, image_out = rest
        image_out[...] = cur[...] * ((now[...] - mid[...]) - (mid[...] - before[...]))
    inj = injection(t, state, spot, pick, at, obs)
    inner(cur, prev, k0, ki, kx, kz, cm, near, deep, inj, part)


def adjoint_first_kernel(flags, cur, prev, k0, ki, kx, kz, cm, near, deep, part):
    inner(cur, prev, k0, ki, kx, kz, cm.at[1], near, deep, None, part)


def turn_kernel(t, flags, part, k0, ki, kx, zm, ym, side, edge, u_part, u_zm, u_ym, spot, pick, at, obs, new, u_new, zo, co, yo):
    outer(flags, part, k0, ki, kx, zm, ym, side, edge, new)
    outer(flags, u_part, k0, ki, kx, u_zm.at[1], u_ym.at[1], side, edge, u_new)
    u_new[...] += injection(t, new, spot, pick, at, obs)
    rims(flags, u_new, zo, co, yo)


def last_kernel(scale, flags, part, k0, ki, kx, zm, ym, side, edge, image, change, vel,
                prev, states, mine, other):
    new = states.at[1]
    states[0] = prev[...]
    outer(flags, part, k0, ki, kx, zm, ym, side, edge, new)
    raw = (image[...] + new[...] * change[...]) * scale / vel[...]
    count, height, lanes = mine.shape
    chunk = raw.shape[1] // (2 * count)
    for n in range(count):
        even, odd = (
            jnp.concatenate(
                [raw[g * height : g * height + height, m * chunk : m * chunk + chunk]
                 for g in range(lanes // chunk)], axis=1)
            for m in (2 * n, 2 * n + 1))
        mine[n] = jnp.where(flags[0] == 0, even, odd)
        other[n] = jnp.where(flags[0] == 0, odd, even)


def join_kernel(flags, mine, got, *outs):
    for s, out in enumerate(outs):
        to = jnp.bitwise_xor(flags[3], s)
        a, b = mine[to], got[to]
        out[0] = jnp.where(flags[0] == 0, a, b)
        out[1] = jnp.where(flags[0] == 0, b, a)


def filter_kernel(flags, *refs):
    *pieces, out = refs
    height, lanes = pieces[0].shape[1:]
    chunk, rows, full = out.shape
    groups = lanes // chunk
    q = flags[3]
    shape = (full, full)
    y = lax.broadcasted_iota(jnp.int32, shape, 1)
    at = lax.broadcasted_iota(jnp.int32, shape, 0)
    within = jnp.bitwise_and(at, 2 * COLS - 1)
    place = jnp.bitwise_xor(q * (2 * COLS), at - within) + within
    weights = jnp.exp(jnp.abs(y - place).astype(F32) * (-1.0 / SMOOTH))
    weights = split(weights / jnp.sum(weights, axis=0, keepdims=True))
    ready = []
    for n in range(height // COLS):
        here = slice(n * COLS, n * COLS + COLS)
        lines = jnp.concatenate([piece[b, here, :] for piece in pieces for b in range(2)], axis=0)
        high, low = split(lines.T)
        done = mm(high, weights[0]) + mm(low, weights[0]) + mm(high, weights[1])
        ready.append(done)
    for g in range(groups):
        lines = jnp.stack([done[g * chunk : g * chunk + chunk] for done in ready], axis=0)
        out[:, g * (rows // groups) : (g + 1) * (rows // groups), :] = jnp.swapaxes(lines, 0, 1)


def shaped(*shape):
    return jax.ShapeDtypeStruct(shape, F32)


def call(kernel, name, outs, *args, weight=0, far=0):
    specs = [pl.BlockSpec(memory_space=pltpu.SMEM)]
    specs += [pl.BlockSpec(memory_space=pl.ANY)] * far
    specs += [pl.BlockSpec(memory_space=pltpu.VMEM)] * (len(args) - 1 - far)
    return pl.pallas_call(
        kernel,
        name=name,
        out_shape=outs,
        in_specs=specs,
        out_specs=[pl.BlockSpec(memory_space=pltpu.VMEM)] * len(outs),
        scratch_shapes=[pltpu.SemaphoreType.DMA((far,))] if far else [],
        compiler_params=pltpu.CompilerParams(vmem_limit_bytes=VMEM_BYTES),
        cost_estimate=pl.CostEstimate(
            flops=1000, bytes_accessed=1000 + int(weight * 3_600_000), transcendentals=0),
    )(*args)


def per_device(plan, fwd_now, fwd_before, adj_now, adj_before, velocity, log_density, observed,
               rec_cells, rec_counts, src_cell, wavelet):
    rows, cols, depth = fwd_now.shape
    size = rows * cols
    steps = wavelet.shape[0]
    nx, nq = plan.nx, plan.nq
    subs = 2 * nx
    xline, c = lax.axis_index("xline"), lax.axis_index("inline")
    q, y = xline // 2, xline % 2
    keep = y == c
    z_perm, c_perm, y_perm, swap_perm = plan.z(), plan.core(), plan.y(), plan.swap()
    stages = [(c_perm, c), (y_perm, y)]
    stages += [(plan.flip(1 << b), (q >> b) & 1) for b in range((nq - 1).bit_length())]
    sub = (2 * q + c) * 2 + y
    flags = jnp.stack([c, y, sub, q] + [bit for pairs, bit in stages]).astype(jnp.int32)
    field = shaped(size, depth)
    side, edge = (size // 2, depth), (4 * cols, depth)
    rim = [shaped(*side), shaped(*side), shaped(*edge)]

    deep = depth_matrix(depth)
    deep = jnp.asarray(np.concatenate([deep, deep]), BF16)
    near = stencil_matrix(GROUP, cols)
    group, own, half = GROUP * cols, near.shape[1] - GROUP * 8, GROUP * 4
    both = [near[:, own : own + half], near[:, own + half :]]
    from_z = [np.concatenate([part[:group], part[2 * group :]]) for part in both]
    inside = jnp.where(c == 0, q > 0, q < nq - 1)
    side = jnp.where(c == 0, jnp.asarray(from_z[0], F32), jnp.asarray(from_z[1], F32))
    side = jnp.where(inside, side, 0.0).astype(BF16)
    side = jnp.concatenate([side, side], axis=1)
    core = jnp.where(c == 0, jnp.asarray(both[1], F32), jnp.asarray(both[0], F32)).astype(BF16)
    edge = jnp.where(y == 1, jnp.asarray(near[: 2 * group, : 4 * cols], F32),
                     jnp.asarray(near[: 2 * group, own - 4 * cols : own], F32)).astype(BF16)
    edge = jnp.concatenate([edge, edge], axis=1)
    near = jnp.asarray(np.concatenate([near[:, :own], near[:, :own]], axis=1), BF16)
    near = jnp.concatenate([near, core, core], axis=1)

    def halo(zo, co, yo):
        return send(zo, z_perm), send(co, c_perm), send(yo, y_perm)

    def after(value, *deps):
        return lax.optimization_barrier((value,) + deps)[0]

    def flat(value):
        return value.reshape(size, depth)

    log_density, fwd_now, velocity = flat(log_density), flat(fwd_now), flat(velocity)
    fwd_before, adj_now, adj_before = flat(fwd_before), flat(adj_now), flat(adj_before)
    got = [send(v, swap_perm) for v in (log_density, fwd_now)]
    stacked = jnp.stack([velocity, fwd_before])
    got_model = send(stacked, swap_perm)
    plane = nx * cols * depth
    src_i = src_cell // plane - y * rows
    src_x = src_cell // depth % (nx * cols) - (2 * q + c) * cols
    ok = (src_i >= 0) & (src_i < rows) & (src_x >= 0) & (src_x < cols)
    srow = jnp.where(ok, src_i * cols + src_x, -1)[None, :]
    sz = (src_cell % depth)[:, None]
    wave = wavelet.T

    slots = subs * CAP
    rec_counts, rec_cells, observed = lax.optimization_barrier(
        (rec_counts, rec_cells, observed, stacked))[:3]
    live = jnp.arange(CAP)[None, :] < rec_counts[0][:, None]
    cells = jnp.where(live, rec_cells[0].reshape(subs, CAP), -1).T.reshape(1, slots).astype(F32)
    worker = (2 * q + c) * 2 + y
    cells = jnp.where(jnp.arange(subs)[:, None] == worker, cells, 0.0)
    traces = observed.reshape(steps, nq, 2, 2, CAP).transpose(1, 3, 2, 4, 0).reshape(subs, CAP * steps)
    spare = jnp.zeros((subs, 128 - CAP * steps), F32)
    lists = jnp.concatenate([cells, traces, spare], axis=1).reshape(subs, -1, 128)
    give = lax.dynamic_index_in_dim(lists.reshape(subs // 2, 2, -1, 128), 1 - c, 1, keepdims=False)
    inj, = call(functools.partial(source_kernel, 0), "source", [field], after(flags, stacked), srow,
                sz, wave, weight=0.6)
    give, flags, inj = lax.optimization_barrier((give, flags, inj))
    got_list = send(give, stages[0][0])

    density, p_now, *out = call(settle_kernel, "settle",
                                [field, field] + [shaped(2, *r.shape) for r in rim],
                                flags, log_density, fwd_now, *got, far=2)
    zm, cm, ym = halo(*out)
    got_adjoint = send(jnp.stack([after(adj_now, density), after(adj_before, density)]), swap_perm)
    vel, p_before = call(settle_pair_kernel, "settle_model", [field, field],
                         flags, velocity, fwd_before, got_model, weight=0.6, far=2)
    parts = call(first_inner_kernel, "first_inner", [field] * 7, flags, density, p_now, cm,
                 near, deep, weight=1.3)

    entries, half_entries = shaped(*lists.shape), shaped(*give.shape)
    new, zo, co, yo, k0, ki, kx, kz, lists, give = call(
        first_outer_kernel, "first_outer", [field] + rim + [field] * 4 + [entries, half_entries],
        flags, p_now, p_before, vel, *parts, inj, zm, ym, side, edge, lists, got_list)
    model = (k0, ki, kx, kz)
    states = [p_before, p_now, new]
    changes = []
    zm, cm, ym = halo(zo, co, yo)
    double = 1
    for t in range(1, steps):
        cur, prev, before = states[:-4:-1]
        stage = t if t < len(stages) else None
        extra = [lists, send(give, stages[t][0])] if stage is not None else []
        part, change = call(
            functools.partial(forward_inner_kernel, t), "forward_inner", [field, field], flags, cur,
            prev, *model, cm, near, deep, srow, sz, wave, before, weight=1.2)
        changes.append(change)
        args = [flags, part, k0, ki, kx, zm, ym, side, edge]
        if t == steps - 1:
            u_part, = call(adjoint_first_kernel, "adjoint_first", [field], flags, u_now, u_before,
                           *model, u_cm, near, deep, weight=1.1)
            receivers = call(
                lists_kernel, "lists",
                [jax.ShapeDtypeStruct((size, slots), BF16),
                 jax.ShapeDtypeStruct((slots, size), BF16), shaped(slots, depth),
                 shaped(slots, steps)], flags, lists, weight=0.8)
            new, u_new, *out = call(
                functools.partial(turn_kernel, t), "turn", [field, field] + rim, *args, u_part,
                u_zm, u_ym, *receivers)
            states.append(new)
            break
        if t == double:
            u_now, u_before = call(settle_pair_kernel, "settle_adjoint", [field, field], flags,
                                   adj_now, adj_before, got_adjoint, weight=0.6, far=2)
            args.append(u_now)
        outs = [field] + ([shaped(2, *r.shape) for r in rim] if t == double else rim)
        if extra:
            outs = outs + [entries] + ([half_entries] if t + 1 < len(stages) else [])
        new, *out = call(functools.partial(outer_kernel, stage, t == double), "forward_outer", outs,
                         *args, *extra)
        if extra:
            out, (lists, *give) = out[:3], out[3:]
            give = give[0] if give else None
        states.append(new)
        zm, cm, ym = halo(*out)
        if t == double:
            u_zm, u_cm, u_ym = zm, cm, ym

    zm, cm, ym = halo(*out)
    u_before, u_now = u_now, u_new
    image = []
    chunk = depth // nx
    half = shaped(nq, size * chunk // 128, 128)
    for j in range(1, steps):
        t = steps - 1 - j
        terms = [changes[t + 1], *image] if image else states[:-4:-1]
        part, *image = call(
            functools.partial(adjoint_inner_kernel, t), "adjoint_inner", [field, field], flags,
            u_now, u_before, *model, cm, near, deep, states[t + 2], *receivers, *terms, weight=1.5)
        args = [part, k0, ki, kx, zm, ym, side, edge]
        if j == steps - 1:
            final, mine, other = call(
                functools.partial(last_kernel, 2.0 / steps), "last",
                [shaped(2, *field.shape), half, half], flags, *args, *image, changes[0], vel, u_now)
            break
        u_before = u_now
        u_now, *out = call(functools.partial(outer_kernel, None, False), "adjoint_outer", [field] + rim,
                           flags, *args)
        zm, cm, ym = halo(*out)

    got = send(final, swap_perm)
    pieces = call(join_kernel, "join", [shaped(2, *half.shape[1:])] * nq, flags, mine,
                  send(other, c_perm))
    pieces = [send(pieces[s], plan.spread(s)) for s in reversed(range(nq))][::-1]
    adj_prev, adj_out = call(select_kernel, "select", [field, field], flags, final, got, weight=1.2)
    gradient, = call(filter_kernel, "filter", [shaped(chunk, rows, nx * cols)],
                     after(flags, adj_out), *pieces)
    block = (rows, cols, depth)
    return gradient, adj_out.reshape(block), adj_prev.reshape(block)


def solution(mesh):
    field = P(("shots", "inline"), "xline", None)
    model = P("inline", "xline", None)
    lists = P(("xline", "inline"), None)
    return jax.shard_map(
        functools.partial(per_device, Plan(mesh)),
        mesh=mesh,
        in_specs=(field, field, field, field, model, model, P("shots", ("xline", "inline")),
                  lists, lists, P("shots"), P("shots", None)),
        out_specs=(P(("shots", "xline"), "inline", None), field, field),
        check_vma=False,
    )
```

```python
import functools

import jax
import jax.numpy as jnp
import numpy as np
from jax import lax
from jax.experimental import pallas as pl
from jax.experimental.pallas import tpu as pltpu
from jax.sharding import PartitionSpec as P

CAP = 8
SMOOTH = 16
SECOND = (-205.0 / 72.0, 8.0 / 5.0, -1.0 / 5.0, 8.0 / 315.0, -1.0 / 560.0)
FIRST = (4.0 / 5.0, -1.0 / 5.0, 4.0 / 105.0, -1.0 / 280.0)
ALL = ("shots", "xline", "inline")
COLS = 8
GROUP = 8
VMEM_BYTES = 8 * 1024 * 1024
F32 = jnp.float32
BF16 = jnp.bfloat16


class Plan:
    def __init__(self, mesh):
        self.shots = mesh.shape["shots"]
        self.nx = mesh.shape["xline"]
        self.nq = self.nx // 2

    def index(self, s, q, y, c):
        return (s * self.nx + 2 * q + y) * 2 + c

    def perm(self, partner):
        pairs = []
        for s in range(self.shots):
            for q in range(self.nq):
                for y in range(2):
                    for c in range(2):
                        t = partner(q, y, c)
                        dst = self.index(s ^ 1, q, y, c) if t is None else self.index(s, *t)
                        pairs.append((self.index(s, q, y, c), dst))
        return pairs

    def swap(self):
        return self.perm(lambda q, y, c: None if y == c else (q, c, y))

    def z(self):
        def partner(q, y, c):
            other = q + 1 if c == 1 else q - 1
            return (other, y, 1 - c) if 0 <= other < self.nq else None

        return self.perm(partner)

    def core(self):
        return self.perm(lambda q, y, c: (q, y, 1 - c))

    def y(self):
        return self.perm(lambda q, y, c: (q, 1 - y, c))

    def flip(self, bit):
        return self.perm(lambda q, y, c: (q ^ bit, y, c) if (q ^ bit) < self.nq else None)

    def spread(self, shift):
        return self.perm(lambda q, y, c: (q ^ shift, c, y))


def send(value, pairs):
    return lax.ppermute(value, ALL, pairs)


def depth_matrix(n):
    m = np.zeros((n, 2 * n), np.float32)
    for k in range(1, 5):
        for j in range(n):
            for i, sign in ((j + k, 1.0), (j - k, -1.0)):
                if 0 <= i < n:
                    m[i, j] = round(SECOND[k] * 5040)
                    m[i, n + j] = sign * round(FIRST[k - 1] * 840)
    return m


def stencil_matrix(rows, cols):
    own = (rows + 8) * cols
    m = np.zeros((3, rows, cols, own + rows * 8), np.float32)
    for i in range(rows):
        for x in range(cols):
            for k in range(1, 5):
                total = round(SECOND[k] * 5040)
                slope = round(FIRST[k - 1] * 840)
                for sign in (1, -1):
                    at = (i + 4 + sign * k) * cols + x
                    m[0, i, x, at] += total
                    m[1, i, x, at] += sign * slope
                    to = x + sign * k
                    if to < 0:
                        at = own + i * 4 + to + 4
                    elif to >= cols:
                        at = own + rows * 4 + i * 4 + to - cols
                    else:
                        at = (i + 4) * cols + to
                    m[0, i, x, at] += total
                    m[2, i, x, at] += sign * slope
    return m.reshape(3 * rows * cols, own + rows * 8)


def split(value):
    high = value.astype(BF16)
    return high, (value - high.astype(F32)).astype(BF16)


def mm(a, b):
    return jnp.dot(a, b, preferred_element_type=F32)


def inner_differences(cur, cm, near, deep):
    depth = cur.shape[1]
    size = GROUP * COLS
    cm = cm.at[0] if len(cm.shape) == 3 else cm
    own = split(cur[...])
    along = mm(jnp.concatenate(own, axis=1), deep[...])
    blank = jnp.zeros((4 * COLS, depth), BF16)
    ext = [jnp.concatenate([blank, part, blank], axis=0) for part in own]
    from_c = split(cm[...])
    for n in range(cur.shape[0] // size):
        here = slice(n * size, n * size + size)
        sides = slice(n * GROUP * 4, n * GROUP * 4 + GROUP * 4)
        rhs = [part[n * size : n * size + size + 8 * COLS] for part in ext]
        rhs += [part[sides] for part in from_c]
        out = mm(near[...], jnp.concatenate(rhs, axis=0))
        yield (here, out[0:size], along[here, 0:depth], out[size : 2 * size], out[2 * size :],
               along[here, depth:])


def side_differences(rows, zm, side):
    size = GROUP * COLS
    zm = zm.at[0] if len(zm.shape) == 3 else zm
    from_z = split(zm[...])
    for n in range(rows // size):
        sides = slice(n * GROUP * 4, n * GROUP * 4 + GROUP * 4)
        out = mm(side[...], jnp.concatenate([part[sides] for part in from_z], axis=0))
        yield slice(n * size, n * size + size), out[0:size], out[size:]


def edge_differences(flags, rows, ym, edge):
    size = GROUP * COLS
    ym = ym.at[0] if len(ym.shape) == 3 else ym
    out = mm(edge[...], jnp.concatenate(split(ym[...]), axis=0))
    start = jnp.where(flags[1] == 1, 0, rows - size)
    return pl.ds(pl.multiple_of(start, size), size), out[0:size], out[size:]


def halves(value):
    rows, depth = value.shape
    pairs = value.reshape(rows // (2 * COLS), 2, COLS, depth)
    a, b = pairs[:, 0], pairs[:, 1]
    low = lax.broadcasted_iota(jnp.int32, a.shape, 1) < 4
    first = jnp.where(low, a, pltpu.roll(b, 4, axis=1))
    last = jnp.where(low, pltpu.roll(a, 4, axis=1), b)
    return first.reshape(rows // 2, depth), last.reshape(rows // 2, depth)


def rims(flags, new, zo, co, yo):
    first, last = halves(new[...])
    zo[...] = jnp.where(flags[0] == 0, first, last)
    co[...] = jnp.where(flags[0] == 0, last, first)
    size = new.shape[0]
    yo[...] = jnp.where(flags[1] == 0, new[size - 4 * COLS :], new[0 : 4 * COLS])


def choose(flags, pairs, sems):
    keep = flags[0] == flags[1]

    @pl.when(keep)
    def _():
        copies = [pltpu.make_async_copy(own, out, sems.at[n])
                  for n, (own, recv, out) in enumerate(pairs)]
        for copy in copies:
            copy.start()
        for copy in copies:
            copy.wait()

    @pl.when(jnp.logical_not(keep))
    def _():
        for own, recv, out in pairs:
            out[...] = recv[...]


def settle_kernel(flags, a, b, recv_a, recv_b, a_out, b_out, zo, co, yo, sems):
    choose(flags, [(a, recv_a, a_out), (b, recv_b, b_out)], sems)
    for n, out in enumerate((a_out, b_out)):
        rims(flags, out, zo.at[n], co.at[n], yo.at[n])


def settle_pair_kernel(flags, a, b, recv, a_out, b_out, sems):
    choose(flags, [(a, recv.at[0], a_out), (b, recv.at[1], b_out)], sems)


def select_kernel(flags, own, recv, *outs):
    keep = flags[0] == flags[1]
    for n, out in enumerate(outs):
        out[...] = jnp.where(keep, own[n], recv[n])


def first_inner_kernel(flags, lr, cur, cm, near, deep, *outs):
    ri, rx, rz, sums_out, di_out, dx_out, dz_out = outs
    for here, spare, spare_z, di, dx, dz in inner_differences(lr, cm.at[0], near, deep):
        ri[here], rx[here], rz[here] = di, dx, dz
    for here, sums, sums_z, di, dx, dz in inner_differences(cur, cm.at[1], near, deep):
        sums_out[here] = sums + sums_z + (3.0 * SECOND[0] * 5040) * cur[here]
        di_out[here], dx_out[here], dz_out[here] = di, dx, dz


def first_outer_kernel(flags, cur, prev, vel, ri, rx, rz, sums, di, dx, dz, inj, zm, ym, side,
                       edge, new, zo, co, yo, k0, ki, kx, kz):
    rows = cur.shape[0]
    kz[...] = sums[...]
    ki[...] = di[...]
    here, more, more_i = edge_differences(flags, rows, ym.at[1], edge)
    kz[here] += more
    ki[here] += more_i
    lr_here, spare, lr_more_i = edge_differences(flags, rows, ym.at[0], edge)
    k0[...] = ri[...]
    k0[lr_here] += lr_more_i
    first = side_differences(rows, zm.at[0], side)
    second = side_differences(rows, zm.at[1], side)
    for (here, spare, more_r), (spare_here, more, more_x) in zip(first, second):
        square = vel[here] * vel[here]
        scaled = square * (1.0 / (840 * 840))
        factor = square * (1.0 / 5040)
        along_i, along_x, along_z = scaled * k0[here], scaled * (rx[here] + more_r), scaled * rz[here]
        change = factor * (kz[here] + more) - (
            along_i * ki[here] + along_x * (dx[here] + more_x) + along_z * dz[here])
        k0[here], ki[here], kx[here], kz[here] = factor, along_i, along_x, along_z
        center = cur[here]
        new[here] = (center - prev[here]) + (center + (change + inj[here]))
    rims(flags, new, zo, co, yo)


def inner(cur, prev, k0, ki, kx, kz, cm, near, deep, inj, out):
    for here, sums, sums_z, di, dx, dz in inner_differences(cur, cm, near, deep):
        center = cur[here]
        change = k0[here] * ((sums + sums_z) + (3.0 * SECOND[0] * 5040) * center)
        change = change - (ki[here] * di + kx[here] * dx + kz[here] * dz)
        if inj is not None:
            change = change + inj[here]
        out[here] = (center - prev[here]) + (center + change)


def outer(flags, part, k0, ki, kx, zm, ym, side, edge, new):
    rows = part.shape[0]
    for here, sums, dx in side_differences(rows, zm, side):
        new[here] = part[here] + (k0[here] * sums - kx[here] * dx)
    here, sums, di = edge_differences(flags, rows, ym, edge)
    new[here] += k0[here] * sums - ki[here] * di


def other_half(stage, flags, count):
    other = 1 - flags[4 + stage]
    for n in range(count // 2):
        high, low = n >> stage, n & ((1 << stage) - 1)
        yield n, (high << (stage + 1)) + (other << stage) + low


def trade(stage, flags, mine, got, out, give=None):
    out[...] = mine[...]
    for n, at in other_half(stage, flags, out.shape[0]):
        out[at] = got[n]
    if give is not None:
        for n, at in other_half(stage + 1, flags, out.shape[0]):
            give[n] = out[at]


def trade_kernel(stage, flags, mine, got, *outs):
    trade(stage, flags, mine, got, *outs)


def source_kernel(step, full, flags, src, wave, out):
    size, depth = out.shape
    count = src.shape[0]
    shift = (depth - 1).bit_length()
    plane = shift + (full - 1).bit_length()
    rows = size // COLS
    lane = lax.broadcasted_iota(jnp.int32, (1, count), 1)
    sub = lax.broadcasted_iota(jnp.int32, (count, 1), 0)
    row = jnp.zeros((1, count), jnp.int32)
    deep = jnp.zeros((count, 1), jnp.int32)
    size_of = jnp.zeros((count, 1), F32)
    for n in range(count):
        cell = src[n]
        i = jnp.right_shift(cell, plane) - flags[1] * rows
        x = jnp.bitwise_and(jnp.right_shift(cell, shift), full - 1)
        x = x - (2 * flags[3] + flags[0]) * COLS
        ok = (i >= 0) & (i < rows) & (x >= 0) & (x < COLS)
        row = jnp.where(lane == n, jnp.where(ok, i * COLS + x, -1), row)
        deep = jnp.where(sub == n, jnp.bitwise_and(cell, depth - 1), deep)
        size_of = jnp.where(sub == n, wave[step, n], size_of)
    spot = lax.broadcasted_iota(jnp.int32, (size, count), 0) == row
    spot = spot.astype(F32).astype(BF16)
    high, low = split(jnp.where(
        lax.broadcasted_iota(jnp.int32, (count, depth), 1) == deep, size_of, 0.0))
    out[...] = mm(spot, high) + mm(spot, low)


def forward_inner_kernel(step, full, flags, src, wave, cur, prev, k0, ki, kx, kz, cm, near, deep,
                         before, part, change):
    source_kernel(step, full, flags, src, wave, change)
    inner(cur, prev, k0, ki, kx, kz, cm, near, deep, change, part)
    change[...] = (cur[...] - prev[...]) - (prev[...] - before[...])


def outer_kernel(stage, double, flags, part, k0, ki, kx, zm, ym, side, edge, *rest):
    rest = list(rest)
    other = rest.pop(0) if double else None
    if stage is not None:
        mine, got, new, zo, co, yo, *lists = rest
        trade(stage, flags, mine, got, *lists)
    else:
        new, zo, co, yo = rest
    outer(flags, part, k0, ki, kx, zm, ym, side, edge, new)
    if double:
        for n, field in enumerate((new, other)):
            rims(flags, field, zo.at[n], co.at[n], yo.at[n])
    else:
        rims(flags, new, zo, co, yo)


def pack_kernel(flags, counts, cells, traces, cells_out, lists, give, counts_v, cells_v, traces_v,
                sems):
    pairs = ((counts, counts_v), (cells, cells_v), (traces, traces_v))
    copies = [pltpu.make_async_copy(a, b, sems.at[n]) for n, (a, b) in enumerate(pairs)]
    for copy in copies:
        copy.start()
    for copy in copies:
        copy.wait()
    subs, n = counts.shape[1], cells.shape[1]
    shape = (subs, n)
    lane = lax.broadcasted_iota(jnp.int32, shape, 1)
    mine = lane // CAP == lax.broadcasted_iota(jnp.int32, shape, 0)
    live = mm(counts_v[...].astype(F32).astype(BF16), mine.astype(F32).astype(BF16))
    slot = jnp.bitwise_and(lane[0:1], CAP - 1)
    cells_out[...] = jnp.where(slot.astype(F32) < live, cells_v[...].astype(F32), -1.0)
    for m in range(subs):
        q, y, c = m >> 2, (m >> 1) & 1, m & 1
        start = ((2 * q + c) * 2 + y) * CAP
        tile = traces_v[:, start // 128 * 128 : start // 128 * 128 + 128]
        lists[m] = pltpu.roll(tile, (128 - start % 128) % 128, axis=1) if start % 128 else tile
    for n, at in other_half(0, flags, subs):
        give[n] = lists[at]


def lists_kernel(flags, lists, own, got, spot, pick, at, obs):
    size, n = spot.shape
    depth = at.shape[1]
    subs, steps = lists.shape[0], obs.shape[1]
    cell = jnp.where(flags[0] == flags[1], own[...], got[...])
    along = jnp.floor((cell + 0.5) * (1.0 / depth))
    same = lax.broadcasted_iota(jnp.int32, (n, n), 0) == lax.broadcasted_iota(jnp.int32, (n, n), 1)

    def column(row):
        return jnp.sum(jnp.where(same, row, 0.0), axis=1, keepdims=True).astype(jnp.int32)

    hot = lax.broadcasted_iota(jnp.int32, (size, n), 0) == along.astype(jnp.int32)
    spot[...] = hot.astype(F32).astype(BF16)
    hot = lax.broadcasted_iota(jnp.int32, (n, size), 1) == column(along)
    pick[...] = hot.astype(F32).astype(BF16)
    hot = lax.broadcasted_iota(jnp.int32, (n, depth), 1) == column(cell - along * depth)
    at[...] = hot.astype(F32)
    traces = lists[...].reshape(subs * steps, 128).T[0:CAP]
    for s in range(subs):
        obs[s * CAP : s * CAP + CAP, :] = traces[:, s * steps : s * steps + steps]


def injection(t, state, spot, pick, at, obs):
    high, low = split(state[...])
    seen = at[...] * (mm(pick[...], high) + mm(pick[...], low))
    residual = jnp.sum(seen, axis=1, keepdims=True) - obs[:, t : t + 1]
    high, low = split(at[...] * residual)
    return mm(spot[...], high) + mm(spot[...], low)


def adjoint_inner_kernel(t, flags, cur, prev, k0, ki, kx, kz, cm, near, deep, state, spot, pick,
                         at, obs, *rest):
    if len(rest) == 4:
        change, image, part, image_out = rest
        image_out[...] = cur[...] * change[...] + image[...]
    else:
        now, mid, before, part, image_out = rest
        image_out[...] = cur[...] * ((now[...] - mid[...]) - (mid[...] - before[...]))
    inj = injection(t, state, spot, pick, at, obs)
    inner(cur, prev, k0, ki, kx, kz, cm, near, deep, inj, part)


def adjoint_first_kernel(flags, cur, prev, k0, ki, kx, kz, cm, near, deep, part):
    inner(cur, prev, k0, ki, kx, kz, cm.at[1], near, deep, None, part)


def turn_kernel(t, flags, part, k0, ki, kx, zm, ym, side, edge, u_part, u_zm, u_ym, spot, pick, at, obs, new, u_new, zo, co, yo):
    outer(flags, part, k0, ki, kx, zm, ym, side, edge, new)
    outer(flags, u_part, k0, ki, kx, u_zm.at[1], u_ym.at[1], side, edge, u_new)
    u_new[...] += injection(t, new, spot, pick, at, obs)
    rims(flags, u_new, zo, co, yo)


def last_kernel(scale, flags, part, k0, ki, kx, zm, ym, side, edge, image, change, vel,
                prev, states, mine, other):
    new = states.at[1]
    states[0] = prev[...]
    outer(flags, part, k0, ki, kx, zm, ym, side, edge, new)
    raw = (image[...] + new[...] * change[...]) * scale / vel[...]
    count, height, lanes = mine.shape
    chunk = raw.shape[1] // (2 * count)
    for n in range(count):
        even, odd = (
            jnp.concatenate(
                [raw[g * height : g * height + height, m * chunk : m * chunk + chunk]
                 for g in range(lanes // chunk)], axis=1)
            for m in (2 * n, 2 * n + 1))
        mine[n] = jnp.where(flags[0] == 0, even, odd)
        other[n] = jnp.where(flags[0] == 0, odd, even)


def join_kernel(flags, mine, got, *outs):
    for s, out in enumerate(outs):
        to = jnp.bitwise_xor(flags[3], s)
        a, b = mine[to], got[to]
        out[0] = jnp.where(flags[0] == 0, a, b)
        out[1] = jnp.where(flags[0] == 0, b, a)


def filter_kernel(flags, *refs):
    *pieces, out = refs
    height, lanes = pieces[0].shape[1:]
    chunk, rows, full = out.shape
    groups = lanes // chunk
    q = flags[3]
    shape = (full, full)
    y = lax.broadcasted_iota(jnp.int32, shape, 1)
    at = lax.broadcasted_iota(jnp.int32, shape, 0)
    within = jnp.bitwise_and(at, 2 * COLS - 1)
    place = jnp.bitwise_xor(q * (2 * COLS), at - within) + within
    weights = jnp.exp(jnp.abs(y - place).astype(F32) * (-1.0 / SMOOTH))
    weights = split(weights / jnp.sum(weights, axis=0, keepdims=True))
    ready = []
    for n in range(height // COLS):
        here = slice(n * COLS, n * COLS + COLS)
        lines = jnp.concatenate([piece[b, here, :] for piece in pieces for b in range(2)], axis=0)
        high, low = split(lines.T)
        done = mm(high, weights[0]) + mm(low, weights[0]) + mm(high, weights[1])
        ready.append(done)
    for g in range(groups):
        lines = jnp.stack([done[g * chunk : g * chunk + chunk] for done in ready], axis=0)
        out[:, g * (rows // groups) : (g + 1) * (rows // groups), :] = jnp.swapaxes(lines, 0, 1)


def shaped(*shape):
    return jax.ShapeDtypeStruct(shape, F32)


def call(kernel, name, outs, *args, weight=0, far=0, scalars=0, scratch=()):
    specs = [pl.BlockSpec(memory_space=pltpu.SMEM)] * (1 + scalars)
    specs += [pl.BlockSpec(memory_space=pl.ANY)] * far
    specs += [pl.BlockSpec(memory_space=pltpu.VMEM)] * (len(args) - 1 - scalars - far)
    return pl.pallas_call(
        kernel,
        name=name,
        out_shape=outs,
        in_specs=specs,
        out_specs=[pl.BlockSpec(memory_space=pltpu.VMEM)] * len(outs),
        scratch_shapes=list(scratch) + ([pltpu.SemaphoreType.DMA((far,))] if far else []),
        compiler_params=pltpu.CompilerParams(vmem_limit_bytes=VMEM_BYTES),
        cost_estimate=pl.CostEstimate(
            flops=1000, bytes_accessed=1000 + int(weight * 3_600_000), transcendentals=0),
    )(*args)


def per_device(plan, fwd_now, fwd_before, adj_now, adj_before, velocity, log_density, observed,
               rec_cells, rec_counts, src_cell, wavelet):
    rows, cols, depth = fwd_now.shape
    size = rows * cols
    steps = wavelet.shape[0]
    nx, nq = plan.nx, plan.nq
    subs = 2 * nx
    xline, c = lax.axis_index("xline"), lax.axis_index("inline")
    q, y = xline // 2, xline % 2
    keep = y == c
    z_perm, c_perm, y_perm, swap_perm = plan.z(), plan.core(), plan.y(), plan.swap()
    stages = [(c_perm, c), (y_perm, y)]
    stages += [(plan.flip(1 << b), (q >> b) & 1) for b in range((nq - 1).bit_length())]
    sub = (2 * q + c) * 2 + y
    flags = jnp.stack([c, y, sub, q] + [bit for pairs, bit in stages]).astype(jnp.int32)
    field = shaped(size, depth)
    side, edge = (size // 2, depth), (4 * cols, depth)
    rim = [shaped(*side), shaped(*side), shaped(*edge)]

    deep = depth_matrix(depth)
    deep = jnp.asarray(np.concatenate([deep, deep]), BF16)
    near = stencil_matrix(GROUP, cols)
    group, own, half = GROUP * cols, near.shape[1] - GROUP * 8, GROUP * 4
    both = [near[:, own : own + half], near[:, own + half :]]
    from_z = [np.concatenate([part[:group], part[2 * group :]]) for part in both]
    inside = jnp.where(c == 0, q > 0, q < nq - 1)
    side = jnp.where(c == 0, jnp.asarray(from_z[0], F32), jnp.asarray(from_z[1], F32))
    side = jnp.where(inside, side, 0.0).astype(BF16)
    side = jnp.concatenate([side, side], axis=1)
    core = jnp.where(c == 0, jnp.asarray(both[1], F32), jnp.asarray(both[0], F32)).astype(BF16)
    edge = jnp.where(y == 1, jnp.asarray(near[: 2 * group, : 4 * cols], F32),
                     jnp.asarray(near[: 2 * group, own - 4 * cols : own], F32)).astype(BF16)
    edge = jnp.concatenate([edge, edge], axis=1)
    near = jnp.asarray(np.concatenate([near[:, :own], near[:, :own]], axis=1), BF16)
    near = jnp.concatenate([near, core, core], axis=1)

    def halo(zo, co, yo):
        return send(zo, z_perm), send(co, c_perm), send(yo, y_perm)

    def after(value, *deps):
        return lax.optimization_barrier((value,) + deps)[0]

    def flat(value):
        return value.reshape(size, depth)

    log_density, fwd_now, velocity = flat(log_density), flat(fwd_now), flat(velocity)
    fwd_before, adj_now, adj_before = flat(fwd_before), flat(adj_now), flat(adj_before)
    got = [send(v, swap_perm) for v in (log_density, fwd_now)]
    stacked = jnp.stack([velocity, fwd_before])
    got_model = send(stacked, swap_perm)
    full = nx * cols
    inj, = call(functools.partial(source_kernel, 0, full), "source", [field], flags, src_cell, wavelet,
                weight=0.7, scalars=2)
    flags_in, inj = lax.optimization_barrier((flags, inj))
    density, p_now, *out = call(settle_kernel, "settle",
                                [field, field] + [shaped(2, *r.shape) for r in rim],
                                flags_in, log_density, fwd_now, *got, far=2)
    zm, cm, ym = halo(*out)
    got_adjoint = send(jnp.stack([after(adj_now, ym), after(adj_before, ym)]), swap_perm)
    vel, p_before = call(settle_pair_kernel, "settle_model", [field, field],
                         flags, velocity, fwd_before, got_model, weight=0.6, far=2)
    parts = call(first_inner_kernel, "first_inner", [field] * 7, flags, density, p_now, cm,
                 near, deep, weight=1.3)

    new, zo, co, yo, k0, ki, kx, kz = call(
        first_outer_kernel, "first_outer", [field] + rim + [field] * 4,
        flags, p_now, p_before, vel, *parts, inj, zm, ym, side, edge)
    model = (k0, ki, kx, kz)
    states = [p_before, p_now, new]
    changes = []
    zm, cm, ym = halo(zo, co, yo)
    double = 1

    slots = subs * CAP
    entries, half_entries = shaped(subs, steps, 128), shaped(subs // 2, steps, 128)
    cells, lists, give = call(
        pack_kernel, "pack", [shaped(1, slots), entries, half_entries], after(flags, k0), rec_counts,
        rec_cells, observed, weight=0.8, far=3,
        scratch=[pltpu.VMEM(rec_counts.shape, jnp.int32), pltpu.VMEM(rec_cells.shape, jnp.int32),
                 pltpu.VMEM(observed.shape, F32)])
    for t in range(1, steps):
        cur, prev, before = states[:-4:-1]
        stage = t - 1 if t <= min(len(stages), steps - 2) else None
        extra = [lists, send(give, stages[stage][0])] if stage is not None else []
        part, change = call(
            functools.partial(forward_inner_kernel, t, full), "forward_inner", [field, field], flags,
            src_cell, wavelet, cur, prev, *model, cm, near, deep, before, weight=1.2, scalars=2)
        changes.append(change)
        args = [flags, part, k0, ki, kx, zm, ym, side, edge]
        if t == steps - 1:
            u_part, = call(adjoint_first_kernel, "adjoint_first", [field], flags, u_now, u_before,
                           *model, u_cm, near, deep, weight=1.1)
            for n in range(steps - 2, len(stages)):
                lists, *give = call(
                    functools.partial(trade_kernel, n), "trade",
                    [entries] + ([half_entries] if n + 1 < len(stages) else []), flags, lists,
                    send(give, stages[n][0]))
                give = give[0] if give else None
            receivers = call(
                lists_kernel, "lists",
                [jax.ShapeDtypeStruct((size, slots), BF16),
                 jax.ShapeDtypeStruct((slots, size), BF16), shaped(slots, depth),
                 shaped(slots, steps)], flags, lists, cells, got_cells, weight=0.8)
            new, u_new, *out = call(
                functools.partial(turn_kernel, t), "turn", [field, field] + rim, *args, u_part,
                u_zm, u_ym, *receivers)
            states.append(new)
            break
        if t == len(stages) - 2:
            got_cells = send(after(cells, part), swap_perm)
        if t == double:
            u_now, u_before = call(settle_pair_kernel, "settle_adjoint", [field, field], flags,
                                   adj_now, adj_before, got_adjoint, weight=0.6, far=2)
            args.append(u_now)
        outs = [field] + ([shaped(2, *r.shape) for r in rim] if t == double else rim)
        if extra:
            outs = outs + [entries] + ([half_entries] if t < len(stages) else [])
        new, *out = call(functools.partial(outer_kernel, stage, t == double), "forward_outer", outs,
                         *args, *extra)
        if extra:
            out, (lists, *give) = out[:3], out[3:]
            give = give[0] if give else None
        states.append(new)
        zm, cm, ym = halo(*out)
        if t == double:
            u_zm, u_cm, u_ym = zm, cm, ym

    zm, cm, ym = halo(*out)
    u_before, u_now = u_now, u_new
    image = []
    chunk = depth // nx
    half = shaped(nq, size * chunk // 128, 128)
    for j in range(1, steps):
        t = steps - 1 - j
        terms = [changes[t + 1], *image] if image else states[:-4:-1]
        part, *image = call(
            functools.partial(adjoint_inner_kernel, t), "adjoint_inner", [field, field], flags,
            u_now, u_before, *model, cm, near, deep, states[t + 2], *receivers, *terms, weight=1.5)
        args = [part, k0, ki, kx, zm, ym, side, edge]
        if j == steps - 1:
            final, mine, other = call(
                functools.partial(last_kernel, 2.0 / steps), "last",
                [shaped(2, *field.shape), half, half], flags, *args, *image, changes[0], vel, u_now)
            break
        u_before = u_now
        u_now, *out = call(functools.partial(outer_kernel, None, False), "adjoint_outer", [field] + rim,
                           flags, *args)
        zm, cm, ym = halo(*out)

    got = send(final, swap_perm)
    pieces = call(join_kernel, "join", [shaped(2, *half.shape[1:])] * nq, flags, mine,
                  send(other, c_perm))
    pieces = [send(pieces[s], plan.spread(s)) for s in reversed(range(nq))][::-1]
    adj_prev, adj_out = call(select_kernel, "select", [field, field], flags, final, got, weight=1.2)
    gradient, = call(filter_kernel, "filter", [shaped(chunk, rows, nx * cols)],
                     after(flags, adj_out), *pieces)
    block = (rows, cols, depth)
    return gradient, adj_out.reshape(block), adj_prev.reshape(block)


def solution(mesh):
    field = P(("shots", "inline"), "xline", None)
    model = P("inline", "xline", None)
    lists = P(("xline", "inline"), None)
    return jax.shard_map(
        functools.partial(per_device, Plan(mesh)),
        mesh=mesh,
        in_specs=(field, field, field, field, model, model, P("shots", ("xline", "inline")),
                  lists, lists, P("shots"), P("shots", None)),
        out_specs=(P(("shots", "xline"), "inline", None), field, field),
        check_vma=False,
    )
```

```python
import functools

import jax
import jax.numpy as jnp
import numpy as np
from jax import lax
from jax.experimental import pallas as pl
from jax.experimental.pallas import tpu as pltpu
from jax.sharding import PartitionSpec as P

CAP = 8
SMOOTH = 16
SECOND = (-205.0 / 72.0, 8.0 / 5.0, -1.0 / 5.0, 8.0 / 315.0, -1.0 / 560.0)
FIRST = (4.0 / 5.0, -1.0 / 5.0, 4.0 / 105.0, -1.0 / 280.0)
ALL = ("shots", "xline", "inline")
COLS = 8
GROUP = 8
VMEM_BYTES = 8 * 1024 * 1024
F32 = jnp.float32
BF16 = jnp.bfloat16


class Plan:
    def __init__(self, mesh):
        self.shots = mesh.shape["shots"]
        self.nx = mesh.shape["xline"]
        self.nq = self.nx // 2

    def index(self, s, q, y, c):
        return (s * self.nx + 2 * q + y) * 2 + c

    def perm(self, partner):
        pairs = []
        for s in range(self.shots):
            for q in range(self.nq):
                for y in range(2):
                    for c in range(2):
                        t = partner(q, y, c)
                        dst = self.index(s ^ 1, q, y, c) if t is None else self.index(s, *t)
                        pairs.append((self.index(s, q, y, c), dst))
        return pairs

    def swap(self):
        return self.perm(lambda q, y, c: None if y == c else (q, c, y))

    def z(self):
        def partner(q, y, c):
            other = q + 1 if c == 1 else q - 1
            return (other, y, 1 - c) if 0 <= other < self.nq else None

        return self.perm(partner)

    def core(self):
        return self.perm(lambda q, y, c: (q, y, 1 - c))

    def y(self):
        return self.perm(lambda q, y, c: (q, 1 - y, c))

    def flip(self, bit):
        return self.perm(lambda q, y, c: (q ^ bit, y, c) if (q ^ bit) < self.nq else None)

    def spread(self, shift):
        return self.perm(lambda q, y, c: (q ^ shift, c, y))


def send(value, pairs):
    return lax.ppermute(value, ALL, pairs)


def depth_matrix(n):
    m = np.zeros((n, 2 * n), np.float32)
    for k in range(1, 5):
        for j in range(n):
            for i, sign in ((j + k, 1.0), (j - k, -1.0)):
                if 0 <= i < n:
                    m[i, j] = round(SECOND[k] * 5040)
                    m[i, n + j] = sign * round(FIRST[k - 1] * 840)
    return m


def stencil_matrix(rows, cols):
    own = (rows + 8) * cols
    m = np.zeros((3, rows, cols, own + rows * 8), np.float32)
    for i in range(rows):
        for x in range(cols):
            for k in range(1, 5):
                total = round(SECOND[k] * 5040)
                slope = round(FIRST[k - 1] * 840)
                for sign in (1, -1):
                    at = (i + 4 + sign * k) * cols + x
                    m[0, i, x, at] += total
                    m[1, i, x, at] += sign * slope
                    to = x + sign * k
                    if to < 0:
                        at = own + i * 4 + to + 4
                    elif to >= cols:
                        at = own + rows * 4 + i * 4 + to - cols
                    else:
                        at = (i + 4) * cols + to
                    m[0, i, x, at] += total
                    m[2, i, x, at] += sign * slope
    return m.reshape(3 * rows * cols, own + rows * 8)


def split(value):
    high = value.astype(BF16)
    return high, (value - high.astype(F32)).astype(BF16)


def mm(a, b):
    return jnp.dot(a, b, preferred_element_type=F32)


def inner_differences(cur, cm, near, deep):
    depth = cur.shape[1]
    size = GROUP * COLS
    cm = cm.at[0] if len(cm.shape) == 3 else cm
    own = split(cur[...])
    along = mm(jnp.concatenate(own, axis=1), deep[...])
    blank = jnp.zeros((4 * COLS, depth), BF16)
    ext = [jnp.concatenate([blank, part, blank], axis=0) for part in own]
    from_c = split(cm[...])
    for n in range(cur.shape[0] // size):
        here = slice(n * size, n * size + size)
        sides = slice(n * GROUP * 4, n * GROUP * 4 + GROUP * 4)
        rhs = [part[n * size : n * size + size + 8 * COLS] for part in ext]
        rhs += [part[sides] for part in from_c]
        out = mm(near[...], jnp.concatenate(rhs, axis=0))
        yield (here, out[0:size], along[here, 0:depth], out[size : 2 * size], out[2 * size :],
               along[here, depth:])


def side_differences(rows, zm, side):
    size = GROUP * COLS
    zm = zm.at[0] if len(zm.shape) == 3 else zm
    from_z = split(zm[...])
    for n in range(rows // size):
        sides = slice(n * GROUP * 4, n * GROUP * 4 + GROUP * 4)
        out = mm(side[...], jnp.concatenate([part[sides] for part in from_z], axis=0))
        yield slice(n * size, n * size + size), out[0:size], out[size:]


def edge_differences(flags, rows, ym, edge):
    size = GROUP * COLS
    ym = ym.at[0] if len(ym.shape) == 3 else ym
    out = mm(edge[...], jnp.concatenate(split(ym[...]), axis=0))
    start = jnp.where(flags[1] == 1, 0, rows - size)
    return pl.ds(pl.multiple_of(start, size), size), out[0:size], out[size:]


def halves(value):
    rows, depth = value.shape
    pairs = value.reshape(rows // (2 * COLS), 2, COLS, depth)
    a, b = pairs[:, 0], pairs[:, 1]
    low = lax.broadcasted_iota(jnp.int32, a.shape, 1) < 4
    first = jnp.where(low, a, pltpu.roll(b, 4, axis=1))
    last = jnp.where(low, pltpu.roll(a, 4, axis=1), b)
    return first.reshape(rows // 2, depth), last.reshape(rows // 2, depth)


def rims(flags, new, zo, co, yo):
    first, last = halves(new[...])
    zo[...] = jnp.where(flags[0] == 0, first, last)
    co[...] = jnp.where(flags[0] == 0, last, first)
    size = new.shape[0]
    yo[...] = jnp.where(flags[1] == 0, new[size - 4 * COLS :], new[0 : 4 * COLS])


def choose(flags, pairs, sems):
    keep = flags[0] == flags[1]

    @pl.when(keep)
    def _():
        copies = [pltpu.make_async_copy(own, out, sems.at[n])
                  for n, (own, recv, out) in enumerate(pairs)]
        for copy in copies:
            copy.start()
        for copy in copies:
            copy.wait()

    @pl.when(jnp.logical_not(keep))
    def _():
        for own, recv, out in pairs:
            out[...] = recv[...]


def settle_kernel(flags, a, b, recv_a, recv_b, a_out, b_out, zo, co, yo, sems):
    choose(flags, [(a, recv_a, a_out), (b, recv_b, b_out)], sems)
    for n, out in enumerate((a_out, b_out)):
        rims(flags, out, zo.at[n], co.at[n], yo.at[n])


def settle_pair_kernel(flags, a, b, recv, a_out, b_out, sems):
    choose(flags, [(a, recv.at[0], a_out), (b, recv.at[1], b_out)], sems)


def select_kernel(flags, own, recv, *outs):
    keep = flags[0] == flags[1]
    for n, out in enumerate(outs):
        out[...] = jnp.where(keep, own[n], recv[n])


def first_inner_kernel(flags, lr, cur, cm, near, deep, *outs):
    ri, rx, rz, sums_out, di_out, dx_out, dz_out = outs
    for here, spare, spare_z, di, dx, dz in inner_differences(lr, cm.at[0], near, deep):
        ri[here], rx[here], rz[here] = di, dx, dz
    for here, sums, sums_z, di, dx, dz in inner_differences(cur, cm.at[1], near, deep):
        sums_out[here] = sums + sums_z + (3.0 * SECOND[0] * 5040) * cur[here]
        di_out[here], dx_out[here], dz_out[here] = di, dx, dz


def first_outer_kernel(flags, cur, prev, vel, ri, rx, rz, sums, di, dx, dz, inj, zm, ym, side,
                       edge, new, zo, co, yo, k0, ki, kx, kz):
    rows = cur.shape[0]
    kz[...] = sums[...]
    ki[...] = di[...]
    here, more, more_i = edge_differences(flags, rows, ym.at[1], edge)
    kz[here] += more
    ki[here] += more_i
    lr_here, spare, lr_more_i = edge_differences(flags, rows, ym.at[0], edge)
    k0[...] = ri[...]
    k0[lr_here] += lr_more_i
    first = side_differences(rows, zm.at[0], side)
    second = side_differences(rows, zm.at[1], side)
    for (here, spare, more_r), (spare_here, more, more_x) in zip(first, second):
        square = vel[here] * vel[here]
        scaled = square * (1.0 / (840 * 840))
        factor = square * (1.0 / 5040)
        along_i, along_x, along_z = scaled * k0[here], scaled * (rx[here] + more_r), scaled * rz[here]
        change = factor * (kz[here] + more) - (
            along_i * ki[here] + along_x * (dx[here] + more_x) + along_z * dz[here])
        k0[here], ki[here], kx[here], kz[here] = factor, along_i, along_x, along_z
        center = cur[here]
        new[here] = (center - prev[here]) + (center + (change + inj[here]))
    rims(flags, new, zo, co, yo)


def inner(cur, prev, k0, ki, kx, kz, cm, near, deep, inj, out):
    for here, sums, sums_z, di, dx, dz in inner_differences(cur, cm, near, deep):
        center = cur[here]
        change = k0[here] * ((sums + sums_z) + (3.0 * SECOND[0] * 5040) * center)
        change = change - (ki[here] * di + kx[here] * dx + kz[here] * dz)
        if inj is not None:
            change = change + inj[here]
        out[here] = (center - prev[here]) + (center + change)


def outer(flags, part, k0, ki, kx, zm, ym, side, edge, new):
    rows = part.shape[0]
    for here, sums, dx in side_differences(rows, zm, side):
        new[here] = part[here] + (k0[here] * sums - kx[here] * dx)
    here, sums, di = edge_differences(flags, rows, ym, edge)
    new[here] += k0[here] * sums - ki[here] * di


def other_half(stage, flags, count):
    other = 1 - flags[4 + stage]
    for n in range(count // 2):
        high, low = n >> stage, n & ((1 << stage) - 1)
        yield n, (high << (stage + 1)) + (other << stage) + low


def trade(stage, flags, mine, got, out, give=None):
    out[...] = mine[...]
    for n, at in other_half(stage, flags, out.shape[0]):
        out[at] = got[n]
    if give is not None:
        for n, at in other_half(stage + 1, flags, out.shape[0]):
            give[n] = out[at]


def trade_kernel(stage, flags, mine, got, *outs):
    trade(stage, flags, mine, got, *outs)


def source_kernel(step, full, flags, src, wave, out):
    size, depth = out.shape
    count = src.shape[0]
    shift = (depth - 1).bit_length()
    plane = shift + (full - 1).bit_length()
    rows = size // COLS
    lane = lax.broadcasted_iota(jnp.int32, (1, count), 1)
    sub = lax.broadcasted_iota(jnp.int32, (count, 1), 0)
    row = jnp.zeros((1, count), jnp.int32)
    deep = jnp.zeros((count, 1), jnp.int32)
    size_of = jnp.zeros((count, 1), F32)
    for n in range(count):
        cell = src[n]
        i = jnp.right_shift(cell, plane) - flags[1] * rows
        x = jnp.bitwise_and(jnp.right_shift(cell, shift), full - 1)
        x = x - (2 * flags[3] + flags[0]) * COLS
        ok = (i >= 0) & (i < rows) & (x >= 0) & (x < COLS)
        row = jnp.where(lane == n, jnp.where(ok, i * COLS + x, -1), row)
        deep = jnp.where(sub == n, jnp.bitwise_and(cell, depth - 1), deep)
        size_of = jnp.where(sub == n, wave[step, n], size_of)
    spot = lax.broadcasted_iota(jnp.int32, (size, count), 0) == row
    spot = spot.astype(F32).astype(BF16)
    high, low = split(jnp.where(
        lax.broadcasted_iota(jnp.int32, (count, depth), 1) == deep, size_of, 0.0))
    out[...] = mm(spot, high) + mm(spot, low)


def forward_inner_kernel(step, full, flags, src, wave, cur, prev, k0, ki, kx, kz, cm, near, deep,
                         before, part, change):
    source_kernel(step, full, flags, src, wave, change)
    inner(cur, prev, k0, ki, kx, kz, cm, near, deep, change, part)
    change[...] = (cur[...] - prev[...]) - (prev[...] - before[...])


def outer_kernel(stage, double, flags, part, k0, ki, kx, zm, ym, side, edge, *rest):
    rest = list(rest)
    other = rest.pop(0) if double else None
    if stage is not None:
        mine, got, new, zo, co, yo, *lists = rest
        trade(stage, flags, mine, got, *lists)
    else:
        new, zo, co, yo = rest
    outer(flags, part, k0, ki, kx, zm, ym, side, edge, new)
    if double:
        for n, field in enumerate((new, other)):
            rims(flags, field, zo.at[n], co.at[n], yo.at[n])
    else:
        rims(flags, new, zo, co, yo)


def pack_kernel(flags, counts, cells, traces, cells_out, lists, give, counts_v, cells_v, traces_v,
                sems):
    pairs = ((counts, counts_v), (cells, cells_v), (traces, traces_v))
    copies = [pltpu.make_async_copy(a, b, sems.at[n]) for n, (a, b) in enumerate(pairs)]
    for copy in copies:
        copy.start()
    for copy in copies:
        copy.wait()
    subs, n = counts.shape[1], cells.shape[1]
    shape = (subs, n)
    lane = lax.broadcasted_iota(jnp.int32, shape, 1)
    mine = lane // CAP == lax.broadcasted_iota(jnp.int32, shape, 0)
    live = mm(counts_v[...].astype(F32).astype(BF16), mine.astype(F32).astype(BF16))
    slot = jnp.bitwise_and(lane[0:1], CAP - 1)
    cells_out[...] = jnp.where(slot.astype(F32) < live, cells_v[...].astype(F32), -1.0)
    for m in range(subs):
        q, y, c = m >> 2, (m >> 1) & 1, m & 1
        start = ((2 * q + c) * 2 + y) * CAP
        tile = traces_v[:, start // 128 * 128 : start // 128 * 128 + 128]
        lists[m] = pltpu.roll(tile, (128 - start % 128) % 128, axis=1) if start % 128 else tile
    for n, at in other_half(0, flags, subs):
        give[n] = lists[at]


def lists_kernel(flags, lists, own, got, spot, pick, at, obs):
    size, n = spot.shape
    depth = at.shape[1]
    subs, steps = lists.shape[0], obs.shape[1]
    cell = jnp.where(flags[0] == flags[1], own[...], got[...])
    along = jnp.floor((cell + 0.5) * (1.0 / depth))
    same = lax.broadcasted_iota(jnp.int32, (n, n), 0) == lax.broadcasted_iota(jnp.int32, (n, n), 1)

    def column(row):
        return jnp.sum(jnp.where(same, row, 0.0), axis=1, keepdims=True).astype(jnp.int32)

    hot = lax.broadcasted_iota(jnp.int32, (size, n), 0) == along.astype(jnp.int32)
    spot[...] = hot.astype(F32).astype(BF16)
    hot = lax.broadcasted_iota(jnp.int32, (n, size), 1) == column(along)
    pick[...] = hot.astype(F32).astype(BF16)
    hot = lax.broadcasted_iota(jnp.int32, (n, depth), 1) == column(cell - along * depth)
    at[...] = hot.astype(F32)
    traces = lists[...].reshape(subs * steps, 128).T[0:CAP]
    for s in range(subs):
        obs[s * CAP : s * CAP + CAP, :] = traces[:, s * steps : s * steps + steps]


def injection(t, state, spot, pick, at, obs):
    high, low = split(state[...])
    seen = at[...] * (mm(pick[...], high) + mm(pick[...], low))
    residual = jnp.sum(seen, axis=1, keepdims=True) - obs[:, t : t + 1]
    high, low = split(at[...] * residual)
    return mm(spot[...], high) + mm(spot[...], low)


def adjoint_inner_kernel(t, flags, cur, prev, k0, ki, kx, kz, cm, near, deep, state, spot, pick,
                         at, obs, *rest):
    if len(rest) == 4:
        change, image, part, image_out = rest
        image_out[...] = cur[...] * change[...] + image[...]
    else:
        now, mid, before, part, image_out = rest
        image_out[...] = cur[...] * ((now[...] - mid[...]) - (mid[...] - before[...]))
    inj = injection(t, state, spot, pick, at, obs)
    inner(cur, prev, k0, ki, kx, kz, cm, near, deep, inj, part)


def adjoint_first_kernel(flags, cur, prev, k0, ki, kx, kz, cm, near, deep, part):
    inner(cur, prev, k0, ki, kx, kz, cm.at[1], near, deep, None, part)


def turn_kernel(t, flags, part, k0, ki, kx, zm, ym, side, edge, u_part, u_zm, u_ym, spot, pick, at, obs, new, u_new, zo, co, yo):
    outer(flags, part, k0, ki, kx, zm, ym, side, edge, new)
    outer(flags, u_part, k0, ki, kx, u_zm.at[1], u_ym.at[1], side, edge, u_new)
    u_new[...] += injection(t, new, spot, pick, at, obs)
    rims(flags, u_new, zo, co, yo)


def last_kernel(scale, flags, part, k0, ki, kx, zm, ym, side, edge, image, change, vel,
                new, mine, other):
    outer(flags, part, k0, ki, kx, zm, ym, side, edge, new)
    raw = (image[...] + new[...] * change[...]) * scale / vel[...]
    count, height, lanes = mine.shape
    chunk = raw.shape[1] // (2 * count)
    for n in range(count):
        even, odd = (
            jnp.concatenate(
                [raw[g * height : g * height + height, m * chunk : m * chunk + chunk]
                 for g in range(lanes // chunk)], axis=1)
            for m in (2 * n, 2 * n + 1))
        mine[n] = jnp.where(flags[0] == 0, even, odd)
        other[n] = jnp.where(flags[0] == 0, odd, even)


def both_kernel(flags, a, b, out):
    out[0] = a[...]
    out[1] = b[...]


def join_kernel(flags, mine, got, *outs):
    for s, out in enumerate(outs):
        to = jnp.bitwise_xor(flags[3], s)
        a, b = mine[to], got[to]
        out[0] = jnp.where(flags[0] == 0, a, b)
        out[1] = jnp.where(flags[0] == 0, b, a)


def filter_kernel(flags, *refs):
    *pieces, out = refs
    height, lanes = pieces[0].shape[1:]
    chunk, rows, full = out.shape
    groups = lanes // chunk
    q = flags[3]
    shape = (full, full)
    y = lax.broadcasted_iota(jnp.int32, shape, 1)
    at = lax.broadcasted_iota(jnp.int32, shape, 0)
    within = jnp.bitwise_and(at, 2 * COLS - 1)
    place = jnp.bitwise_xor(q * (2 * COLS), at - within) + within
    weights = jnp.exp(jnp.abs(y - place).astype(F32) * (-1.0 / SMOOTH))
    weights = split(weights / jnp.sum(weights, axis=0, keepdims=True))
    ready = []
    for n in range(height // COLS):
        here = slice(n * COLS, n * COLS + COLS)
        lines = jnp.concatenate([piece[b, here, :] for piece in pieces for b in range(2)], axis=0)
        high, low = split(lines.T)
        done = mm(high, weights[0]) + mm(low, weights[0]) + mm(high, weights[1])
        ready.append(done)
    for g in range(groups):
        lines = jnp.stack([done[g * chunk : g * chunk + chunk] for done in ready], axis=0)
        out[:, g * (rows // groups) : (g + 1) * (rows // groups), :] = jnp.swapaxes(lines, 0, 1)


def shaped(*shape):
    return jax.ShapeDtypeStruct(shape, F32)


def call(kernel, name, outs, *args, weight=0, far=0, scalars=0, scratch=()):
    specs = [pl.BlockSpec(memory_space=pltpu.SMEM)] * (1 + scalars)
    specs += [pl.BlockSpec(memory_space=pl.ANY)] * far
    specs += [pl.BlockSpec(memory_space=pltpu.VMEM)] * (len(args) - 1 - scalars - far)
    return pl.pallas_call(
        kernel,
        name=name,
        out_shape=outs,
        in_specs=specs,
        out_specs=[pl.BlockSpec(memory_space=pltpu.VMEM)] * len(outs),
        scratch_shapes=list(scratch) + ([pltpu.SemaphoreType.DMA((far,))] if far else []),
        compiler_params=pltpu.CompilerParams(vmem_limit_bytes=VMEM_BYTES),
        cost_estimate=pl.CostEstimate(
            flops=1000, bytes_accessed=1000 + int(weight * 3_600_000), transcendentals=0),
    )(*args)


def per_device(plan, fwd_now, fwd_before, adj_now, adj_before, velocity, log_density, observed,
               rec_cells, rec_counts, src_cell, wavelet):
    rows, cols, depth = fwd_now.shape
    size = rows * cols
    steps = wavelet.shape[0]
    nx, nq = plan.nx, plan.nq
    subs = 2 * nx
    xline, c = lax.axis_index("xline"), lax.axis_index("inline")
    q, y = xline // 2, xline % 2
    keep = y == c
    z_perm, c_perm, y_perm, swap_perm = plan.z(), plan.core(), plan.y(), plan.swap()
    stages = [(c_perm, c), (y_perm, y)]
    stages += [(plan.flip(1 << b), (q >> b) & 1) for b in range((nq - 1).bit_length())]
    sub = (2 * q + c) * 2 + y
    flags = jnp.stack([c, y, sub, q] + [bit for pairs, bit in stages]).astype(jnp.int32)
    field = shaped(size, depth)
    side, edge = (size // 2, depth), (4 * cols, depth)
    rim = [shaped(*side), shaped(*side), shaped(*edge)]

    deep = depth_matrix(depth)
    deep = jnp.asarray(np.concatenate([deep, deep]), BF16)
    near = stencil_matrix(GROUP, cols)
    group, own, half = GROUP * cols, near.shape[1] - GROUP * 8, GROUP * 4
    both = [near[:, own : own + half], near[:, own + half :]]
    from_z = [np.concatenate([part[:group], part[2 * group :]]) for part in both]
    inside = jnp.where(c == 0, q > 0, q < nq - 1)
    side = jnp.where(c == 0, jnp.asarray(from_z[0], F32), jnp.asarray(from_z[1], F32))
    side = jnp.where(inside, side, 0.0).astype(BF16)
    side = jnp.concatenate([side, side], axis=1)
    core = jnp.where(c == 0, jnp.asarray(both[1], F32), jnp.asarray(both[0], F32)).astype(BF16)
    edge = jnp.where(y == 1, jnp.asarray(near[: 2 * group, : 4 * cols], F32),
                     jnp.asarray(near[: 2 * group, own - 4 * cols : own], F32)).astype(BF16)
    edge = jnp.concatenate([edge, edge], axis=1)
    near = jnp.asarray(np.concatenate([near[:, :own], near[:, :own]], axis=1), BF16)
    near = jnp.concatenate([near, core, core], axis=1)

    def halo(zo, co, yo):
        return send(zo, z_perm), send(co, c_perm), send(yo, y_perm)

    def after(value, *deps):
        return lax.optimization_barrier((value,) + deps)[0]

    def flat(value):
        return value.reshape(size, depth)

    log_density, fwd_now, velocity = flat(log_density), flat(fwd_now), flat(velocity)
    fwd_before, adj_now, adj_before = flat(fwd_before), flat(adj_now), flat(adj_before)
    got = [send(v, swap_perm) for v in (log_density, fwd_now)]
    stacked = jnp.stack([velocity, fwd_before])
    got_model = send(stacked, swap_perm)
    full = nx * cols
    inj, = call(functools.partial(source_kernel, 0, full), "source", [field], flags, src_cell, wavelet,
                weight=0.7, scalars=2)
    flags_in, inj = lax.optimization_barrier((flags, inj))
    density, p_now, *out = call(settle_kernel, "settle",
                                [field, field] + [shaped(2, *r.shape) for r in rim],
                                flags_in, log_density, fwd_now, *got, far=2)
    zm, cm = send(out[0], z_perm), send(out[1], c_perm)
    ym = send(after(out[2], cm), y_perm)
    vel, p_before = call(settle_pair_kernel, "settle_model", [field, field],
                         flags, velocity, fwd_before, got_model, weight=0.6, far=2)
    parts = call(first_inner_kernel, "first_inner", [field] * 7, flags, density, p_now, cm,
                 near, deep, weight=1.3)
    got_adjoint = send(
        jnp.stack([after(adj_now, parts[0]), after(adj_before, parts[0])]), swap_perm)

    new, zo, co, yo, k0, ki, kx, kz = call(
        first_outer_kernel, "first_outer", [field] + rim + [field] * 4,
        flags, p_now, p_before, vel, *parts, inj, zm, ym, side, edge)
    model = (k0, ki, kx, kz)
    states = [p_before, p_now, new]
    changes = []
    zm, cm, ym = halo(zo, co, yo)
    double = 1
    late = steps - 2 if len(stages) < steps - 2 else steps - 1

    slots = subs * CAP
    entries, half_entries = shaped(subs, steps, 128), shaped(subs // 2, steps, 128)
    cells, lists, give = call(
        pack_kernel, "pack", [shaped(1, slots), entries, half_entries], after(flags, k0), rec_counts,
        rec_cells, observed, weight=0.8, far=3,
        scratch=[pltpu.VMEM(rec_counts.shape, jnp.int32), pltpu.VMEM(rec_cells.shape, jnp.int32),
                 pltpu.VMEM(observed.shape, F32)])
    for t in range(1, steps):
        cur, prev, before = states[:-4:-1]
        stage = t - 1 if t <= min(len(stages), steps - 2) else None
        extra = [lists, send(give, stages[stage][0])] if stage is not None else []
        part, change = call(
            functools.partial(forward_inner_kernel, t, full), "forward_inner", [field, field], flags,
            src_cell, wavelet, cur, prev, *model, cm, near, deep, before, weight=1.2, scalars=2)
        changes.append(change)
        args = [flags, part, k0, ki, kx, zm, ym, side, edge]
        if t == steps - 3:
            u_part, = call(adjoint_first_kernel, "adjoint_first", [field], flags, u_now, u_before,
                           *model, u_cm, near, deep, weight=1.1)
            args[1] = after(part, u_part)
        if t == late:
            for n in range(steps - 2, len(stages)):
                lists, *give = call(
                    functools.partial(trade_kernel, n), "trade",
                    [entries] + ([half_entries] if n + 1 < len(stages) else []), flags, lists,
                    send(give, stages[n][0]))
                give = give[0] if give else None
            receivers = call(
                lists_kernel, "lists",
                [jax.ShapeDtypeStruct((size, slots), BF16),
                 jax.ShapeDtypeStruct((slots, size), BF16), shaped(slots, depth),
                 shaped(slots, steps)], flags, lists, cells, got_cells, weight=0.8)
            args[1] = after(part, receivers[0])
        if t == steps - 1:
            new, u_new, *out = call(
                functools.partial(turn_kernel, t), "turn", [field, field] + rim, *args, u_part,
                u_zm, u_ym, *receivers)
            states.append(new)
            break
        if t == len(stages) - 2:
            got_cells = send(after(cells, part), swap_perm)
        if t == len(stages) - 1:
            args[1] = after(part, got_cells)
        if t == double:
            u_now, u_before = call(settle_pair_kernel, "settle_adjoint", [field, field], flags,
                                   adj_now, adj_before, got_adjoint, weight=0.6, far=2)
            args.append(u_now)
        outs = [field] + ([shaped(2, *r.shape) for r in rim] if t == double else rim)
        if extra:
            outs = outs + [entries] + ([half_entries] if t < len(stages) else [])
        new, *out = call(functools.partial(outer_kernel, stage, t == double), "forward_outer", outs,
                         *args, *extra)
        if extra:
            out, (lists, *give) = out[:3], out[3:]
            give = give[0] if give else None
        states.append(new)
        zm, cm, ym = halo(*out)
        if t == double:
            u_zm, u_cm, u_ym = zm, cm, ym

    zm, cm, ym = halo(*out)
    u_before, u_now = u_now, u_new
    image = []
    chunk = depth // nx
    half = shaped(nq, size * chunk // 128, 128)
    for j in range(1, steps):
        t = steps - 1 - j
        terms = [changes[t + 1], *image] if image else states[:-4:-1]
        part, *image = call(
            functools.partial(adjoint_inner_kernel, t), "adjoint_inner", [field, field], flags,
            u_now, u_before, *model, cm, near, deep, states[t + 2], *receivers, *terms, weight=1.5)
        args = [part, k0, ki, kx, zm, ym, side, edge]
        if j == steps - 1:
            u_last, mine, other = call(
                functools.partial(last_kernel, 2.0 / steps), "last", [field, half, half], flags,
                *args, *image, changes[0], vel)
            break
        u_before = u_now
        u_now, *out = call(functools.partial(outer_kernel, None, False), "adjoint_outer", [field] + rim,
                           flags, *args)
        zm, cm, ym = halo(*out)

    final, = call(both_kernel, "both", [shaped(2, *field.shape)], flags, u_now, u_last, weight=0.4)
    got = send(final, swap_perm)
    pieces = call(join_kernel, "join", [shaped(2, *half.shape[1:])] * nq, flags, mine,
                  send(other, c_perm))
    pieces = [send(pieces[s], plan.spread(s)) for s in reversed(range(nq))][::-1]
    adj_prev, adj_out = call(select_kernel, "select", [field, field], flags, final, got, weight=1.2)
    gradient, = call(filter_kernel, "filter", [shaped(chunk, rows, nx * cols)],
                     after(flags, adj_out), *pieces)
    block = (rows, cols, depth)
    return gradient, adj_out.reshape(block), adj_prev.reshape(block)


def solution(mesh):
    field = P(("shots", "inline"), "xline", None)
    model = P("inline", "xline", None)
    lists = P(("xline", "inline"), None)
    return jax.shard_map(
        functools.partial(per_device, Plan(mesh)),
        mesh=mesh,
        in_specs=(field, field, field, field, model, model, P("shots", ("xline", "inline")),
                  lists, lists, P("shots"), P("shots", None)),
        out_specs=(P(("shots", "xline"), "inline", None), field, field),
        check_vma=False,
    )
```

```python
import functools

import jax
import jax.numpy as jnp
import numpy as np
from jax import lax
from jax.experimental import pallas as pl
from jax.experimental.pallas import tpu as pltpu
from jax.sharding import PartitionSpec as P

CAP = 8
SMOOTH = 16
SECOND = (-205.0 / 72.0, 8.0 / 5.0, -1.0 / 5.0, 8.0 / 315.0, -1.0 / 560.0)
FIRST = (4.0 / 5.0, -1.0 / 5.0, 4.0 / 105.0, -1.0 / 280.0)
ALL = ("shots", "xline", "inline")
COLS = 8
GROUP = 8
VMEM_BYTES = 8 * 1024 * 1024
F32 = jnp.float32
BF16 = jnp.bfloat16


class Plan:
    def __init__(self, mesh):
        self.shots = mesh.shape["shots"]
        self.nx = mesh.shape["xline"]
        self.nq = self.nx // 2

    def index(self, s, q, y, c):
        return (s * self.nx + 2 * q + y) * 2 + c

    def perm(self, partner):
        pairs = []
        for s in range(self.shots):
            for q in range(self.nq):
                for y in range(2):
                    for c in range(2):
                        t = partner(q, y, c)
                        dst = self.index(s ^ 1, q, y, c) if t is None else self.index(s, *t)
                        pairs.append((self.index(s, q, y, c), dst))
        return pairs

    def swap(self):
        return self.perm(lambda q, y, c: None if y == c else (q, c, y))

    def z(self):
        def partner(q, y, c):
            other = q + 1 if c == 1 else q - 1
            return (other, y, 1 - c) if 0 <= other < self.nq else None

        return self.perm(partner)

    def core(self):
        return self.perm(lambda q, y, c: (q, y, 1 - c))

    def y(self):
        return self.perm(lambda q, y, c: (q, 1 - y, c))

    def flip(self, bit):
        return self.perm(lambda q, y, c: (q ^ bit, y, c) if (q ^ bit) < self.nq else None)

    def spread(self, shift):
        return self.perm(lambda q, y, c: (q ^ shift, c, y))


def send(value, pairs):
    return lax.ppermute(value, ALL, pairs)


def depth_matrix(n):
    m = np.zeros((n, 2 * n), np.float32)
    for k in range(1, 5):
        for j in range(n):
            for i, sign in ((j + k, 1.0), (j - k, -1.0)):
                if 0 <= i < n:
                    m[i, j] = round(SECOND[k] * 5040)
                    m[i, n + j] = sign * round(FIRST[k - 1] * 840)
    return m


def stencil_matrix(rows, cols):
    own = (rows + 8) * cols
    m = np.zeros((3, rows, cols, own + rows * 8), np.float32)
    for i in range(rows):
        for x in range(cols):
            for k in range(1, 5):
                total = round(SECOND[k] * 5040)
                slope = round(FIRST[k - 1] * 840)
                for sign in (1, -1):
                    at = (i + 4 + sign * k) * cols + x
                    m[0, i, x, at] += total
                    m[1, i, x, at] += sign * slope
                    to = x + sign * k
                    if to < 0:
                        at = own + i * 4 + to + 4
                    elif to >= cols:
                        at = own + rows * 4 + i * 4 + to - cols
                    else:
                        at = (i + 4) * cols + to
                    m[0, i, x, at] += total
                    m[2, i, x, at] += sign * slope
    return m.reshape(3 * rows * cols, own + rows * 8)


def split(value):
    high = value.astype(BF16)
    return high, (value - high.astype(F32)).astype(BF16)


def mm(a, b):
    return jnp.dot(a, b, preferred_element_type=F32)


def inner_differences(cur, cm, near, deep):
    depth = cur.shape[1]
    size = GROUP * COLS
    cm = cm.at[0] if len(cm.shape) == 3 else cm
    own = split(cur[...])
    along = mm(jnp.concatenate(own, axis=1), deep[...])
    blank = jnp.zeros((4 * COLS, depth), BF16)
    ext = [jnp.concatenate([blank, part, blank], axis=0) for part in own]
    from_c = split(cm[...])
    for n in range(cur.shape[0] // size):
        here = slice(n * size, n * size + size)
        sides = slice(n * GROUP * 4, n * GROUP * 4 + GROUP * 4)
        rhs = [part[n * size : n * size + size + 8 * COLS] for part in ext]
        rhs += [part[sides] for part in from_c]
        out = mm(near[...], jnp.concatenate(rhs, axis=0))
        yield (here, out[0:size], along[here, 0:depth], out[size : 2 * size], out[2 * size :],
               along[here, depth:])


def side_differences(rows, zm, side):
    size = GROUP * COLS
    zm = zm.at[0] if len(zm.shape) == 3 else zm
    from_z = split(zm[...])
    for n in range(rows // size):
        sides = slice(n * GROUP * 4, n * GROUP * 4 + GROUP * 4)
        out = mm(side[...], jnp.concatenate([part[sides] for part in from_z], axis=0))
        yield slice(n * size, n * size + size), out[0:size], out[size:]


def edge_differences(flags, rows, ym, edge):
    size = GROUP * COLS
    ym = ym.at[0] if len(ym.shape) == 3 else ym
    out = mm(edge[...], jnp.concatenate(split(ym[...]), axis=0))
    start = jnp.where(flags[1] == 1, 0, rows - size)
    return pl.ds(pl.multiple_of(start, size), size), out[0:size], out[size:]


def halves(value):
    rows, depth = value.shape
    pairs = value.reshape(rows // (2 * COLS), 2, COLS, depth)
    a, b = pairs[:, 0], pairs[:, 1]
    low = lax.broadcasted_iota(jnp.int32, a.shape, 1) < 4
    first = jnp.where(low, a, pltpu.roll(b, 4, axis=1))
    last = jnp.where(low, pltpu.roll(a, 4, axis=1), b)
    return first.reshape(rows // 2, depth), last.reshape(rows // 2, depth)


def rims(flags, new, zo, co, yo):
    first, last = halves(new[...])
    zo[...] = jnp.where(flags[0] == 0, first, last)
    co[...] = jnp.where(flags[0] == 0, last, first)
    size = new.shape[0]
    yo[...] = jnp.where(flags[1] == 0, new[size - 4 * COLS :], new[0 : 4 * COLS])


def choose(flags, pairs, sems):
    keep = flags[0] == flags[1]

    @pl.when(keep)
    def _():
        copies = [pltpu.make_async_copy(own, out, sems.at[n])
                  for n, (own, recv, out) in enumerate(pairs)]
        for copy in copies:
            copy.start()
        for copy in copies:
            copy.wait()

    @pl.when(jnp.logical_not(keep))
    def _():
        for own, recv, out in pairs:
            out[...] = recv[...]


def settle_kernel(flags, a, b, recv_a, recv_b, a_out, b_out, zo, co, yo, sems):
    choose(flags, [(a, recv_a, a_out), (b, recv_b, b_out)], sems)
    for n, out in enumerate((a_out, b_out)):
        rims(flags, out, zo.at[n], co.at[n], yo.at[n])


def settle_pair_kernel(flags, a, b, *rest):
    *recv, a_out, b_out, sems = rest
    recv = recv if len(recv) == 2 else (recv[0].at[0], recv[0].at[1])
    choose(flags, [(a, recv[0], a_out), (b, recv[1], b_out)], sems)


def select_kernel(flags, own, recv, *outs):
    keep = flags[0] == flags[1]
    for n, out in enumerate(outs):
        out[...] = jnp.where(keep, own[n], recv[n])


def first_inner_kernel(flags, lr, cur, cm, near, deep, *outs):
    ri, rx, rz, sums_out, di_out, dx_out, dz_out = outs
    for here, spare, spare_z, di, dx, dz in inner_differences(lr, cm.at[0], near, deep):
        ri[here], rx[here], rz[here] = di, dx, dz
    for here, sums, sums_z, di, dx, dz in inner_differences(cur, cm.at[1], near, deep):
        sums_out[here] = sums + sums_z + (3.0 * SECOND[0] * 5040) * cur[here]
        di_out[here], dx_out[here], dz_out[here] = di, dx, dz


def first_outer_kernel(flags, cur, prev, vel, ri, rx, rz, sums, di, dx, dz, inj, zm, ym, side,
                       edge, new, zo, co, yo, k0, ki, kx, kz):
    rows = cur.shape[0]
    kz[...] = sums[...]
    ki[...] = di[...]
    here, more, more_i = edge_differences(flags, rows, ym.at[1], edge)
    kz[here] += more
    ki[here] += more_i
    lr_here, spare, lr_more_i = edge_differences(flags, rows, ym.at[0], edge)
    k0[...] = ri[...]
    k0[lr_here] += lr_more_i
    first = side_differences(rows, zm.at[0], side)
    second = side_differences(rows, zm.at[1], side)
    for (here, spare, more_r), (spare_here, more, more_x) in zip(first, second):
        square = vel[here] * vel[here]
        scaled = square * (1.0 / (840 * 840))
        factor = square * (1.0 / 5040)
        along_i, along_x, along_z = scaled * k0[here], scaled * (rx[here] + more_r), scaled * rz[here]
        change = factor * (kz[here] + more) - (
            along_i * ki[here] + along_x * (dx[here] + more_x) + along_z * dz[here])
        k0[here], ki[here], kx[here], kz[here] = factor, along_i, along_x, along_z
        center = cur[here]
        new[here] = (center - prev[here]) + (center + (change + inj[here]))
    rims(flags, new, zo, co, yo)


def inner(cur, prev, k0, ki, kx, kz, cm, near, deep, inj, out):
    for here, sums, sums_z, di, dx, dz in inner_differences(cur, cm, near, deep):
        center = cur[here]
        change = k0[here] * ((sums + sums_z) + (3.0 * SECOND[0] * 5040) * center)
        change = change - (ki[here] * di + kx[here] * dx + kz[here] * dz)
        if inj is not None:
            change = change + inj[here]
        out[here] = (center - prev[here]) + (center + change)


def outer(flags, part, k0, ki, kx, zm, ym, side, edge, new):
    rows = part.shape[0]
    for here, sums, dx in side_differences(rows, zm, side):
        new[here] = part[here] + (k0[here] * sums - kx[here] * dx)
    here, sums, di = edge_differences(flags, rows, ym, edge)
    new[here] += k0[here] * sums - ki[here] * di


def other_half(stage, flags, count):
    other = 1 - flags[4 + stage]
    for n in range(count // 2):
        high, low = n >> stage, n & ((1 << stage) - 1)
        yield n, (high << (stage + 1)) + (other << stage) + low


def trade(stage, flags, mine, got, out, give=None):
    out[...] = mine[...]
    for n, at in other_half(stage, flags, out.shape[0]):
        out[at] = got[n]
    if give is not None:
        for n, at in other_half(stage + 1, flags, out.shape[0]):
            give[n] = out[at]


def trade_kernel(stage, flags, mine, got, *outs):
    trade(stage, flags, mine, got, *outs)


def source_kernel(step, full, flags, src, wave, out):
    size, depth = out.shape
    count = src.shape[0]
    shift = (depth - 1).bit_length()
    plane = shift + (full - 1).bit_length()
    rows = size // COLS
    lane = lax.broadcasted_iota(jnp.int32, (1, count), 1)
    sub = lax.broadcasted_iota(jnp.int32, (count, 1), 0)
    row = jnp.zeros((1, count), jnp.int32)
    deep = jnp.zeros((count, 1), jnp.int32)
    size_of = jnp.zeros((count, 1), F32)
    for n in range(count):
        cell = src[n]
        i = jnp.right_shift(cell, plane) - flags[1] * rows
        x = jnp.bitwise_and(jnp.right_shift(cell, shift), full - 1)
        x = x - (2 * flags[3] + flags[0]) * COLS
        ok = (i >= 0) & (i < rows) & (x >= 0) & (x < COLS)
        row = jnp.where(lane == n, jnp.where(ok, i * COLS + x, -1), row)
        deep = jnp.where(sub == n, jnp.bitwise_and(cell, depth - 1), deep)
        size_of = jnp.where(sub == n, wave[step, n], size_of)
    spot = lax.broadcasted_iota(jnp.int32, (size, count), 0) == row
    spot = spot.astype(F32).astype(BF16)
    high, low = split(jnp.where(
        lax.broadcasted_iota(jnp.int32, (count, depth), 1) == deep, size_of, 0.0))
    out[...] = mm(spot, high) + mm(spot, low)


def forward_inner_kernel(step, full, flags, src, wave, cur, prev, k0, ki, kx, kz, cm, near, deep,
                         before, part, change):
    source_kernel(step, full, flags, src, wave, change)
    inner(cur, prev, k0, ki, kx, kz, cm, near, deep, change, part)
    change[...] = (cur[...] - prev[...]) - (prev[...] - before[...])


def outer_kernel(stage, double, flags, part, k0, ki, kx, zm, ym, side, edge, *rest):
    rest = list(rest)
    other = rest.pop(0) if double else None
    if stage is not None:
        mine, got, new, zo, co, yo, *lists = rest
        trade(stage, flags, mine, got, *lists)
    else:
        new, zo, co, yo = rest
    outer(flags, part, k0, ki, kx, zm, ym, side, edge, new)
    if double:
        for n, field in enumerate((new, other)):
            rims(flags, field, zo.at[n], co.at[n], yo.at[n])
    else:
        rims(flags, new, zo, co, yo)


def pack_kernel(flags, counts, cells, traces, cells_out, lists, give, counts_v, cells_v, traces_v,
                sems):
    pairs = ((counts, counts_v), (cells, cells_v), (traces, traces_v))
    copies = [pltpu.make_async_copy(a, b, sems.at[n]) for n, (a, b) in enumerate(pairs)]
    for copy in copies:
        copy.start()
    for copy in copies:
        copy.wait()
    subs, n = counts.shape[1], cells.shape[1]
    shape = (subs, n)
    lane = lax.broadcasted_iota(jnp.int32, shape, 1)
    mine = lane // CAP == lax.broadcasted_iota(jnp.int32, shape, 0)
    live = mm(counts_v[...].astype(F32).astype(BF16), mine.astype(F32).astype(BF16))
    slot = jnp.bitwise_and(lane[0:1], CAP - 1)
    cells_out[...] = jnp.where(slot.astype(F32) < live, cells_v[...].astype(F32), -1.0)
    for m in range(subs):
        q, y, c = m >> 2, (m >> 1) & 1, m & 1
        start = ((2 * q + c) * 2 + y) * CAP
        tile = traces_v[:, start // 128 * 128 : start // 128 * 128 + 128]
        lists[m] = pltpu.roll(tile, (128 - start % 128) % 128, axis=1) if start % 128 else tile
    for n, at in other_half(0, flags, subs):
        give[n] = lists[at]


def lists_kernel(flags, lists, own, got, spot, pick, at, obs):
    size, n = spot.shape
    depth = at.shape[1]
    subs, steps = lists.shape[0], obs.shape[1]
    cell = jnp.where(flags[0] == flags[1], own[...], got[...])
    along = jnp.floor((cell + 0.5) * (1.0 / depth))
    same = lax.broadcasted_iota(jnp.int32, (n, n), 0) == lax.broadcasted_iota(jnp.int32, (n, n), 1)

    def column(row):
        return jnp.sum(jnp.where(same, row, 0.0), axis=1, keepdims=True).astype(jnp.int32)

    hot = lax.broadcasted_iota(jnp.int32, (size, n), 0) == along.astype(jnp.int32)
    spot[...] = hot.astype(F32).astype(BF16)
    hot = lax.broadcasted_iota(jnp.int32, (n, size), 1) == column(along)
    pick[...] = hot.astype(F32).astype(BF16)
    hot = lax.broadcasted_iota(jnp.int32, (n, depth), 1) == column(cell - along * depth)
    at[...] = hot.astype(F32)
    traces = lists[...].reshape(subs * steps, 128).T[0:CAP]
    for s in range(subs):
        obs[s * CAP : s * CAP + CAP, :] = traces[:, s * steps : s * steps + steps]


def injection(t, state, spot, pick, at, obs):
    high, low = split(state[...])
    seen = at[...] * (mm(pick[...], high) + mm(pick[...], low))
    residual = jnp.sum(seen, axis=1, keepdims=True) - obs[:, t : t + 1]
    high, low = split(at[...] * residual)
    return mm(spot[...], high) + mm(spot[...], low)


def adjoint_inner_kernel(t, flags, cur, prev, k0, ki, kx, kz, cm, near, deep, state, spot, pick,
                         at, obs, *rest):
    if len(rest) == 4:
        change, image, part, image_out = rest
        image_out[...] = cur[...] * change[...] + image[...]
    else:
        now, mid, before, part, image_out = rest
        image_out[...] = cur[...] * ((now[...] - mid[...]) - (mid[...] - before[...]))
    inj = injection(t, state, spot, pick, at, obs)
    inner(cur, prev, k0, ki, kx, kz, cm, near, deep, inj, part)


def adjoint_first_kernel(flags, cur, prev, k0, ki, kx, kz, cm, near, deep, part):
    inner(cur, prev, k0, ki, kx, kz, cm.at[1], near, deep, None, part)


def turn_kernel(t, flags, part, k0, ki, kx, zm, ym, side, edge, u_part, u_zm, u_ym, spot, pick, at, obs, new, u_new, zo, co, yo):
    outer(flags, part, k0, ki, kx, zm, ym, side, edge, new)
    outer(flags, u_part, k0, ki, kx, u_zm.at[1], u_ym.at[1], side, edge, u_new)
    u_new[...] += injection(t, new, spot, pick, at, obs)
    rims(flags, u_new, zo, co, yo)


def last_kernel(scale, flags, part, k0, ki, kx, zm, ym, side, edge, image, change, vel,
                new, mine, other):
    outer(flags, part, k0, ki, kx, zm, ym, side, edge, new)
    raw = (image[...] + new[...] * change[...]) * scale / vel[...]
    count, height, lanes = mine.shape
    chunk = raw.shape[1] // (2 * count)
    for n in range(count):
        even, odd = (
            jnp.concatenate(
                [raw[g * height : g * height + height, m * chunk : m * chunk + chunk]
                 for g in range(lanes // chunk)], axis=1)
            for m in (2 * n, 2 * n + 1))
        mine[n] = jnp.where(flags[0] == 0, even, odd)
        other[n] = jnp.where(flags[0] == 0, odd, even)


def both_kernel(flags, a, b, out):
    out[0] = a[...]
    out[1] = b[...]


def join_kernel(flags, mine, got, *outs):
    for s, out in enumerate(outs):
        to = jnp.bitwise_xor(flags[3], s)
        a, b = mine[to], got[to]
        out[0] = jnp.where(flags[0] == 0, a, b)
        out[1] = jnp.where(flags[0] == 0, b, a)


def filter_kernel(flags, *refs):
    *pieces, out = refs
    height, lanes = pieces[0].shape[1:]
    chunk, rows, full = out.shape
    groups = lanes // chunk
    q = flags[3]
    shape = (full, full)
    y = lax.broadcasted_iota(jnp.int32, shape, 1)
    at = lax.broadcasted_iota(jnp.int32, shape, 0)
    within = jnp.bitwise_and(at, 2 * COLS - 1)
    place = jnp.bitwise_xor(q * (2 * COLS), at - within) + within
    weights = jnp.exp(jnp.abs(y - place).astype(F32) * (-1.0 / SMOOTH))
    weights = split(weights / jnp.sum(weights, axis=0, keepdims=True))
    ready = []
    for n in range(height // COLS):
        here = slice(n * COLS, n * COLS + COLS)
        lines = jnp.concatenate([piece[b, here, :] for piece in pieces for b in range(2)], axis=0)
        high, low = split(lines.T)
        done = mm(high, weights[0]) + mm(low, weights[0]) + mm(high, weights[1])
        ready.append(done)
    for g in range(groups):
        lines = jnp.stack([done[g * chunk : g * chunk + chunk] for done in ready], axis=0)
        out[:, g * (rows // groups) : (g + 1) * (rows // groups), :] = jnp.swapaxes(lines, 0, 1)


def shaped(*shape):
    return jax.ShapeDtypeStruct(shape, F32)


def call(kernel, name, outs, *args, weight=0, far=0, scalars=0, scratch=()):
    specs = [pl.BlockSpec(memory_space=pltpu.SMEM)] * (1 + scalars)
    specs += [pl.BlockSpec(memory_space=pl.ANY)] * far
    specs += [pl.BlockSpec(memory_space=pltpu.VMEM)] * (len(args) - 1 - scalars - far)
    return pl.pallas_call(
        kernel,
        name=name,
        out_shape=outs,
        in_specs=specs,
        out_specs=[pl.BlockSpec(memory_space=pltpu.VMEM)] * len(outs),
        scratch_shapes=list(scratch) + ([pltpu.SemaphoreType.DMA((far,))] if far else []),
        compiler_params=pltpu.CompilerParams(vmem_limit_bytes=VMEM_BYTES),
        cost_estimate=pl.CostEstimate(
            flops=1000, bytes_accessed=1000 + int(weight * 3_600_000), transcendentals=0),
    )(*args)


def per_device(plan, fwd_now, fwd_before, adj_now, adj_before, velocity, log_density, observed,
               rec_cells, rec_counts, src_cell, wavelet):
    rows, cols, depth = fwd_now.shape
    size = rows * cols
    steps = wavelet.shape[0]
    nx, nq = plan.nx, plan.nq
    subs = 2 * nx
    xline, c = lax.axis_index("xline"), lax.axis_index("inline")
    q, y = xline // 2, xline % 2
    keep = y == c
    z_perm, c_perm, y_perm, swap_perm = plan.z(), plan.core(), plan.y(), plan.swap()
    stages = [(c_perm, c), (y_perm, y)]
    stages += [(plan.flip(1 << b), (q >> b) & 1) for b in range((nq - 1).bit_length())]
    sub = (2 * q + c) * 2 + y
    flags = jnp.stack([c, y, sub, q] + [bit for pairs, bit in stages]).astype(jnp.int32)
    field = shaped(size, depth)
    side, edge = (size // 2, depth), (4 * cols, depth)
    rim = [shaped(*side), shaped(*side), shaped(*edge)]

    deep = depth_matrix(depth)
    deep = jnp.asarray(np.concatenate([deep, deep]), BF16)
    near = stencil_matrix(GROUP, cols)
    group, own, half = GROUP * cols, near.shape[1] - GROUP * 8, GROUP * 4
    both = [near[:, own : own + half], near[:, own + half :]]
    from_z = [np.concatenate([part[:group], part[2 * group :]]) for part in both]
    inside = jnp.where(c == 0, q > 0, q < nq - 1)
    side = jnp.where(c == 0, jnp.asarray(from_z[0], F32), jnp.asarray(from_z[1], F32))
    side = jnp.where(inside, side, 0.0).astype(BF16)
    side = jnp.concatenate([side, side], axis=1)
    core = jnp.where(c == 0, jnp.asarray(both[1], F32), jnp.asarray(both[0], F32)).astype(BF16)
    edge = jnp.where(y == 1, jnp.asarray(near[: 2 * group, : 4 * cols], F32),
                     jnp.asarray(near[: 2 * group, own - 4 * cols : own], F32)).astype(BF16)
    edge = jnp.concatenate([edge, edge], axis=1)
    near = jnp.asarray(np.concatenate([near[:, :own], near[:, :own]], axis=1), BF16)
    near = jnp.concatenate([near, core, core], axis=1)

    def halo(zo, co, yo):
        return send(zo, z_perm), send(co, c_perm), send(yo, y_perm)

    def after(value, *deps):
        return lax.optimization_barrier((value,) + deps)[0]

    def flat(value):
        return value.reshape(size, depth)

    log_density, fwd_now, velocity = flat(log_density), flat(fwd_now), flat(velocity)
    fwd_before, adj_now, adj_before = flat(fwd_before), flat(adj_now), flat(adj_before)
    got = [send(v, swap_perm) for v in (log_density, fwd_now)]
    stacked = jnp.stack([velocity, fwd_before])
    got_model = send(stacked, swap_perm)
    full = nx * cols
    inj, = call(functools.partial(source_kernel, 0, full), "source", [field], flags, src_cell, wavelet,
                weight=0.7, scalars=2)
    flags_in, inj = lax.optimization_barrier((flags, inj))
    density, p_now, *out = call(settle_kernel, "settle",
                                [field, field] + [shaped(2, *r.shape) for r in rim],
                                flags_in, log_density, fwd_now, *got, far=2)
    zm, cm, ym = halo(*out)
    vel, p_before = call(settle_pair_kernel, "settle_model", [field, field],
                         flags, velocity, fwd_before, got_model, weight=0.6, far=2)
    parts = call(first_inner_kernel, "first_inner", [field] * 7, flags, density, p_now, cm,
                 near, deep, weight=1.3)
    got_adjoint = [send(after(v, parts[0]), swap_perm) for v in (adj_now, adj_before)]

    new, zo, co, yo, k0, ki, kx, kz = call(
        first_outer_kernel, "first_outer", [field] + rim + [field] * 4,
        flags, p_now, p_before, vel, *parts, inj, zm, ym, side, edge)
    model = (k0, ki, kx, kz)
    states = [p_before, p_now, new]
    changes = []
    zm, cm, ym = halo(zo, co, yo)
    double = 1
    late = steps - 2 if len(stages) < steps - 2 else steps - 1

    slots = subs * CAP
    entries, half_entries = shaped(subs, steps, 128), shaped(subs // 2, steps, 128)
    cells, lists, give = call(
        pack_kernel, "pack", [shaped(1, slots), entries, half_entries], after(flags, k0), rec_counts,
        rec_cells, observed, weight=0.8, far=3,
        scratch=[pltpu.VMEM(rec_counts.shape, jnp.int32), pltpu.VMEM(rec_cells.shape, jnp.int32),
                 pltpu.VMEM(observed.shape, F32)])
    for t in range(1, steps):
        cur, prev, before = states[:-4:-1]
        stage = t - 1 if t <= min(len(stages), steps - 2) else None
        extra = [lists, send(give, stages[stage][0])] if stage is not None else []
        part, change = call(
            functools.partial(forward_inner_kernel, t, full), "forward_inner", [field, field], flags,
            src_cell, wavelet, cur, prev, *model, cm, near, deep, before, weight=1.2, scalars=2)
        changes.append(change)
        args = [flags, part, k0, ki, kx, zm, ym, side, edge]
        if t == steps - 3:
            u_part, = call(adjoint_first_kernel, "adjoint_first", [field], flags, u_now, u_before,
                           *model, u_cm, near, deep, weight=1.1)
            args[1] = after(part, u_part)
        if t == late:
            for n in range(steps - 2, len(stages)):
                lists, *give = call(
                    functools.partial(trade_kernel, n), "trade",
                    [entries] + ([half_entries] if n + 1 < len(stages) else []), flags, lists,
                    send(give, stages[n][0]))
                give = give[0] if give else None
            receivers = call(
                lists_kernel, "lists",
                [jax.ShapeDtypeStruct((size, slots), BF16),
                 jax.ShapeDtypeStruct((slots, size), BF16), shaped(slots, depth),
                 shaped(slots, steps)], flags, lists, cells, got_cells, weight=0.8)
            args[1] = after(part, receivers[0])
        if t == steps - 1:
            new, u_new, *out = call(
                functools.partial(turn_kernel, t), "turn", [field, field] + rim, *args, u_part,
                u_zm, u_ym, *receivers)
            states.append(new)
            break
        if t == len(stages) - 2:
            got_cells = send(after(cells, part), swap_perm)
        if t == len(stages) - 1:
            args[1] = after(part, got_cells)
        if t == double:
            u_now, u_before = call(settle_pair_kernel, "settle_adjoint", [field, field], flags,
                                   adj_now, adj_before, *got_adjoint, weight=0.6, far=2)
            args.append(u_now)
        outs = [field] + ([shaped(2, *r.shape) for r in rim] if t == double else rim)
        if extra:
            outs = outs + [entries] + ([half_entries] if t < len(stages) else [])
        new, *out = call(functools.partial(outer_kernel, stage, t == double), "forward_outer", outs,
                         *args, *extra)
        if extra:
            out, (lists, *give) = out[:3], out[3:]
            give = give[0] if give else None
        states.append(new)
        zm, cm, ym = halo(*out)
        if t == double:
            u_zm, u_cm, u_ym = zm, cm, ym

    zm, cm, ym = halo(*out)
    u_before, u_now = u_now, u_new
    image = []
    chunk = depth // nx
    half = shaped(nq, size * chunk // 128, 128)
    for j in range(1, steps):
        t = steps - 1 - j
        terms = [changes[t + 1], *image] if image else states[:-4:-1]
        part, *image = call(
            functools.partial(adjoint_inner_kernel, t), "adjoint_inner", [field, field], flags,
            u_now, u_before, *model, cm, near, deep, states[t + 2], *receivers, *terms, weight=1.5)
        args = [part, k0, ki, kx, zm, ym, side, edge]
        if j == steps - 1:
            u_last, mine, other = call(
                functools.partial(last_kernel, 2.0 / steps), "last", [field, half, half], flags,
                *args, *image, changes[0], vel)
            break
        u_before = u_now
        u_now, *out = call(functools.partial(outer_kernel, None, False), "adjoint_outer", [field] + rim,
                           flags, *args)
        zm, cm, ym = halo(*out)

    final, = call(both_kernel, "both", [shaped(2, *field.shape)], flags, u_now, u_last, weight=0.4)
    got = send(final, swap_perm)
    pieces = call(join_kernel, "join", [shaped(2, *half.shape[1:])] * nq, flags, mine,
                  send(other, c_perm))
    pieces = [send(pieces[s], plan.spread(s)) for s in reversed(range(nq))][::-1]
    adj_prev, adj_out = call(select_kernel, "select", [field, field], flags, final, got, weight=1.2)
    gradient, = call(filter_kernel, "filter", [shaped(chunk, rows, nx * cols)],
                     after(flags, adj_out), *pieces)
    block = (rows, cols, depth)
    return gradient, adj_out.reshape(block), adj_prev.reshape(block)


def solution(mesh):
    field = P(("shots", "inline"), "xline", None)
    model = P("inline", "xline", None)
    lists = P(("xline", "inline"), None)
    return jax.shard_map(
        functools.partial(per_device, Plan(mesh)),
        mesh=mesh,
        in_specs=(field, field, field, field, model, model, P("shots", ("xline", "inline")),
                  lists, lists, P("shots"), P("shots", None)),
        out_specs=(P(("shots", "xline"), "inline", None), field, field),
        check_vma=False,
    )
```

```python
import functools

import jax
import jax.numpy as jnp
import numpy as np
from jax import lax
from jax.experimental import pallas as pl
from jax.experimental.pallas import tpu as pltpu
from jax.sharding import PartitionSpec as P

CAP = 8
SMOOTH = 16
SECOND = (-205.0 / 72.0, 8.0 / 5.0, -1.0 / 5.0, 8.0 / 315.0, -1.0 / 560.0)
FIRST = (4.0 / 5.0, -1.0 / 5.0, 4.0 / 105.0, -1.0 / 280.0)
ALL = ("shots", "xline", "inline")
COLS = 8
GROUP = 8
VMEM_BYTES = 8 * 1024 * 1024
F32 = jnp.float32
BF16 = jnp.bfloat16


class Plan:
    def __init__(self, mesh):
        self.shots = mesh.shape["shots"]
        self.nx = mesh.shape["xline"]
        self.nq = self.nx // 2

    def index(self, s, q, y, c):
        return (s * self.nx + 2 * q + y) * 2 + c

    def perm(self, partner):
        pairs = []
        for s in range(self.shots):
            for q in range(self.nq):
                for y in range(2):
                    for c in range(2):
                        t = partner(q, y, c)
                        dst = self.index(s ^ 1, q, y, c) if t is None else self.index(s, *t)
                        pairs.append((self.index(s, q, y, c), dst))
        return pairs

    def swap(self):
        return self.perm(lambda q, y, c: None if y == c else (q, c, y))

    def z(self):
        def partner(q, y, c):
            other = q + 1 if c == 1 else q - 1
            return (other, y, 1 - c) if 0 <= other < self.nq else None

        return self.perm(partner)

    def core(self):
        return self.perm(lambda q, y, c: (q, y, 1 - c))

    def y(self):
        return self.perm(lambda q, y, c: (q, 1 - y, c))

    def flip(self, bit):
        return self.perm(lambda q, y, c: (q ^ bit, y, c) if (q ^ bit) < self.nq else None)

    def spread(self, shift):
        return self.perm(lambda q, y, c: (q ^ shift, c, y))


def send(value, pairs):
    return lax.ppermute(value, ALL, pairs)


def depth_matrix(n):
    m = np.zeros((n, 2 * n), np.float32)
    for k in range(1, 5):
        for j in range(n):
            for i, sign in ((j + k, 1.0), (j - k, -1.0)):
                if 0 <= i < n:
                    m[i, j] = round(SECOND[k] * 5040)
                    m[i, n + j] = sign * round(FIRST[k - 1] * 840)
    return m


def stencil_matrix(rows, cols):
    own = (rows + 8) * cols
    m = np.zeros((3, rows, cols, own + rows * 8), np.float32)
    for i in range(rows):
        for x in range(cols):
            for k in range(1, 5):
                total = round(SECOND[k] * 5040)
                slope = round(FIRST[k - 1] * 840)
                for sign in (1, -1):
                    at = (i + 4 + sign * k) * cols + x
                    m[0, i, x, at] += total
                    m[1, i, x, at] += sign * slope
                    to = x + sign * k
                    if to < 0:
                        at = own + i * 4 + to + 4
                    elif to >= cols:
                        at = own + rows * 4 + i * 4 + to - cols
                    else:
                        at = (i + 4) * cols + to
                    m[0, i, x, at] += total
                    m[2, i, x, at] += sign * slope
    return m.reshape(3 * rows * cols, own + rows * 8)


def halved(rows, cols, c):
    at = np.arange(rows)[:, None] * cols
    z_side = (at + 4 * c + np.arange(4)).reshape(-1)
    return np.concatenate([z_side, (at + 4 * (1 - c) + np.arange(4)).reshape(-1)])


def near_matrix(rows, cols, c):
    m = stencil_matrix(rows, cols)
    own = (rows + 8) * cols
    place = halved(rows, cols, c)
    out = np.concatenate([place + k * rows * cols for k in range(3)])
    side = own + (1 - c) * rows * 4 + np.arange(rows * 4)
    return m[out][:, np.concatenate([halved(rows + 8, cols, c), side])]


def side_matrix(rows, c):
    m = np.zeros((2, rows, 4, rows, 4), np.float32)
    for x in range(4):
        for k in range(4):
            d = x + 4 - k if c == 0 else k + 4 - x
            if d <= 4:
                for i in range(rows):
                    m[0, i, x, i, k] = round(SECOND[d] * 5040)
                    m[1, i, x, i, k] = round(FIRST[d - 1] * 840) * (-1 if c == 0 else 1)
    return m.reshape(2 * rows * 4, rows * 4)


def edge_matrix(y):
    m = np.zeros((2, 2, 4, 4, 2, 4, 4), np.float32)
    for i in range(4):
        for k in range(4):
            d = i + 4 - k if y == 1 else k + 4 - i
            if d <= 4:
                for part in range(2):
                    for x in range(4):
                        m[0, part, i, x, part, k, x] = round(SECOND[d] * 5040)
                        m[1, part, i, x, part, k, x] = round(FIRST[d - 1] * 840) * (-1 if y == 1 else 1)
    return m.reshape(64, 32)


def split(value):
    high = value.astype(BF16)
    return high, (value - high.astype(F32)).astype(BF16)


def mm(a, b):
    return jnp.dot(a, b, preferred_element_type=F32)


def inner_differences(cur, cm, near, deep):
    size, depth = cur.shape
    half = size // 2
    cm = cm.at[0] if len(cm.shape) == 3 else cm
    own = split(cur[...])
    along = mm(jnp.concatenate(own, axis=1), deep[...])
    blank = jnp.zeros((16, depth), BF16)
    ext = [[jnp.concatenate([blank, part[h * half : h * half + half], blank], axis=0)
            for h in range(2)] for part in own]
    from_c = split(cm[...])
    step = GROUP * 4
    for n in range(half // step):
        rhs = [part[h][n * step : n * step + step + 32] for part in ext for h in range(2)]
        rhs += [part[n * step : n * step + step] for part in from_c]
        out = mm(near[...], jnp.concatenate(rhs, axis=0))
        for h in range(2):
            here = slice(h * half + n * step, h * half + n * step + step)
            sums, di, dx = (out[(2 * k + h) * step : (2 * k + h + 1) * step] for k in range(3))
            yield here, sums, along[here, 0:depth], di, dx, along[here, depth:]


def side_differences(zm, side):
    zm = zm.at[0] if len(zm.shape) == 3 else zm
    out = mm(side[...], jnp.concatenate(split(zm[...]), axis=0))
    half = out.shape[0] // 2
    return out[0:half], out[half:]


def edge_differences(flags, size, ym, edge):
    ym = ym.at[0] if len(ym.shape) == 3 else ym
    out = mm(edge[...], jnp.concatenate(split(ym[...]), axis=0))
    start = jnp.where(flags[1] == 1, 0, size // 2 - 16)
    for h in range(2):
        at = pl.ds(pl.multiple_of(start + h * (size // 2), 16), 16)
        yield at, out[h * 16 : h * 16 + 16], out[32 + h * 16 : 48 + h * 16]


def to_halves(flags, value):
    rows, depth = value.shape
    pairs = value.reshape(rows // (2 * COLS), 2, COLS, depth)
    a, b = pairs[:, 0], pairs[:, 1]
    low = lax.broadcasted_iota(jnp.int32, a.shape, 1) < 4
    first = jnp.where(low, a, pltpu.roll(b, 4, axis=1)).reshape(rows // 2, depth)
    last = jnp.where(low, pltpu.roll(a, 4, axis=1), b).reshape(rows // 2, depth)
    return jnp.where(flags[0] == 0, first, last), jnp.where(flags[0] == 0, last, first)


def from_halves(flags, value):
    rows, depth = value.shape
    z_side, c_side = value[0 : rows // 2], value[rows // 2 :]
    shape = (rows // (2 * COLS), COLS, depth)
    first = jnp.where(flags[0] == 0, z_side, c_side).reshape(shape)
    last = jnp.where(flags[0] == 0, c_side, z_side).reshape(shape)
    low = lax.broadcasted_iota(jnp.int32, shape, 1) < 4
    a = jnp.where(low, first, pltpu.roll(last, 4, axis=1))
    b = jnp.where(low, pltpu.roll(first, 4, axis=1), last)
    return jnp.stack([a, b], axis=1).reshape(rows, depth)


def place_of(flags, size, i, x):
    near = x - 4 * flags[0]
    return i * 4 + jnp.where((near >= 0) & (near < 4), near, size // 2 + x - 4 * (1 - flags[0]))


def rims(flags, new, zo, co, yo):
    size = new.shape[0]
    half = size // 2
    zo[...] = new[0:half]
    co[...] = new[half:]
    last = jnp.concatenate([new[half - 16 : half], new[size - 16 :]], axis=0)
    first = jnp.concatenate([new[0:16], new[half : half + 16]], axis=0)
    yo[...] = jnp.where(flags[1] == 0, last, first)


def choose(flags, pairs, sems):
    keep = flags[0] == flags[1]

    @pl.when(keep)
    def _():
        copies = [pltpu.make_async_copy(own, out, sems.at[n])
                  for n, (own, recv, out) in enumerate(pairs)]
        for copy in copies:
            copy.start()
        for copy in copies:
            copy.wait()

    @pl.when(jnp.logical_not(keep))
    def _():
        for own, recv, out in pairs:
            out[...] = recv[...]

    for own, recv, out in pairs:
        half = out.shape[0] // 2
        z_side, c_side = to_halves(flags, out[...])
        out[0:half] = z_side
        out[half:] = c_side


def settle_kernel(flags, a, b, recv_a, recv_b, a_out, b_out, zo, co, yo, sems):
    choose(flags, [(a, recv_a, a_out), (b, recv_b, b_out)], sems)
    for n, out in enumerate((a_out, b_out)):
        rims(flags, out, zo.at[n], co.at[n], yo.at[n])


def settle_pair_kernel(flags, a, b, *rest):
    *recv, a_out, b_out, sems = rest
    recv = recv if len(recv) == 2 else (recv[0].at[0], recv[0].at[1])
    choose(flags, [(a, recv[0], a_out), (b, recv[1], b_out)], sems)


def select_kernel(flags, own, recv, *outs):
    keep = flags[0] == flags[1]
    for n, out in enumerate(outs):
        out[...] = jnp.where(keep, own[n], recv[n])


def first_inner_kernel(flags, lr, cur, cm, near, deep, *outs):
    ri, rx, rz, sums_out, di_out, dx_out, dz_out = outs
    for here, spare, spare_z, di, dx, dz in inner_differences(lr, cm.at[0], near, deep):
        ri[here], rx[here], rz[here] = di, dx, dz
    for here, sums, sums_z, di, dx, dz in inner_differences(cur, cm.at[1], near, deep):
        sums_out[here] = sums + sums_z + (3.0 * SECOND[0] * 5040) * cur[here]
        di_out[here], dx_out[here], dz_out[here] = di, dx, dz


def first_outer_kernel(flags, cur, prev, vel, ri, rx, rz, sums, di, dx, dz, inj, zm, ym, side,
                       edge, new, zo, co, yo, k0, ki, kx, kz):
    size = cur.shape[0]
    half = size // 2
    kz[...], ki[...], kx[...] = sums[...], di[...], dx[...]
    k0[...], new[...] = ri[...], rx[...]
    more, more_x = side_differences(zm.at[1], side)
    kz[0:half] += more
    kx[0:half] += more_x
    spare, more_x = side_differences(zm.at[0], side)
    new[0:half] += more_x
    for here, more, more_i in edge_differences(flags, size, ym.at[1], edge):
        kz[here] += more
        ki[here] += more_i
    for here, spare, more_i in edge_differences(flags, size, ym.at[0], edge):
        k0[here] += more_i
    for n in range(4):
        here = slice(n * (size // 4), (n + 1) * (size // 4))
        square = vel[here] * vel[here]
        scaled = square * (1.0 / (840 * 840))
        factor = square * (1.0 / 5040)
        along_i, along_x, along_z = scaled * k0[here], scaled * new[here], scaled * rz[here]
        change = factor * kz[here] - (
            along_i * ki[here] + along_x * kx[here] + along_z * dz[here])
        k0[here], ki[here], kx[here], kz[here] = factor, along_i, along_x, along_z
        center = cur[here]
        new[here] = (center - prev[here]) + (center + (change + inj[here]))
    rims(flags, new, zo, co, yo)


def inner(cur, prev, k0, ki, kx, kz, cm, near, deep, inj, out):
    for here, sums, sums_z, di, dx, dz in inner_differences(cur, cm, near, deep):
        center = cur[here]
        change = k0[here] * ((sums + sums_z) + (3.0 * SECOND[0] * 5040) * center)
        change = change - (ki[here] * di + kx[here] * dx + kz[here] * dz)
        if inj is not None:
            change = change + inj[here]
        out[here] = (center - prev[here]) + (center + change)


def outer(flags, part, k0, ki, kx, zm, ym, side, edge, new):
    size = part.shape[0]
    half = size // 2
    sums, dx = side_differences(zm, side)
    new[0:half] = part[0:half] + (k0[0:half] * sums - kx[0:half] * dx)
    new[half:] = part[half:]
    for here, sums, di in edge_differences(flags, size, ym, edge):
        new[here] += k0[here] * sums - ki[here] * di


def other_half(stage, flags, count):
    other = 1 - flags[4 + stage]
    for n in range(count // 2):
        high, low = n >> stage, n & ((1 << stage) - 1)
        yield n, (high << (stage + 1)) + (other << stage) + low


def trade(stage, flags, mine, got, out, give=None):
    out[...] = mine[...]
    for n, at in other_half(stage, flags, out.shape[0]):
        out[at] = got[n]
    if give is not None:
        for n, at in other_half(stage + 1, flags, out.shape[0]):
            give[n] = out[at]


def trade_kernel(stage, flags, mine, got, *outs):
    trade(stage, flags, mine, got, *outs)


def source_kernel(step, full, flags, src, wave, out):
    size, depth = out.shape
    count = src.shape[0]
    shift = (depth - 1).bit_length()
    plane = shift + (full - 1).bit_length()
    rows = size // COLS
    lane = lax.broadcasted_iota(jnp.int32, (1, count), 1)
    sub = lax.broadcasted_iota(jnp.int32, (count, 1), 0)
    row = jnp.zeros((1, count), jnp.int32)
    deep = jnp.zeros((count, 1), jnp.int32)
    size_of = jnp.zeros((count, 1), F32)
    for n in range(count):
        cell = src[n]
        i = jnp.right_shift(cell, plane) - flags[1] * rows
        x = jnp.bitwise_and(jnp.right_shift(cell, shift), full - 1)
        x = x - (2 * flags[3] + flags[0]) * COLS
        ok = (i >= 0) & (i < rows) & (x >= 0) & (x < COLS)
        row = jnp.where(lane == n, jnp.where(ok, place_of(flags, size, i, x), -1), row)
        deep = jnp.where(sub == n, jnp.bitwise_and(cell, depth - 1), deep)
        size_of = jnp.where(sub == n, wave[step, n], size_of)
    spot = lax.broadcasted_iota(jnp.int32, (size, count), 0) == row
    spot = spot.astype(F32).astype(BF16)
    high, low = split(jnp.where(
        lax.broadcasted_iota(jnp.int32, (count, depth), 1) == deep, size_of, 0.0))
    out[...] = mm(spot, high) + mm(spot, low)


def forward_inner_kernel(step, full, flags, src, wave, cur, prev, k0, ki, kx, kz, cm, near, deep,
                         before, part, change):
    source_kernel(step, full, flags, src, wave, change)
    inner(cur, prev, k0, ki, kx, kz, cm, near, deep, change, part)
    change[...] = (cur[...] - prev[...]) - (prev[...] - before[...])


def outer_kernel(stage, double, flags, part, k0, ki, kx, zm, ym, side, edge, *rest):
    rest = list(rest)
    other = rest.pop(0) if double else None
    if stage is not None:
        mine, got, new, zo, co, yo, *lists = rest
        trade(stage, flags, mine, got, *lists)
    else:
        new, zo, co, yo = rest
    outer(flags, part, k0, ki, kx, zm, ym, side, edge, new)
    if double:
        for n, field in enumerate((new, other)):
            rims(flags, field, zo.at[n], co.at[n], yo.at[n])
    else:
        rims(flags, new, zo, co, yo)


def pack_kernel(flags, counts, cells, traces, cells_out, lists, give, counts_v, cells_v, traces_v,
                sems):
    pairs = ((counts, counts_v), (cells, cells_v), (traces, traces_v))
    copies = [pltpu.make_async_copy(a, b, sems.at[n]) for n, (a, b) in enumerate(pairs)]
    for copy in copies:
        copy.start()
    for copy in copies:
        copy.wait()
    subs, n = counts.shape[1], cells.shape[1]
    shape = (subs, n)
    lane = lax.broadcasted_iota(jnp.int32, shape, 1)
    mine = lane // CAP == lax.broadcasted_iota(jnp.int32, shape, 0)
    live = mm(counts_v[...].astype(F32).astype(BF16), mine.astype(F32).astype(BF16))
    slot = jnp.bitwise_and(lane[0:1], CAP - 1)
    cells_out[...] = jnp.where(slot.astype(F32) < live, cells_v[...].astype(F32), -1.0)
    for m in range(subs):
        q, y, c = m >> 2, (m >> 1) & 1, m & 1
        start = ((2 * q + c) * 2 + y) * CAP
        tile = traces_v[:, start // 128 * 128 : start // 128 * 128 + 128]
        lists[m] = pltpu.roll(tile, (128 - start % 128) % 128, axis=1) if start % 128 else tile
    for n, at in other_half(0, flags, subs):
        give[n] = lists[at]


def lists_kernel(flags, lists, own, got, spot, pick, at, obs):
    size, n = spot.shape
    depth = at.shape[1]
    subs, steps = lists.shape[0], obs.shape[1]
    cell = jnp.where(flags[0] == flags[1], own[...], got[...])
    along = jnp.floor((cell + 0.5) * (1.0 / depth))
    place = along.astype(jnp.int32)
    place = jnp.where(place < 0, -1, place_of(
        flags, size, jnp.right_shift(place, 3), jnp.bitwise_and(place, COLS - 1)))
    same = lax.broadcasted_iota(jnp.int32, (n, n), 0) == lax.broadcasted_iota(jnp.int32, (n, n), 1)

    def column(row):
        return jnp.sum(jnp.where(same, row, 0.0), axis=1, keepdims=True).astype(jnp.int32)

    hot = lax.broadcasted_iota(jnp.int32, (size, n), 0) == place
    spot[...] = hot.astype(F32).astype(BF16)
    hot = lax.broadcasted_iota(jnp.int32, (n, size), 1) == column(place.astype(F32))
    pick[...] = hot.astype(F32).astype(BF16)
    hot = lax.broadcasted_iota(jnp.int32, (n, depth), 1) == column(cell - along * depth)
    at[...] = hot.astype(F32)
    traces = lists[...].reshape(subs * steps, 128).T[0:CAP]
    for s in range(subs):
        obs[s * CAP : s * CAP + CAP, :] = traces[:, s * steps : s * steps + steps]


def injection(t, state, spot, pick, at, obs):
    high, low = split(state[...])
    seen = at[...] * (mm(pick[...], high) + mm(pick[...], low))
    residual = jnp.sum(seen, axis=1, keepdims=True) - obs[:, t : t + 1]
    high, low = split(at[...] * residual)
    return mm(spot[...], high) + mm(spot[...], low)


def adjoint_inner_kernel(t, flags, cur, prev, k0, ki, kx, kz, cm, near, deep, state, spot, pick,
                         at, obs, *rest):
    if len(rest) == 4:
        change, image, part, image_out = rest
        image_out[...] = cur[...] * change[...] + image[...]
    else:
        now, mid, before, part, image_out = rest
        image_out[...] = cur[...] * ((now[...] - mid[...]) - (mid[...] - before[...]))
    inj = injection(t, state, spot, pick, at, obs)
    inner(cur, prev, k0, ki, kx, kz, cm, near, deep, inj, part)


def adjoint_first_kernel(flags, cur, prev, k0, ki, kx, kz, cm, near, deep, part):
    inner(cur, prev, k0, ki, kx, kz, cm.at[1], near, deep, None, part)


def turn_kernel(t, flags, part, k0, ki, kx, zm, ym, side, edge, u_part, u_zm, u_ym, spot, pick, at, obs, new, u_new, zo, co, yo):
    outer(flags, part, k0, ki, kx, zm, ym, side, edge, new)
    outer(flags, u_part, k0, ki, kx, u_zm.at[1], u_ym.at[1], side, edge, u_new)
    u_new[...] += injection(t, new, spot, pick, at, obs)
    rims(flags, u_new, zo, co, yo)


def last_kernel(scale, flags, part, k0, ki, kx, zm, ym, side, edge, image, change, vel,
                new, mine, other):
    outer(flags, part, k0, ki, kx, zm, ym, side, edge, new)
    raw = from_halves(flags, (image[...] + new[...] * change[...]) * scale / vel[...])
    count, height, lanes = mine.shape
    chunk = raw.shape[1] // (2 * count)
    for n in range(count):
        even, odd = (
            jnp.concatenate(
                [raw[g * height : g * height + height, m * chunk : m * chunk + chunk]
                 for g in range(lanes // chunk)], axis=1)
            for m in (2 * n, 2 * n + 1))
        mine[n] = jnp.where(flags[0] == 0, even, odd)
        other[n] = jnp.where(flags[0] == 0, odd, even)


def both_kernel(flags, a, b, out):
    out[0] = from_halves(flags, a[...])
    out[1] = from_halves(flags, b[...])


def join_kernel(flags, mine, got, *outs):
    for s, out in enumerate(outs):
        to = jnp.bitwise_xor(flags[3], s)
        a, b = mine[to], got[to]
        out[0] = jnp.where(flags[0] == 0, a, b)
        out[1] = jnp.where(flags[0] == 0, b, a)


def filter_kernel(flags, *refs):
    *pieces, out = refs
    height, lanes = pieces[0].shape[1:]
    chunk, rows, full = out.shape
    groups = lanes // chunk
    q = flags[3]
    shape = (full, full)
    y = lax.broadcasted_iota(jnp.int32, shape, 1)
    at = lax.broadcasted_iota(jnp.int32, shape, 0)
    within = jnp.bitwise_and(at, 2 * COLS - 1)
    place = jnp.bitwise_xor(q * (2 * COLS), at - within) + within
    weights = jnp.exp(jnp.abs(y - place).astype(F32) * (-1.0 / SMOOTH))
    weights = split(weights / jnp.sum(weights, axis=0, keepdims=True))
    ready = []
    for n in range(height // COLS):
        here = slice(n * COLS, n * COLS + COLS)
        lines = jnp.concatenate([piece[b, here, :] for piece in pieces for b in range(2)], axis=0)
        high, low = split(lines.T)
        done = mm(high, weights[0]) + mm(low, weights[0]) + mm(high, weights[1])
        ready.append(done)
    for g in range(groups):
        lines = jnp.stack([done[g * chunk : g * chunk + chunk] for done in ready], axis=0)
        out[:, g * (rows // groups) : (g + 1) * (rows // groups), :] = jnp.swapaxes(lines, 0, 1)


def shaped(*shape):
    return jax.ShapeDtypeStruct(shape, F32)


def call(kernel, name, outs, *args, weight=0, far=0, scalars=0, scratch=()):
    specs = [pl.BlockSpec(memory_space=pltpu.SMEM)] * (1 + scalars)
    specs += [pl.BlockSpec(memory_space=pl.ANY)] * far
    specs += [pl.BlockSpec(memory_space=pltpu.VMEM)] * (len(args) - 1 - scalars - far)
    return pl.pallas_call(
        kernel,
        name=name,
        out_shape=outs,
        in_specs=specs,
        out_specs=[pl.BlockSpec(memory_space=pltpu.VMEM)] * len(outs),
        scratch_shapes=list(scratch) + ([pltpu.SemaphoreType.DMA((far,))] if far else []),
        compiler_params=pltpu.CompilerParams(vmem_limit_bytes=VMEM_BYTES),
        cost_estimate=pl.CostEstimate(
            flops=1000, bytes_accessed=1000 + int(weight * 3_600_000), transcendentals=0),
    )(*args)


def per_device(plan, fwd_now, fwd_before, adj_now, adj_before, velocity, log_density, observed,
               rec_cells, rec_counts, src_cell, wavelet):
    rows, cols, depth = fwd_now.shape
    size = rows * cols
    steps = wavelet.shape[0]
    nx, nq = plan.nx, plan.nq
    subs = 2 * nx
    xline, c = lax.axis_index("xline"), lax.axis_index("inline")
    q, y = xline // 2, xline % 2
    keep = y == c
    z_perm, c_perm, y_perm, swap_perm = plan.z(), plan.core(), plan.y(), plan.swap()
    stages = [(c_perm, c), (y_perm, y)]
    stages += [(plan.flip(1 << b), (q >> b) & 1) for b in range((nq - 1).bit_length())]
    sub = (2 * q + c) * 2 + y
    flags = jnp.stack([c, y, sub, q] + [bit for pairs, bit in stages]).astype(jnp.int32)
    field = shaped(size, depth)
    rim = [shaped(size // 2, depth), shaped(size // 2, depth), shaped(4 * cols, depth)]

    deep = depth_matrix(depth)
    deep = jnp.asarray(np.concatenate([deep, deep]), BF16)
    inside = jnp.where(c == 0, q > 0, q < nq - 1)
    near = [near_matrix(GROUP, cols, k) for k in range(2)]
    wide = (GROUP + 8) * cols
    near = [np.concatenate([m[:, :wide], m[:, :wide], m[:, wide:], m[:, wide:]], axis=1) for m in near]
    near = jnp.where(c == 0, jnp.asarray(near[0], F32), jnp.asarray(near[1], F32)).astype(BF16)
    side = [side_matrix(rows, k) for k in range(2)]
    side = jnp.where(c == 0, jnp.asarray(side[0], BF16), jnp.asarray(side[1], BF16))
    side = jnp.where(inside, side, jnp.zeros_like(side))
    side = jnp.concatenate([side, side], axis=1)
    edge = [edge_matrix(k) for k in range(2)]
    edge = jnp.where(y == 0, jnp.asarray(edge[0], F32), jnp.asarray(edge[1], F32)).astype(BF16)
    edge = jnp.concatenate([edge, edge], axis=1)

    def halo(zo, co, yo):
        return send(zo, z_perm), send(co, c_perm), send(yo, y_perm)

    def after(value, *deps):
        return lax.optimization_barrier((value,) + deps)[0]

    def flat(value):
        return value.reshape(size, depth)

    log_density, fwd_now, velocity = flat(log_density), flat(fwd_now), flat(velocity)
    fwd_before, adj_now, adj_before = flat(fwd_before), flat(adj_now), flat(adj_before)
    got = [send(v, swap_perm) for v in (log_density, fwd_now)]
    stacked = jnp.stack([velocity, fwd_before])
    got_model = send(stacked, swap_perm)
    full = nx * cols
    inj, = call(functools.partial(source_kernel, 0, full), "source", [field], flags, src_cell, wavelet,
                weight=0.7, scalars=2)
    flags_in, inj = lax.optimization_barrier((flags, inj))
    density, p_now, *out = call(settle_kernel, "settle",
                                [field, field] + [shaped(2, *r.shape) for r in rim],
                                flags_in, log_density, fwd_now, *got, far=2)
    zm, cm, ym = halo(*out)
    vel, p_before = call(settle_pair_kernel, "settle_model", [field, field],
                         flags, velocity, fwd_before, got_model, weight=0.6, far=2)
    parts = call(first_inner_kernel, "first_inner", [field] * 7, flags, density, p_now, cm,
                 near, deep, weight=1.3)
    got_adjoint = [send(after(v, parts[0]), swap_perm) for v in (adj_now, adj_before)]

    new, zo, co, yo, k0, ki, kx, kz = call(
        first_outer_kernel, "first_outer", [field] + rim + [field] * 4,
        flags, p_now, p_before, vel, *parts, inj, zm, ym, side, edge)
    model = (k0, ki, kx, kz)
    states = [p_before, p_now, new]
    changes = []
    zm, cm, ym = halo(zo, co, yo)
    double = 1
    late = steps - 2 if len(stages) < steps - 2 else steps - 1

    slots = subs * CAP
    entries, half_entries = shaped(subs, steps, 128), shaped(subs // 2, steps, 128)
    cells, lists, give = call(
        pack_kernel, "pack", [shaped(1, slots), entries, half_entries], after(flags, k0), rec_counts,
        rec_cells, observed, weight=0.8, far=3,
        scratch=[pltpu.VMEM(rec_counts.shape, jnp.int32), pltpu.VMEM(rec_cells.shape, jnp.int32),
                 pltpu.VMEM(observed.shape, F32)])
    for t in range(1, steps):
        cur, prev, before = states[:-4:-1]
        stage = t - 1 if t <= min(len(stages), steps - 2) else None
        extra = [lists, send(give, stages[stage][0])] if stage is not None else []
        part, change = call(
            functools.partial(forward_inner_kernel, t, full), "forward_inner", [field, field], flags,
            src_cell, wavelet, cur, prev, *model, cm, near, deep, before, weight=1.2, scalars=2)
        changes.append(change)
        args = [flags, part, k0, ki, kx, zm, ym, side, edge]
        if t == steps - 3:
            u_part, = call(adjoint_first_kernel, "adjoint_first", [field], flags, u_now, u_before,
                           *model, u_cm, near, deep, weight=1.1)
            args[1] = after(part, u_part)
        if t == late:
            for n in range(steps - 2, len(stages)):
                lists, *give = call(
                    functools.partial(trade_kernel, n), "trade",
                    [entries] + ([half_entries] if n + 1 < len(stages) else []), flags, lists,
                    send(give, stages[n][0]))
                give = give[0] if give else None
            receivers = call(
                lists_kernel, "lists",
                [jax.ShapeDtypeStruct((size, slots), BF16),
                 jax.ShapeDtypeStruct((slots, size), BF16), shaped(slots, depth),
                 shaped(slots, steps)], flags, lists, cells, got_cells, weight=0.8)
            args[1] = after(part, receivers[0])
        if t == steps - 1:
            new, u_new, *out = call(
                functools.partial(turn_kernel, t), "turn", [field, field] + rim, *args, u_part,
                u_zm, u_ym, *receivers)
            states.append(new)
            break
        if t == len(stages) - 2:
            got_cells = send(after(cells, part), swap_perm)
        if t == len(stages) - 1:
            args[1] = after(part, got_cells)
        if t == double:
            u_now, u_before = call(settle_pair_kernel, "settle_adjoint", [field, field], flags,
                                   adj_now, adj_before, *got_adjoint, weight=0.6, far=2)
            args.append(u_now)
        outs = [field] + ([shaped(2, *r.shape) for r in rim] if t == double else rim)
        if extra:
            outs = outs + [entries] + ([half_entries] if t < len(stages) else [])
        new, *out = call(functools.partial(outer_kernel, stage, t == double), "forward_outer", outs,
                         *args, *extra)
        if extra:
            out, (lists, *give) = out[:3], out[3:]
            give = give[0] if give else None
        states.append(new)
        zm, cm, ym = halo(*out)
        if t == double:
            u_zm, u_cm, u_ym = zm, cm, ym

    zm, cm, ym = halo(*out)
    u_before, u_now = u_now, u_new
    image = []
    chunk = depth // nx
    half = shaped(nq, size * chunk // 128, 128)
    for j in range(1, steps):
        t = steps - 1 - j
        terms = [changes[t + 1], *image] if image else states[:-4:-1]
        part, *image = call(
            functools.partial(adjoint_inner_kernel, t), "adjoint_inner", [field, field], flags,
            u_now, u_before, *model, cm, near, deep, states[t + 2], *receivers, *terms, weight=1.5)
        args = [part, k0, ki, kx, zm, ym, side, edge]
        if j == steps - 1:
            u_last, mine, other = call(
                functools.partial(last_kernel, 2.0 / steps), "last", [field, half, half], flags,
                *args, *image, changes[0], vel)
            break
        u_before = u_now
        u_now, *out = call(functools.partial(outer_kernel, None, False), "adjoint_outer", [field] + rim,
                           flags, *args)
        zm, cm, ym = halo(*out)

    final, = call(both_kernel, "both", [shaped(2, *field.shape)], flags, u_now, u_last, weight=0.4)
    got = send(final, swap_perm)
    pieces = call(join_kernel, "join", [shaped(2, *half.shape[1:])] * nq, flags, mine,
                  send(other, c_perm))
    pieces = [send(pieces[s], plan.spread(s)) for s in reversed(range(nq))][::-1]
    adj_prev, adj_out = call(select_kernel, "select", [field, field], flags, final, got, weight=1.2)
    gradient, = call(filter_kernel, "filter", [shaped(chunk, rows, nx * cols)],
                     after(flags, adj_out), *pieces)
    block = (rows, cols, depth)
    return gradient, adj_out.reshape(block), adj_prev.reshape(block)


def solution(mesh):
    field = P(("shots", "inline"), "xline", None)
    model = P("inline", "xline", None)
    lists = P(("xline", "inline"), None)
    return jax.shard_map(
        functools.partial(per_device, Plan(mesh)),
        mesh=mesh,
        in_specs=(field, field, field, field, model, model, P("shots", ("xline", "inline")),
                  lists, lists, P("shots"), P("shots", None)),
        out_specs=(P(("shots", "xline"), "inline", None), field, field),
        check_vma=False,
    )
```

```python
import functools

import jax
import jax.numpy as jnp
import numpy as np
from jax import lax
from jax.experimental import pallas as pl
from jax.experimental.pallas import tpu as pltpu
from jax.sharding import PartitionSpec as P

CAP = 8
SMOOTH = 16
SECOND = (-205.0 / 72.0, 8.0 / 5.0, -1.0 / 5.0, 8.0 / 315.0, -1.0 / 560.0)
FIRST = (4.0 / 5.0, -1.0 / 5.0, 4.0 / 105.0, -1.0 / 280.0)
ALL = ("shots", "xline", "inline")
COLS = 8
GROUP = 8
VMEM_BYTES = 8 * 1024 * 1024
F32 = jnp.float32
BF16 = jnp.bfloat16


class Plan:
    def __init__(self, mesh):
        self.shots = mesh.shape["shots"]
        self.nx = mesh.shape["xline"]
        self.nq = self.nx // 2

    def index(self, s, q, y, c):
        return (s * self.nx + 2 * q + y) * 2 + c

    def perm(self, partner):
        pairs = []
        for s in range(self.shots):
            for q in range(self.nq):
                for y in range(2):
                    for c in range(2):
                        t = partner(q, y, c)
                        dst = self.index(s ^ 1, q, y, c) if t is None else self.index(s, *t)
                        pairs.append((self.index(s, q, y, c), dst))
        return pairs

    def swap(self):
        return self.perm(lambda q, y, c: None if y == c else (q, c, y))

    def z(self):
        def partner(q, y, c):
            other = q + 1 if c == 1 else q - 1
            return (other, y, 1 - c) if 0 <= other < self.nq else None

        return self.perm(partner)

    def core(self):
        return self.perm(lambda q, y, c: (q, y, 1 - c))

    def y(self):
        return self.perm(lambda q, y, c: (q, 1 - y, c))

    def flip(self, bit):
        return self.perm(lambda q, y, c: (q ^ bit, y, c) if (q ^ bit) < self.nq else None)

    def spread(self, shift):
        return self.perm(lambda q, y, c: (q ^ shift, c, y))


def send(value, pairs):
    return lax.ppermute(value, ALL, pairs)


def depth_matrix(n):
    m = np.zeros((n, 2 * n), np.float32)
    for k in range(1, 5):
        for j in range(n):
            for i, sign in ((j + k, 1.0), (j - k, -1.0)):
                if 0 <= i < n:
                    m[i, j] = round(SECOND[k] * 5040)
                    m[i, n + j] = sign * round(FIRST[k - 1] * 840)
    return m


def stencil_matrix(rows, cols):
    own = (rows + 8) * cols
    m = np.zeros((3, rows, cols, own + rows * 8), np.float32)
    for i in range(rows):
        for x in range(cols):
            for k in range(1, 5):
                total = round(SECOND[k] * 5040)
                slope = round(FIRST[k - 1] * 840)
                for sign in (1, -1):
                    at = (i + 4 + sign * k) * cols + x
                    m[0, i, x, at] += total
                    m[1, i, x, at] += sign * slope
                    to = x + sign * k
                    if to < 0:
                        at = own + i * 4 + to + 4
                    elif to >= cols:
                        at = own + rows * 4 + i * 4 + to - cols
                    else:
                        at = (i + 4) * cols + to
                    m[0, i, x, at] += total
                    m[2, i, x, at] += sign * slope
    return m.reshape(3 * rows * cols, own + rows * 8)


def halved(rows, cols, c):
    at = np.arange(rows)[:, None] * cols
    z_side = (at + 4 * c + np.arange(4)).reshape(-1)
    return np.concatenate([z_side, (at + 4 * (1 - c) + np.arange(4)).reshape(-1)])


def near_matrix(rows, cols, c):
    m = stencil_matrix(rows, cols)
    own = (rows + 8) * cols
    place = halved(rows, cols, c)
    out = np.concatenate([place + k * rows * cols for k in range(3)])
    side = own + (1 - c) * rows * 4 + np.arange(rows * 4)
    return m[out][:, np.concatenate([halved(rows + 8, cols, c), side])]


def side_matrix(rows, c):
    m = np.zeros((2, rows, 4, rows, 4), np.float32)
    for x in range(4):
        for k in range(4):
            d = x + 4 - k if c == 0 else k + 4 - x
            if d <= 4:
                for i in range(rows):
                    m[0, i, x, i, k] = round(SECOND[d] * 5040)
                    m[1, i, x, i, k] = round(FIRST[d - 1] * 840) * (-1 if c == 0 else 1)
    return m.reshape(2 * rows * 4, rows * 4)


def edge_matrix(y):
    m = np.zeros((2, 2, 4, 4, 2, 4, 4), np.float32)
    for i in range(4):
        for k in range(4):
            d = i + 4 - k if y == 1 else k + 4 - i
            if d <= 4:
                for part in range(2):
                    for x in range(4):
                        m[0, part, i, x, part, k, x] = round(SECOND[d] * 5040)
                        m[1, part, i, x, part, k, x] = round(FIRST[d - 1] * 840) * (-1 if y == 1 else 1)
    return m.reshape(64, 32)


def split(value):
    high = value.astype(BF16)
    return high, (value - high.astype(F32)).astype(BF16)


def mm(a, b):
    return jnp.dot(a, b, preferred_element_type=F32)


def inner_differences(cur, cm, near, deep):
    size, depth = cur.shape
    half = size // 2
    cm = cm.at[0] if len(cm.shape) == 3 else cm
    own = split(cur[...])
    along = mm(jnp.concatenate(own, axis=1), deep[...])
    blank = jnp.zeros((16, depth), BF16)
    ext = [[jnp.concatenate([blank, part[h * half : h * half + half], blank], axis=0)
            for h in range(2)] for part in own]
    from_c = split(cm[...])
    step = GROUP * 4
    for n in range(half // step):
        rhs = [part[h][n * step : n * step + step + 32] for part in ext for h in range(2)]
        rhs += [part[n * step : n * step + step] for part in from_c]
        out = mm(near[...], jnp.concatenate(rhs, axis=0))
        for h in range(2):
            here = slice(h * half + n * step, h * half + n * step + step)
            sums, di, dx = (out[(2 * k + h) * step : (2 * k + h + 1) * step] for k in range(3))
            yield here, sums, along[here, 0:depth], di, dx, along[here, depth:]


def side_differences(zm, side):
    zm = zm.at[0] if len(zm.shape) == 3 else zm
    out = mm(side[...], jnp.concatenate(split(zm[...]), axis=0))
    half = out.shape[0] // 2
    return out[0:half], out[half:]


def edge_differences(flags, size, ym, edge):
    ym = ym.at[0] if len(ym.shape) == 3 else ym
    out = mm(edge[...], jnp.concatenate(split(ym[...]), axis=0))
    start = jnp.where(flags[1] == 1, 0, size // 2 - 16)
    for h in range(2):
        at = pl.ds(pl.multiple_of(start + h * (size // 2), 16), 16)
        yield at, out[h * 16 : h * 16 + 16], out[32 + h * 16 : 48 + h * 16]


def to_halves(flags, value):
    rows, depth = value.shape
    pairs = value.reshape(rows // (2 * COLS), 2, COLS, depth)
    a, b = pairs[:, 0], pairs[:, 1]
    low = lax.broadcasted_iota(jnp.int32, a.shape, 1) < 4
    first = jnp.where(low, a, pltpu.roll(b, 4, axis=1)).reshape(rows // 2, depth)
    last = jnp.where(low, pltpu.roll(a, 4, axis=1), b).reshape(rows // 2, depth)
    return jnp.where(flags[0] == 0, first, last), jnp.where(flags[0] == 0, last, first)


def from_halves(flags, value):
    rows, depth = value.shape
    z_side, c_side = value[0 : rows // 2], value[rows // 2 :]
    shape = (rows // (2 * COLS), COLS, depth)
    first = jnp.where(flags[0] == 0, z_side, c_side).reshape(shape)
    last = jnp.where(flags[0] == 0, c_side, z_side).reshape(shape)
    low = lax.broadcasted_iota(jnp.int32, shape, 1) < 4
    a = jnp.where(low, first, pltpu.roll(last, 4, axis=1))
    b = jnp.where(low, pltpu.roll(first, 4, axis=1), last)
    return jnp.stack([a, b], axis=1).reshape(rows, depth)


def place_of(flags, size, i, x):
    near = x - 4 * flags[0]
    return i * 4 + jnp.where((near >= 0) & (near < 4), near, size // 2 + x - 4 * (1 - flags[0]))


def rims(flags, new, zo, co, yo):
    size = new.shape[0]
    half = size // 2
    zo[...] = new[0:half]
    co[...] = new[half:]
    last = jnp.concatenate([new[half - 16 : half], new[size - 16 :]], axis=0)
    first = jnp.concatenate([new[0:16], new[half : half + 16]], axis=0)
    yo[...] = jnp.where(flags[1] == 0, last, first)


def choose(flags, pairs, sems):
    keep = flags[0] == flags[1]

    @pl.when(keep)
    def _():
        copies = [pltpu.make_async_copy(own, out, sems.at[n])
                  for n, (own, recv, out) in enumerate(pairs)]
        for copy in copies:
            copy.start()
        for copy in copies:
            copy.wait()

    @pl.when(jnp.logical_not(keep))
    def _():
        for own, recv, out in pairs:
            out[...] = recv[...]

    for own, recv, out in pairs:
        half = out.shape[0] // 2
        z_side, c_side = to_halves(flags, out[...])
        out[0:half] = z_side
        out[half:] = c_side


def settle_kernel(flags, a, b, recv_a, recv_b, a_out, b_out, zo, co, yo, sems):
    choose(flags, [(a, recv_a, a_out), (b, recv_b, b_out)], sems)
    for n, out in enumerate((a_out, b_out)):
        rims(flags, out, zo.at[n], co.at[n], yo.at[n])


def settle_pair_kernel(flags, a, b, *rest):
    *recv, a_out, b_out, sems = rest
    recv = recv if len(recv) == 2 else (recv[0].at[0], recv[0].at[1])
    choose(flags, [(a, recv[0], a_out), (b, recv[1], b_out)], sems)


def select_kernel(flags, own, recv, *outs):
    keep = flags[0] == flags[1]
    for n, out in enumerate(outs):
        out[...] = jnp.where(keep, own[n], recv[n])


def first_inner_kernel(flags, lr, cur, cm, near, deep, *outs):
    ri, rx, rz, sums_out, di_out, dx_out, dz_out = outs
    for here, spare, spare_z, di, dx, dz in inner_differences(lr, cm.at[0], near, deep):
        ri[here], rx[here], rz[here] = di, dx, dz
    for here, sums, sums_z, di, dx, dz in inner_differences(cur, cm.at[1], near, deep):
        sums_out[here] = sums + sums_z + (3.0 * SECOND[0] * 5040) * cur[here]
        di_out[here], dx_out[here], dz_out[here] = di, dx, dz


def first_outer_kernel(flags, cur, prev, vel, ri, rx, rz, sums, di, dx, dz, inj, zm, ym, side,
                       edge, new, zo, co, yo, k0, ki, kx, kz):
    size = cur.shape[0]
    half = size // 2
    kz[...], ki[...], kx[...] = sums[...], di[...], dx[...]
    k0[...], new[...] = ri[...], rx[...]
    more, more_x = side_differences(zm.at[1], side)
    kz[0:half] += more
    kx[0:half] += more_x
    spare, more_x = side_differences(zm.at[0], side)
    new[0:half] += more_x
    for here, more, more_i in edge_differences(flags, size, ym.at[1], edge):
        kz[here] += more
        ki[here] += more_i
    for here, spare, more_i in edge_differences(flags, size, ym.at[0], edge):
        k0[here] += more_i
    for n in range(4):
        here = slice(n * (size // 4), (n + 1) * (size // 4))
        square = vel[here] * vel[here]
        scaled = square * (1.0 / (840 * 840))
        factor = square * (1.0 / 5040)
        along_i, along_x, along_z = scaled * k0[here], scaled * new[here], scaled * rz[here]
        change = factor * kz[here] - (
            along_i * ki[here] + along_x * kx[here] + along_z * dz[here])
        k0[here], ki[here], kx[here], kz[here] = factor, along_i, along_x, along_z
        center = cur[here]
        new[here] = (center - prev[here]) + (center + (change + inj[here]))
    rims(flags, new, zo, co, yo)


def inner(cur, prev, k0, ki, kx, kz, cm, near, deep, inj, out):
    for here, sums, sums_z, di, dx, dz in inner_differences(cur, cm, near, deep):
        center = cur[here]
        change = k0[here] * ((sums + sums_z) + (3.0 * SECOND[0] * 5040) * center)
        change = change - (ki[here] * di + kx[here] * dx + kz[here] * dz)
        if inj is not None:
            change = change + inj[here]
        out[here] = (center - prev[here]) + (center + change)


def outer(flags, part, k0, ki, kx, zm, ym, side, edge, new):
    size = part.shape[0]
    half = size // 2
    sums, dx = side_differences(zm, side)
    new[0:half] = part[0:half] + (k0[0:half] * sums - kx[0:half] * dx)
    new[half:] = part[half:]
    for here, sums, di in edge_differences(flags, size, ym, edge):
        new[here] += k0[here] * sums - ki[here] * di


def other_half(stage, flags, count):
    other = 1 - flags[4 + stage]
    for n in range(count // 2):
        high, low = n >> stage, n & ((1 << stage) - 1)
        yield n, (high << (stage + 1)) + (other << stage) + low


def trade(stage, flags, mine, got, out, give=None):
    out[...] = mine[...]
    for n, at in other_half(stage, flags, out.shape[0]):
        out[at] = got[n]
    if give is not None:
        for n, at in other_half(stage + 1, flags, out.shape[0]):
            give[n] = out[at]


def trade_kernel(stage, flags, mine, got, *outs):
    trade(stage, flags, mine, got, *outs)


def source_kernel(step, full, flags, src, wave, out):
    size, depth = out.shape
    count = src.shape[0]
    shift = (depth - 1).bit_length()
    plane = shift + (full - 1).bit_length()
    rows = size // COLS
    lane = lax.broadcasted_iota(jnp.int32, (1, count), 1)
    sub = lax.broadcasted_iota(jnp.int32, (count, 1), 0)
    row = jnp.zeros((1, count), jnp.int32)
    deep = jnp.zeros((count, 1), jnp.int32)
    size_of = jnp.zeros((count, 1), F32)
    for n in range(count):
        cell = src[n]
        i = jnp.right_shift(cell, plane) - flags[1] * rows
        x = jnp.bitwise_and(jnp.right_shift(cell, shift), full - 1)
        x = x - (2 * flags[3] + flags[0]) * COLS
        ok = (i >= 0) & (i < rows) & (x >= 0) & (x < COLS)
        row = jnp.where(lane == n, jnp.where(ok, place_of(flags, size, i, x), -1), row)
        deep = jnp.where(sub == n, jnp.bitwise_and(cell, depth - 1), deep)
        size_of = jnp.where(sub == n, wave[step, n], size_of)
    spot = lax.broadcasted_iota(jnp.int32, (size, count), 0) == row
    spot = spot.astype(F32).astype(BF16)
    high, low = split(jnp.where(
        lax.broadcasted_iota(jnp.int32, (count, depth), 1) == deep, size_of, 0.0))
    out[...] = mm(spot, high) + mm(spot, low)


def forward_inner_kernel(step, full, flags, src, wave, cur, prev, k0, ki, kx, kz, cm, near, deep,
                         before, part, change):
    source_kernel(step, full, flags, src, wave, change)
    inner(cur, prev, k0, ki, kx, kz, cm, near, deep, change, part)
    change[...] = (cur[...] - prev[...]) - (prev[...] - before[...])


def outer_kernel(stage, double, flags, part, k0, ki, kx, zm, ym, side, edge, *rest):
    rest = list(rest)
    other = rest.pop(0) if double else None
    if stage is not None:
        mine, got, new, zo, co, yo, *lists = rest
        trade(stage, flags, mine, got, *lists)
    else:
        new, zo, co, yo = rest
    outer(flags, part, k0, ki, kx, zm, ym, side, edge, new)
    if double:
        for n, field in enumerate((new, other)):
            rims(flags, field, zo.at[n], co.at[n], yo.at[n])
    else:
        rims(flags, new, zo, co, yo)


def pack_kernel(flags, counts, cells, traces, cells_out, lists, give, counts_v, cells_v, traces_v,
                sems):
    pairs = ((counts, counts_v), (cells, cells_v), (traces, traces_v))
    copies = [pltpu.make_async_copy(a, b, sems.at[n]) for n, (a, b) in enumerate(pairs)]
    for copy in copies:
        copy.start()
    for copy in copies:
        copy.wait()
    subs, n = counts.shape[1], cells.shape[1]
    shape = (subs, n)
    lane = lax.broadcasted_iota(jnp.int32, shape, 1)
    mine = lane // CAP == lax.broadcasted_iota(jnp.int32, shape, 0)
    live = mm(counts_v[...].astype(F32).astype(BF16), mine.astype(F32).astype(BF16))
    slot = jnp.bitwise_and(lane[0:1], CAP - 1)
    cells_out[...] = jnp.where(slot.astype(F32) < live, cells_v[...].astype(F32), -1.0)
    for m in range(subs):
        q, y, c = m >> 2, (m >> 1) & 1, m & 1
        start = ((2 * q + c) * 2 + y) * CAP
        tile = traces_v[:, start // 128 * 128 : start // 128 * 128 + 128]
        lists[m] = pltpu.roll(tile, (128 - start % 128) % 128, axis=1) if start % 128 else tile
    for n, at in other_half(0, flags, subs):
        give[n] = lists[at]


def lists_kernel(flags, lists, own, got, spot, pick, at, obs):
    size, n = spot.shape
    depth = at.shape[1]
    subs, steps = lists.shape[0], obs.shape[1]
    cell = jnp.where(flags[0] == flags[1], own[...], got[...])
    along = jnp.floor((cell + 0.5) * (1.0 / depth))
    place = along.astype(jnp.int32)
    place = jnp.where(place < 0, -1, place_of(
        flags, size, jnp.right_shift(place, 3), jnp.bitwise_and(place, COLS - 1)))
    same = lax.broadcasted_iota(jnp.int32, (n, n), 0) == lax.broadcasted_iota(jnp.int32, (n, n), 1)

    def column(row):
        return jnp.sum(jnp.where(same, row, 0.0), axis=1, keepdims=True).astype(jnp.int32)

    hot = lax.broadcasted_iota(jnp.int32, (size, n), 0) == place
    spot[...] = hot.astype(F32).astype(BF16)
    hot = lax.broadcasted_iota(jnp.int32, (n, size), 1) == column(place.astype(F32))
    pick[...] = hot.astype(F32).astype(BF16)
    hot = lax.broadcasted_iota(jnp.int32, (n, depth), 1) == column(cell - along * depth)
    at[...] = hot.astype(F32)
    traces = lists[...].reshape(subs * steps, 128).T[0:CAP]
    for s in range(subs):
        obs[s * CAP : s * CAP + CAP, :] = traces[:, s * steps : s * steps + steps]


def injection(t, state, spot, pick, at, obs):
    high, low = split(state[...])
    seen = at[...] * (mm(pick[...], high) + mm(pick[...], low))
    residual = jnp.sum(seen, axis=1, keepdims=True) - obs[:, t : t + 1]
    high, low = split(at[...] * residual)
    return mm(spot[...], high) + mm(spot[...], low)


def adjoint_inner_kernel(t, flags, cur, prev, k0, ki, kx, kz, cm, near, deep, state, spot, pick,
                         at, obs, *rest):
    if len(rest) == 4:
        change, image, part, image_out = rest
        image_out[...] = cur[...] * change[...] + image[...]
    else:
        now, mid, before, part, image_out = rest
        image_out[...] = cur[...] * ((now[...] - mid[...]) - (mid[...] - before[...]))
    inj = injection(t, state, spot, pick, at, obs)
    inner(cur, prev, k0, ki, kx, kz, cm, near, deep, inj, part)


def adjoint_first_kernel(flags, cur, prev, k0, ki, kx, kz, cm, near, deep, part):
    inner(cur, prev, k0, ki, kx, kz, cm.at[1], near, deep, None, part)


def turn_kernel(t, flags, part, k0, ki, kx, zm, ym, side, edge, u_part, u_zm, u_ym, spot, pick, at, obs, new, u_new, zo, co, yo):
    outer(flags, part, k0, ki, kx, zm, ym, side, edge, new)
    outer(flags, u_part, k0, ki, kx, u_zm.at[1], u_ym.at[1], side, edge, u_new)
    u_new[...] += injection(t, new, spot, pick, at, obs)
    rims(flags, u_new, zo, co, yo)


def last_kernel(scale, flags, part, k0, ki, kx, zm, ym, side, edge, image, change, vel,
                prev, states, mine, other):
    new = states.at[1]
    outer(flags, part, k0, ki, kx, zm, ym, side, edge, new)
    raw = from_halves(flags, (image[...] + new[...] * change[...]) * scale / vel[...])
    new[...] = from_halves(flags, new[...])
    states[0] = from_halves(flags, prev[...])
    count, height, lanes = mine.shape
    chunk = raw.shape[1] // (2 * count)
    for n in range(count):
        even, odd = (
            jnp.concatenate(
                [raw[g * height : g * height + height, m * chunk : m * chunk + chunk]
                 for g in range(lanes // chunk)], axis=1)
            for m in (2 * n, 2 * n + 1))
        mine[n] = jnp.where(flags[0] == 0, even, odd)
        other[n] = jnp.where(flags[0] == 0, odd, even)


def join_kernel(flags, mine, got, *outs):
    for s, out in enumerate(outs):
        to = jnp.bitwise_xor(flags[3], s)
        a, b = mine[to], got[to]
        out[0] = jnp.where(flags[0] == 0, a, b)
        out[1] = jnp.where(flags[0] == 0, b, a)


def filter_kernel(flags, *refs):
    *pieces, out = refs
    height, lanes = pieces[0].shape[1:]
    chunk, rows, full = out.shape
    groups = lanes // chunk
    q = flags[3]
    shape = (full, full)
    y = lax.broadcasted_iota(jnp.int32, shape, 1)
    at = lax.broadcasted_iota(jnp.int32, shape, 0)
    within = jnp.bitwise_and(at, 2 * COLS - 1)
    place = jnp.bitwise_xor(q * (2 * COLS), at - within) + within
    weights = jnp.exp(jnp.abs(y - place).astype(F32) * (-1.0 / SMOOTH))
    weights = split(weights / jnp.sum(weights, axis=0, keepdims=True))
    ready = []
    for n in range(height // COLS):
        here = slice(n * COLS, n * COLS + COLS)
        lines = jnp.concatenate([piece[b, here, :] for piece in pieces for b in range(2)], axis=0)
        high, low = split(lines.T)
        done = mm(high, weights[0]) + mm(low, weights[0]) + mm(high, weights[1])
        ready.append(done)
    for g in range(groups):
        lines = jnp.stack([done[g * chunk : g * chunk + chunk] for done in ready], axis=0)
        out[:, g * (rows // groups) : (g + 1) * (rows // groups), :] = jnp.swapaxes(lines, 0, 1)


def shaped(*shape):
    return jax.ShapeDtypeStruct(shape, F32)


class Flags:
    def __getitem__(self, n):
        if n == 0:
            return lax.axis_index("inline")
        xline = lax.axis_index("xline")
        if n == 1:
            return jnp.bitwise_and(xline, 1)
        if n == 3:
            return jnp.right_shift(xline, 1)
        place = 2 * xline + lax.axis_index("inline")
        return jnp.bitwise_and(jnp.right_shift(place, n - 4), 1)


def call(kernel, name, outs, *args, weight=0, far=0, scalars=0, scratch=()):
    specs = [pl.BlockSpec(memory_space=pltpu.SMEM)] * scalars
    specs += [pl.BlockSpec(memory_space=pl.ANY)] * far
    specs += [pl.BlockSpec(memory_space=pltpu.VMEM)] * (len(args) - scalars - far)
    return pl.pallas_call(
        functools.partial(kernel, Flags()),
        name=name,
        out_shape=outs,
        in_specs=specs,
        out_specs=[pl.BlockSpec(memory_space=pltpu.VMEM)] * len(outs),
        scratch_shapes=list(scratch) + ([pltpu.SemaphoreType.DMA((far,))] if far else []),
        compiler_params=pltpu.CompilerParams(vmem_limit_bytes=VMEM_BYTES),
        cost_estimate=pl.CostEstimate(
            flops=1000, bytes_accessed=1000 + int(weight * 3_600_000), transcendentals=0),
    )(*args)


def per_device(plan, fwd_now, fwd_before, adj_now, adj_before, velocity, log_density, observed,
               rec_cells, rec_counts, src_cell, wavelet):
    rows, cols, depth = fwd_now.shape
    size = rows * cols
    steps = wavelet.shape[0]
    nx, nq = plan.nx, plan.nq
    subs = 2 * nx
    xline, c = lax.axis_index("xline"), lax.axis_index("inline")
    q, y = xline // 2, xline % 2
    keep = y == c
    z_perm, c_perm, y_perm, swap_perm = plan.z(), plan.core(), plan.y(), plan.swap()
    stages = [(c_perm, c), (y_perm, y)]
    stages += [(plan.flip(1 << b), (q >> b) & 1) for b in range((nq - 1).bit_length())]
    field = shaped(size, depth)
    rim = [shaped(size // 2, depth), shaped(size // 2, depth), shaped(4 * cols, depth)]

    deep = depth_matrix(depth)
    deep = jnp.asarray(np.concatenate([deep, deep]), BF16)
    inside = jnp.where(c == 0, q > 0, q < nq - 1)
    near = [near_matrix(GROUP, cols, k) for k in range(2)]
    wide = (GROUP + 8) * cols
    near = [np.concatenate([m[:, :wide], m[:, :wide], m[:, wide:], m[:, wide:]], axis=1) for m in near]
    near = jnp.where(c == 0, jnp.asarray(near[0], F32), jnp.asarray(near[1], F32)).astype(BF16)
    side = [side_matrix(rows, k) for k in range(2)]
    side = jnp.where(c == 0, jnp.asarray(side[0], BF16), jnp.asarray(side[1], BF16))
    side = jnp.where(inside, side, jnp.zeros_like(side))
    side = jnp.concatenate([side, side], axis=1)
    edge = [edge_matrix(k) for k in range(2)]
    edge = jnp.where(y == 0, jnp.asarray(edge[0], F32), jnp.asarray(edge[1], F32)).astype(BF16)
    edge = jnp.concatenate([edge, edge], axis=1)

    def halo(zo, co, yo):
        return send(zo, z_perm), send(co, c_perm), send(yo, y_perm)

    def after(value, *deps):
        return lax.optimization_barrier((value,) + deps)[0]

    def flat(value):
        return value.reshape(size, depth)

    log_density, fwd_now, velocity = flat(log_density), flat(fwd_now), flat(velocity)
    fwd_before, adj_now, adj_before = flat(fwd_before), flat(adj_now), flat(adj_before)
    got = [send(v, swap_perm) for v in (log_density, fwd_now)]
    stacked = jnp.stack([velocity, fwd_before])
    got_model = send(stacked, swap_perm)
    full = nx * cols
    inj, = call(functools.partial(source_kernel, 0, full), "source", [field], src_cell, wavelet,
                weight=0.7, scalars=2)
    got[0], inj = lax.optimization_barrier((got[0], inj))
    density, p_now, *out = call(settle_kernel, "settle",
                                [field, field] + [shaped(2, *r.shape) for r in rim],
                                log_density, fwd_now, *got, far=2)
    zm, cm, ym = halo(*out)
    vel, p_before = call(settle_pair_kernel, "settle_model", [field, field],
                         velocity, fwd_before, got_model, weight=0.6, far=2)
    parts = call(first_inner_kernel, "first_inner", [field] * 7, density, p_now, cm,
                 near, deep, weight=1.3)
    got_adjoint = [send(after(v, parts[0]), swap_perm) for v in (adj_now, adj_before)]

    new, zo, co, yo, k0, ki, kx, kz = call(
        first_outer_kernel, "first_outer", [field] + rim + [field] * 4,
        p_now, p_before, vel, *parts, inj, zm, ym, side, edge)
    model = (k0, ki, kx, kz)
    states = [p_before, p_now, new]
    changes = []
    zm, cm, ym = halo(zo, co, yo)
    double = 1
    late = steps - 2 if len(stages) < steps - 2 else steps - 1

    slots = subs * CAP
    entries, half_entries = shaped(subs, steps, 128), shaped(subs // 2, steps, 128)
    cells, lists, give = call(
        pack_kernel, "pack", [shaped(1, slots), entries, half_entries], after(rec_counts, k0),
        rec_cells, observed, weight=0.8, far=3,
        scratch=[pltpu.VMEM(rec_counts.shape, jnp.int32), pltpu.VMEM(rec_cells.shape, jnp.int32),
                 pltpu.VMEM(observed.shape, F32)])
    for t in range(1, steps):
        cur, prev, before = states[:-4:-1]
        stage = t - 1 if t <= min(len(stages), steps - 2) else None
        extra = [lists, send(give, stages[stage][0])] if stage is not None else []
        part, change = call(
            functools.partial(forward_inner_kernel, t, full), "forward_inner", [field, field], src_cell, wavelet, cur, prev, *model, cm, near, deep, before, weight=1.2, scalars=2)
        changes.append(change)
        args = [part, k0, ki, kx, zm, ym, side, edge]
        if t == steps - 3:
            u_part, = call(adjoint_first_kernel, "adjoint_first", [field], u_now, u_before,
                           *model, u_cm, near, deep, weight=1.1)
            args[0] = after(part, u_part)
        if t == late:
            for n in range(steps - 2, len(stages)):
                lists, *give = call(
                    functools.partial(trade_kernel, n), "trade",
                    [entries] + ([half_entries] if n + 1 < len(stages) else []), lists,
                    send(give, stages[n][0]))
                give = give[0] if give else None
            receivers = call(
                lists_kernel, "lists",
                [jax.ShapeDtypeStruct((size, slots), BF16),
                 jax.ShapeDtypeStruct((slots, size), BF16), shaped(slots, depth),
                 shaped(slots, steps)], lists, cells, got_cells, weight=0.8)
            args[0] = after(part, receivers[0])
        if t == steps - 1:
            new, u_new, *out = call(
                functools.partial(turn_kernel, t), "turn", [field, field] + rim, *args, u_part,
                u_zm, u_ym, *receivers)
            states.append(new)
            break
        if t == len(stages) - 2:
            got_cells = send(after(cells, part), swap_perm)
        if t == len(stages) - 1:
            args[0] = after(part, got_cells)
        if t == double:
            u_now, u_before = call(settle_pair_kernel, "settle_adjoint", [field, field], adj_now, adj_before, *got_adjoint, weight=0.6, far=2)
            args.append(u_now)
        outs = [field] + ([shaped(2, *r.shape) for r in rim] if t == double else rim)
        if extra:
            outs = outs + [entries] + ([half_entries] if t < len(stages) else [])
        new, *out = call(functools.partial(outer_kernel, stage, t == double), "forward_outer", outs,
                         *args, *extra)
        if extra:
            out, (lists, *give) = out[:3], out[3:]
            give = give[0] if give else None
        states.append(new)
        zm, cm, ym = halo(*out)
        if t == double:
            u_zm, u_cm, u_ym = zm, cm, ym

    zm, cm, ym = halo(*out)
    u_before, u_now = u_now, u_new
    image = []
    chunk = depth // nx
    half = shaped(nq, size * chunk // 128, 128)
    for j in range(1, steps):
        t = steps - 1 - j
        terms = [changes[t + 1], *image] if image else states[:-4:-1]
        part, *image = call(
            functools.partial(adjoint_inner_kernel, t), "adjoint_inner", [field, field], u_now, u_before, *model, cm, near, deep, states[t + 2], *receivers, *terms, weight=1.5)
        args = [part, k0, ki, kx, zm, ym, side, edge]
        if j == steps - 1:
            final, mine, other = call(
                functools.partial(last_kernel, 2.0 / steps), "last",
                [shaped(2, *field.shape), half, half], *args, *image, changes[0], vel, u_now)
            break
        u_before = u_now
        u_now, *out = call(functools.partial(outer_kernel, None, False), "adjoint_outer", [field] + rim,
                           *args)
        zm, cm, ym = halo(*out)

    got = send(final, swap_perm)
    pieces = call(join_kernel, "join", [shaped(2, *half.shape[1:])] * nq, mine,
                  send(other, c_perm))
    pieces = [send(pieces[s], plan.spread(s)) for s in reversed(range(nq))][::-1]
    adj_prev, adj_out = call(select_kernel, "select", [field, field], final, got, weight=1.2)
    gradient, = call(filter_kernel, "filter", [shaped(chunk, rows, nx * cols)],
                     after(pieces[0], adj_out), *pieces[1:])
    block = (rows, cols, depth)
    return gradient, adj_out.reshape(block), adj_prev.reshape(block)


def solution(mesh):
    field = P(("shots", "inline"), "xline", None)
    model = P("inline", "xline", None)
    lists = P(("xline", "inline"), None)
    return jax.shard_map(
        functools.partial(per_device, Plan(mesh)),
        mesh=mesh,
        in_specs=(field, field, field, field, model, model, P("shots", ("xline", "inline")),
                  lists, lists, P("shots"), P("shots", None)),
        out_specs=(P(("shots", "xline"), "inline", None), field, field),
        check_vma=False,
    )
```

```python
import functools

import jax
import jax.numpy as jnp
import numpy as np
from jax import lax
from jax.experimental import pallas as pl
from jax.experimental.pallas import tpu as pltpu
from jax.sharding import PartitionSpec as P

CAP = 8
SMOOTH = 16
SECOND = (-205.0 / 72.0, 8.0 / 5.0, -1.0 / 5.0, 8.0 / 315.0, -1.0 / 560.0)
FIRST = (4.0 / 5.0, -1.0 / 5.0, 4.0 / 105.0, -1.0 / 280.0)
ALL = ("shots", "xline", "inline")
COLS = 8
GROUP = 8
VMEM_BYTES = 8 * 1024 * 1024
F32 = jnp.float32
BF16 = jnp.bfloat16


class Plan:
    def __init__(self, mesh):
        self.shots = mesh.shape["shots"]
        self.nx = mesh.shape["xline"]
        self.nq = self.nx // 2

    def index(self, s, q, y, c):
        return (s * self.nx + 2 * q + y) * 2 + c

    def perm(self, partner):
        pairs = []
        for s in range(self.shots):
            for q in range(self.nq):
                for y in range(2):
                    for c in range(2):
                        t = partner(q, y, c)
                        dst = self.index(s ^ 1, q, y, c) if t is None else self.index(s, *t)
                        pairs.append((self.index(s, q, y, c), dst))
        return pairs

    def swap(self):
        return self.perm(lambda q, y, c: None if y == c else (q, c, y))

    def z(self):
        def partner(q, y, c):
            other = q + 1 if c == 1 else q - 1
            return (other, y, 1 - c) if 0 <= other < self.nq else None

        return self.perm(partner)

    def core(self):
        return self.perm(lambda q, y, c: (q, y, 1 - c))

    def y(self):
        return self.perm(lambda q, y, c: (q, 1 - y, c))

    def flip(self, bit):
        return self.perm(lambda q, y, c: (q ^ bit, y, c) if (q ^ bit) < self.nq else None)

    def spread(self, shift):
        return self.perm(lambda q, y, c: (q ^ shift, c, y))


def send(value, pairs):
    return lax.ppermute(value, ALL, pairs)


def depth_matrix(n):
    m = np.zeros((n, 2 * n), np.float32)
    for k in range(1, 5):
        for j in range(n):
            for i, sign in ((j + k, 1.0), (j - k, -1.0)):
                if 0 <= i < n:
                    m[i, j] = round(SECOND[k] * 5040)
                    m[i, n + j] = sign * round(FIRST[k - 1] * 840)
    return m


def stencil_matrix(rows, cols):
    own = (rows + 8) * cols
    m = np.zeros((3, rows, cols, own + rows * 8), np.float32)
    for i in range(rows):
        for x in range(cols):
            for k in range(1, 5):
                total = round(SECOND[k] * 5040)
                slope = round(FIRST[k - 1] * 840)
                for sign in (1, -1):
                    at = (i + 4 + sign * k) * cols + x
                    m[0, i, x, at] += total
                    m[1, i, x, at] += sign * slope
                    to = x + sign * k
                    if to < 0:
                        at = own + i * 4 + to + 4
                    elif to >= cols:
                        at = own + rows * 4 + i * 4 + to - cols
                    else:
                        at = (i + 4) * cols + to
                    m[0, i, x, at] += total
                    m[2, i, x, at] += sign * slope
    return m.reshape(3 * rows * cols, own + rows * 8)


def halved(rows, cols, c):
    at = np.arange(rows)[:, None] * cols
    z_side = (at + 4 * c + np.arange(4)).reshape(-1)
    return np.concatenate([z_side, (at + 4 * (1 - c) + np.arange(4)).reshape(-1)])


def near_matrix(rows, cols, c):
    m = stencil_matrix(rows, cols)
    own = (rows + 8) * cols
    place = halved(rows, cols, c)
    out = np.concatenate([place + k * rows * cols for k in range(3)])
    side = own + (1 - c) * rows * 4 + np.arange(rows * 4)
    return m[out][:, np.concatenate([halved(rows + 8, cols, c), side])]


def side_matrix(rows, c):
    m = np.zeros((2, rows, 4, rows, 4), np.float32)
    for x in range(4):
        for k in range(4):
            d = x + 4 - k if c == 0 else k + 4 - x
            if d <= 4:
                for i in range(rows):
                    m[0, i, x, i, k] = round(SECOND[d] * 5040)
                    m[1, i, x, i, k] = round(FIRST[d - 1] * 840) * (-1 if c == 0 else 1)
    return m.reshape(2 * rows * 4, rows * 4)


def edge_matrix(y):
    m = np.zeros((2, 2, 4, 4, 2, 4, 4), np.float32)
    for i in range(4):
        for k in range(4):
            d = i + 4 - k if y == 1 else k + 4 - i
            if d <= 4:
                for part in range(2):
                    for x in range(4):
                        m[0, part, i, x, part, k, x] = round(SECOND[d] * 5040)
                        m[1, part, i, x, part, k, x] = round(FIRST[d - 1] * 840) * (-1 if y == 1 else 1)
    return m.reshape(64, 32)


def split(value):
    high = value.astype(BF16)
    return high, (value - high.astype(F32)).astype(BF16)


def mm(a, b):
    return jnp.dot(a, b, preferred_element_type=F32)


def inner_differences(cur, cm, near, deep):
    size, depth = cur.shape
    half = size // 2
    cm = cm.at[0] if len(cm.shape) == 3 else cm
    own = split(cur[...])
    along = mm(jnp.concatenate(own, axis=1), deep[...])
    blank = jnp.zeros((16, depth), BF16)
    ext = [[jnp.concatenate([blank, part[h * half : h * half + half], blank], axis=0)
            for h in range(2)] for part in own]
    from_c = split(cm[0:half])
    step = GROUP * 4
    for n in range(half // step):
        rhs = [part[h][n * step : n * step + step + 32] for part in ext for h in range(2)]
        rhs += [part[n * step : n * step + step] for part in from_c]
        out = mm(near[...], jnp.concatenate(rhs, axis=0))
        for h in range(2):
            here = slice(h * half + n * step, h * half + n * step + step)
            sums, di, dx = (out[(2 * k + h) * step : (2 * k + h + 1) * step] for k in range(3))
            yield here, sums, along[here, 0:depth], di, dx, along[here, depth:]


def side_differences(zm, side):
    zm = zm.at[0] if len(zm.shape) == 3 else zm
    out = mm(side[...], jnp.concatenate(split(zm[...]), axis=0))
    half = out.shape[0] // 2
    return out[0:half], out[half:]


def edge_differences(flags, size, ym, edge):
    ym = ym.at[0] if len(ym.shape) == 3 else ym
    out = mm(edge[...], jnp.concatenate(split(ym[0:32]), axis=0))
    start = jnp.where(flags[1] == 1, 0, size // 2 - 16)
    for h in range(2):
        at = pl.ds(pl.multiple_of(start + h * (size // 2), 16), 16)
        yield at, out[h * 16 : h * 16 + 16], out[32 + h * 16 : 48 + h * 16]


def to_halves(flags, value):
    rows, depth = value.shape
    pairs = value.reshape(rows // (2 * COLS), 2, COLS, depth)
    a, b = pairs[:, 0], pairs[:, 1]
    low = lax.broadcasted_iota(jnp.int32, a.shape, 1) < 4
    first = jnp.where(low, a, pltpu.roll(b, 4, axis=1)).reshape(rows // 2, depth)
    last = jnp.where(low, pltpu.roll(a, 4, axis=1), b).reshape(rows // 2, depth)
    return jnp.where(flags[0] == 0, first, last), jnp.where(flags[0] == 0, last, first)


def from_halves(flags, value):
    rows, depth = value.shape
    z_side, c_side = value[0 : rows // 2], value[rows // 2 :]
    shape = (rows // (2 * COLS), COLS, depth)
    first = jnp.where(flags[0] == 0, z_side, c_side).reshape(shape)
    last = jnp.where(flags[0] == 0, c_side, z_side).reshape(shape)
    low = lax.broadcasted_iota(jnp.int32, shape, 1) < 4
    a = jnp.where(low, first, pltpu.roll(last, 4, axis=1))
    b = jnp.where(low, pltpu.roll(first, 4, axis=1), last)
    return jnp.stack([a, b], axis=1).reshape(rows, depth)


def place_of(flags, size, i, x):
    near = x - 4 * flags[0]
    return i * 4 + jnp.where((near >= 0) & (near < 4), near, size // 2 + x - 4 * (1 - flags[0]))


def rims(flags, new, zo, co, yo):
    size = new.shape[0]
    half = size // 2
    zo[...] = new[0:half]
    co[...] = new[half:]
    last = jnp.concatenate([new[half - 16 : half], new[size - 16 :]], axis=0)
    first = jnp.concatenate([new[0:16], new[half : half + 16]], axis=0)
    yo[...] = jnp.where(flags[1] == 0, last, first)


def choose(flags, pairs, sems):
    keep = flags[0] == flags[1]

    @pl.when(keep)
    def _():
        copies = [pltpu.make_async_copy(own, out, sems.at[n])
                  for n, (own, recv, out) in enumerate(pairs)]
        for copy in copies:
            copy.start()
        for copy in copies:
            copy.wait()

    @pl.when(jnp.logical_not(keep))
    def _():
        for own, recv, out in pairs:
            out[...] = recv[...]

    for own, recv, out in pairs:
        half = out.shape[0] // 2
        z_side, c_side = to_halves(flags, out[...])
        out[0:half] = z_side
        out[half:] = c_side


def settle_kernel(flags, a, b, recv_a, recv_b, a_out, b_out, zo, co, yo, sems):
    choose(flags, [(a, recv_a, a_out), (b, recv_b, b_out)], sems)
    for n, out in enumerate((a_out, b_out)):
        rims(flags, out, zo.at[n], co.at[n], yo.at[n])


def settle_pair_kernel(flags, a, b, *rest):
    *recv, a_out, b_out, sems = rest
    recv = recv if len(recv) == 2 else (recv[0].at[0], recv[0].at[1])
    choose(flags, [(a, recv[0], a_out), (b, recv[1], b_out)], sems)


def select_kernel(flags, own, recv, *outs):
    keep = flags[0] == flags[1]
    for n, out in enumerate(outs):
        out[...] = jnp.where(keep, own[n], recv[n])


def first_inner_kernel(flags, lr, cur, cm, near, deep, *outs):
    ri, rx, rz, sums_out, di_out, dx_out, dz_out = outs
    for here, spare, spare_z, di, dx, dz in inner_differences(lr, cm.at[0], near, deep):
        ri[here], rx[here], rz[here] = di, dx, dz
    for here, sums, sums_z, di, dx, dz in inner_differences(cur, cm.at[1], near, deep):
        sums_out[here] = sums + sums_z + (3.0 * SECOND[0] * 5040) * cur[here]
        di_out[here], dx_out[here], dz_out[here] = di, dx, dz


def first_outer_kernel(flags, cur, prev, vel, ri, rx, rz, sums, di, dx, dz, inj, zm, ym, side,
                       edge, give, cells, new, zo, co, yo, k0, ki, kx, kz):
    size = cur.shape[0]
    half = size // 2
    kz[...], ki[...], kx[...] = sums[...], di[...], dx[...]
    k0[...], new[...] = ri[...], rx[...]
    more, more_x = side_differences(zm.at[1], side)
    kz[0:half] += more
    kx[0:half] += more_x
    spare, more_x = side_differences(zm.at[0], side)
    new[0:half] += more_x
    for here, more, more_i in edge_differences(flags, size, ym.at[1], edge):
        kz[here] += more
        ki[here] += more_i
    for here, spare, more_i in edge_differences(flags, size, ym.at[0], edge):
        k0[here] += more_i
    for n in range(4):
        here = slice(n * (size // 4), (n + 1) * (size // 4))
        square = vel[here] * vel[here]
        scaled = square * (1.0 / (840 * 840))
        factor = square * (1.0 / 5040)
        along_i, along_x, along_z = scaled * k0[here], scaled * new[here], scaled * rz[here]
        change = factor * kz[here] - (
            along_i * ki[here] + along_x * kx[here] + along_z * dz[here])
        k0[here], ki[here], kx[here], kz[here] = factor, along_i, along_x, along_z
        center = cur[here]
        new[here] = (center - prev[here]) + (center + (change + inj[here]))
    rims(flags, new, zo, co.at[pl.ds(0, half)], yo)
    load(co, half, lambda n: give[n], give.shape[0], [cells[...]])


def inner(cur, prev, k0, ki, kx, kz, cm, near, deep, inj, out):
    for here, sums, sums_z, di, dx, dz in inner_differences(cur, cm, near, deep):
        center = cur[here]
        change = k0[here] * ((sums + sums_z) + (3.0 * SECOND[0] * 5040) * center)
        change = change - (ki[here] * di + kx[here] * dx + kz[here] * dz)
        if inj is not None:
            change = change + inj[here]
        out[here] = (center - prev[here]) + (center + change)


def outer(flags, part, k0, ki, kx, zm, ym, side, edge, new):
    size = part.shape[0]
    half = size // 2
    sums, dx = side_differences(zm, side)
    new[0:half] = part[0:half] + (k0[0:half] * sums - kx[0:half] * dx)
    new[half:] = part[half:]
    for here, sums, di in edge_differences(flags, size, ym, edge):
        new[here] += k0[here] * sums - ki[here] * di


def other_half(stage, flags, count):
    other = 1 - flags[4 + stage]
    for n in range(count // 2):
        high, low = n >> stage, n & ((1 << stage) - 1)
        yield n, (high << (stage + 1)) + (other << stage) + low


def trade(stage, flags, mine, got, out, give=None):
    out[...] = mine[...]
    for n, at in other_half(stage, flags, out.shape[0]):
        out[at] = got(n) if callable(got) else got[n]
    if give is not None:
        for n, at in other_half(stage + 1, flags, out.shape[0]):
            give[n] = out[at]


def load(message, rim, entry, count, cells):
    for n in range(count):
        message[rim + n // 2 * 8 : rim + n // 2 * 8 + 8, n % 2 * 128 : n % 2 * 128 + 128] = entry(n)
    at = rim + count // 2 * 8
    wide = message.shape[1]
    for k, row in enumerate(cells):
        for m in range(row.shape[1] // 128):
            lane = k * row.shape[1] + m * 128
            message[at + lane // wide : at + lane // wide + 1, lane % wide : lane % wide + 128] = (
                row[:, m * 128 : m * 128 + 128])


def unload(message, rim, count, rows, slots):
    wide = message.shape[1]
    at = rim + count // 2 * 8

    def entry(n):
        return message[rim + n // 2 * 8 : rim + n // 2 * 8 + 8, n % 2 * 128 : n % 2 * 128 + 128]

    cells = []
    for k in range(rows):
        tiles = []
        for m in range(slots // 128):
            lane = k * slots + m * 128
            tiles.append(message[at + lane // wide : at + lane // wide + 1,
                                 lane % wide : lane % wide + 128])
        cells.append(jnp.concatenate(tiles, axis=1) if len(tiles) > 1 else tiles[0])
    return entry, cells


def trade_kernel(stage, flags, mine, got, *outs):
    trade(stage, flags, mine, got, *outs)


def source_kernel(step, full, flags, src, wave, out):
    size, depth = out.shape
    count = src.shape[0]
    shift = (depth - 1).bit_length()
    plane = shift + (full - 1).bit_length()
    rows = size // COLS
    lane = lax.broadcasted_iota(jnp.int32, (1, count), 1)
    sub = lax.broadcasted_iota(jnp.int32, (count, 1), 0)
    row = jnp.zeros((1, count), jnp.int32)
    deep = jnp.zeros((count, 1), jnp.int32)
    size_of = jnp.zeros((count, 1), F32)
    for n in range(count):
        cell = src[n]
        i = jnp.right_shift(cell, plane) - flags[1] * rows
        x = jnp.bitwise_and(jnp.right_shift(cell, shift), full - 1)
        x = x - (2 * flags[3] + flags[0]) * COLS
        ok = (i >= 0) & (i < rows) & (x >= 0) & (x < COLS)
        row = jnp.where(lane == n, jnp.where(ok, place_of(flags, size, i, x), -1), row)
        deep = jnp.where(sub == n, jnp.bitwise_and(cell, depth - 1), deep)
        size_of = jnp.where(sub == n, wave[step, n], size_of)
    spot = lax.broadcasted_iota(jnp.int32, (size, count), 0) == row
    spot = spot.astype(F32).astype(BF16)
    high, low = split(jnp.where(
        lax.broadcasted_iota(jnp.int32, (count, depth), 1) == deep, size_of, 0.0))
    out[...] = mm(spot, high) + mm(spot, low)


def forward_inner_kernel(step, full, flags, src, wave, cur, prev, k0, ki, kx, kz, cm, near, deep,
                         before, part, change):
    source_kernel(step, full, flags, src, wave, change)
    inner(cur, prev, k0, ki, kx, kz, cm, near, deep, change, part)
    change[...] = (cur[...] - prev[...]) - (prev[...] - before[...])


def outer_kernel(stage, flags, part, k0, ki, kx, zm, ym, side, edge, *rest):
    if stage is not None:
        mine, got, new, zo, co, yo, *lists = rest
        trade(stage, flags, mine, got, *lists)
    else:
        new, zo, co, yo = rest
    outer(flags, part, k0, ki, kx, zm, ym, side, edge, new)
    rims(flags, new, zo, co, yo)


def pack_kernel(flags, counts, cells, traces, cells_out, lists, give, counts_v, cells_v, traces_v,
                sems):
    pairs = ((counts, counts_v), (cells, cells_v), (traces, traces_v))
    copies = [pltpu.make_async_copy(a, b, sems.at[n]) for n, (a, b) in enumerate(pairs)]
    for copy in copies:
        copy.start()
    for copy in copies:
        copy.wait()
    subs, n = counts.shape[1], cells.shape[1]
    shape = (subs, n)
    lane = lax.broadcasted_iota(jnp.int32, shape, 1)
    mine = lane // CAP == lax.broadcasted_iota(jnp.int32, shape, 0)
    live = mm(counts_v[...].astype(F32).astype(BF16), mine.astype(F32).astype(BF16))
    slot = jnp.bitwise_and(lane[0:1], CAP - 1)
    cells_out[...] = jnp.where(slot.astype(F32) < live, cells_v[...].astype(F32), -1.0)
    for m in range(subs):
        q, y, c = m >> 2, (m >> 1) & 1, m & 1
        start = ((2 * q + c) * 2 + y) * CAP
        tile = traces_v[:, start // 128 * 128 : start // 128 * 128 + 128]
        lists[m] = pltpu.roll(tile, (128 - start % 128) % 128, axis=1) if start % 128 else tile
    for n, at in other_half(0, flags, subs):
        give[n] = lists[at]


def core_stage_kernel(flags, part, k0, ki, kx, zm, ym, side, edge, lists, cells, cm, new, zo, co, yo,
                      lists_out, pair):
    outer(flags, part, k0, ki, kx, zm, ym, side, edge, new)
    count, half = lists.shape[0] // 2, new.shape[0] // 2
    entry, (theirs,) = unload(cm, half, count, 1, cells.shape[1])
    trade(0, flags, lists, entry, lists_out)
    mine = cells[...]
    pair[0:1] = jnp.where(flags[0] == 0, mine, theirs)
    pair[1:2] = jnp.where(flags[0] == 0, theirs, mine)
    rims(flags, new, zo, co, yo.at[pl.ds(0, 32)])
    at = [k for n, k in other_half(1, flags, lists.shape[0])]
    load(yo, 32, lambda n: lists_out[at[n]], count, [pair[0:1], pair[1:2]])


def y_stage_kernel(flags, part, k0, ki, kx, zm, ym, side, edge, lists, pair, other, new, zo, co, yo,
                   lists_out, give, cells):
    outer(flags, part, k0, ki, kx, zm, ym, side, edge, new)
    for n, field in enumerate((new, other)):
        rims(flags, field, zo.at[n], co.at[n], yo.at[n])
    entry, theirs = unload(ym, 32, lists.shape[0] // 2, 2, pair.shape[1])
    trade(1, flags, lists, entry, lists_out, give)
    away = flags[0] != flags[1]
    low = jnp.where(away, theirs[0], pair[0:1])
    high = jnp.where(away, theirs[1], pair[1:2])
    cells[...] = jnp.where(flags[1] == 0, low, high)


def lists_kernel(flags, lists, cells, spot, pick, at, obs):
    size, n = spot.shape
    depth = at.shape[1]
    subs, steps = lists.shape[0], obs.shape[1]
    cell = cells[...]
    along = jnp.floor((cell + 0.5) * (1.0 / depth))
    place = along.astype(jnp.int32)
    place = jnp.where(place < 0, -1, place_of(
        flags, size, jnp.right_shift(place, 3), jnp.bitwise_and(place, COLS - 1)))
    same = lax.broadcasted_iota(jnp.int32, (n, n), 0) == lax.broadcasted_iota(jnp.int32, (n, n), 1)

    def column(row):
        return jnp.sum(jnp.where(same, row, 0.0), axis=1, keepdims=True).astype(jnp.int32)

    hot = lax.broadcasted_iota(jnp.int32, (size, n), 0) == place
    spot[...] = hot.astype(F32).astype(BF16)
    hot = lax.broadcasted_iota(jnp.int32, (n, size), 1) == column(place.astype(F32))
    pick[...] = hot.astype(F32).astype(BF16)
    hot = lax.broadcasted_iota(jnp.int32, (n, depth), 1) == column(cell - along * depth)
    at[...] = hot.astype(F32)
    traces = lists[...].reshape(subs * steps, 128).T[0:CAP]
    for s in range(subs):
        obs[s * CAP : s * CAP + CAP, :] = traces[:, s * steps : s * steps + steps]


def injection(t, state, spot, pick, at, obs):
    high, low = split(state[...])
    seen = at[...] * (mm(pick[...], high) + mm(pick[...], low))
    residual = jnp.sum(seen, axis=1, keepdims=True) - obs[:, t : t + 1]
    high, low = split(at[...] * residual)
    return mm(spot[...], high) + mm(spot[...], low)


def adjoint_inner_kernel(t, flags, cur, prev, k0, ki, kx, kz, cm, near, deep, state, spot, pick,
                         at, obs, *rest):
    if len(rest) == 4:
        change, image, part, image_out = rest
        image_out[...] = cur[...] * change[...] + image[...]
    else:
        now, mid, before, part, image_out = rest
        image_out[...] = cur[...] * ((now[...] - mid[...]) - (mid[...] - before[...]))
    inj = injection(t, state, spot, pick, at, obs)
    inner(cur, prev, k0, ki, kx, kz, cm, near, deep, inj, part)


def adjoint_first_kernel(flags, cur, prev, k0, ki, kx, kz, cm, near, deep, part):
    inner(cur, prev, k0, ki, kx, kz, cm.at[1], near, deep, None, part)


def turn_kernel(t, flags, part, k0, ki, kx, zm, ym, side, edge, u_part, u_zm, u_ym, spot, pick, at, obs, new, u_new, zo, co, yo):
    outer(flags, part, k0, ki, kx, zm, ym, side, edge, new)
    outer(flags, u_part, k0, ki, kx, u_zm.at[1], u_ym.at[1], side, edge, u_new)
    u_new[...] += injection(t, new, spot, pick, at, obs)
    rims(flags, u_new, zo, co, yo)


def last_kernel(scale, flags, part, k0, ki, kx, zm, ym, side, edge, image, change, vel,
                prev, states, mine, other):
    new = states.at[1]
    outer(flags, part, k0, ki, kx, zm, ym, side, edge, new)
    raw = from_halves(flags, (image[...] + new[...] * change[...]) * scale / vel[...])
    new[...] = from_halves(flags, new[...])
    states[0] = from_halves(flags, prev[...])
    count, height, lanes = mine.shape
    chunk = raw.shape[1] // (2 * count)
    for n in range(count):
        even, odd = (
            jnp.concatenate(
                [raw[g * height : g * height + height, m * chunk : m * chunk + chunk]
                 for g in range(lanes // chunk)], axis=1)
            for m in (2 * n, 2 * n + 1))
        mine[n] = jnp.where(flags[0] == 0, even, odd)
        other[n] = jnp.where(flags[0] == 0, odd, even)


def join_kernel(flags, mine, got, *outs):
    for s, out in enumerate(outs):
        to = jnp.bitwise_xor(flags[3], s)
        a, b = mine[to], got[to]
        out[0] = jnp.where(flags[0] == 0, a, b)
        out[1] = jnp.where(flags[0] == 0, b, a)


def filter_kernel(flags, *refs):
    *pieces, out = refs
    height, lanes = pieces[0].shape[1:]
    chunk, rows, full = out.shape
    groups = lanes // chunk
    q = flags[3]
    shape = (full, full)
    y = lax.broadcasted_iota(jnp.int32, shape, 1)
    at = lax.broadcasted_iota(jnp.int32, shape, 0)
    within = jnp.bitwise_and(at, 2 * COLS - 1)
    place = jnp.bitwise_xor(q * (2 * COLS), at - within) + within
    weights = jnp.exp(jnp.abs(y - place).astype(F32) * (-1.0 / SMOOTH))
    weights = split(weights / jnp.sum(weights, axis=0, keepdims=True))
    ready = []
    for n in range(height // COLS):
        here = slice(n * COLS, n * COLS + COLS)
        lines = jnp.concatenate([piece[b, here, :] for piece in pieces for b in range(2)], axis=0)
        high, low = split(lines.T)
        done = mm(high, weights[0]) + mm(low, weights[0]) + mm(high, weights[1])
        ready.append(done)
    for g in range(groups):
        lines = jnp.stack([done[g * chunk : g * chunk + chunk] for done in ready], axis=0)
        out[:, g * (rows // groups) : (g + 1) * (rows // groups), :] = jnp.swapaxes(lines, 0, 1)


def shaped(*shape):
    return jax.ShapeDtypeStruct(shape, F32)


class Flags:
    def __getitem__(self, n):
        if n == 0:
            return lax.axis_index("inline")
        xline = lax.axis_index("xline")
        if n == 1:
            return jnp.bitwise_and(xline, 1)
        if n == 3:
            return jnp.right_shift(xline, 1)
        place = 2 * xline + lax.axis_index("inline")
        return jnp.bitwise_and(jnp.right_shift(place, n - 4), 1)


def call(kernel, name, outs, *args, weight=0, far=0, scalars=0, scratch=()):
    specs = [pl.BlockSpec(memory_space=pltpu.SMEM)] * scalars
    specs += [pl.BlockSpec(memory_space=pl.ANY)] * far
    specs += [pl.BlockSpec(memory_space=pltpu.VMEM)] * (len(args) - scalars - far)
    return pl.pallas_call(
        functools.partial(kernel, Flags()),
        name=name,
        out_shape=outs,
        in_specs=specs,
        out_specs=[pl.BlockSpec(memory_space=pltpu.VMEM)] * len(outs),
        scratch_shapes=list(scratch) + ([pltpu.SemaphoreType.DMA((far,))] if far else []),
        compiler_params=pltpu.CompilerParams(vmem_limit_bytes=VMEM_BYTES),
        cost_estimate=pl.CostEstimate(
            flops=1000, bytes_accessed=1000 + int(weight * 3_600_000), transcendentals=0),
    )(*args)


def per_device(plan, fwd_now, fwd_before, adj_now, adj_before, velocity, log_density, observed,
               rec_cells, rec_counts, src_cell, wavelet):
    rows, cols, depth = fwd_now.shape
    size = rows * cols
    steps = wavelet.shape[0]
    nx, nq = plan.nx, plan.nq
    subs = 2 * nx
    xline, c = lax.axis_index("xline"), lax.axis_index("inline")
    q, y = xline // 2, xline % 2
    keep = y == c
    z_perm, c_perm, y_perm, swap_perm = plan.z(), plan.core(), plan.y(), plan.swap()
    stages = [(c_perm, c), (y_perm, y)]
    stages += [(plan.flip(1 << b), (q >> b) & 1) for b in range((nq - 1).bit_length())]
    field = shaped(size, depth)
    rim = [shaped(size // 2, depth), shaped(size // 2, depth), shaped(4 * cols, depth)]

    deep = depth_matrix(depth)
    deep = jnp.asarray(np.concatenate([deep, deep]), BF16)
    inside = jnp.where(c == 0, q > 0, q < nq - 1)
    near = [near_matrix(GROUP, cols, k) for k in range(2)]
    wide = (GROUP + 8) * cols
    near = [np.concatenate([m[:, :wide], m[:, :wide], m[:, wide:], m[:, wide:]], axis=1) for m in near]
    near = jnp.where(c == 0, jnp.asarray(near[0], F32), jnp.asarray(near[1], F32)).astype(BF16)
    side = [side_matrix(rows, k) for k in range(2)]
    side = jnp.where(c == 0, jnp.asarray(side[0], BF16), jnp.asarray(side[1], BF16))
    side = jnp.where(inside, side, jnp.zeros_like(side))
    side = jnp.concatenate([side, side], axis=1)
    edge = [edge_matrix(k) for k in range(2)]
    edge = jnp.where(y == 0, jnp.asarray(edge[0], F32), jnp.asarray(edge[1], F32)).astype(BF16)
    edge = jnp.concatenate([edge, edge], axis=1)

    def halo(zo, co, yo):
        return send(zo, z_perm), send(co, c_perm), send(yo, y_perm)

    def after(value, *deps):
        return lax.optimization_barrier((value,) + deps)[0]

    def flat(value):
        return value.reshape(size, depth)

    log_density, fwd_now, velocity = flat(log_density), flat(fwd_now), flat(velocity)
    fwd_before, adj_now, adj_before = flat(fwd_before), flat(adj_now), flat(adj_before)
    got = [send(v, swap_perm) for v in (log_density, fwd_now)]
    stacked = jnp.stack([velocity, fwd_before])
    got_model = send(stacked, swap_perm)
    full = nx * cols
    inj, = call(functools.partial(source_kernel, 0, full), "source", [field], src_cell, wavelet,
                weight=0.7, scalars=2)
    got[0], inj = lax.optimization_barrier((got[0], inj))
    density, p_now, *out = call(settle_kernel, "settle",
                                [field, field] + [shaped(2, *r.shape) for r in rim],
                                log_density, fwd_now, *got, far=2)
    zm, cm, ym = halo(*out)
    vel, p_before = call(settle_pair_kernel, "settle_model", [field, field],
                         velocity, fwd_before, got_model, weight=0.6, far=2)
    parts = call(first_inner_kernel, "first_inner", [field] * 7, density, p_now, cm,
                 near, deep, weight=1.3)
    got_adjoint = [send(after(v, parts[0]), swap_perm) for v in (adj_now, adj_before)]

    slots = subs * CAP
    entries, half_entries = shaped(subs, steps, 128), shaped(subs // 2, steps, 128)
    cells, lists, give = call(
        pack_kernel, "pack", [shaped(1, slots), entries, half_entries], after(rec_counts, density),
        rec_cells, observed, weight=0.2, far=3,
        scratch=[pltpu.VMEM(rec_counts.shape, jnp.int32), pltpu.VMEM(rec_cells.shape, jnp.int32),
                 pltpu.VMEM(observed.shape, F32)])
    riders = subs // 4 * 8 + 8
    core_rim = shaped(size // 2 + riders, depth)
    y_rim = shaped(4 * cols + riders, depth)

    new, zo, co, yo, k0, ki, kx, kz = call(
        first_outer_kernel, "first_outer", [field, rim[0], core_rim, rim[2]] + [field] * 4,
        p_now, p_before, vel, *parts, inj, zm, ym, side, edge, give, cells)
    model = (k0, ki, kx, kz)
    states = [p_before, p_now, new]
    changes = []
    zm, cm, ym = halo(zo, co, yo)
    late = steps - 2 if len(stages) < steps - 1 else steps - 1
    for t in range(1, steps):
        cur, prev, before = states[:-4:-1]
        stage = t - 1 if 2 < t <= min(len(stages), steps - 2) else None
        extra = [lists, send(give, stages[stage][0])] if stage is not None else []
        part, change = call(
            functools.partial(forward_inner_kernel, t, full), "forward_inner", [field, field], src_cell, wavelet, cur, prev, *model, cm, near, deep, before, weight=1.2, scalars=2)
        changes.append(change)
        args = [part, k0, ki, kx, zm, ym, side, edge]
        if t == steps - 3:
            u_part, = call(adjoint_first_kernel, "adjoint_first", [field], u_now, u_before,
                           *model, u_cm, near, deep, weight=1.1)
            args[0] = after(part, u_part)
        if t == late:
            for n in range(steps - 2, len(stages)):
                lists, *give = call(
                    functools.partial(trade_kernel, n), "trade",
                    [entries] + ([half_entries] if n + 1 < len(stages) else []), lists,
                    send(give, stages[n][0]))
                give = give[0] if give else None
            receivers = call(
                lists_kernel, "lists",
                [jax.ShapeDtypeStruct((size, slots), BF16),
                 jax.ShapeDtypeStruct((slots, size), BF16), shaped(slots, depth),
                 shaped(slots, steps)], lists, cells, weight=0.3)
            args[0] = after(part, receivers[0])
        if t == steps - 1:
            new, u_new, *out = call(
                functools.partial(turn_kernel, t), "turn", [field, field] + rim, *args, u_part,
                u_zm, u_ym, *receivers)
            states.append(new)
            break
        if t == 1:
            new, *out, lists, pair = call(
                core_stage_kernel, "forward_outer",
                [field, rim[0], rim[1], y_rim, entries, shaped(2, slots)], *args, lists, cells, cm)
            states.append(new)
            zm, cm, ym = halo(*out)
            continue
        if t == 2:
            u_now, u_before = call(settle_pair_kernel, "settle_adjoint", [field, field], adj_now,
                                   adj_before, *got_adjoint, weight=0.3, far=2)
            new, *out, lists, give, cells = call(
                y_stage_kernel, "forward_outer",
                [field] + [shaped(2, *r.shape) for r in rim] + [entries, half_entries,
                                                                shaped(1, slots)],
                *args, lists, pair, u_now)
            states.append(new)
            zm, cm, ym = halo(*out)
            u_zm, u_cm, u_ym = zm, cm, ym
            continue
        outs = [field] + rim
        if extra:
            outs = outs + [entries] + ([half_entries] if t < len(stages) else [])
        new, *out = call(functools.partial(outer_kernel, stage), "forward_outer", outs,
                         *args, *extra)
        if extra:
            out, (lists, *give) = out[:3], out[3:]
            give = give[0] if give else None
        states.append(new)
        zm, cm, ym = halo(*out)

    zm, cm, ym = halo(*out)
    u_before, u_now = u_now, u_new
    image = []
    chunk = depth // nx
    half = shaped(nq, size * chunk // 128, 128)
    for j in range(1, steps):
        t = steps - 1 - j
        terms = [changes[t + 1], *image] if image else states[:-4:-1]
        part, *image = call(
            functools.partial(adjoint_inner_kernel, t), "adjoint_inner", [field, field], u_now, u_before, *model, cm, near, deep, states[t + 2], *receivers, *terms, weight=1.5)
        args = [part, k0, ki, kx, zm, ym, side, edge]
        if j == steps - 1:
            final, mine, other = call(
                functools.partial(last_kernel, 2.0 / steps), "last",
                [shaped(2, *field.shape), half, half], *args, *image, changes[0], vel, u_now)
            break
        u_before = u_now
        u_now, *out = call(functools.partial(outer_kernel, None), "adjoint_outer", [field] + rim,
                           *args)
        zm, cm, ym = halo(*out)

    got = send(final, swap_perm)
    pieces = call(join_kernel, "join", [shaped(2, *half.shape[1:])] * nq, mine,
                  send(other, c_perm))
    pieces = [send(pieces[s], plan.spread(s)) for s in reversed(range(nq))][::-1]
    adj_prev, adj_out = call(select_kernel, "select", [field, field], final, got, weight=1.2)
    gradient, = call(filter_kernel, "filter", [shaped(chunk, rows, nx * cols)],
                     after(pieces[0], adj_out), *pieces[1:])
    block = (rows, cols, depth)
    return gradient, adj_out.reshape(block), adj_prev.reshape(block)


def solution(mesh):
    field = P(("shots", "inline"), "xline", None)
    model = P("inline", "xline", None)
    lists = P(("xline", "inline"), None)
    return jax.shard_map(
        functools.partial(per_device, Plan(mesh)),
        mesh=mesh,
        in_specs=(field, field, field, field, model, model, P("shots", ("xline", "inline")),
                  lists, lists, P("shots"), P("shots", None)),
        out_specs=(P(("shots", "xline"), "inline", None), field, field),
        check_vma=False,
    )
```

```python
import functools

import jax
import jax.numpy as jnp
import numpy as np
from jax import lax
from jax.experimental import pallas as pl
from jax.experimental.pallas import tpu as pltpu
from jax.sharding import PartitionSpec as P

CAP = 8
SMOOTH = 16
SECOND = (-205.0 / 72.0, 8.0 / 5.0, -1.0 / 5.0, 8.0 / 315.0, -1.0 / 560.0)
FIRST = (4.0 / 5.0, -1.0 / 5.0, 4.0 / 105.0, -1.0 / 280.0)
ALL = ("shots", "xline", "inline")
COLS = 8
GROUP = 8
VMEM_BYTES = 8 * 1024 * 1024
F32 = jnp.float32
BF16 = jnp.bfloat16


class Plan:
    def __init__(self, mesh):
        self.shots = mesh.shape["shots"]
        self.nx = mesh.shape["xline"]
        self.nq = self.nx // 2

    def index(self, s, q, y, c):
        return (s * self.nx + 2 * q + y) * 2 + c

    def perm(self, partner):
        pairs = []
        for s in range(self.shots):
            for q in range(self.nq):
                for y in range(2):
                    for c in range(2):
                        t = partner(q, y, c)
                        dst = self.index(s ^ 1, q, y, c) if t is None else self.index(s, *t)
                        pairs.append((self.index(s, q, y, c), dst))
        return pairs

    def swap(self):
        return self.perm(lambda q, y, c: None if y == c else (q, c, y))

    def z(self):
        def partner(q, y, c):
            other = q + 1 if c == 1 else q - 1
            return (other, y, 1 - c) if 0 <= other < self.nq else None

        return self.perm(partner)

    def core(self):
        return self.perm(lambda q, y, c: (q, y, 1 - c))

    def y(self):
        return self.perm(lambda q, y, c: (q, 1 - y, c))

    def flip(self, bit):
        return self.perm(lambda q, y, c: (q ^ bit, y, c) if (q ^ bit) < self.nq else None)

    def spread(self, shift):
        return self.perm(lambda q, y, c: (q ^ shift, c, y))


def send(value, pairs):
    return lax.ppermute(value, ALL, pairs)


def depth_matrix(n):
    m = np.zeros((n, 2 * n), np.float32)
    for k in range(1, 5):
        for j in range(n):
            for i, sign in ((j + k, 1.0), (j - k, -1.0)):
                if 0 <= i < n:
                    m[i, j] = round(SECOND[k] * 5040)
                    m[i, n + j] = sign * round(FIRST[k - 1] * 840)
    return m


def stencil_matrix(rows, cols):
    own = (rows + 8) * cols
    m = np.zeros((3, rows, cols, own + rows * 8), np.float32)
    for i in range(rows):
        for x in range(cols):
            for k in range(1, 5):
                total = round(SECOND[k] * 5040)
                slope = round(FIRST[k - 1] * 840)
                for sign in (1, -1):
                    at = (i + 4 + sign * k) * cols + x
                    m[0, i, x, at] += total
                    m[1, i, x, at] += sign * slope
                    to = x + sign * k
                    if to < 0:
                        at = own + i * 4 + to + 4
                    elif to >= cols:
                        at = own + rows * 4 + i * 4 + to - cols
                    else:
                        at = (i + 4) * cols + to
                    m[0, i, x, at] += total
                    m[2, i, x, at] += sign * slope
    return m.reshape(3 * rows * cols, own + rows * 8)


def halved(rows, cols, c):
    at = np.arange(rows)[:, None] * cols
    z_side = (at + 4 * c + np.arange(4)).reshape(-1)
    return np.concatenate([z_side, (at + 4 * (1 - c) + np.arange(4)).reshape(-1)])


def near_matrix(rows, cols, c):
    m = stencil_matrix(rows, cols)
    own = (rows + 8) * cols
    place = halved(rows, cols, c)
    out = np.concatenate([place + k * rows * cols for k in range(3)])
    side = own + (1 - c) * rows * 4 + np.arange(rows * 4)
    return m[out][:, np.concatenate([halved(rows + 8, cols, c), side])]


def side_matrix(rows, c):
    m = np.zeros((2, rows, 4, rows, 4), np.float32)
    for x in range(4):
        for k in range(4):
            d = x + 4 - k if c == 0 else k + 4 - x
            if d <= 4:
                for i in range(rows):
                    m[0, i, x, i, k] = round(SECOND[d] * 5040)
                    m[1, i, x, i, k] = round(FIRST[d - 1] * 840) * (-1 if c == 0 else 1)
    return m.reshape(2 * rows * 4, rows * 4)


def edge_matrix(y):
    m = np.zeros((2, 2, 4, 4, 2, 4, 4), np.float32)
    for i in range(4):
        for k in range(4):
            d = i + 4 - k if y == 1 else k + 4 - i
            if d <= 4:
                for part in range(2):
                    for x in range(4):
                        m[0, part, i, x, part, k, x] = round(SECOND[d] * 5040)
                        m[1, part, i, x, part, k, x] = round(FIRST[d - 1] * 840) * (-1 if y == 1 else 1)
    return m.reshape(64, 32)


def split(value):
    high = value.astype(BF16)
    return high, (value - high.astype(F32)).astype(BF16)


def mm(a, b):
    return jnp.dot(a, b, preferred_element_type=F32)


def inner_differences(cur, cm, near, deep):
    size, depth = cur.shape
    half = size // 2
    cm = cm.at[0] if len(cm.shape) == 3 else cm
    own = split(cur[...])
    along = mm(jnp.concatenate(own, axis=1), deep[...])
    blank = jnp.zeros((16, depth), BF16)
    ext = [[jnp.concatenate([blank, part[h * half : h * half + half], blank], axis=0)
            for h in range(2)] for part in own]
    from_c = split(cm[0:half])
    step = GROUP * 4
    for n in range(half // step):
        rhs = [part[h][n * step : n * step + step + 32] for part in ext for h in range(2)]
        rhs += [part[n * step : n * step + step] for part in from_c]
        out = mm(near[...], jnp.concatenate(rhs, axis=0))
        for h in range(2):
            here = slice(h * half + n * step, h * half + n * step + step)
            sums, di, dx = (out[(2 * k + h) * step : (2 * k + h + 1) * step] for k in range(3))
            yield here, sums, along[here, 0:depth], di, dx, along[here, depth:]


def side_differences(zm, side):
    zm = zm.at[0] if len(zm.shape) == 3 else zm
    out = mm(side[...], jnp.concatenate(split(zm[...]), axis=0))
    half = out.shape[0] // 2
    return out[0:half], out[half:]


def edge_differences(flags, size, ym, edge):
    ym = ym.at[0] if len(ym.shape) == 3 else ym
    out = mm(edge[...], jnp.concatenate(split(ym[0:32]), axis=0))
    start = jnp.where(flags[1] == 1, 0, size // 2 - 16)
    for h in range(2):
        at = pl.ds(pl.multiple_of(start + h * (size // 2), 16), 16)
        yield at, out[h * 16 : h * 16 + 16], out[32 + h * 16 : 48 + h * 16]


def to_halves(flags, value):
    rows, depth = value.shape
    pairs = value.reshape(rows // (2 * COLS), 2, COLS, depth)
    a, b = pairs[:, 0], pairs[:, 1]
    low = lax.broadcasted_iota(jnp.int32, a.shape, 1) < 4
    first = jnp.where(low, a, pltpu.roll(b, 4, axis=1)).reshape(rows // 2, depth)
    last = jnp.where(low, pltpu.roll(a, 4, axis=1), b).reshape(rows // 2, depth)
    return jnp.where(flags[0] == 0, first, last), jnp.where(flags[0] == 0, last, first)


def from_halves(flags, value):
    rows, depth = value.shape
    z_side, c_side = value[0 : rows // 2], value[rows // 2 :]
    shape = (rows // (2 * COLS), COLS, depth)
    first = jnp.where(flags[0] == 0, z_side, c_side).reshape(shape)
    last = jnp.where(flags[0] == 0, c_side, z_side).reshape(shape)
    low = lax.broadcasted_iota(jnp.int32, shape, 1) < 4
    a = jnp.where(low, first, pltpu.roll(last, 4, axis=1))
    b = jnp.where(low, pltpu.roll(first, 4, axis=1), last)
    return jnp.stack([a, b], axis=1).reshape(rows, depth)


def place_of(flags, size, i, x):
    near = x - 4 * flags[0]
    return i * 4 + jnp.where((near >= 0) & (near < 4), near, size // 2 + x - 4 * (1 - flags[0]))


def rims(flags, new, zo, co, yo):
    size = new.shape[0]
    half = size // 2
    zo[...] = new[0:half]
    co[...] = new[half:]
    last = jnp.concatenate([new[half - 16 : half], new[size - 16 :]], axis=0)
    first = jnp.concatenate([new[0:16], new[half : half + 16]], axis=0)
    yo[...] = jnp.where(flags[1] == 0, last, first)


def choose(flags, pairs, sems):
    keep = flags[0] == flags[1]

    @pl.when(keep)
    def _():
        copies = [pltpu.make_async_copy(own, out, sems.at[n])
                  for n, (own, recv, out) in enumerate(pairs)]
        for copy in copies:
            copy.start()
        for copy in copies:
            copy.wait()

    @pl.when(jnp.logical_not(keep))
    def _():
        for own, recv, out in pairs:
            out[...] = recv[...]

    for own, recv, out in pairs:
        half = out.shape[0] // 2
        z_side, c_side = to_halves(flags, out[...])
        out[0:half] = z_side
        out[half:] = c_side


def settle_kernel(flags, a, b, recv_a, recv_b, a_out, b_out, zo, co, yo, sems):
    choose(flags, [(a, recv_a, a_out), (b, recv_b, b_out)], sems)
    for n, out in enumerate((a_out, b_out)):
        rims(flags, out, zo.at[n], co.at[n], yo.at[n])


def settle_pair_kernel(flags, a, b, *rest):
    *recv, a_out, b_out, sems = rest
    recv = recv if len(recv) == 2 else (recv[0].at[0], recv[0].at[1])
    choose(flags, [(a, recv[0], a_out), (b, recv[1], b_out)], sems)


def select_kernel(flags, own, recv, *outs):
    keep = flags[0] == flags[1]
    for n, out in enumerate(outs):
        out[...] = jnp.where(keep, own[n], recv[n])


def first_inner_kernel(flags, lr, cur, cm, near, deep, *outs):
    ri, rx, rz, sums_out, di_out, dx_out, dz_out = outs
    for here, spare, spare_z, di, dx, dz in inner_differences(lr, cm.at[0], near, deep):
        ri[here], rx[here], rz[here] = di, dx, dz
    for here, sums, sums_z, di, dx, dz in inner_differences(cur, cm.at[1], near, deep):
        sums_out[here] = sums + sums_z + (3.0 * SECOND[0] * 5040) * cur[here]
        di_out[here], dx_out[here], dz_out[here] = di, dx, dz


def first_outer_kernel(flags, cur, prev, vel, ri, rx, rz, sums, di, dx, dz, inj, zm, ym, side,
                       edge, give, cells, new, zo, co, yo, k0, ki, kx, kz):
    size = cur.shape[0]
    half = size // 2
    kz[...], ki[...], kx[...] = sums[...], di[...], dx[...]
    k0[...], new[...] = ri[...], rx[...]
    more, more_x = side_differences(zm.at[1], side)
    kz[0:half] += more
    kx[0:half] += more_x
    spare, more_x = side_differences(zm.at[0], side)
    new[0:half] += more_x
    for here, more, more_i in edge_differences(flags, size, ym.at[1], edge):
        kz[here] += more
        ki[here] += more_i
    for here, spare, more_i in edge_differences(flags, size, ym.at[0], edge):
        k0[here] += more_i
    for n in range(4):
        here = slice(n * (size // 4), (n + 1) * (size // 4))
        square = vel[here] * vel[here]
        scaled = square * (1.0 / (840 * 840))
        factor = square * (1.0 / 5040)
        along_i, along_x, along_z = scaled * k0[here], scaled * new[here], scaled * rz[here]
        change = factor * kz[here] - (
            along_i * ki[here] + along_x * kx[here] + along_z * dz[here])
        k0[here], ki[here], kx[here], kz[here] = factor, along_i, along_x, along_z
        center = cur[here]
        new[here] = (center - prev[here]) + (center + (change + inj[here]))
    rims(flags, new, zo, co.at[pl.ds(0, half)], yo)
    load(co, half, lambda n: give[n], give.shape[0], [cells[...]])


def inner(cur, prev, k0, ki, kx, kz, cm, near, deep, inj, out):
    for here, sums, sums_z, di, dx, dz in inner_differences(cur, cm, near, deep):
        center = cur[here]
        change = k0[here] * ((sums + sums_z) + (3.0 * SECOND[0] * 5040) * center)
        change = change - (ki[here] * di + kx[here] * dx + kz[here] * dz)
        if inj is not None:
            change = change + inj[here]
        out[here] = (center - prev[here]) + (center + change)


def outer(flags, part, k0, ki, kx, zm, ym, side, edge, new):
    size = part.shape[0]
    half = size // 2
    sums, dx = side_differences(zm, side)
    new[0:half] = part[0:half] + (k0[0:half] * sums - kx[0:half] * dx)
    new[half:] = part[half:]
    for here, sums, di in edge_differences(flags, size, ym, edge):
        new[here] += k0[here] * sums - ki[here] * di


def other_half(stage, flags, count):
    other = 1 - flags[4 + stage]
    for n in range(count // 2):
        high, low = n >> stage, n & ((1 << stage) - 1)
        yield n, (high << (stage + 1)) + (other << stage) + low


def trade(stage, flags, mine, got, out, give=None):
    out[...] = mine[...]
    for n, at in other_half(stage, flags, out.shape[0]):
        out[at] = got(n) if callable(got) else got[n]
    if give is not None:
        for n, at in other_half(stage + 1, flags, out.shape[0]):
            give[n] = out[at]


def load(message, rim, entry, count, cells):
    for n in range(count):
        message[rim + n // 2 * 8 : rim + n // 2 * 8 + 8, n % 2 * 128 : n % 2 * 128 + 128] = entry(n)
    at = rim + count // 2 * 8
    wide = message.shape[1]
    for k, row in enumerate(cells):
        for m in range(row.shape[1] // 128):
            lane = k * row.shape[1] + m * 128
            message[at + lane // wide : at + lane // wide + 1, lane % wide : lane % wide + 128] = (
                row[:, m * 128 : m * 128 + 128])


def unload(message, rim, count, rows, slots):
    wide = message.shape[1]
    at = rim + count // 2 * 8

    def entry(n):
        return message[rim + n // 2 * 8 : rim + n // 2 * 8 + 8, n % 2 * 128 : n % 2 * 128 + 128]

    cells = []
    for k in range(rows):
        tiles = []
        for m in range(slots // 128):
            lane = k * slots + m * 128
            tiles.append(message[at + lane // wide : at + lane // wide + 1,
                                 lane % wide : lane % wide + 128])
        cells.append(jnp.concatenate(tiles, axis=1) if len(tiles) > 1 else tiles[0])
    return entry, cells


def trade_kernel(stage, flags, mine, got, *outs):
    trade(stage, flags, mine, got, *outs)


def source_kernel(step, full, flags, src, wave, out):
    size, depth = out.shape
    count = src.shape[0]
    shift = (depth - 1).bit_length()
    plane = shift + (full - 1).bit_length()
    rows = size // COLS
    lane = lax.broadcasted_iota(jnp.int32, (1, count), 1)
    sub = lax.broadcasted_iota(jnp.int32, (count, 1), 0)
    row = jnp.zeros((1, count), jnp.int32)
    deep = jnp.zeros((count, 1), jnp.int32)
    size_of = jnp.zeros((count, 1), F32)
    for n in range(count):
        cell = src[n]
        i = jnp.right_shift(cell, plane) - flags[1] * rows
        x = jnp.bitwise_and(jnp.right_shift(cell, shift), full - 1)
        x = x - (2 * flags[3] + flags[0]) * COLS
        ok = (i >= 0) & (i < rows) & (x >= 0) & (x < COLS)
        row = jnp.where(lane == n, jnp.where(ok, place_of(flags, size, i, x), -1), row)
        deep = jnp.where(sub == n, jnp.bitwise_and(cell, depth - 1), deep)
        size_of = jnp.where(sub == n, wave[step, n], size_of)
    spot = lax.broadcasted_iota(jnp.int32, (size, count), 0) == row
    spot = spot.astype(F32).astype(BF16)
    high, low = split(jnp.where(
        lax.broadcasted_iota(jnp.int32, (count, depth), 1) == deep, size_of, 0.0))
    out[...] = mm(spot, high) + mm(spot, low)


def forward_inner_kernel(step, full, flags, src, wave, cur, prev, k0, ki, kx, kz, cm, near, deep,
                         before, part, change):
    source_kernel(step, full, flags, src, wave, change)
    inner(cur, prev, k0, ki, kx, kz, cm, near, deep, change, part)
    change[...] = (cur[...] - prev[...]) - (prev[...] - before[...])


def outer_kernel(stage, flags, part, k0, ki, kx, zm, ym, side, edge, *rest):
    if stage is not None:
        mine, got, new, zo, co, yo, *lists = rest
        trade(stage, flags, mine, got, *lists)
    else:
        new, zo, co, yo = rest
    outer(flags, part, k0, ki, kx, zm, ym, side, edge, new)
    rims(flags, new, zo, co, yo)


def pack_kernel(flags, counts, cells, traces, cells_out, lists, give, counts_v, cells_v, traces_v,
                sems):
    pairs = ((counts, counts_v), (cells, cells_v), (traces, traces_v))
    copies = [pltpu.make_async_copy(a, b, sems.at[n]) for n, (a, b) in enumerate(pairs)]
    for copy in copies:
        copy.start()
    for copy in copies:
        copy.wait()
    subs, n = counts.shape[1], cells.shape[1]
    shape = (subs, n)
    lane = lax.broadcasted_iota(jnp.int32, shape, 1)
    mine = lane // CAP == lax.broadcasted_iota(jnp.int32, shape, 0)
    live = mm(counts_v[...].astype(F32).astype(BF16), mine.astype(F32).astype(BF16))
    slot = jnp.bitwise_and(lane[0:1], CAP - 1)
    cells_out[...] = jnp.where(slot.astype(F32) < live, cells_v[...].astype(F32), -1.0)
    for m in range(subs):
        q, y, c = m >> 2, (m >> 1) & 1, m & 1
        start = ((2 * q + c) * 2 + y) * CAP
        tile = traces_v[:, start // 128 * 128 : start // 128 * 128 + 128]
        lists[m] = pltpu.roll(tile, (128 - start % 128) % 128, axis=1) if start % 128 else tile
    for n, at in other_half(0, flags, subs):
        give[n] = lists[at]


def core_stage_kernel(flags, part, k0, ki, kx, zm, ym, side, edge, lists, cells, cm, new, zo, co, yo,
                      lists_out, pair):
    outer(flags, part, k0, ki, kx, zm, ym, side, edge, new)
    count, half = lists.shape[0] // 2, new.shape[0] // 2
    entry, (theirs,) = unload(cm, half, count, 1, cells.shape[1])
    trade(0, flags, lists, entry, lists_out)
    mine = cells[...]
    pair[0:1] = jnp.where(flags[0] == 0, mine, theirs)
    pair[1:2] = jnp.where(flags[0] == 0, theirs, mine)
    rims(flags, new, zo, co, yo.at[pl.ds(0, 32)])
    at = [k for n, k in other_half(1, flags, lists.shape[0])]
    load(yo, 32, lambda n: lists_out[at[n]], count, [pair[0:1], pair[1:2]])


def y_stage_kernel(flags, part, k0, ki, kx, zm, ym, side, edge, lists, pair, other, new, zo, co, yo,
                   lists_out, give, cells):
    outer(flags, part, k0, ki, kx, zm, ym, side, edge, new)
    for n, field in enumerate((new, other)):
        rims(flags, field, zo.at[n], co.at[n], yo.at[n])
    entry, theirs = unload(ym, 32, lists.shape[0] // 2, 2, pair.shape[1])
    trade(1, flags, lists, entry, lists_out, give)
    away = flags[0] != flags[1]
    low = jnp.where(away, theirs[0], pair[0:1])
    high = jnp.where(away, theirs[1], pair[1:2])
    cells[...] = jnp.where(flags[1] == 0, low, high)


def lists_kernel(flags, lists, cells, spot, pick, at, obs):
    size, n = spot.shape
    depth = at.shape[1]
    subs, steps = lists.shape[0], obs.shape[1]
    cell = cells[...]
    along = jnp.floor((cell + 0.5) * (1.0 / depth))
    place = along.astype(jnp.int32)
    place = jnp.where(place < 0, -1, place_of(
        flags, size, jnp.right_shift(place, 3), jnp.bitwise_and(place, COLS - 1)))
    same = lax.broadcasted_iota(jnp.int32, (n, n), 0) == lax.broadcasted_iota(jnp.int32, (n, n), 1)

    def column(row):
        return jnp.sum(jnp.where(same, row, 0.0), axis=1, keepdims=True).astype(jnp.int32)

    hot = lax.broadcasted_iota(jnp.int32, (size, n), 0) == place
    spot[...] = hot.astype(F32).astype(BF16)
    hot = lax.broadcasted_iota(jnp.int32, (n, size), 1) == column(place.astype(F32))
    pick[...] = hot.astype(F32).astype(BF16)
    hot = lax.broadcasted_iota(jnp.int32, (n, depth), 1) == column(cell - along * depth)
    at[...] = hot.astype(F32)
    traces = lists[...].reshape(subs * steps, 128).T[0:CAP]
    for s in range(subs):
        obs[s * CAP : s * CAP + CAP, :] = traces[:, s * steps : s * steps + steps]


def injection(t, state, spot, pick, at, obs):
    high, low = split(state[...])
    seen = at[...] * (mm(pick[...], high) + mm(pick[...], low))
    residual = jnp.sum(seen, axis=1, keepdims=True) - obs[:, t : t + 1]
    high, low = split(at[...] * residual)
    return mm(spot[...], high) + mm(spot[...], low)


def adjoint_inner_kernel(t, flags, cur, prev, k0, ki, kx, kz, cm, near, deep, state, spot, pick,
                         at, obs, *rest):
    if len(rest) == 4:
        change, image, part, image_out = rest
        image_out[...] = cur[...] * change[...] + image[...]
    else:
        now, mid, before, part, image_out = rest
        image_out[...] = cur[...] * ((now[...] - mid[...]) - (mid[...] - before[...]))
    inj = injection(t, state, spot, pick, at, obs)
    inner(cur, prev, k0, ki, kx, kz, cm, near, deep, inj, part)


def adjoint_first_kernel(flags, cur, prev, k0, ki, kx, kz, cm, near, deep, part):
    inner(cur, prev, k0, ki, kx, kz, cm.at[1], near, deep, None, part)


def turn_kernel(t, flags, part, k0, ki, kx, zm, ym, side, edge, u_part, u_zm, u_ym, spot, pick, at, obs, new, u_new, zo, co, yo):
    outer(flags, part, k0, ki, kx, zm, ym, side, edge, new)
    outer(flags, u_part, k0, ki, kx, u_zm.at[1], u_ym.at[1], side, edge, u_new)
    u_new[...] += injection(t, new, spot, pick, at, obs)
    rims(flags, u_new, zo, co, yo)


def last_kernel(scale, flags, part, k0, ki, kx, zm, ym, side, edge, image, change, vel,
                prev, states, mine, other):
    new = states.at[1]
    outer(flags, part, k0, ki, kx, zm, ym, side, edge, new)
    raw = from_halves(flags, (image[...] + new[...] * change[...]) * scale / vel[...])
    new[...] = from_halves(flags, new[...])
    states[0] = from_halves(flags, prev[...])
    count, height, lanes = mine.shape
    chunk = raw.shape[1] // (2 * count)
    for n in range(count):
        even, odd = (
            jnp.concatenate(
                [raw[g * height : g * height + height, m * chunk : m * chunk + chunk]
                 for g in range(lanes // chunk)], axis=1)
            for m in (2 * n, 2 * n + 1))
        mine[n] = jnp.where(flags[0] == 0, even, odd)
        other[n] = jnp.where(flags[0] == 0, odd, even)


def join_kernel(flags, mine, got, *outs):
    for s, out in enumerate(outs):
        to = jnp.bitwise_xor(flags[3], s)
        a, b = mine[to], got[to]
        out[0] = jnp.where(flags[0] == 0, a, b)
        out[1] = jnp.where(flags[0] == 0, b, a)


def filter_kernel(flags, *refs):
    *pieces, out = refs
    height, lanes = pieces[0].shape[1:]
    chunk, rows, full = out.shape
    groups = lanes // chunk
    q = flags[3]
    shape = (full, full)
    y = lax.broadcasted_iota(jnp.int32, shape, 1)
    at = lax.broadcasted_iota(jnp.int32, shape, 0)
    within = jnp.bitwise_and(at, 2 * COLS - 1)
    place = jnp.bitwise_xor(q * (2 * COLS), at - within) + within
    weights = jnp.exp(jnp.abs(y - place).astype(F32) * (-1.0 / SMOOTH))
    weights = split(weights / jnp.sum(weights, axis=0, keepdims=True))
    ready = []
    for n in range(height // COLS):
        here = slice(n * COLS, n * COLS + COLS)
        lines = jnp.concatenate([piece[b, here, :] for piece in pieces for b in range(2)], axis=0)
        high, low = split(lines.T)
        done = mm(high, weights[0]) + mm(low, weights[0]) + mm(high, weights[1])
        ready.append(done)
    for g in range(groups):
        lines = jnp.stack([done[g * chunk : g * chunk + chunk] for done in ready], axis=0)
        out[:, g * (rows // groups) : (g + 1) * (rows // groups), :] = jnp.swapaxes(lines, 0, 1)


def shaped(*shape):
    return jax.ShapeDtypeStruct(shape, F32)


class Flags:
    def __getitem__(self, n):
        if n == 0:
            return lax.axis_index("inline")
        xline = lax.axis_index("xline")
        if n == 1:
            return jnp.bitwise_and(xline, 1)
        if n == 3:
            return jnp.right_shift(xline, 1)
        place = 2 * xline + lax.axis_index("inline")
        return jnp.bitwise_and(jnp.right_shift(place, n - 4), 1)


def call(kernel, name, outs, *args, weight=0, far=0, scalars=0, scratch=()):
    specs = [pl.BlockSpec(memory_space=pltpu.SMEM)] * scalars
    specs += [pl.BlockSpec(memory_space=pl.ANY)] * far
    specs += [pl.BlockSpec(memory_space=pltpu.VMEM)] * (len(args) - scalars - far)
    return pl.pallas_call(
        functools.partial(kernel, Flags()),
        name=name,
        out_shape=outs,
        in_specs=specs,
        out_specs=[pl.BlockSpec(memory_space=pltpu.VMEM)] * len(outs),
        scratch_shapes=list(scratch) + ([pltpu.SemaphoreType.DMA((far,))] if far else []),
        compiler_params=pltpu.CompilerParams(vmem_limit_bytes=VMEM_BYTES),
        cost_estimate=pl.CostEstimate(
            flops=1000, bytes_accessed=1000 + int(weight * 3_600_000), transcendentals=0),
    )(*args)


def per_device(plan, fwd_now, fwd_before, adj_now, adj_before, velocity, log_density, observed,
               rec_cells, rec_counts, src_cell, wavelet):
    rows, cols, depth = fwd_now.shape
    size = rows * cols
    steps = wavelet.shape[0]
    nx, nq = plan.nx, plan.nq
    subs = 2 * nx
    xline, c = lax.axis_index("xline"), lax.axis_index("inline")
    q, y = xline // 2, xline % 2
    keep = y == c
    z_perm, c_perm, y_perm, swap_perm = plan.z(), plan.core(), plan.y(), plan.swap()
    stages = [(c_perm, c), (y_perm, y)]
    stages += [(plan.flip(1 << b), (q >> b) & 1) for b in range((nq - 1).bit_length())]
    field = shaped(size, depth)
    rim = [shaped(size // 2, depth), shaped(size // 2, depth), shaped(4 * cols, depth)]

    deep = depth_matrix(depth)
    deep = jnp.asarray(np.concatenate([deep, deep]), BF16)
    inside = jnp.where(c == 0, q > 0, q < nq - 1)
    near = [near_matrix(GROUP, cols, k) for k in range(2)]
    wide = (GROUP + 8) * cols
    near = [np.concatenate([m[:, :wide], m[:, :wide], m[:, wide:], m[:, wide:]], axis=1) for m in near]
    near = jnp.where(c == 0, jnp.asarray(near[0], F32), jnp.asarray(near[1], F32)).astype(BF16)
    side = [side_matrix(rows, k) for k in range(2)]
    side = jnp.where(c == 0, jnp.asarray(side[0], BF16), jnp.asarray(side[1], BF16))
    side = jnp.where(inside, side, jnp.zeros_like(side))
    side = jnp.concatenate([side, side], axis=1)
    edge = [edge_matrix(k) for k in range(2)]
    edge = jnp.where(y == 0, jnp.asarray(edge[0], F32), jnp.asarray(edge[1], F32)).astype(BF16)
    edge = jnp.concatenate([edge, edge], axis=1)

    def halo(zo, co, yo):
        return send(zo, z_perm), send(co, c_perm), send(yo, y_perm)

    def after(value, *deps):
        return lax.optimization_barrier((value,) + deps)[0]

    def flat(value):
        return value.reshape(size, depth)

    log_density, fwd_now, velocity = flat(log_density), flat(fwd_now), flat(velocity)
    fwd_before, adj_now, adj_before = flat(fwd_before), flat(adj_now), flat(adj_before)
    got = [send(v, swap_perm) for v in (log_density, fwd_now)]
    stacked = jnp.stack([velocity, fwd_before])
    got_model = send(stacked, swap_perm)
    full = nx * cols
    inj, = call(functools.partial(source_kernel, 0, full), "source", [field], src_cell, wavelet,
                weight=0.7, scalars=2)
    got[0], inj = lax.optimization_barrier((got[0], inj))
    density, p_now, *out = call(settle_kernel, "settle",
                                [field, field] + [shaped(2, *r.shape) for r in rim],
                                log_density, fwd_now, *got, far=2)
    zm, cm, ym = halo(*out)
    vel, p_before = call(settle_pair_kernel, "settle_model", [field, field],
                         velocity, fwd_before, got_model, weight=0.6, far=2)
    parts = call(first_inner_kernel, "first_inner", [field] * 7, density, p_now, cm,
                 near, deep, weight=1.3)
    got_adjoint = [send(after(v, parts[0]), swap_perm) for v in (adj_now, adj_before)]

    slots = subs * CAP
    entries, half_entries = shaped(subs, steps, 128), shaped(subs // 2, steps, 128)
    cells, lists, give = call(
        pack_kernel, "pack", [shaped(1, slots), entries, half_entries], after(rec_counts, density),
        rec_cells, observed, weight=0.2, far=3,
        scratch=[pltpu.VMEM(rec_counts.shape, jnp.int32), pltpu.VMEM(rec_cells.shape, jnp.int32),
                 pltpu.VMEM(observed.shape, F32)])
    riders = subs // 4 * 8 + 8
    core_rim = shaped(size // 2 + riders, depth)
    y_rim = shaped(4 * cols + riders, depth)

    new, zo, co, yo, k0, ki, kx, kz = call(
        first_outer_kernel, "first_outer", [field, rim[0], core_rim, rim[2]] + [field] * 4,
        p_now, p_before, vel, *parts, inj, zm, ym, side, edge, give, cells)
    model = (k0, ki, kx, kz)
    states = [p_before, p_now, new]
    changes = []
    zm, cm, ym = halo(zo, co, yo)
    late = steps - 2 if len(stages) < steps - 1 else steps - 1
    for t in range(1, steps):
        cur, prev, before = states[:-4:-1]
        stage = t - 1 if 2 < t <= min(len(stages), steps - 2) else None
        extra = [lists, send(give, stages[stage][0])] if stage is not None else []
        part, change = call(
            functools.partial(forward_inner_kernel, t, full), "forward_inner", [field, field], src_cell, wavelet, cur, prev, *model, cm, near, deep, before, weight=1.2, scalars=2)
        changes.append(change)
        args = [part, k0, ki, kx, zm, ym, side, edge]
        if t == steps - 3:
            u_part, = call(adjoint_first_kernel, "adjoint_first", [field], u_now, u_before,
                           *model, u_cm, near, deep, weight=1.1)
            args[0] = after(part, u_part)
        if t == late:
            for n in range(steps - 2, len(stages)):
                lists, *give = call(
                    functools.partial(trade_kernel, n), "trade",
                    [entries] + ([half_entries] if n + 1 < len(stages) else []), lists,
                    send(give, stages[n][0]))
                give = give[0] if give else None
            receivers = call(
                lists_kernel, "lists",
                [jax.ShapeDtypeStruct((size, slots), BF16),
                 jax.ShapeDtypeStruct((slots, size), BF16), shaped(slots, depth),
                 shaped(slots, steps)], lists, cells, weight=0.3)
            args[0] = after(part, receivers[0])
        if t == steps - 1:
            new, u_new, *out = call(
                functools.partial(turn_kernel, t), "turn", [field, field] + rim, *args, u_part,
                u_zm, u_ym, *receivers)
            states.append(new)
            break
        if t == 1:
            u_now, u_before = call(settle_pair_kernel, "settle_adjoint", [field, field], adj_now,
                                   adj_before, *got_adjoint, weight=0.6, far=2)
            args[0] = after(part, u_now)
            new, *out, lists, pair = call(
                core_stage_kernel, "forward_outer",
                [field, rim[0], rim[1], y_rim, entries, shaped(2, slots)], *args, lists, cells, cm)
            states.append(new)
            zm, cm, ym = halo(*out)
            continue
        if t == 2:
            new, *out, lists, give, cells = call(
                y_stage_kernel, "forward_outer",
                [field] + [shaped(2, *r.shape) for r in rim] + [entries, half_entries,
                                                                shaped(1, slots)],
                *args, lists, pair, u_now)
            states.append(new)
            zm, cm, ym = halo(*out)
            u_zm, u_cm, u_ym = zm, cm, ym
            continue
        outs = [field] + rim
        if extra:
            outs = outs + [entries] + ([half_entries] if t < len(stages) else [])
        new, *out = call(functools.partial(outer_kernel, stage), "forward_outer", outs,
                         *args, *extra)
        if extra:
            out, (lists, *give) = out[:3], out[3:]
            give = give[0] if give else None
        states.append(new)
        zm, cm, ym = halo(*out)

    zm, cm, ym = halo(*out)
    u_before, u_now = u_now, u_new
    image = []
    chunk = depth // nx
    half = shaped(nq, size * chunk // 128, 128)
    for j in range(1, steps):
        t = steps - 1 - j
        terms = [changes[t + 1], *image] if image else states[:-4:-1]
        part, *image = call(
            functools.partial(adjoint_inner_kernel, t), "adjoint_inner", [field, field], u_now, u_before, *model, cm, near, deep, states[t + 2], *receivers, *terms, weight=1.5)
        args = [part, k0, ki, kx, zm, ym, side, edge]
        if j == steps - 1:
            final, mine, other = call(
                functools.partial(last_kernel, 2.0 / steps), "last",
                [shaped(2, *field.shape), half, half], *args, *image, changes[0], vel, u_now)
            break
        u_before = u_now
        u_now, *out = call(functools.partial(outer_kernel, None), "adjoint_outer", [field] + rim,
                           *args)
        zm, cm, ym = halo(*out)

    got = send(final, swap_perm)
    pieces = call(join_kernel, "join", [shaped(2, *half.shape[1:])] * nq, mine,
                  send(other, c_perm))
    pieces = [send(pieces[s], plan.spread(s)) for s in reversed(range(nq))][::-1]
    adj_prev, adj_out = call(select_kernel, "select", [field, field], final, got, weight=1.2)
    gradient, = call(filter_kernel, "filter", [shaped(chunk, rows, nx * cols)],
                     after(pieces[0], adj_out), *pieces[1:])
    block = (rows, cols, depth)
    return gradient, adj_out.reshape(block), adj_prev.reshape(block)


def solution(mesh):
    field = P(("shots", "inline"), "xline", None)
    model = P("inline", "xline", None)
    lists = P(("xline", "inline"), None)
    return jax.shard_map(
        functools.partial(per_device, Plan(mesh)),
        mesh=mesh,
        in_specs=(field, field, field, field, model, model, P("shots", ("xline", "inline")),
                  lists, lists, P("shots"), P("shots", None)),
        out_specs=(P(("shots", "xline"), "inline", None), field, field),
        check_vma=False,
    )
```

```python
import functools

import jax
import jax.numpy as jnp
import numpy as np
from jax import lax
from jax.experimental import pallas as pl
from jax.experimental.pallas import tpu as pltpu
from jax.sharding import PartitionSpec as P

CAP = 8
SMOOTH = 16
SECOND = (-205.0 / 72.0, 8.0 / 5.0, -1.0 / 5.0, 8.0 / 315.0, -1.0 / 560.0)
FIRST = (4.0 / 5.0, -1.0 / 5.0, 4.0 / 105.0, -1.0 / 280.0)
ALL = ("shots", "xline", "inline")
COLS = 8
GROUP = 8
VMEM_BYTES = 8 * 1024 * 1024
F32 = jnp.float32
BF16 = jnp.bfloat16


class Plan:
    def __init__(self, mesh):
        self.shots = mesh.shape["shots"]
        self.nx = mesh.shape["xline"]
        self.nq = self.nx // 2

    def index(self, s, q, y, c):
        return (s * self.nx + 2 * q + y) * 2 + c

    def perm(self, partner):
        pairs = []
        for s in range(self.shots):
            for q in range(self.nq):
                for y in range(2):
                    for c in range(2):
                        t = partner(q, y, c)
                        dst = self.index(s ^ 1, q, y, c) if t is None else self.index(s, *t)
                        pairs.append((self.index(s, q, y, c), dst))
        return pairs

    def swap(self):
        return self.perm(lambda q, y, c: None if y == c else (q, c, y))

    def z(self):
        def partner(q, y, c):
            other = q + 1 if c == 1 else q - 1
            return (other, y, 1 - c) if 0 <= other < self.nq else None

        return self.perm(partner)

    def core(self):
        return self.perm(lambda q, y, c: (q, y, 1 - c))

    def y(self):
        return self.perm(lambda q, y, c: (q, 1 - y, c))

    def flip(self, bit):
        return self.perm(lambda q, y, c: (q ^ bit, y, c) if (q ^ bit) < self.nq else None)

    def spread(self, shift):
        return self.perm(lambda q, y, c: (q ^ shift, c, y))


def send(value, pairs):
    return lax.ppermute(value, ALL, pairs)


def depth_matrix(n):
    m = np.zeros((n, 2 * n), np.float32)
    for k in range(1, 5):
        for j in range(n):
            for i, sign in ((j + k, 1.0), (j - k, -1.0)):
                if 0 <= i < n:
                    m[i, j] = round(SECOND[k] * 5040)
                    m[i, n + j] = sign * round(FIRST[k - 1] * 840)
    return m


def stencil_matrix(rows, cols):
    own = (rows + 8) * cols
    m = np.zeros((3, rows, cols, own + rows * 8), np.float32)
    for i in range(rows):
        for x in range(cols):
            for k in range(1, 5):
                total = round(SECOND[k] * 5040)
                slope = round(FIRST[k - 1] * 840)
                for sign in (1, -1):
                    at = (i + 4 + sign * k) * cols + x
                    m[0, i, x, at] += total
                    m[1, i, x, at] += sign * slope
                    to = x + sign * k
                    if to < 0:
                        at = own + i * 4 + to + 4
                    elif to >= cols:
                        at = own + rows * 4 + i * 4 + to - cols
                    else:
                        at = (i + 4) * cols + to
                    m[0, i, x, at] += total
                    m[2, i, x, at] += sign * slope
    return m.reshape(3 * rows * cols, own + rows * 8)


def halved(rows, cols, c):
    at = np.arange(rows)[:, None] * cols
    z_side = (at + 4 * c + np.arange(4)).reshape(-1)
    return np.concatenate([z_side, (at + 4 * (1 - c) + np.arange(4)).reshape(-1)])


def near_matrix(rows, cols, c):
    m = stencil_matrix(rows, cols)
    own = (rows + 8) * cols
    place = halved(rows, cols, c)
    out = np.concatenate([place + k * rows * cols for k in range(3)])
    side = own + (1 - c) * rows * 4 + np.arange(rows * 4)
    return m[out][:, np.concatenate([halved(rows + 8, cols, c), side])]


def side_matrix(rows, c):
    m = np.zeros((2, rows, 4, rows, 4), np.float32)
    for x in range(4):
        for k in range(4):
            d = x + 4 - k if c == 0 else k + 4 - x
            if d <= 4:
                for i in range(rows):
                    m[0, i, x, i, k] = round(SECOND[d] * 5040)
                    m[1, i, x, i, k] = round(FIRST[d - 1] * 840) * (-1 if c == 0 else 1)
    return m.reshape(2 * rows * 4, rows * 4)


def edge_matrix(y):
    m = np.zeros((2, 2, 4, 4, 2, 4, 4), np.float32)
    for i in range(4):
        for k in range(4):
            d = i + 4 - k if y == 1 else k + 4 - i
            if d <= 4:
                for part in range(2):
                    for x in range(4):
                        m[0, part, i, x, part, k, x] = round(SECOND[d] * 5040)
                        m[1, part, i, x, part, k, x] = round(FIRST[d - 1] * 840) * (-1 if y == 1 else 1)
    return m.reshape(64, 32)


def split(value):
    high = value.astype(BF16)
    return high, (value - high.astype(F32)).astype(BF16)


def mm(a, b):
    return jnp.dot(a, b, preferred_element_type=F32)


def inner_differences(cur, cm, near, deep):
    size, depth = cur.shape
    half = size // 2
    cm = cm.at[0] if len(cm.shape) == 3 else cm
    own = split(cur[...])
    along = mm(jnp.concatenate(own, axis=1), deep[...])
    blank = jnp.zeros((16, depth), BF16)
    ext = [[jnp.concatenate([blank, part[h * half : h * half + half], blank], axis=0)
            for h in range(2)] for part in own]
    from_c = split(cm[0:half])
    step = GROUP * 4
    for n in range(half // step):
        rhs = [part[h][n * step : n * step + step + 32] for part in ext for h in range(2)]
        rhs += [part[n * step : n * step + step] for part in from_c]
        out = mm(near[...], jnp.concatenate(rhs, axis=0))
        for h in range(2):
            here = slice(h * half + n * step, h * half + n * step + step)
            sums, di, dx = (out[(2 * k + h) * step : (2 * k + h + 1) * step] for k in range(3))
            yield here, sums, along[here, 0:depth], di, dx, along[here, depth:]


def side_differences(zm, side):
    zm = zm.at[0] if len(zm.shape) == 3 else zm
    out = mm(side[...], jnp.concatenate(split(zm[...]), axis=0))
    half = out.shape[0] // 2
    return out[0:half], out[half:]


def edge_differences(flags, size, ym, edge):
    ym = ym.at[0] if len(ym.shape) == 3 else ym
    out = mm(edge[...], jnp.concatenate(split(ym[0:32]), axis=0))
    start = jnp.where(flags[1] == 1, 0, size // 2 - 16)
    for h in range(2):
        at = pl.ds(pl.multiple_of(start + h * (size // 2), 16), 16)
        yield at, out[h * 16 : h * 16 + 16], out[32 + h * 16 : 48 + h * 16]


def to_halves(flags, value):
    rows, depth = value.shape
    pairs = value.reshape(rows // (2 * COLS), 2, COLS, depth)
    a, b = pairs[:, 0], pairs[:, 1]
    low = lax.broadcasted_iota(jnp.int32, a.shape, 1) < 4
    first = jnp.where(low, a, pltpu.roll(b, 4, axis=1)).reshape(rows // 2, depth)
    last = jnp.where(low, pltpu.roll(a, 4, axis=1), b).reshape(rows // 2, depth)
    return jnp.where(flags[0] == 0, first, last), jnp.where(flags[0] == 0, last, first)


def from_halves(flags, value):
    rows, depth = value.shape
    z_side, c_side = value[0 : rows // 2], value[rows // 2 :]
    shape = (rows // (2 * COLS), COLS, depth)
    first = jnp.where(flags[0] == 0, z_side, c_side).reshape(shape)
    last = jnp.where(flags[0] == 0, c_side, z_side).reshape(shape)
    low = lax.broadcasted_iota(jnp.int32, shape, 1) < 4
    a = jnp.where(low, first, pltpu.roll(last, 4, axis=1))
    b = jnp.where(low, pltpu.roll(first, 4, axis=1), last)
    return jnp.stack([a, b], axis=1).reshape(rows, depth)


def place_of(flags, size, i, x):
    near = x - 4 * flags[0]
    return i * 4 + jnp.where((near >= 0) & (near < 4), near, size // 2 + x - 4 * (1 - flags[0]))


def rims(flags, new, zo, co, yo):
    size = new.shape[0]
    half = size // 2
    zo[...] = new[0:half]
    co[...] = new[half:]
    last = jnp.concatenate([new[half - 16 : half], new[size - 16 :]], axis=0)
    first = jnp.concatenate([new[0:16], new[half : half + 16]], axis=0)
    yo[...] = jnp.where(flags[1] == 0, last, first)


def choose(flags, pairs, sems):
    keep = flags[0] == flags[1]

    @pl.when(keep)
    def _():
        copies = [pltpu.make_async_copy(own, out, sems.at[n])
                  for n, (own, recv, out) in enumerate(pairs)]
        for copy in copies:
            copy.start()
        for copy in copies:
            copy.wait()

    @pl.when(jnp.logical_not(keep))
    def _():
        for own, recv, out in pairs:
            out[...] = recv[...]

    for own, recv, out in pairs:
        half = out.shape[0] // 2
        z_side, c_side = to_halves(flags, out[...])
        out[0:half] = z_side
        out[half:] = c_side


def settle_kernel(flags, a, recv, out, zo, co, yo, sems):
    choose(flags, [(a, recv, out)], sems)
    rims(flags, out, zo, co, yo)


def settle_pair_kernel(flags, a, b, *rest):
    *recv, a_out, b_out, sems = rest
    recv = recv if len(recv) == 2 else (recv[0].at[0], recv[0].at[1])
    choose(flags, [(a, recv[0], a_out), (b, recv[1], b_out)], sems)


def select_kernel(flags, own, recv, *outs):
    keep = flags[0] == flags[1]
    for n, out in enumerate(outs):
        out[...] = jnp.where(keep, own[n], recv[n])


def first_inner_kernel(flags, lr, cur, lr_cm, cm, near, deep, *outs):
    ri, rx, rz, sums_out, di_out, dx_out, dz_out = outs
    for here, spare, spare_z, di, dx, dz in inner_differences(lr, lr_cm, near, deep):
        ri[here], rx[here], rz[here] = di, dx, dz
    for here, sums, sums_z, di, dx, dz in inner_differences(cur, cm, near, deep):
        sums_out[here] = sums + sums_z + (3.0 * SECOND[0] * 5040) * cur[here]
        di_out[here], dx_out[here], dz_out[here] = di, dx, dz


def first_outer_kernel(flags, cur, prev, vel, ri, rx, rz, sums, di, dx, dz, inj, lr_zm, lr_ym, zm, ym,
                       side, edge, give, cells, new, zo, co, yo, k0, ki, kx, kz):
    size = cur.shape[0]
    half = size // 2
    kz[...], ki[...], kx[...] = sums[...], di[...], dx[...]
    k0[...], new[...] = ri[...], rx[...]
    more, more_x = side_differences(zm, side)
    kz[0:half] += more
    kx[0:half] += more_x
    spare, more_x = side_differences(lr_zm, side)
    new[0:half] += more_x
    for here, more, more_i in edge_differences(flags, size, ym, edge):
        kz[here] += more
        ki[here] += more_i
    for here, spare, more_i in edge_differences(flags, size, lr_ym, edge):
        k0[here] += more_i
    for n in range(4):
        here = slice(n * (size // 4), (n + 1) * (size // 4))
        square = vel[here] * vel[here]
        scaled = square * (1.0 / (840 * 840))
        factor = square * (1.0 / 5040)
        along_i, along_x, along_z = scaled * k0[here], scaled * new[here], scaled * rz[here]
        change = factor * kz[here] - (
            along_i * ki[here] + along_x * kx[here] + along_z * dz[here])
        k0[here], ki[here], kx[here], kz[here] = factor, along_i, along_x, along_z
        center = cur[here]
        new[here] = (center - prev[here]) + (center + (change + inj[here]))
    rims(flags, new, zo, co.at[pl.ds(0, half)], yo)
    load(co, half, lambda n: give[n], give.shape[0], [cells[...]])


def inner(cur, prev, k0, ki, kx, kz, cm, near, deep, inj, out):
    for here, sums, sums_z, di, dx, dz in inner_differences(cur, cm, near, deep):
        center = cur[here]
        change = k0[here] * ((sums + sums_z) + (3.0 * SECOND[0] * 5040) * center)
        change = change - (ki[here] * di + kx[here] * dx + kz[here] * dz)
        if inj is not None:
            change = change + inj[here]
        out[here] = (center - prev[here]) + (center + change)


def outer(flags, part, k0, ki, kx, zm, ym, side, edge, new):
    size = part.shape[0]
    half = size // 2
    sums, dx = side_differences(zm, side)
    new[0:half] = part[0:half] + (k0[0:half] * sums - kx[0:half] * dx)
    new[half:] = part[half:]
    for here, sums, di in edge_differences(flags, size, ym, edge):
        new[here] += k0[here] * sums - ki[here] * di


def other_half(stage, flags, count):
    other = 1 - flags[4 + stage]
    for n in range(count // 2):
        high, low = n >> stage, n & ((1 << stage) - 1)
        yield n, (high << (stage + 1)) + (other << stage) + low


def trade(stage, flags, mine, got, out, give=None):
    out[...] = mine[...]
    for n, at in other_half(stage, flags, out.shape[0]):
        out[at] = got(n) if callable(got) else got[n]
    if give is not None:
        for n, at in other_half(stage + 1, flags, out.shape[0]):
            give[n] = out[at]


def load(message, rim, entry, count, cells):
    for n in range(count):
        message[rim + n // 2 * 8 : rim + n // 2 * 8 + 8, n % 2 * 128 : n % 2 * 128 + 128] = entry(n)
    at = rim + count // 2 * 8
    wide = message.shape[1]
    for k, row in enumerate(cells):
        for m in range(row.shape[1] // 128):
            lane = k * row.shape[1] + m * 128
            message[at + lane // wide : at + lane // wide + 1, lane % wide : lane % wide + 128] = (
                row[:, m * 128 : m * 128 + 128])


def unload(message, rim, count, rows, slots):
    wide = message.shape[1]
    at = rim + count // 2 * 8

    def entry(n):
        return message[rim + n // 2 * 8 : rim + n // 2 * 8 + 8, n % 2 * 128 : n % 2 * 128 + 128]

    cells = []
    for k in range(rows):
        tiles = []
        for m in range(slots // 128):
            lane = k * slots + m * 128
            tiles.append(message[at + lane // wide : at + lane // wide + 1,
                                 lane % wide : lane % wide + 128])
        cells.append(jnp.concatenate(tiles, axis=1) if len(tiles) > 1 else tiles[0])
    return entry, cells


def trade_kernel(stage, flags, mine, got, *outs):
    trade(stage, flags, mine, got, *outs)


def source_kernel(step, full, flags, src, wave, out):
    size, depth = out.shape
    count = src.shape[0]
    shift = (depth - 1).bit_length()
    plane = shift + (full - 1).bit_length()
    rows = size // COLS
    lane = lax.broadcasted_iota(jnp.int32, (1, count), 1)
    sub = lax.broadcasted_iota(jnp.int32, (count, 1), 0)
    row = jnp.zeros((1, count), jnp.int32)
    deep = jnp.zeros((count, 1), jnp.int32)
    size_of = jnp.zeros((count, 1), F32)
    for n in range(count):
        cell = src[n]
        i = jnp.right_shift(cell, plane) - flags[1] * rows
        x = jnp.bitwise_and(jnp.right_shift(cell, shift), full - 1)
        x = x - (2 * flags[3] + flags[0]) * COLS
        ok = (i >= 0) & (i < rows) & (x >= 0) & (x < COLS)
        row = jnp.where(lane == n, jnp.where(ok, place_of(flags, size, i, x), -1), row)
        deep = jnp.where(sub == n, jnp.bitwise_and(cell, depth - 1), deep)
        size_of = jnp.where(sub == n, wave[step, n], size_of)
    spot = lax.broadcasted_iota(jnp.int32, (size, count), 0) == row
    spot = spot.astype(F32).astype(BF16)
    high, low = split(jnp.where(
        lax.broadcasted_iota(jnp.int32, (count, depth), 1) == deep, size_of, 0.0))
    out[...] = mm(spot, high) + mm(spot, low)


def forward_inner_kernel(step, full, flags, src, wave, cur, prev, k0, ki, kx, kz, cm, near, deep,
                         before, part, change):
    source_kernel(step, full, flags, src, wave, change)
    inner(cur, prev, k0, ki, kx, kz, cm, near, deep, change, part)
    change[...] = (cur[...] - prev[...]) - (prev[...] - before[...])


def outer_kernel(stage, flags, part, k0, ki, kx, zm, ym, side, edge, *rest):
    if stage is not None:
        mine, got, new, zo, co, yo, *lists = rest
        trade(stage, flags, mine, got, *lists)
    else:
        new, zo, co, yo = rest
    outer(flags, part, k0, ki, kx, zm, ym, side, edge, new)
    rims(flags, new, zo, co, yo)


def pack_kernel(flags, counts, cells, traces, cells_out, lists, give, counts_v, cells_v, traces_v,
                sems):
    pairs = ((counts, counts_v), (cells, cells_v), (traces, traces_v))
    copies = [pltpu.make_async_copy(a, b, sems.at[n]) for n, (a, b) in enumerate(pairs)]
    for copy in copies:
        copy.start()
    for copy in copies:
        copy.wait()
    subs, n = counts.shape[1], cells.shape[1]
    shape = (subs, n)
    lane = lax.broadcasted_iota(jnp.int32, shape, 1)
    mine = lane // CAP == lax.broadcasted_iota(jnp.int32, shape, 0)
    live = mm(counts_v[...].astype(F32).astype(BF16), mine.astype(F32).astype(BF16))
    slot = jnp.bitwise_and(lane[0:1], CAP - 1)
    cells_out[...] = jnp.where(slot.astype(F32) < live, cells_v[...].astype(F32), -1.0)
    for m in range(subs):
        q, y, c = m >> 2, (m >> 1) & 1, m & 1
        start = ((2 * q + c) * 2 + y) * CAP
        tile = traces_v[:, start // 128 * 128 : start // 128 * 128 + 128]
        lists[m] = pltpu.roll(tile, (128 - start % 128) % 128, axis=1) if start % 128 else tile
    for n, at in other_half(0, flags, subs):
        give[n] = lists[at]


def core_stage_kernel(flags, part, k0, ki, kx, zm, ym, side, edge, lists, cells, cm, new, zo, co, yo,
                      lists_out, pair):
    outer(flags, part, k0, ki, kx, zm, ym, side, edge, new)
    count, half = lists.shape[0] // 2, new.shape[0] // 2
    entry, (theirs,) = unload(cm, half, count, 1, cells.shape[1])
    trade(0, flags, lists, entry, lists_out)
    mine = cells[...]
    pair[0:1] = jnp.where(flags[0] == 0, mine, theirs)
    pair[1:2] = jnp.where(flags[0] == 0, theirs, mine)
    rims(flags, new, zo, co, yo.at[pl.ds(0, 32)])
    at = [k for n, k in other_half(1, flags, lists.shape[0])]
    load(yo, 32, lambda n: lists_out[at[n]], count, [pair[0:1], pair[1:2]])


def y_stage_kernel(flags, part, k0, ki, kx, zm, ym, side, edge, lists, pair, other, new, zo, co, yo,
                   lists_out, give, cells):
    outer(flags, part, k0, ki, kx, zm, ym, side, edge, new)
    for n, field in enumerate((new, other)):
        rims(flags, field, zo.at[n], co.at[n], yo.at[n])
    entry, theirs = unload(ym, 32, lists.shape[0] // 2, 2, pair.shape[1])
    trade(1, flags, lists, entry, lists_out, give)
    away = flags[0] != flags[1]
    low = jnp.where(away, theirs[0], pair[0:1])
    high = jnp.where(away, theirs[1], pair[1:2])
    cells[...] = jnp.where(flags[1] == 0, low, high)


def lists_kernel(flags, lists, cells, spot, pick, at, obs):
    size, n = spot.shape
    depth = at.shape[1]
    subs, steps = lists.shape[0], obs.shape[1]
    cell = cells[...]
    along = jnp.floor((cell + 0.5) * (1.0 / depth))
    place = along.astype(jnp.int32)
    place = jnp.where(place < 0, -1, place_of(
        flags, size, jnp.right_shift(place, 3), jnp.bitwise_and(place, COLS - 1)))
    same = lax.broadcasted_iota(jnp.int32, (n, n), 0) == lax.broadcasted_iota(jnp.int32, (n, n), 1)

    def column(row):
        return jnp.sum(jnp.where(same, row, 0.0), axis=1, keepdims=True).astype(jnp.int32)

    hot = lax.broadcasted_iota(jnp.int32, (size, n), 0) == place
    spot[...] = hot.astype(F32).astype(BF16)
    hot = lax.broadcasted_iota(jnp.int32, (n, size), 1) == column(place.astype(F32))
    pick[...] = hot.astype(F32).astype(BF16)
    hot = lax.broadcasted_iota(jnp.int32, (n, depth), 1) == column(cell - along * depth)
    at[...] = hot.astype(F32)
    traces = lists[...].reshape(subs * steps, 128).T[0:CAP]
    for s in range(subs):
        obs[s * CAP : s * CAP + CAP, :] = traces[:, s * steps : s * steps + steps]


def injection(t, state, spot, pick, at, obs):
    high, low = split(state[...])
    seen = at[...] * (mm(pick[...], high) + mm(pick[...], low))
    residual = jnp.sum(seen, axis=1, keepdims=True) - obs[:, t : t + 1]
    high, low = split(at[...] * residual)
    return mm(spot[...], high) + mm(spot[...], low)


def adjoint_inner_kernel(t, flags, cur, prev, k0, ki, kx, kz, cm, near, deep, state, spot, pick,
                         at, obs, *rest):
    if len(rest) == 4:
        change, image, part, image_out = rest
        image_out[...] = cur[...] * change[...] + image[...]
    else:
        now, mid, before, part, image_out = rest
        image_out[...] = cur[...] * ((now[...] - mid[...]) - (mid[...] - before[...]))
    inj = injection(t, state, spot, pick, at, obs)
    inner(cur, prev, k0, ki, kx, kz, cm, near, deep, inj, part)


def adjoint_first_kernel(flags, cur, prev, k0, ki, kx, kz, cm, near, deep, part):
    inner(cur, prev, k0, ki, kx, kz, cm.at[1], near, deep, None, part)


def turn_kernel(t, flags, part, k0, ki, kx, zm, ym, side, edge, u_part, u_zm, u_ym, spot, pick, at, obs, new, u_new, zo, co, yo):
    outer(flags, part, k0, ki, kx, zm, ym, side, edge, new)
    outer(flags, u_part, k0, ki, kx, u_zm.at[1], u_ym.at[1], side, edge, u_new)
    u_new[...] += injection(t, new, spot, pick, at, obs)
    rims(flags, u_new, zo, co, yo)


def last_kernel(scale, flags, part, k0, ki, kx, zm, ym, side, edge, image, change, vel,
                prev, states, mine, other):
    new = states.at[1]
    outer(flags, part, k0, ki, kx, zm, ym, side, edge, new)
    raw = from_halves(flags, (image[...] + new[...] * change[...]) * scale / vel[...])
    new[...] = from_halves(flags, new[...])
    states[0] = from_halves(flags, prev[...])
    count, height, lanes = mine.shape
    chunk = raw.shape[1] // (2 * count)
    for n in range(count):
        even, odd = (
            jnp.concatenate(
                [raw[g * height : g * height + height, m * chunk : m * chunk + chunk]
                 for g in range(lanes // chunk)], axis=1)
            for m in (2 * n, 2 * n + 1))
        mine[n] = jnp.where(flags[0] == 0, even, odd)
        other[n] = jnp.where(flags[0] == 0, odd, even)


def join_kernel(flags, mine, got, *outs):
    for s, out in enumerate(outs):
        to = jnp.bitwise_xor(flags[3], s)
        a, b = mine[to], got[to]
        out[0] = jnp.where(flags[0] == 0, a, b)
        out[1] = jnp.where(flags[0] == 0, b, a)


def filter_kernel(flags, *refs):
    *pieces, out = refs
    pieces = pieces[::-1]
    height, lanes = pieces[0].shape[1:]
    chunk, rows, full = out.shape
    groups = lanes // chunk
    q = flags[3]
    shape = (full, full)
    y = lax.broadcasted_iota(jnp.int32, shape, 1)
    at = lax.broadcasted_iota(jnp.int32, shape, 0)
    within = jnp.bitwise_and(at, 2 * COLS - 1)
    place = jnp.bitwise_xor(q * (2 * COLS), at - within) + within
    weights = jnp.exp(jnp.abs(y - place).astype(F32) * (-1.0 / SMOOTH))
    weights = split(weights / jnp.sum(weights, axis=0, keepdims=True))
    ready = []
    for n in range(height // COLS):
        here = slice(n * COLS, n * COLS + COLS)
        lines = jnp.concatenate([piece[b, here, :] for piece in pieces for b in range(2)], axis=0)
        high, low = split(lines.T)
        done = mm(high, weights[0]) + mm(low, weights[0]) + mm(high, weights[1])
        ready.append(done)
    for g in range(groups):
        lines = jnp.stack([done[g * chunk : g * chunk + chunk] for done in ready], axis=0)
        out[:, g * (rows // groups) : (g + 1) * (rows // groups), :] = jnp.swapaxes(lines, 0, 1)


def shaped(*shape):
    return jax.ShapeDtypeStruct(shape, F32)


class Flags:
    def __getitem__(self, n):
        if n == 0:
            return lax.axis_index("inline")
        xline = lax.axis_index("xline")
        if n == 1:
            return jnp.bitwise_and(xline, 1)
        if n == 3:
            return jnp.right_shift(xline, 1)
        place = 2 * xline + lax.axis_index("inline")
        return jnp.bitwise_and(jnp.right_shift(place, n - 4), 1)


def call(kernel, name, outs, *args, weight=0, far=0, scalars=0, scratch=()):
    specs = [pl.BlockSpec(memory_space=pltpu.SMEM)] * scalars
    specs += [pl.BlockSpec(memory_space=pl.ANY)] * far
    specs += [pl.BlockSpec(memory_space=pltpu.VMEM)] * (len(args) - scalars - far)
    return pl.pallas_call(
        functools.partial(kernel, Flags()),
        name=name,
        out_shape=outs,
        in_specs=specs,
        out_specs=[pl.BlockSpec(memory_space=pltpu.VMEM)] * len(outs),
        scratch_shapes=list(scratch) + ([pltpu.SemaphoreType.DMA((far,))] if far else []),
        compiler_params=pltpu.CompilerParams(vmem_limit_bytes=VMEM_BYTES),
        cost_estimate=pl.CostEstimate(
            flops=1000, bytes_accessed=1000 + int(weight * 3_600_000), transcendentals=0),
    )(*args)


def per_device(plan, fwd_now, fwd_before, adj_now, adj_before, velocity, log_density, observed,
               rec_cells, rec_counts, src_cell, wavelet):
    rows, cols, depth = fwd_now.shape
    size = rows * cols
    steps = wavelet.shape[0]
    nx, nq = plan.nx, plan.nq
    subs = 2 * nx
    xline, c = lax.axis_index("xline"), lax.axis_index("inline")
    q, y = xline // 2, xline % 2
    keep = y == c
    z_perm, c_perm, y_perm, swap_perm = plan.z(), plan.core(), plan.y(), plan.swap()
    stages = [(c_perm, c), (y_perm, y)]
    stages += [(plan.flip(1 << b), (q >> b) & 1) for b in range((nq - 1).bit_length())]
    field = shaped(size, depth)
    rim = [shaped(size // 2, depth), shaped(size // 2, depth), shaped(4 * cols, depth)]

    deep = depth_matrix(depth)
    deep = jnp.asarray(np.concatenate([deep, deep]), BF16)
    inside = jnp.where(c == 0, q > 0, q < nq - 1)
    near = [near_matrix(GROUP, cols, k) for k in range(2)]
    wide = (GROUP + 8) * cols
    near = [np.concatenate([m[:, :wide], m[:, :wide], m[:, wide:], m[:, wide:]], axis=1) for m in near]
    near = jnp.where(c == 0, jnp.asarray(near[0], F32), jnp.asarray(near[1], F32)).astype(BF16)
    side = [side_matrix(rows, k) for k in range(2)]
    side = jnp.where(c == 0, jnp.asarray(side[0], BF16), jnp.asarray(side[1], BF16))
    side = jnp.where(inside, side, jnp.zeros_like(side))
    side = jnp.concatenate([side, side], axis=1)
    edge = [edge_matrix(k) for k in range(2)]
    edge = jnp.where(y == 0, jnp.asarray(edge[0], F32), jnp.asarray(edge[1], F32)).astype(BF16)
    edge = jnp.concatenate([edge, edge], axis=1)

    def halo(zo, co, yo):
        return send(zo, z_perm), send(co, c_perm), send(yo, y_perm)

    def after(value, *deps):
        return lax.optimization_barrier((value,) + deps)[0]

    def flat(value):
        return value.reshape(size, depth)

    log_density, fwd_now, velocity = flat(log_density), flat(fwd_now), flat(velocity)
    fwd_before, adj_now, adj_before = flat(fwd_before), flat(adj_now), flat(adj_before)
    got_density = send(log_density, swap_perm)
    stacked = jnp.stack([velocity, fwd_before])
    got_now = send(after(fwd_now, stacked), swap_perm)
    got_model = send(stacked, swap_perm)
    full = nx * cols
    inj, = call(functools.partial(source_kernel, 0, full), "source", [field], src_cell, wavelet,
                weight=0.7, scalars=2)
    got_density, inj = lax.optimization_barrier((got_density, inj))
    density, *out = call(settle_kernel, "settle_density", [field] + rim, log_density, got_density,
                         weight=0.2, far=1)
    lr_zm, lr_cm, lr_ym = halo(*out)
    p_now, *out = call(settle_kernel, "settle", [field] + rim, fwd_now, got_now, weight=0.2, far=1)
    zm, cm, ym = halo(*out)
    vel, p_before = call(settle_pair_kernel, "settle_model", [field, field],
                         velocity, fwd_before, got_model, weight=0.6, far=2)
    parts = call(first_inner_kernel, "first_inner", [field] * 7, density, p_now, lr_cm, cm, near,
                 deep, weight=0.8)
    got_adjoint = [send(after(v, parts[0]), swap_perm) for v in (adj_now, adj_before)]

    slots = subs * CAP
    entries, half_entries = shaped(subs, steps, 128), shaped(subs // 2, steps, 128)
    cells, lists, give = call(
        pack_kernel, "pack", [shaped(1, slots), entries, half_entries], after(rec_counts, density),
        rec_cells, observed, weight=0.2, far=3,
        scratch=[pltpu.VMEM(rec_counts.shape, jnp.int32), pltpu.VMEM(rec_cells.shape, jnp.int32),
                 pltpu.VMEM(observed.shape, F32)])
    riders = subs // 4 * 8 + 8
    core_rim = shaped(size // 2 + riders, depth)
    y_rim = shaped(4 * cols + riders, depth)

    new, zo, co, yo, k0, ki, kx, kz = call(
        first_outer_kernel, "first_outer", [field, rim[0], core_rim, rim[2]] + [field] * 4,
        p_now, p_before, vel, *parts, inj, lr_zm, lr_ym, zm, ym, side, edge, give, cells)
    model = (k0, ki, kx, kz)
    states = [p_before, p_now, new]
    changes = []
    zm, cm, ym = halo(zo, co, yo)
    late = steps - 2 if len(stages) < steps - 1 else steps - 1
    for t in range(1, steps):
        cur, prev, before = states[:-4:-1]
        stage = t - 1 if 2 < t <= min(len(stages), steps - 2) else None
        extra = [lists, send(give, stages[stage][0])] if stage is not None else []
        part, change = call(
            functools.partial(forward_inner_kernel, t, full), "forward_inner", [field, field], src_cell, wavelet, cur, prev, *model, cm, near, deep, before, weight=1.2, scalars=2)
        changes.append(change)
        args = [part, k0, ki, kx, zm, ym, side, edge]
        if t == steps - 3:
            u_part, = call(adjoint_first_kernel, "adjoint_first", [field], u_now, u_before,
                           *model, u_cm, near, deep, weight=1.1)
            args[0] = after(part, u_part)
        if t == late:
            for n in range(steps - 2, len(stages)):
                lists, *give = call(
                    functools.partial(trade_kernel, n), "trade",
                    [entries] + ([half_entries] if n + 1 < len(stages) else []), lists,
                    send(give, stages[n][0]))
                give = give[0] if give else None
            receivers = call(
                lists_kernel, "lists",
                [jax.ShapeDtypeStruct((size, slots), BF16),
                 jax.ShapeDtypeStruct((slots, size), BF16), shaped(slots, depth),
                 shaped(slots, steps)], lists, cells, weight=0.3)
            args[0] = after(part, receivers[0])
        if t == steps - 1:
            new, u_new, *out = call(
                functools.partial(turn_kernel, t), "turn", [field, field] + rim, *args, u_part,
                u_zm, u_ym, *receivers)
            states.append(new)
            break
        if t == 1:
            u_now, u_before = call(settle_pair_kernel, "settle_adjoint", [field, field], adj_now,
                                   adj_before, *got_adjoint, weight=0.6, far=2)
            args[0] = after(part, u_now)
            new, *out, lists, pair = call(
                core_stage_kernel, "forward_outer",
                [field, rim[0], rim[1], y_rim, entries, shaped(2, slots)], *args, lists, cells, cm)
            states.append(new)
            zm, cm, ym = halo(*out)
            continue
        if t == 2:
            new, *out, lists, give, cells = call(
                y_stage_kernel, "forward_outer",
                [field] + [shaped(2, *r.shape) for r in rim] + [entries, half_entries,
                                                                shaped(1, slots)],
                *args, lists, pair, u_now)
            states.append(new)
            zm, cm, ym = halo(*out)
            u_zm, u_cm, u_ym = zm, cm, ym
            continue
        outs = [field] + rim
        if extra:
            outs = outs + [entries] + ([half_entries] if t < len(stages) else [])
        new, *out = call(functools.partial(outer_kernel, stage), "forward_outer", outs,
                         *args, *extra)
        if extra:
            out, (lists, *give) = out[:3], out[3:]
            give = give[0] if give else None
        states.append(new)
        zm, cm, ym = halo(*out)

    zm, cm, ym = halo(*out)
    u_before, u_now = u_now, u_new
    image = []
    chunk = depth // nx
    half = shaped(nq, size * chunk // 128, 128)
    for j in range(1, steps):
        t = steps - 1 - j
        terms = [changes[t + 1], *image] if image else states[:-4:-1]
        part, *image = call(
            functools.partial(adjoint_inner_kernel, t), "adjoint_inner", [field, field], u_now, u_before, *model, cm, near, deep, states[t + 2], *receivers, *terms, weight=1.5)
        args = [part, k0, ki, kx, zm, ym, side, edge]
        if j == steps - 1:
            final, mine, other = call(
                functools.partial(last_kernel, 2.0 / steps), "last",
                [shaped(2, *field.shape), half, half], *args, *image, changes[0], vel, u_now)
            break
        u_before = u_now
        u_now, *out = call(functools.partial(outer_kernel, None), "adjoint_outer", [field] + rim,
                           *args)
        zm, cm, ym = halo(*out)

    got = send(final, swap_perm)
    pieces = call(join_kernel, "join", [shaped(2, *half.shape[1:])] * nq, mine,
                  send(other, c_perm))
    pieces = [send(pieces[s], plan.spread(s)) for s in reversed(range(nq))][::-1]
    adj_prev, adj_out = call(select_kernel, "select", [field, field], final, got, weight=1.2)
    gradient, = call(filter_kernel, "filter", [shaped(chunk, rows, nx * cols)],
                     after(pieces[-1], adj_out), *pieces[-2::-1])
    block = (rows, cols, depth)
    return gradient, adj_out.reshape(block), adj_prev.reshape(block)


def solution(mesh):
    field = P(("shots", "inline"), "xline", None)
    model = P("inline", "xline", None)
    lists = P(("xline", "inline"), None)
    return jax.shard_map(
        functools.partial(per_device, Plan(mesh)),
        mesh=mesh,
        in_specs=(field, field, field, field, model, model, P("shots", ("xline", "inline")),
                  lists, lists, P("shots"), P("shots", None)),
        out_specs=(P(("shots", "xline"), "inline", None), field, field),
        check_vma=False,
    )
```

```python
import functools

import jax
import jax.numpy as jnp
import numpy as np
from jax import lax
from jax.experimental import pallas as pl
from jax.experimental.pallas import tpu as pltpu
from jax.sharding import PartitionSpec as P

CAP = 8
SMOOTH = 16
SECOND = (-205.0 / 72.0, 8.0 / 5.0, -1.0 / 5.0, 8.0 / 315.0, -1.0 / 560.0)
FIRST = (4.0 / 5.0, -1.0 / 5.0, 4.0 / 105.0, -1.0 / 280.0)
ALL = ("shots", "xline", "inline")
COLS = 8
GROUP = 8
VMEM_BYTES = 8 * 1024 * 1024
F32 = jnp.float32
BF16 = jnp.bfloat16


class Plan:
    def __init__(self, mesh):
        self.shots = mesh.shape["shots"]
        self.nx = mesh.shape["xline"]
        self.nq = self.nx // 2

    def index(self, s, q, y, c):
        return (s * self.nx + 2 * q + y) * 2 + c

    def perm(self, partner):
        pairs = []
        for s in range(self.shots):
            for q in range(self.nq):
                for y in range(2):
                    for c in range(2):
                        t = partner(q, y, c)
                        dst = self.index(s ^ 1, q, y, c) if t is None else self.index(s, *t)
                        pairs.append((self.index(s, q, y, c), dst))
        return pairs

    def swap(self):
        return self.perm(lambda q, y, c: None if y == c else (q, c, y))

    def z(self):
        def partner(q, y, c):
            other = q + 1 if c == 1 else q - 1
            return (other, y, 1 - c) if 0 <= other < self.nq else None

        return self.perm(partner)

    def core(self):
        return self.perm(lambda q, y, c: (q, y, 1 - c))

    def y(self):
        return self.perm(lambda q, y, c: (q, 1 - y, c))

    def flip(self, bit):
        return self.perm(lambda q, y, c: (q ^ bit, y, c) if (q ^ bit) < self.nq else None)

    def spread(self, shift):
        return self.perm(lambda q, y, c: (q ^ shift, c, y))


def send(value, pairs):
    return lax.ppermute(value, ALL, pairs)


def depth_matrix(n):
    m = np.zeros((n, 2 * n), np.float32)
    for k in range(1, 5):
        for j in range(n):
            for i, sign in ((j + k, 1.0), (j - k, -1.0)):
                if 0 <= i < n:
                    m[i, j] = round(SECOND[k] * 5040)
                    m[i, n + j] = sign * round(FIRST[k - 1] * 840)
    return m


def stencil_matrix(rows, cols):
    own = (rows + 8) * cols
    m = np.zeros((3, rows, cols, own + rows * 8), np.float32)
    for i in range(rows):
        for x in range(cols):
            for k in range(1, 5):
                total = round(SECOND[k] * 5040)
                slope = round(FIRST[k - 1] * 840)
                for sign in (1, -1):
                    at = (i + 4 + sign * k) * cols + x
                    m[0, i, x, at] += total
                    m[1, i, x, at] += sign * slope
                    to = x + sign * k
                    if to < 0:
                        at = own + i * 4 + to + 4
                    elif to >= cols:
                        at = own + rows * 4 + i * 4 + to - cols
                    else:
                        at = (i + 4) * cols + to
                    m[0, i, x, at] += total
                    m[2, i, x, at] += sign * slope
    return m.reshape(3 * rows * cols, own + rows * 8)


def halved(rows, cols, c):
    at = np.arange(rows)[:, None] * cols
    z_side = (at + 4 * c + np.arange(4)).reshape(-1)
    return np.concatenate([z_side, (at + 4 * (1 - c) + np.arange(4)).reshape(-1)])


def near_matrix(rows, cols, c):
    m = stencil_matrix(rows, cols)
    own = (rows + 8) * cols
    place = halved(rows, cols, c)
    out = np.concatenate([place + k * rows * cols for k in range(3)])
    side = own + (1 - c) * rows * 4 + np.arange(rows * 4)
    return m[out][:, np.concatenate([halved(rows + 8, cols, c), side])]


def side_matrix(rows, c):
    m = np.zeros((2, rows, 4, rows, 4), np.float32)
    for x in range(4):
        for k in range(4):
            d = x + 4 - k if c == 0 else k + 4 - x
            if d <= 4:
                for i in range(rows):
                    m[0, i, x, i, k] = round(SECOND[d] * 5040)
                    m[1, i, x, i, k] = round(FIRST[d - 1] * 840) * (-1 if c == 0 else 1)
    return m.reshape(2 * rows * 4, rows * 4)


def edge_matrix(y):
    m = np.zeros((2, 2, 4, 4, 2, 4, 4), np.float32)
    for i in range(4):
        for k in range(4):
            d = i + 4 - k if y == 1 else k + 4 - i
            if d <= 4:
                for part in range(2):
                    for x in range(4):
                        m[0, part, i, x, part, k, x] = round(SECOND[d] * 5040)
                        m[1, part, i, x, part, k, x] = round(FIRST[d - 1] * 840) * (-1 if y == 1 else 1)
    return m.reshape(64, 32)


def split(value):
    high = value.astype(BF16)
    return high, (value - high.astype(F32)).astype(BF16)


def mm(a, b):
    return jnp.dot(a, b, preferred_element_type=F32)


def inner_differences(cur, cm, near, deep):
    size, depth = cur.shape
    half = size // 2
    cm = cm.at[0] if len(cm.shape) == 3 else cm
    own = split(cur[...])
    along = mm(jnp.concatenate(own, axis=1), deep[...])
    blank = jnp.zeros((16, depth), BF16)
    ext = [[jnp.concatenate([blank, part[h * half : h * half + half], blank], axis=0)
            for h in range(2)] for part in own]
    from_c = split(cm[0:half])
    step = GROUP * 4
    for n in range(half // step):
        rhs = [part[h][n * step : n * step + step + 32] for part in ext for h in range(2)]
        rhs += [part[n * step : n * step + step] for part in from_c]
        out = mm(near[...], jnp.concatenate(rhs, axis=0))
        for h in range(2):
            here = slice(h * half + n * step, h * half + n * step + step)
            sums, di, dx = (out[(2 * k + h) * step : (2 * k + h + 1) * step] for k in range(3))
            yield here, sums, along[here, 0:depth], di, dx, along[here, depth:]


def side_differences(zm, side):
    zm = zm.at[0] if len(zm.shape) == 3 else zm
    out = mm(side[...], jnp.concatenate(split(zm[...]), axis=0))
    half = out.shape[0] // 2
    return out[0:half], out[half:]


def edge_differences(flags, size, ym, edge):
    ym = ym.at[0] if len(ym.shape) == 3 else ym
    out = mm(edge[...], jnp.concatenate(split(ym[0:32]), axis=0))
    start = jnp.where(flags[1] == 1, 0, size // 2 - 16)
    for h in range(2):
        at = pl.ds(pl.multiple_of(start + h * (size // 2), 16), 16)
        yield at, out[h * 16 : h * 16 + 16], out[32 + h * 16 : 48 + h * 16]


def to_halves(flags, value):
    rows, depth = value.shape
    pairs = value.reshape(rows // (2 * COLS), 2, COLS, depth)
    a, b = pairs[:, 0], pairs[:, 1]
    low = lax.broadcasted_iota(jnp.int32, a.shape, 1) < 4
    first = jnp.where(low, a, pltpu.roll(b, 4, axis=1)).reshape(rows // 2, depth)
    last = jnp.where(low, pltpu.roll(a, 4, axis=1), b).reshape(rows // 2, depth)
    return jnp.where(flags[0] == 0, first, last), jnp.where(flags[0] == 0, last, first)


def from_halves(flags, value):
    rows, depth = value.shape
    z_side, c_side = value[0 : rows // 2], value[rows // 2 :]
    shape = (rows // (2 * COLS), COLS, depth)
    first = jnp.where(flags[0] == 0, z_side, c_side).reshape(shape)
    last = jnp.where(flags[0] == 0, c_side, z_side).reshape(shape)
    low = lax.broadcasted_iota(jnp.int32, shape, 1) < 4
    a = jnp.where(low, first, pltpu.roll(last, 4, axis=1))
    b = jnp.where(low, pltpu.roll(first, 4, axis=1), last)
    return jnp.stack([a, b], axis=1).reshape(rows, depth)


def place_of(flags, size, i, x):
    near = x - 4 * flags[0]
    return i * 4 + jnp.where((near >= 0) & (near < 4), near, size // 2 + x - 4 * (1 - flags[0]))


def rims(flags, new, zo, co, yo):
    size = new.shape[0]
    half = size // 2
    zo[...] = new[0:half]
    co[...] = new[half:]
    last = jnp.concatenate([new[half - 16 : half], new[size - 16 :]], axis=0)
    first = jnp.concatenate([new[0:16], new[half : half + 16]], axis=0)
    yo[...] = jnp.where(flags[1] == 0, last, first)


def choose(flags, pairs, sems):
    keep = flags[0] == flags[1]

    @pl.when(keep)
    def _():
        copies = [pltpu.make_async_copy(own, out, sems.at[n])
                  for n, (own, recv, out) in enumerate(pairs)]
        for copy in copies:
            copy.start()
        for copy in copies:
            copy.wait()

    @pl.when(jnp.logical_not(keep))
    def _():
        for own, recv, out in pairs:
            out[...] = recv[...]

    for own, recv, out in pairs:
        half = out.shape[0] // 2
        z_side, c_side = to_halves(flags, out[...])
        out[0:half] = z_side
        out[half:] = c_side


def settle_kernel(flags, a, b, recv_a, recv_b, a_out, b_out, zo, co, yo, sems):
    choose(flags, [(a, recv_a, a_out), (b, recv_b, b_out)], sems)
    for n, out in enumerate((a_out, b_out)):
        rims(flags, out, zo.at[n], co.at[n], yo.at[n])


def settle_pair_kernel(flags, a, b, *rest):
    *recv, a_out, b_out, sems = rest
    recv = recv if len(recv) == 2 else (recv[0].at[0], recv[0].at[1])
    choose(flags, [(a, recv[0], a_out), (b, recv[1], b_out)], sems)


def select_kernel(flags, own, recv, *outs):
    keep = flags[0] == flags[1]
    for n, out in enumerate(outs):
        out[...] = jnp.where(keep, own[n], recv[n])


def first_inner_kernel(flags, lr, cur, cm, near, deep, *outs):
    ri, rx, rz, sums_out, di_out, dx_out, dz_out = outs
    for here, spare, spare_z, di, dx, dz in inner_differences(lr, cm.at[0], near, deep):
        ri[here], rx[here], rz[here] = di, dx, dz
    for here, sums, sums_z, di, dx, dz in inner_differences(cur, cm.at[1], near, deep):
        sums_out[here] = sums + sums_z + (3.0 * SECOND[0] * 5040) * cur[here]
        di_out[here], dx_out[here], dz_out[here] = di, dx, dz


def first_outer_kernel(flags, cur, prev, vel, ri, rx, rz, sums, di, dx, dz, inj, zm, ym, side,
                       edge, give, cells, new, zo, co, yo, k0, ki, kx, kz):
    size = cur.shape[0]
    half = size // 2
    kz[...], ki[...], kx[...] = sums[...], di[...], dx[...]
    k0[...], new[...] = ri[...], rx[...]
    more, more_x = side_differences(zm.at[1], side)
    kz[0:half] += more
    kx[0:half] += more_x
    spare, more_x = side_differences(zm.at[0], side)
    new[0:half] += more_x
    for here, more, more_i in edge_differences(flags, size, ym.at[1], edge):
        kz[here] += more
        ki[here] += more_i
    for here, spare, more_i in edge_differences(flags, size, ym.at[0], edge):
        k0[here] += more_i
    for n in range(4):
        here = slice(n * (size // 4), (n + 1) * (size // 4))
        square = vel[here] * vel[here]
        scaled = square * (1.0 / (840 * 840))
        factor = square * (1.0 / 5040)
        along_i, along_x, along_z = scaled * k0[here], scaled * new[here], scaled * rz[here]
        change = factor * kz[here] - (
            along_i * ki[here] + along_x * kx[here] + along_z * dz[here])
        k0[here], ki[here], kx[here], kz[here] = factor, along_i, along_x, along_z
        center = cur[here]
        new[here] = (center - prev[here]) + (center + (change + inj[here]))
    rims(flags, new, zo, co.at[pl.ds(0, half)], yo)
    load(co, half, lambda n: give[n], give.shape[0], [cells[...]])


def inner(cur, prev, k0, ki, kx, kz, cm, near, deep, inj, out):
    for here, sums, sums_z, di, dx, dz in inner_differences(cur, cm, near, deep):
        center = cur[here]
        change = k0[here] * ((sums + sums_z) + (3.0 * SECOND[0] * 5040) * center)
        change = change - (ki[here] * di + kx[here] * dx + kz[here] * dz)
        if inj is not None:
            change = change + inj[here]
        out[here] = (center - prev[here]) + (center + change)


def outer(flags, part, k0, ki, kx, zm, ym, side, edge, new):
    size = part.shape[0]
    half = size // 2
    sums, dx = side_differences(zm, side)
    new[0:half] = part[0:half] + (k0[0:half] * sums - kx[0:half] * dx)
    new[half:] = part[half:]
    for here, sums, di in edge_differences(flags, size, ym, edge):
        new[here] += k0[here] * sums - ki[here] * di


def other_half(stage, flags, count):
    other = 1 - flags[4 + stage]
    for n in range(count // 2):
        high, low = n >> stage, n & ((1 << stage) - 1)
        yield n, (high << (stage + 1)) + (other << stage) + low


def trade(stage, then, flags, mine, got, out, give=None):
    out[...] = mine[...]
    for n, at in other_half(stage, flags, out.shape[0]):
        out[at] = got(n) if callable(got) else got[n]
    if give is not None:
        for n, at in other_half(then, flags, out.shape[0]):
            give[n] = out[at]


def load(message, rim, entry, count, cells):
    for n in range(count):
        message[rim + n // 2 * 8 : rim + n // 2 * 8 + 8, n % 2 * 128 : n % 2 * 128 + 128] = entry(n)
    at = rim + count // 2 * 8
    wide = message.shape[1]
    for k, row in enumerate(cells):
        for m in range(row.shape[1] // 128):
            lane = k * row.shape[1] + m * 128
            message[at + lane // wide : at + lane // wide + 1, lane % wide : lane % wide + 128] = (
                row[:, m * 128 : m * 128 + 128])


def unload(message, rim, count, rows, slots):
    wide = message.shape[1]
    at = rim + count // 2 * 8

    def entry(n):
        return message[rim + n // 2 * 8 : rim + n // 2 * 8 + 8, n % 2 * 128 : n % 2 * 128 + 128]

    cells = []
    for k in range(rows):
        tiles = []
        for m in range(slots // 128):
            lane = k * slots + m * 128
            tiles.append(message[at + lane // wide : at + lane // wide + 1,
                                 lane % wide : lane % wide + 128])
        cells.append(jnp.concatenate(tiles, axis=1) if len(tiles) > 1 else tiles[0])
    return entry, cells


def trade_kernel(stage, then, flags, mine, got, out, give):
    trade(stage, then, flags, mine, got, out, give)


def source_kernel(step, full, flags, src, wave, out):
    size, depth = out.shape
    count = src.shape[0]
    shift = (depth - 1).bit_length()
    plane = shift + (full - 1).bit_length()
    rows = size // COLS
    lane = lax.broadcasted_iota(jnp.int32, (1, count), 1)
    sub = lax.broadcasted_iota(jnp.int32, (count, 1), 0)
    row = jnp.zeros((1, count), jnp.int32)
    deep = jnp.zeros((count, 1), jnp.int32)
    size_of = jnp.zeros((count, 1), F32)
    for n in range(count):
        cell = src[n]
        i = jnp.right_shift(cell, plane) - flags[1] * rows
        x = jnp.bitwise_and(jnp.right_shift(cell, shift), full - 1)
        x = x - (2 * flags[3] + flags[0]) * COLS
        ok = (i >= 0) & (i < rows) & (x >= 0) & (x < COLS)
        row = jnp.where(lane == n, jnp.where(ok, place_of(flags, size, i, x), -1), row)
        deep = jnp.where(sub == n, jnp.bitwise_and(cell, depth - 1), deep)
        size_of = jnp.where(sub == n, wave[step, n], size_of)
    spot = lax.broadcasted_iota(jnp.int32, (size, count), 0) == row
    spot = spot.astype(F32).astype(BF16)
    high, low = split(jnp.where(
        lax.broadcasted_iota(jnp.int32, (count, depth), 1) == deep, size_of, 0.0))
    out[...] = mm(spot, high) + mm(spot, low)


def forward_inner_kernel(step, full, flags, src, wave, cur, prev, k0, ki, kx, kz, cm, near, deep,
                         before, part, change):
    source_kernel(step, full, flags, src, wave, change)
    inner(cur, prev, k0, ki, kx, kz, cm, near, deep, change, part)
    change[...] = (cur[...] - prev[...]) - (prev[...] - before[...])


def outer_kernel(flags, part, k0, ki, kx, zm, ym, side, edge, new, zo, co, yo):
    outer(flags, part, k0, ki, kx, zm, ym, side, edge, new)
    rims(flags, new, zo, co, yo)


def pack_kernel(stage, flags, counts, cells, traces, cells_out, lists, give, counts_v, cells_v, traces_v,
                sems):
    pairs = ((counts, counts_v), (cells, cells_v), (traces, traces_v))
    copies = [pltpu.make_async_copy(a, b, sems.at[n]) for n, (a, b) in enumerate(pairs)]
    for copy in copies:
        copy.start()
    for copy in copies:
        copy.wait()
    subs, n = counts.shape[1], cells.shape[1]
    shape = (subs, n)
    lane = lax.broadcasted_iota(jnp.int32, shape, 1)
    mine = lane // CAP == lax.broadcasted_iota(jnp.int32, shape, 0)
    live = mm(counts_v[...].astype(F32).astype(BF16), mine.astype(F32).astype(BF16))
    slot = jnp.bitwise_and(lane[0:1], CAP - 1)
    cells_out[...] = jnp.where(slot.astype(F32) < live, cells_v[...].astype(F32), -1.0)
    for m in range(subs):
        q, y, c = m >> 2, (m >> 1) & 1, m & 1
        start = ((2 * q + c) * 2 + y) * CAP
        tile = traces_v[:, start // 128 * 128 : start // 128 * 128 + 128]
        lists[m] = pltpu.roll(tile, (128 - start % 128) % 128, axis=1) if start % 128 else tile
    for n, at in other_half(stage, flags, subs):
        give[n] = lists[at]


def core_stage_kernel(flags, part, k0, ki, kx, zm, ym, side, edge, lists, cells, cm, new, zo, co, yo,
                      lists_out, pair):
    outer(flags, part, k0, ki, kx, zm, ym, side, edge, new)
    count, half = lists.shape[0] // 2, new.shape[0] // 2
    entry, (theirs,) = unload(cm, half, count, 1, cells.shape[1])
    trade(0, None, flags, lists, entry, lists_out)
    mine = cells[...]
    pair[0:1] = jnp.where(flags[0] == 0, mine, theirs)
    pair[1:2] = jnp.where(flags[0] == 0, theirs, mine)
    rims(flags, new, zo, co, yo.at[pl.ds(0, 32)])
    at = [k for n, k in other_half(1, flags, lists.shape[0])]
    load(yo, 32, lambda n: lists_out[at[n]], count, [pair[0:1], pair[1:2]])


def y_stage_kernel(flags, part, k0, ki, kx, zm, ym, side, edge, lists, pair, other, new, zo, co, yo,
                   lists_out, cells):
    outer(flags, part, k0, ki, kx, zm, ym, side, edge, new)
    for n, field in enumerate((new, other)):
        rims(flags, field, zo.at[n], co.at[n], yo.at[n])
    entry, theirs = unload(ym, 32, lists.shape[0] // 2, 2, pair.shape[1])
    trade(1, None, flags, lists, entry, lists_out)
    away = flags[0] != flags[1]
    low = jnp.where(away, theirs[0], pair[0:1])
    high = jnp.where(away, theirs[1], pair[1:2])
    cells[...] = jnp.where(flags[1] == 0, low, high)


def lists_kernel(flags, lists, cells, spot, pick, at, obs):
    size, n = spot.shape
    depth = at.shape[1]
    subs, steps = lists.shape[0], obs.shape[1]
    cell = cells[...]
    along = jnp.floor((cell + 0.5) * (1.0 / depth))
    place = along.astype(jnp.int32)
    place = jnp.where(place < 0, -1, place_of(
        flags, size, jnp.right_shift(place, 3), jnp.bitwise_and(place, COLS - 1)))
    same = lax.broadcasted_iota(jnp.int32, (n, n), 0) == lax.broadcasted_iota(jnp.int32, (n, n), 1)

    def column(row):
        return jnp.sum(jnp.where(same, row, 0.0), axis=1, keepdims=True).astype(jnp.int32)

    hot = lax.broadcasted_iota(jnp.int32, (size, n), 0) == place
    spot[...] = hot.astype(F32).astype(BF16)
    hot = lax.broadcasted_iota(jnp.int32, (n, size), 1) == column(place.astype(F32))
    pick[...] = hot.astype(F32).astype(BF16)
    hot = lax.broadcasted_iota(jnp.int32, (n, depth), 1) == column(cell - along * depth)
    at[...] = hot.astype(F32)
    traces = lists[...].reshape(subs * steps, 128).T[0:CAP]
    for s in range(subs):
        obs[s * CAP : s * CAP + CAP, :] = traces[:, s * steps : s * steps + steps]


def injection(t, state, spot, pick, at, obs):
    high, low = split(state[...])
    seen = at[...] * (mm(pick[...], high) + mm(pick[...], low))
    residual = jnp.sum(seen, axis=1, keepdims=True) - obs[:, t : t + 1]
    high, low = split(at[...] * residual)
    return mm(spot[...], high) + mm(spot[...], low)


def adjoint_inner_kernel(t, flags, cur, prev, k0, ki, kx, kz, cm, near, deep, state, spot, pick,
                         at, obs, *rest):
    if len(rest) == 4:
        change, image, part, image_out = rest
        image_out[...] = cur[...] * change[...] + image[...]
    else:
        now, mid, before, part, image_out = rest
        image_out[...] = cur[...] * ((now[...] - mid[...]) - (mid[...] - before[...]))
    inj = injection(t, state, spot, pick, at, obs)
    inner(cur, prev, k0, ki, kx, kz, cm, near, deep, inj, part)


def adjoint_first_kernel(flags, cur, prev, k0, ki, kx, kz, cm, near, deep, part):
    inner(cur, prev, k0, ki, kx, kz, cm.at[1], near, deep, None, part)


def turn_kernel(t, flags, part, k0, ki, kx, zm, ym, side, edge, u_part, u_zm, u_ym, spot, pick, at, obs, new, u_new, zo, co, yo):
    outer(flags, part, k0, ki, kx, zm, ym, side, edge, new)
    outer(flags, u_part, k0, ki, kx, u_zm.at[1], u_ym.at[1], side, edge, u_new)
    u_new[...] += injection(t, new, spot, pick, at, obs)
    rims(flags, u_new, zo, co, yo)


def last_kernel(scale, flags, part, k0, ki, kx, zm, ym, side, edge, image, change, vel,
                prev, states, mine, other):
    new = states.at[1]
    outer(flags, part, k0, ki, kx, zm, ym, side, edge, new)
    raw = from_halves(flags, (image[...] + new[...] * change[...]) * scale / vel[...])
    new[...] = from_halves(flags, new[...])
    states[0] = from_halves(flags, prev[...])
    count, height, lanes = mine.shape
    chunk = raw.shape[1] // (2 * count)
    for n in range(count):
        even, odd = (
            jnp.concatenate(
                [raw[g * height : g * height + height, m * chunk : m * chunk + chunk]
                 for g in range(lanes // chunk)], axis=1)
            for m in (2 * n, 2 * n + 1))
        mine[n] = jnp.where(flags[0] == 0, even, odd)
        other[n] = jnp.where(flags[0] == 0, odd, even)


def join_kernel(flags, mine, got, *outs):
    for s, out in enumerate(outs):
        to = jnp.bitwise_xor(flags[3], s)
        a, b = mine[to], got[to]
        out[0] = jnp.where(flags[0] == 0, a, b)
        out[1] = jnp.where(flags[0] == 0, b, a)


def filter_kernel(flags, *refs):
    *pieces, out = refs
    pieces = pieces[::-1]
    height, lanes = pieces[0].shape[1:]
    chunk, rows, full = out.shape
    groups = lanes // chunk
    q = flags[3]
    shape = (full, full)
    y = lax.broadcasted_iota(jnp.int32, shape, 1)
    at = lax.broadcasted_iota(jnp.int32, shape, 0)
    within = jnp.bitwise_and(at, 2 * COLS - 1)
    place = jnp.bitwise_xor(q * (2 * COLS), at - within) + within
    weights = jnp.exp(jnp.abs(y - place).astype(F32) * (-1.0 / SMOOTH))
    weights = split(weights / jnp.sum(weights, axis=0, keepdims=True))
    ready = []
    for n in range(height // COLS):
        here = slice(n * COLS, n * COLS + COLS)
        lines = jnp.concatenate([piece[b, here, :] for piece in pieces for b in range(2)], axis=0)
        high, low = split(lines.T)
        done = mm(high, weights[0]) + mm(low, weights[0]) + mm(high, weights[1])
        ready.append(done)
    for g in range(groups):
        lines = jnp.stack([done[g * chunk : g * chunk + chunk] for done in ready], axis=0)
        out[:, g * (rows // groups) : (g + 1) * (rows // groups), :] = jnp.swapaxes(lines, 0, 1)


def shaped(*shape):
    return jax.ShapeDtypeStruct(shape, F32)


class Flags:
    def __getitem__(self, n):
        if n == 0:
            return lax.axis_index("inline")
        xline = lax.axis_index("xline")
        if n == 1:
            return jnp.bitwise_and(xline, 1)
        if n == 3:
            return jnp.right_shift(xline, 1)
        place = 2 * xline + lax.axis_index("inline")
        return jnp.bitwise_and(jnp.right_shift(place, n - 4), 1)


def call(kernel, name, outs, *args, weight=0, far=0, scalars=0, scratch=()):
    specs = [pl.BlockSpec(memory_space=pltpu.SMEM)] * scalars
    specs += [pl.BlockSpec(memory_space=pl.ANY)] * far
    specs += [pl.BlockSpec(memory_space=pltpu.VMEM)] * (len(args) - scalars - far)
    return pl.pallas_call(
        functools.partial(kernel, Flags()),
        name=name,
        out_shape=outs,
        in_specs=specs,
        out_specs=[pl.BlockSpec(memory_space=pltpu.VMEM)] * len(outs),
        scratch_shapes=list(scratch) + ([pltpu.SemaphoreType.DMA((far,))] if far else []),
        compiler_params=pltpu.CompilerParams(vmem_limit_bytes=VMEM_BYTES),
        cost_estimate=pl.CostEstimate(
            flops=1000, bytes_accessed=1000 + int(weight * 3_600_000), transcendentals=0),
    )(*args)


def per_device(plan, fwd_now, fwd_before, adj_now, adj_before, velocity, log_density, observed,
               rec_cells, rec_counts, src_cell, wavelet):
    rows, cols, depth = fwd_now.shape
    size = rows * cols
    steps = wavelet.shape[0]
    nx, nq = plan.nx, plan.nq
    subs = 2 * nx
    xline, c = lax.axis_index("xline"), lax.axis_index("inline")
    q, y = xline // 2, xline % 2
    keep = y == c
    z_perm, c_perm, y_perm, swap_perm = plan.z(), plan.core(), plan.y(), plan.swap()
    stages = [(c_perm, c), (y_perm, y)]
    stages += [(plan.flip(1 << b), (q >> b) & 1) for b in range((nq - 1).bit_length())]
    field = shaped(size, depth)
    rim = [shaped(size // 2, depth), shaped(size // 2, depth), shaped(4 * cols, depth)]

    deep = depth_matrix(depth)
    deep = jnp.asarray(np.concatenate([deep, deep]), BF16)
    inside = jnp.where(c == 0, q > 0, q < nq - 1)
    near = [near_matrix(GROUP, cols, k) for k in range(2)]
    wide = (GROUP + 8) * cols
    near = [np.concatenate([m[:, :wide], m[:, :wide], m[:, wide:], m[:, wide:]], axis=1) for m in near]
    near = jnp.where(c == 0, jnp.asarray(near[0], F32), jnp.asarray(near[1], F32)).astype(BF16)
    side = [side_matrix(rows, k) for k in range(2)]
    side = jnp.where(c == 0, jnp.asarray(side[0], BF16), jnp.asarray(side[1], BF16))
    side = jnp.where(inside, side, jnp.zeros_like(side))
    side = jnp.concatenate([side, side], axis=1)
    edge = [edge_matrix(k) for k in range(2)]
    edge = jnp.where(y == 0, jnp.asarray(edge[0], F32), jnp.asarray(edge[1], F32)).astype(BF16)
    edge = jnp.concatenate([edge, edge], axis=1)

    def halo(zo, co, yo):
        return send(zo, z_perm), send(co, c_perm), send(yo, y_perm)

    def after(value, *deps):
        return lax.optimization_barrier((value,) + deps)[0]

    def flat(value):
        return value.reshape(size, depth)

    log_density, fwd_now, velocity = flat(log_density), flat(fwd_now), flat(velocity)
    fwd_before, adj_now, adj_before = flat(fwd_before), flat(adj_now), flat(adj_before)
    got = [send(v, swap_perm) for v in (log_density, fwd_now)]
    stacked = jnp.stack([velocity, fwd_before])
    got_model = send(stacked, swap_perm)
    full = nx * cols
    inj, = call(functools.partial(source_kernel, 0, full), "source", [field], src_cell, wavelet,
                weight=0.7, scalars=2)
    got[0], inj = lax.optimization_barrier((got[0], inj))
    slots = subs * CAP
    entries, half_entries = shaped(subs, steps, 128), shaped(subs // 2, steps, 128)
    order = [*range(2, len(stages)), 0]
    cells, lists, give = call(
        functools.partial(pack_kernel, order[0]), "pack", [shaped(1, slots), entries, half_entries], after(rec_counts, stacked),
        rec_cells, observed, weight=0.2, far=3,
        scratch=[pltpu.VMEM(rec_counts.shape, jnp.int32), pltpu.VMEM(rec_cells.shape, jnp.int32),
                 pltpu.VMEM(observed.shape, F32)])
    for n, bit in enumerate(order[:-1]):
        lists, give = call(
            functools.partial(trade_kernel, bit, order[n + 1]), "trade", [entries, half_entries],
            lists, send(give, stages[bit][0]), weight=0.1)
        if n == 0:
            got[0], give = lax.optimization_barrier((got[0], give))

    density, p_now, *out = call(settle_kernel, "settle",
                                [field, field] + [shaped(2, *r.shape) for r in rim],
                                log_density, fwd_now, *got, far=2)
    zm, cm, ym = halo(*out)
    vel, p_before = call(settle_pair_kernel, "settle_model", [field, field],
                         velocity, fwd_before, got_model, weight=0.6, far=2)
    parts = call(first_inner_kernel, "first_inner", [field] * 7, density, p_now, cm,
                 near, deep, weight=1.3)
    got_adjoint = [send(after(v, parts[0]), swap_perm) for v in (adj_now, adj_before)]

    riders = subs // 4 * 8 + 8
    core_rim = shaped(size // 2 + riders, depth)
    y_rim = shaped(4 * cols + riders, depth)

    new, zo, co, yo, k0, ki, kx, kz = call(
        first_outer_kernel, "first_outer", [field, rim[0], core_rim, rim[2]] + [field] * 4,
        p_now, p_before, vel, *parts, inj, zm, ym, side, edge, give, cells)
    model = (k0, ki, kx, kz)
    states = [p_before, p_now, new]
    changes = []
    zm, cm, ym = halo(zo, co, yo)
    for t in range(1, steps):
        cur, prev, before = states[:-4:-1]
        part, change = call(
            functools.partial(forward_inner_kernel, t, full), "forward_inner", [field, field], src_cell, wavelet, cur, prev, *model, cm, near, deep, before, weight=1.2, scalars=2)
        changes.append(change)
        args = [part, k0, ki, kx, zm, ym, side, edge]
        if t == steps - 3:
            u_part, = call(adjoint_first_kernel, "adjoint_first", [field], u_now, u_before,
                           *model, u_cm, near, deep, weight=1.1)
            args[0] = after(part, u_part)
        if t == steps - 2:
            receivers = call(
                lists_kernel, "lists",
                [jax.ShapeDtypeStruct((size, slots), BF16),
                 jax.ShapeDtypeStruct((slots, size), BF16), shaped(slots, depth),
                 shaped(slots, steps)], lists, cells, weight=0.3)
            args[0] = after(part, receivers[0])
        if t == steps - 1:
            new, u_new, *out = call(
                functools.partial(turn_kernel, t), "turn", [field, field] + rim, *args, u_part,
                u_zm, u_ym, *receivers)
            states.append(new)
            break
        if t == 1:
            u_now, u_before = call(settle_pair_kernel, "settle_adjoint", [field, field], adj_now,
                                   adj_before, *got_adjoint, weight=0.6, far=2)
            args[0] = after(part, u_now)
            new, *out, lists, pair = call(
                core_stage_kernel, "forward_outer",
                [field, rim[0], rim[1], y_rim, entries, shaped(2, slots)], *args, lists, cells, cm)
            states.append(new)
            zm, cm, ym = halo(*out)
            continue
        if t == 2:
            new, *out, lists, cells = call(
                y_stage_kernel, "forward_outer",
                [field] + [shaped(2, *r.shape) for r in rim] + [entries, shaped(1, slots)],
                *args, lists, pair, u_now)
            states.append(new)
            zm, cm, ym = halo(*out)
            u_zm, u_cm, u_ym = zm, cm, ym
            continue
        new, *out = call(outer_kernel, "forward_outer", [field] + rim, *args)
        states.append(new)
        zm, cm, ym = halo(*out)

    zm, cm, ym = halo(*out)
    u_before, u_now = u_now, u_new
    image = []
    chunk = depth // nx
    half = shaped(nq, size * chunk // 128, 128)
    for j in range(1, steps):
        t = steps - 1 - j
        terms = [changes[t + 1], *image] if image else states[:-4:-1]
        part, *image = call(
            functools.partial(adjoint_inner_kernel, t), "adjoint_inner", [field, field], u_now, u_before, *model, cm, near, deep, states[t + 2], *receivers, *terms, weight=1.5)
        args = [part, k0, ki, kx, zm, ym, side, edge]
        if j == steps - 1:
            final, mine, other = call(
                functools.partial(last_kernel, 2.0 / steps), "last",
                [shaped(2, *field.shape), half, half], *args, *image, changes[0], vel, u_now)
            break
        u_before = u_now
        u_now, *out = call(outer_kernel, "adjoint_outer", [field] + rim,
                           *args)
        zm, cm, ym = halo(*out)

    got = send(final, swap_perm)
    pieces = call(join_kernel, "join", [shaped(2, *half.shape[1:])] * nq, mine,
                  send(other, c_perm))
    pieces = [send(pieces[s], plan.spread(s)) for s in reversed(range(nq))][::-1]
    adj_prev, adj_out = call(select_kernel, "select", [field, field], final, got, weight=1.2)
    gradient, = call(filter_kernel, "filter", [shaped(chunk, rows, nx * cols)],
                     after(pieces[-1], adj_out), *pieces[-2::-1])
    block = (rows, cols, depth)
    return gradient, adj_out.reshape(block), adj_prev.reshape(block)


def solution(mesh):
    field = P(("shots", "inline"), "xline", None)
    model = P("inline", "xline", None)
    lists = P(("xline", "inline"), None)
    return jax.shard_map(
        functools.partial(per_device, Plan(mesh)),
        mesh=mesh,
        in_specs=(field, field, field, field, model, model, P("shots", ("xline", "inline")),
                  lists, lists, P("shots"), P("shots", None)),
        out_specs=(P(("shots", "xline"), "inline", None), field, field),
        check_vma=False,
    )
```

```python
import functools

import jax
import jax.numpy as jnp
import numpy as np
from jax import lax
from jax.experimental import pallas as pl
from jax.experimental.pallas import tpu as pltpu
from jax.sharding import PartitionSpec as P

CAP = 8
SMOOTH = 16
SECOND = (-205.0 / 72.0, 8.0 / 5.0, -1.0 / 5.0, 8.0 / 315.0, -1.0 / 560.0)
FIRST = (4.0 / 5.0, -1.0 / 5.0, 4.0 / 105.0, -1.0 / 280.0)
ALL = ("shots", "xline", "inline")
COLS = 8
GROUP = 8
VMEM_BYTES = 8 * 1024 * 1024
F32 = jnp.float32
BF16 = jnp.bfloat16


class Plan:
    def __init__(self, mesh):
        self.shots = mesh.shape["shots"]
        self.nx = mesh.shape["xline"]
        self.nq = self.nx // 2

    def index(self, s, q, y, c):
        return (s * self.nx + 2 * q + y) * 2 + c

    def perm(self, partner):
        pairs = []
        for s in range(self.shots):
            for q in range(self.nq):
                for y in range(2):
                    for c in range(2):
                        t = partner(q, y, c)
                        dst = self.index(s ^ 1, q, y, c) if t is None else self.index(s, *t)
                        pairs.append((self.index(s, q, y, c), dst))
        return pairs

    def swap(self):
        return self.perm(lambda q, y, c: None if y == c else (q, c, y))

    def z(self):
        def partner(q, y, c):
            other = q + 1 if c == 1 else q - 1
            return (other, y, 1 - c) if 0 <= other < self.nq else None

        return self.perm(partner)

    def core(self):
        return self.perm(lambda q, y, c: (q, y, 1 - c))

    def y(self):
        return self.perm(lambda q, y, c: (q, 1 - y, c))

    def flip(self, bit):
        return self.perm(lambda q, y, c: (q ^ bit, y, c) if (q ^ bit) < self.nq else None)

    def spread(self, shift):
        return self.perm(lambda q, y, c: (q ^ shift, c, y))


def send(value, pairs):
    return lax.ppermute(value, ALL, pairs)


def depth_matrix(n):
    m = np.zeros((n, 2 * n), np.float32)
    for k in range(1, 5):
        for j in range(n):
            for i, sign in ((j + k, 1.0), (j - k, -1.0)):
                if 0 <= i < n:
                    m[i, j] = round(SECOND[k] * 5040)
                    m[i, n + j] = sign * round(FIRST[k - 1] * 840)
    return m


def stencil_matrix(rows, cols):
    own = (rows + 8) * cols
    m = np.zeros((3, rows, cols, own + rows * 8), np.float32)
    for i in range(rows):
        for x in range(cols):
            for k in range(1, 5):
                total = round(SECOND[k] * 5040)
                slope = round(FIRST[k - 1] * 840)
                for sign in (1, -1):
                    at = (i + 4 + sign * k) * cols + x
                    m[0, i, x, at] += total
                    m[1, i, x, at] += sign * slope
                    to = x + sign * k
                    if to < 0:
                        at = own + i * 4 + to + 4
                    elif to >= cols:
                        at = own + rows * 4 + i * 4 + to - cols
                    else:
                        at = (i + 4) * cols + to
                    m[0, i, x, at] += total
                    m[2, i, x, at] += sign * slope
    return m.reshape(3 * rows * cols, own + rows * 8)


def halved(rows, cols, c):
    at = np.arange(rows)[:, None] * cols
    z_side = (at + 4 * c + np.arange(4)).reshape(-1)
    return np.concatenate([z_side, (at + 4 * (1 - c) + np.arange(4)).reshape(-1)])


def near_matrix(rows, cols, c):
    m = stencil_matrix(rows, cols)
    own = (rows + 8) * cols
    place = halved(rows, cols, c)
    out = np.concatenate([place + k * rows * cols for k in range(3)])
    side = own + (1 - c) * rows * 4 + np.arange(rows * 4)
    return m[out][:, np.concatenate([halved(rows + 8, cols, c), side])]


def side_matrix(rows, c):
    m = np.zeros((2, rows, 4, rows, 4), np.float32)
    for x in range(4):
        for k in range(4):
            d = x + 4 - k if c == 0 else k + 4 - x
            if d <= 4:
                for i in range(rows):
                    m[0, i, x, i, k] = round(SECOND[d] * 5040)
                    m[1, i, x, i, k] = round(FIRST[d - 1] * 840) * (-1 if c == 0 else 1)
    return m.reshape(2 * rows * 4, rows * 4)


def edge_matrix(y):
    m = np.zeros((2, 2, 4, 4, 2, 4, 4), np.float32)
    for i in range(4):
        for k in range(4):
            d = i + 4 - k if y == 1 else k + 4 - i
            if d <= 4:
                for part in range(2):
                    for x in range(4):
                        m[0, part, i, x, part, k, x] = round(SECOND[d] * 5040)
                        m[1, part, i, x, part, k, x] = round(FIRST[d - 1] * 840) * (-1 if y == 1 else 1)
    return m.reshape(64, 32)


def split(value):
    high = value.astype(BF16)
    return high, (value - high.astype(F32)).astype(BF16)


def mm(a, b):
    return jnp.dot(a, b, preferred_element_type=F32)


def inner_differences(cur, cm, near, deep):
    size, depth = cur.shape
    half = size // 2
    cm = cm.at[0] if len(cm.shape) == 3 else cm
    own = split(cur[...])
    along = mm(jnp.concatenate(own, axis=1), deep[...])
    blank = jnp.zeros((16, depth), BF16)
    ext = [[jnp.concatenate([blank, part[h * half : h * half + half], blank], axis=0)
            for h in range(2)] for part in own]
    from_c = split(cm[0:half])
    step = GROUP * 4
    for n in range(half // step):
        rhs = [part[h][n * step : n * step + step + 32] for part in ext for h in range(2)]
        rhs += [part[n * step : n * step + step] for part in from_c]
        out = mm(near[...], jnp.concatenate(rhs, axis=0))
        for h in range(2):
            here = slice(h * half + n * step, h * half + n * step + step)
            sums, di, dx = (out[(2 * k + h) * step : (2 * k + h + 1) * step] for k in range(3))
            yield here, sums, along[here, 0:depth], di, dx, along[here, depth:]


def side_differences(zm, side):
    zm = zm.at[0] if len(zm.shape) == 3 else zm
    out = mm(side[...], jnp.concatenate(split(zm[...]), axis=0))
    half = out.shape[0] // 2
    return out[0:half], out[half:]


def edge_differences(flags, size, ym, edge):
    ym = ym.at[0] if len(ym.shape) == 3 else ym
    out = mm(edge[...], jnp.concatenate(split(ym[0:32]), axis=0))
    start = jnp.where(flags[1] == 1, 0, size // 2 - 16)
    for h in range(2):
        at = pl.ds(pl.multiple_of(start + h * (size // 2), 16), 16)
        yield at, out[h * 16 : h * 16 + 16], out[32 + h * 16 : 48 + h * 16]


def to_halves(flags, value):
    rows, depth = value.shape
    pairs = value.reshape(rows // (2 * COLS), 2, COLS, depth)
    a, b = pairs[:, 0], pairs[:, 1]
    low = lax.broadcasted_iota(jnp.int32, a.shape, 1) < 4
    first = jnp.where(low, a, pltpu.roll(b, 4, axis=1)).reshape(rows // 2, depth)
    last = jnp.where(low, pltpu.roll(a, 4, axis=1), b).reshape(rows // 2, depth)
    return jnp.where(flags[0] == 0, first, last), jnp.where(flags[0] == 0, last, first)


def from_halves(flags, value):
    rows, depth = value.shape
    z_side, c_side = value[0 : rows // 2], value[rows // 2 :]
    shape = (rows // (2 * COLS), COLS, depth)
    first = jnp.where(flags[0] == 0, z_side, c_side).reshape(shape)
    last = jnp.where(flags[0] == 0, c_side, z_side).reshape(shape)
    low = lax.broadcasted_iota(jnp.int32, shape, 1) < 4
    a = jnp.where(low, first, pltpu.roll(last, 4, axis=1))
    b = jnp.where(low, pltpu.roll(first, 4, axis=1), last)
    return jnp.stack([a, b], axis=1).reshape(rows, depth)


def place_of(flags, size, i, x):
    near = x - 4 * flags[0]
    return i * 4 + jnp.where((near >= 0) & (near < 4), near, size // 2 + x - 4 * (1 - flags[0]))


def rims(flags, new, zo, co, yo):
    size = new.shape[0]
    half = size // 2
    zo[...] = new[0:half]
    co[...] = new[half:]
    last = jnp.concatenate([new[half - 16 : half], new[size - 16 :]], axis=0)
    first = jnp.concatenate([new[0:16], new[half : half + 16]], axis=0)
    yo[...] = jnp.where(flags[1] == 0, last, first)


def choose(flags, pairs, sems):
    keep = flags[0] == flags[1]

    @pl.when(keep)
    def _():
        copies = [pltpu.make_async_copy(own, out, sems.at[n])
                  for n, (own, recv, out) in enumerate(pairs)]
        for copy in copies:
            copy.start()
        for copy in copies:
            copy.wait()

    @pl.when(jnp.logical_not(keep))
    def _():
        for own, recv, out in pairs:
            out[...] = recv[...]

    for own, recv, out in pairs:
        half = out.shape[0] // 2
        z_side, c_side = to_halves(flags, out[...])
        out[0:half] = z_side
        out[half:] = c_side


def settle_kernel(flags, a, b, recv_a, recv_b, a_out, b_out, zo, co, yo, sems):
    choose(flags, [(a, recv_a, a_out), (b, recv_b, b_out)], sems)
    for n, out in enumerate((a_out, b_out)):
        rims(flags, out, zo.at[n], co.at[n], yo.at[n])


def settle_pair_kernel(flags, a, b, *rest):
    *recv, a_out, b_out, sems = rest
    recv = recv if len(recv) == 2 else (recv[0].at[0], recv[0].at[1])
    choose(flags, [(a, recv[0], a_out), (b, recv[1], b_out)], sems)


def gather_kernel(flags, a, b, out, sems):
    copies = [pltpu.make_async_copy(part, out.at[n], sems.at[n]) for n, part in enumerate((a, b))]
    for copy in copies:
        copy.start()
    for copy in copies:
        copy.wait()


def select_kernel(flags, own, recv, *outs):
    keep = flags[0] == flags[1]
    for n, out in enumerate(outs):
        out[...] = jnp.where(keep, own[n], recv[n])


def first_inner_kernel(flags, lr, cur, cm, near, deep, *outs):
    ri, rx, rz, sums_out, di_out, dx_out, dz_out = outs
    for here, spare, spare_z, di, dx, dz in inner_differences(lr, cm.at[0], near, deep):
        ri[here], rx[here], rz[here] = di, dx, dz
    for here, sums, sums_z, di, dx, dz in inner_differences(cur, cm.at[1], near, deep):
        sums_out[here] = sums + sums_z + (3.0 * SECOND[0] * 5040) * cur[here]
        di_out[here], dx_out[here], dz_out[here] = di, dx, dz


def first_outer_kernel(flags, cur, prev, vel, ri, rx, rz, sums, di, dx, dz, inj, zm, ym, side,
                       edge, give, cells, new, zo, co, yo, k0, ki, kx, kz):
    size = cur.shape[0]
    half = size // 2
    kz[...], ki[...], kx[...] = sums[...], di[...], dx[...]
    k0[...], new[...] = ri[...], rx[...]
    more, more_x = side_differences(zm.at[1], side)
    kz[0:half] += more
    kx[0:half] += more_x
    spare, more_x = side_differences(zm.at[0], side)
    new[0:half] += more_x
    for here, more, more_i in edge_differences(flags, size, ym.at[1], edge):
        kz[here] += more
        ki[here] += more_i
    for here, spare, more_i in edge_differences(flags, size, ym.at[0], edge):
        k0[here] += more_i
    for n in range(4):
        here = slice(n * (size // 4), (n + 1) * (size // 4))
        square = vel[here] * vel[here]
        scaled = square * (1.0 / (840 * 840))
        factor = square * (1.0 / 5040)
        along_i, along_x, along_z = scaled * k0[here], scaled * new[here], scaled * rz[here]
        change = factor * kz[here] - (
            along_i * ki[here] + along_x * kx[here] + along_z * dz[here])
        k0[here], ki[here], kx[here], kz[here] = factor, along_i, along_x, along_z
        center = cur[here]
        new[here] = (center - prev[here]) + (center + (change + inj[here]))
    rims(flags, new, zo, co.at[pl.ds(0, half)], yo)
    load(co, half, lambda n: give[n], give.shape[0], [cells[...]])


def inner(cur, prev, k0, ki, kx, kz, cm, near, deep, inj, out):
    for here, sums, sums_z, di, dx, dz in inner_differences(cur, cm, near, deep):
        center = cur[here]
        change = k0[here] * ((sums + sums_z) + (3.0 * SECOND[0] * 5040) * center)
        change = change - (ki[here] * di + kx[here] * dx + kz[here] * dz)
        if inj is not None:
            change = change + inj[here]
        out[here] = (center - prev[here]) + (center + change)


def outer(flags, part, k0, ki, kx, zm, ym, side, edge, new):
    size = part.shape[0]
    half = size // 2
    sums, dx = side_differences(zm, side)
    new[0:half] = part[0:half] + (k0[0:half] * sums - kx[0:half] * dx)
    new[half:] = part[half:]
    for here, sums, di in edge_differences(flags, size, ym, edge):
        new[here] += k0[here] * sums - ki[here] * di


def other_half(stage, flags, count):
    other = 1 - flags[4 + stage]
    for n in range(count // 2):
        high, low = n >> stage, n & ((1 << stage) - 1)
        yield n, (high << (stage + 1)) + (other << stage) + low


def trade(stage, then, flags, mine, got, out, give=None):
    out[...] = mine[...]
    for n, at in other_half(stage, flags, out.shape[0]):
        out[at] = got(n) if callable(got) else got[n]
    if give is not None:
        for n, at in other_half(then, flags, out.shape[0]):
            give[n] = out[at]


def load(message, rim, entry, count, cells):
    for n in range(count):
        message[rim + n // 2 * 8 : rim + n // 2 * 8 + 8, n % 2 * 128 : n % 2 * 128 + 128] = entry(n)
    at = rim + count // 2 * 8
    wide = message.shape[1]
    for k, row in enumerate(cells):
        for m in range(row.shape[1] // 128):
            lane = k * row.shape[1] + m * 128
            message[at + lane // wide : at + lane // wide + 1, lane % wide : lane % wide + 128] = (
                row[:, m * 128 : m * 128 + 128])


def unload(message, rim, count, rows, slots):
    wide = message.shape[1]
    at = rim + count // 2 * 8

    def entry(n):
        return message[rim + n // 2 * 8 : rim + n // 2 * 8 + 8, n % 2 * 128 : n % 2 * 128 + 128]

    cells = []
    for k in range(rows):
        tiles = []
        for m in range(slots // 128):
            lane = k * slots + m * 128
            tiles.append(message[at + lane // wide : at + lane // wide + 1,
                                 lane % wide : lane % wide + 128])
        cells.append(jnp.concatenate(tiles, axis=1) if len(tiles) > 1 else tiles[0])
    return entry, cells


def trade_kernel(stage, then, flags, mine, got, out, give):
    trade(stage, then, flags, mine, got, out, give)


def source_kernel(step, full, flags, src, wave, out):
    size, depth = out.shape
    count = src.shape[0]
    shift = (depth - 1).bit_length()
    plane = shift + (full - 1).bit_length()
    rows = size // COLS
    lane = lax.broadcasted_iota(jnp.int32, (1, count), 1)
    sub = lax.broadcasted_iota(jnp.int32, (count, 1), 0)
    row = jnp.zeros((1, count), jnp.int32)
    deep = jnp.zeros((count, 1), jnp.int32)
    size_of = jnp.zeros((count, 1), F32)
    for n in range(count):
        cell = src[n]
        i = jnp.right_shift(cell, plane) - flags[1] * rows
        x = jnp.bitwise_and(jnp.right_shift(cell, shift), full - 1)
        x = x - (2 * flags[3] + flags[0]) * COLS
        ok = (i >= 0) & (i < rows) & (x >= 0) & (x < COLS)
        row = jnp.where(lane == n, jnp.where(ok, place_of(flags, size, i, x), -1), row)
        deep = jnp.where(sub == n, jnp.bitwise_and(cell, depth - 1), deep)
        size_of = jnp.where(sub == n, wave[step, n], size_of)
    spot = lax.broadcasted_iota(jnp.int32, (size, count), 0) == row
    spot = spot.astype(F32).astype(BF16)
    high, low = split(jnp.where(
        lax.broadcasted_iota(jnp.int32, (count, depth), 1) == deep, size_of, 0.0))
    out[...] = mm(spot, high) + mm(spot, low)


def forward_inner_kernel(step, full, flags, src, wave, cur, prev, k0, ki, kx, kz, cm, near, deep,
                         before, part, change):
    source_kernel(step, full, flags, src, wave, change)
    inner(cur, prev, k0, ki, kx, kz, cm, near, deep, change, part)
    change[...] = (cur[...] - prev[...]) - (prev[...] - before[...])


def outer_kernel(flags, part, k0, ki, kx, zm, ym, side, edge, new, zo, co, yo):
    outer(flags, part, k0, ki, kx, zm, ym, side, edge, new)
    rims(flags, new, zo, co, yo)


def pack_kernel(stage, flags, counts, cells, traces, cells_out, lists, give, counts_v, cells_v, traces_v,
                sems):
    pairs = ((counts, counts_v), (cells, cells_v), (traces, traces_v))
    copies = [pltpu.make_async_copy(a, b, sems.at[n]) for n, (a, b) in enumerate(pairs)]
    for copy in copies:
        copy.start()
    for copy in copies:
        copy.wait()
    subs, n = counts.shape[1], cells.shape[1]
    shape = (subs, n)
    lane = lax.broadcasted_iota(jnp.int32, shape, 1)
    mine = lane // CAP == lax.broadcasted_iota(jnp.int32, shape, 0)
    live = mm(counts_v[...].astype(F32).astype(BF16), mine.astype(F32).astype(BF16))
    slot = jnp.bitwise_and(lane[0:1], CAP - 1)
    cells_out[...] = jnp.where(slot.astype(F32) < live, cells_v[...].astype(F32), -1.0)
    for m in range(subs):
        q, y, c = m >> 2, (m >> 1) & 1, m & 1
        start = ((2 * q + c) * 2 + y) * CAP
        tile = traces_v[:, start // 128 * 128 : start // 128 * 128 + 128]
        lists[m] = pltpu.roll(tile, (128 - start % 128) % 128, axis=1) if start % 128 else tile
    for n, at in other_half(stage, flags, subs):
        give[n] = lists[at]


def core_stage_kernel(flags, part, k0, ki, kx, zm, ym, side, edge, lists, cells, cm, new, zo, co, yo,
                      lists_out, pair):
    outer(flags, part, k0, ki, kx, zm, ym, side, edge, new)
    count, half = lists.shape[0] // 2, new.shape[0] // 2
    entry, (theirs,) = unload(cm, half, count, 1, cells.shape[1])
    trade(0, None, flags, lists, entry, lists_out)
    mine = cells[...]
    pair[0:1] = jnp.where(flags[0] == 0, mine, theirs)
    pair[1:2] = jnp.where(flags[0] == 0, theirs, mine)
    rims(flags, new, zo, co, yo.at[pl.ds(0, 32)])
    at = [k for n, k in other_half(1, flags, lists.shape[0])]
    load(yo, 32, lambda n: lists_out[at[n]], count, [pair[0:1], pair[1:2]])


def y_stage_kernel(flags, part, k0, ki, kx, zm, ym, side, edge, lists, pair, other, new, zo, co, yo,
                   lists_out, cells):
    outer(flags, part, k0, ki, kx, zm, ym, side, edge, new)
    for n, field in enumerate((new, other)):
        rims(flags, field, zo.at[n], co.at[n], yo.at[n])
    entry, theirs = unload(ym, 32, lists.shape[0] // 2, 2, pair.shape[1])
    trade(1, None, flags, lists, entry, lists_out)
    away = flags[0] != flags[1]
    low = jnp.where(away, theirs[0], pair[0:1])
    high = jnp.where(away, theirs[1], pair[1:2])
    cells[...] = jnp.where(flags[1] == 0, low, high)


def lists_kernel(flags, lists, cells, spot, pick, at, obs):
    size, n = spot.shape
    depth = at.shape[1]
    subs, steps = lists.shape[0], obs.shape[1]
    cell = cells[...]
    along = jnp.floor((cell + 0.5) * (1.0 / depth))
    place = along.astype(jnp.int32)
    place = jnp.where(place < 0, -1, place_of(
        flags, size, jnp.right_shift(place, 3), jnp.bitwise_and(place, COLS - 1)))
    same = lax.broadcasted_iota(jnp.int32, (n, n), 0) == lax.broadcasted_iota(jnp.int32, (n, n), 1)

    def column(row):
        return jnp.sum(jnp.where(same, row, 0.0), axis=1, keepdims=True).astype(jnp.int32)

    hot = lax.broadcasted_iota(jnp.int32, (size, n), 0) == place
    spot[...] = hot.astype(F32).astype(BF16)
    hot = lax.broadcasted_iota(jnp.int32, (n, size), 1) == column(place.astype(F32))
    pick[...] = hot.astype(F32).astype(BF16)
    hot = lax.broadcasted_iota(jnp.int32, (n, depth), 1) == column(cell - along * depth)
    at[...] = hot.astype(F32)
    traces = lists[...].reshape(subs * steps, 128).T[0:CAP]
    for s in range(subs):
        obs[s * CAP : s * CAP + CAP, :] = traces[:, s * steps : s * steps + steps]


def injection(t, state, spot, pick, at, obs):
    high, low = split(state[...])
    seen = at[...] * (mm(pick[...], high) + mm(pick[...], low))
    residual = jnp.sum(seen, axis=1, keepdims=True) - obs[:, t : t + 1]
    high, low = split(at[...] * residual)
    return mm(spot[...], high) + mm(spot[...], low)


def adjoint_inner_kernel(t, flags, cur, prev, k0, ki, kx, kz, cm, near, deep, state, spot, pick,
                         at, obs, *rest):
    if len(rest) == 4:
        change, image, part, image_out = rest
        image_out[...] = cur[...] * change[...] + image[...]
    else:
        now, mid, before, part, image_out = rest
        image_out[...] = cur[...] * ((now[...] - mid[...]) - (mid[...] - before[...]))
    inj = injection(t, state, spot, pick, at, obs)
    inner(cur, prev, k0, ki, kx, kz, cm, near, deep, inj, part)


def adjoint_first_kernel(flags, cur, prev, k0, ki, kx, kz, cm, near, deep, part):
    inner(cur, prev, k0, ki, kx, kz, cm.at[1], near, deep, None, part)


def turn_kernel(t, flags, part, k0, ki, kx, zm, ym, side, edge, u_part, u_zm, u_ym, spot, pick, at, obs, new, u_new, zo, co, yo):
    outer(flags, part, k0, ki, kx, zm, ym, side, edge, new)
    outer(flags, u_part, k0, ki, kx, u_zm.at[1], u_ym.at[1], side, edge, u_new)
    u_new[...] += injection(t, new, spot, pick, at, obs)
    rims(flags, u_new, zo, co, yo)


def last_kernel(scale, flags, part, k0, ki, kx, zm, ym, side, edge, image, change, vel,
                prev, states, mine, other):
    new = states.at[1]
    outer(flags, part, k0, ki, kx, zm, ym, side, edge, new)
    raw = from_halves(flags, (image[...] + new[...] * change[...]) * scale / vel[...])
    new[...] = from_halves(flags, new[...])
    states[0] = from_halves(flags, prev[...])
    count, height, lanes = mine.shape
    chunk = raw.shape[1] // (2 * count)
    for n in range(count):
        even, odd = (
            jnp.concatenate(
                [raw[g * height : g * height + height, m * chunk : m * chunk + chunk]
                 for g in range(lanes // chunk)], axis=1)
            for m in (2 * n, 2 * n + 1))
        mine[n] = jnp.where(flags[0] == 0, even, odd)
        other[n] = jnp.where(flags[0] == 0, odd, even)


def join_kernel(flags, mine, got, *outs):
    for s, out in enumerate(outs):
        to = jnp.bitwise_xor(flags[3], s)
        a, b = mine[to], got[to]
        out[0] = jnp.where(flags[0] == 0, a, b)
        out[1] = jnp.where(flags[0] == 0, b, a)


def filter_kernel(flags, *refs):
    *pieces, out = refs
    pieces = pieces[::-1]
    height, lanes = pieces[0].shape[1:]
    chunk, rows, full = out.shape
    groups = lanes // chunk
    q = flags[3]
    shape = (full, full)
    y = lax.broadcasted_iota(jnp.int32, shape, 1)
    at = lax.broadcasted_iota(jnp.int32, shape, 0)
    within = jnp.bitwise_and(at, 2 * COLS - 1)
    place = jnp.bitwise_xor(q * (2 * COLS), at - within) + within
    weights = jnp.exp(jnp.abs(y - place).astype(F32) * (-1.0 / SMOOTH))
    weights = split(weights / jnp.sum(weights, axis=0, keepdims=True))
    ready = []
    for n in range(height // COLS):
        here = slice(n * COLS, n * COLS + COLS)
        lines = jnp.concatenate([piece[b, here, :] for piece in pieces for b in range(2)], axis=0)
        high, low = split(lines.T)
        done = mm(high, weights[0]) + mm(low, weights[0]) + mm(high, weights[1])
        ready.append(done)
    for g in range(groups):
        lines = jnp.stack([done[g * chunk : g * chunk + chunk] for done in ready], axis=0)
        out[:, g * (rows // groups) : (g + 1) * (rows // groups), :] = jnp.swapaxes(lines, 0, 1)


def shaped(*shape):
    return jax.ShapeDtypeStruct(shape, F32)


class Flags:
    def __getitem__(self, n):
        if n == 0:
            return lax.axis_index("inline")
        xline = lax.axis_index("xline")
        if n == 1:
            return jnp.bitwise_and(xline, 1)
        if n == 3:
            return jnp.right_shift(xline, 1)
        place = 2 * xline + lax.axis_index("inline")
        return jnp.bitwise_and(jnp.right_shift(place, n - 4), 1)


def call(kernel, name, outs, *args, weight=0, far=0, scalars=0, scratch=()):
    specs = [pl.BlockSpec(memory_space=pltpu.SMEM)] * scalars
    specs += [pl.BlockSpec(memory_space=pl.ANY)] * far
    specs += [pl.BlockSpec(memory_space=pltpu.VMEM)] * (len(args) - scalars - far)
    return pl.pallas_call(
        functools.partial(kernel, Flags()),
        name=name,
        out_shape=outs,
        in_specs=specs,
        out_specs=[pl.BlockSpec(memory_space=pltpu.VMEM)] * len(outs),
        scratch_shapes=list(scratch) + ([pltpu.SemaphoreType.DMA((far,))] if far else []),
        compiler_params=pltpu.CompilerParams(vmem_limit_bytes=VMEM_BYTES),
        cost_estimate=pl.CostEstimate(
            flops=1000, bytes_accessed=1000 + int(weight * 3_600_000), transcendentals=0),
    )(*args)


def per_device(plan, fwd_now, fwd_before, adj_now, adj_before, velocity, log_density, observed,
               rec_cells, rec_counts, src_cell, wavelet):
    rows, cols, depth = fwd_now.shape
    size = rows * cols
    steps = wavelet.shape[0]
    nx, nq = plan.nx, plan.nq
    subs = 2 * nx
    xline, c = lax.axis_index("xline"), lax.axis_index("inline")
    q, y = xline // 2, xline % 2
    keep = y == c
    z_perm, c_perm, y_perm, swap_perm = plan.z(), plan.core(), plan.y(), plan.swap()
    stages = [(c_perm, c), (y_perm, y)]
    stages += [(plan.flip(1 << b), (q >> b) & 1) for b in range((nq - 1).bit_length())]
    field = shaped(size, depth)
    rim = [shaped(size // 2, depth), shaped(size // 2, depth), shaped(4 * cols, depth)]

    deep = depth_matrix(depth)
    deep = jnp.asarray(np.concatenate([deep, deep]), BF16)
    inside = jnp.where(c == 0, q > 0, q < nq - 1)
    near = [near_matrix(GROUP, cols, k) for k in range(2)]
    wide = (GROUP + 8) * cols
    near = [np.concatenate([m[:, :wide], m[:, :wide], m[:, wide:], m[:, wide:]], axis=1) for m in near]
    near = jnp.where(c == 0, jnp.asarray(near[0], F32), jnp.asarray(near[1], F32)).astype(BF16)
    side = [side_matrix(rows, k) for k in range(2)]
    side = jnp.where(c == 0, jnp.asarray(side[0], BF16), jnp.asarray(side[1], BF16))
    side = jnp.where(inside, side, jnp.zeros_like(side))
    side = jnp.concatenate([side, side], axis=1)
    edge = [edge_matrix(k) for k in range(2)]
    edge = jnp.where(y == 0, jnp.asarray(edge[0], F32), jnp.asarray(edge[1], F32)).astype(BF16)
    edge = jnp.concatenate([edge, edge], axis=1)

    def halo(zo, co, yo):
        return send(zo, z_perm), send(co, c_perm), send(yo, y_perm)

    def after(value, *deps):
        return lax.optimization_barrier((value,) + deps)[0]

    def flat(value):
        return value.reshape(size, depth)

    log_density, fwd_now, velocity = flat(log_density), flat(fwd_now), flat(velocity)
    fwd_before, adj_now, adj_before = flat(fwd_before), flat(adj_now), flat(adj_before)
    got = [send(v, swap_perm) for v in (log_density, fwd_now)]
    stacked = jnp.stack([velocity, fwd_before])
    got_model = send(stacked, swap_perm)
    full = nx * cols
    inj, = call(functools.partial(source_kernel, 0, full), "source", [field], src_cell, wavelet,
                weight=0.7, scalars=2)
    adjoint, = call(gather_kernel, "gather", [shaped(2, *field.shape)], after(adj_now, stacked),
                    adj_before, weight=0.3, far=2)
    got[0], inj, adjoint = lax.optimization_barrier((got[0], inj, adjoint))
    slots = subs * CAP
    entries, half_entries = shaped(subs, steps, 128), shaped(subs // 2, steps, 128)
    order = [*range(2, len(stages)), 0]
    cells, lists, give = call(
        functools.partial(pack_kernel, order[0]), "pack", [shaped(1, slots), entries, half_entries], after(rec_counts, stacked),
        rec_cells, observed, weight=0.2, far=3,
        scratch=[pltpu.VMEM(rec_counts.shape, jnp.int32), pltpu.VMEM(rec_cells.shape, jnp.int32),
                 pltpu.VMEM(observed.shape, F32)])
    for n, bit in enumerate(order[:-1]):
        lists, give = call(
            functools.partial(trade_kernel, bit, order[n + 1]), "trade", [entries, half_entries],
            lists, send(give, stages[bit][0]), weight=0.1)
        if n == 0:
            got[0], give = lax.optimization_barrier((got[0], give))

    density, p_now, *out = call(settle_kernel, "settle",
                                [field, field] + [shaped(2, *r.shape) for r in rim],
                                log_density, fwd_now, *got, far=2)
    zm, cm, ym = halo(*out)
    vel, p_before = call(settle_pair_kernel, "settle_model", [field, field],
                         velocity, fwd_before, got_model, weight=0.6, far=2)
    parts = call(first_inner_kernel, "first_inner", [field] * 7, density, p_now, cm,
                 near, deep, weight=1.3)
    got_adjoint = send(after(adjoint, parts[0]), swap_perm)

    riders = subs // 4 * 8 + 8
    core_rim = shaped(size // 2 + riders, depth)
    y_rim = shaped(4 * cols + riders, depth)

    new, zo, co, yo, k0, ki, kx, kz = call(
        first_outer_kernel, "first_outer", [field, rim[0], core_rim, rim[2]] + [field] * 4,
        p_now, p_before, vel, *parts, inj, zm, ym, side, edge, give, cells)
    model = (k0, ki, kx, kz)
    states = [p_before, p_now, new]
    changes = []
    zm, cm, ym = halo(zo, co, yo)
    for t in range(1, steps):
        cur, prev, before = states[:-4:-1]
        part, change = call(
            functools.partial(forward_inner_kernel, t, full), "forward_inner", [field, field], src_cell, wavelet, cur, prev, *model, cm, near, deep, before, weight=1.2, scalars=2)
        changes.append(change)
        args = [part, k0, ki, kx, zm, ym, side, edge]
        if t == steps - 3:
            u_part, = call(adjoint_first_kernel, "adjoint_first", [field], u_now, u_before,
                           *model, u_cm, near, deep, weight=1.1)
            args[0] = after(part, u_part)
        if t == steps - 2:
            receivers = call(
                lists_kernel, "lists",
                [jax.ShapeDtypeStruct((size, slots), BF16),
                 jax.ShapeDtypeStruct((slots, size), BF16), shaped(slots, depth),
                 shaped(slots, steps)], lists, cells, weight=0.3)
            args[0] = after(part, receivers[0])
        if t == steps - 1:
            new, u_new, *out = call(
                functools.partial(turn_kernel, t), "turn", [field, field] + rim, *args, u_part,
                u_zm, u_ym, *receivers)
            states.append(new)
            break
        if t == 1:
            u_now, u_before = call(settle_pair_kernel, "settle_adjoint", [field, field], adj_now,
                                   adj_before, got_adjoint, weight=0.6, far=2)
            args[0] = after(part, u_now)
            new, *out, lists, pair = call(
                core_stage_kernel, "forward_outer",
                [field, rim[0], rim[1], y_rim, entries, shaped(2, slots)], *args, lists, cells, cm)
            states.append(new)
            zm, cm, ym = halo(*out)
            continue
        if t == 2:
            new, *out, lists, cells = call(
                y_stage_kernel, "forward_outer",
                [field] + [shaped(2, *r.shape) for r in rim] + [entries, shaped(1, slots)],
                *args, lists, pair, u_now)
            states.append(new)
            zm, cm, ym = halo(*out)
            u_zm, u_cm, u_ym = zm, cm, ym
            continue
        new, *out = call(outer_kernel, "forward_outer", [field] + rim, *args)
        states.append(new)
        zm, cm, ym = halo(*out)

    zm, cm, ym = halo(*out)
    u_before, u_now = u_now, u_new
    image = []
    chunk = depth // nx
    half = shaped(nq, size * chunk // 128, 128)
    for j in range(1, steps):
        t = steps - 1 - j
        terms = [changes[t + 1], *image] if image else states[:-4:-1]
        part, *image = call(
            functools.partial(adjoint_inner_kernel, t), "adjoint_inner", [field, field], u_now, u_before, *model, cm, near, deep, states[t + 2], *receivers, *terms, weight=1.5)
        args = [part, k0, ki, kx, zm, ym, side, edge]
        if j == steps - 1:
            final, mine, other = call(
                functools.partial(last_kernel, 2.0 / steps), "last",
                [shaped(2, *field.shape), half, half], *args, *image, changes[0], vel, u_now)
            break
        u_before = u_now
        u_now, *out = call(outer_kernel, "adjoint_outer", [field] + rim,
                           *args)
        zm, cm, ym = halo(*out)

    got = send(final, swap_perm)
    pieces = call(join_kernel, "join", [shaped(2, *half.shape[1:])] * nq, mine,
                  send(other, c_perm))
    pieces = [send(pieces[s], plan.spread(s)) for s in reversed(range(nq))][::-1]
    adj_prev, adj_out = call(select_kernel, "select", [field, field], final, got, weight=1.2)
    gradient, = call(filter_kernel, "filter", [shaped(chunk, rows, nx * cols)],
                     after(pieces[-1], adj_out), *pieces[-2::-1])
    block = (rows, cols, depth)
    return gradient, adj_out.reshape(block), adj_prev.reshape(block)


def solution(mesh):
    field = P(("shots", "inline"), "xline", None)
    model = P("inline", "xline", None)
    lists = P(("xline", "inline"), None)
    return jax.shard_map(
        functools.partial(per_device, Plan(mesh)),
        mesh=mesh,
        in_specs=(field, field, field, field, model, model, P("shots", ("xline", "inline")),
                  lists, lists, P("shots"), P("shots", None)),
        out_specs=(P(("shots", "xline"), "inline", None), field, field),
        check_vma=False,
    )
```

```python
import functools

import jax
import jax.numpy as jnp
import numpy as np
from jax import lax
from jax.experimental import pallas as pl
from jax.experimental.pallas import tpu as pltpu
from jax.sharding import PartitionSpec as P

CAP = 8
SMOOTH = 16
SECOND = (-205.0 / 72.0, 8.0 / 5.0, -1.0 / 5.0, 8.0 / 315.0, -1.0 / 560.0)
FIRST = (4.0 / 5.0, -1.0 / 5.0, 4.0 / 105.0, -1.0 / 280.0)
ALL = ("shots", "xline", "inline")
COLS = 8
GROUP = 8
VMEM_BYTES = 8 * 1024 * 1024
F32 = jnp.float32
BF16 = jnp.bfloat16


class Plan:
    def __init__(self, mesh):
        self.shots = mesh.shape["shots"]
        self.nx = mesh.shape["xline"]
        self.nq = self.nx // 2

    def index(self, s, q, y, c):
        return (s * self.nx + 2 * q + y) * 2 + c

    def perm(self, partner):
        pairs = []
        for s in range(self.shots):
            for q in range(self.nq):
                for y in range(2):
                    for c in range(2):
                        t = partner(q, y, c)
                        dst = self.index(s ^ 1, q, y, c) if t is None else self.index(s, *t)
                        pairs.append((self.index(s, q, y, c), dst))
        return pairs

    def swap(self):
        return self.perm(lambda q, y, c: None if y == c else (q, c, y))

    def z(self):
        def partner(q, y, c):
            other = q + 1 if c == 1 else q - 1
            return (other, y, 1 - c) if 0 <= other < self.nq else None

        return self.perm(partner)

    def core(self):
        return self.perm(lambda q, y, c: (q, y, 1 - c))

    def y(self):
        return self.perm(lambda q, y, c: (q, 1 - y, c))

    def flip(self, bit):
        return self.perm(lambda q, y, c: (q ^ bit, y, c) if (q ^ bit) < self.nq else None)

    def spread(self, shift):
        return self.perm(lambda q, y, c: (q ^ shift, c, y))


def send(value, pairs):
    return lax.ppermute(value, ALL, pairs)


def depth_matrix(n):
    m = np.zeros((n, 2 * n), np.float32)
    for k in range(1, 5):
        for j in range(n):
            for i, sign in ((j + k, 1.0), (j - k, -1.0)):
                if 0 <= i < n:
                    m[i, j] = round(SECOND[k] * 5040)
                    m[i, n + j] = sign * round(FIRST[k - 1] * 840)
    return m


def stencil_matrix(rows, cols):
    own = (rows + 8) * cols
    m = np.zeros((3, rows, cols, own + rows * 8), np.float32)
    for i in range(rows):
        for x in range(cols):
            for k in range(1, 5):
                total = round(SECOND[k] * 5040)
                slope = round(FIRST[k - 1] * 840)
                for sign in (1, -1):
                    at = (i + 4 + sign * k) * cols + x
                    m[0, i, x, at] += total
                    m[1, i, x, at] += sign * slope
                    to = x + sign * k
                    if to < 0:
                        at = own + i * 4 + to + 4
                    elif to >= cols:
                        at = own + rows * 4 + i * 4 + to - cols
                    else:
                        at = (i + 4) * cols + to
                    m[0, i, x, at] += total
                    m[2, i, x, at] += sign * slope
    return m.reshape(3 * rows * cols, own + rows * 8)


def halved(rows, cols, c):
    at = np.arange(rows)[:, None] * cols
    z_side = (at + 4 * c + np.arange(4)).reshape(-1)
    return np.concatenate([z_side, (at + 4 * (1 - c) + np.arange(4)).reshape(-1)])


def near_matrix(rows, cols, c):
    m = stencil_matrix(rows, cols)
    own = (rows + 8) * cols
    place = halved(rows, cols, c)
    out = np.concatenate([place + k * rows * cols for k in range(3)])
    side = own + (1 - c) * rows * 4 + np.arange(rows * 4)
    return m[out][:, np.concatenate([halved(rows + 8, cols, c), side])]


def side_matrix(rows, c):
    m = np.zeros((2, rows, 4, rows, 4), np.float32)
    for x in range(4):
        for k in range(4):
            d = x + 4 - k if c == 0 else k + 4 - x
            if d <= 4:
                for i in range(rows):
                    m[0, i, x, i, k] = round(SECOND[d] * 5040)
                    m[1, i, x, i, k] = round(FIRST[d - 1] * 840) * (-1 if c == 0 else 1)
    return m.reshape(2 * rows * 4, rows * 4)


def edge_matrix(y):
    m = np.zeros((2, 2, 4, 4, 2, 4, 4), np.float32)
    for i in range(4):
        for k in range(4):
            d = i + 4 - k if y == 1 else k + 4 - i
            if d <= 4:
                for part in range(2):
                    for x in range(4):
                        m[0, part, i, x, part, k, x] = round(SECOND[d] * 5040)
                        m[1, part, i, x, part, k, x] = round(FIRST[d - 1] * 840) * (-1 if y == 1 else 1)
    return m.reshape(64, 32)


def split(value):
    high = value.astype(BF16)
    return high, (value - high.astype(F32)).astype(BF16)


def mm(a, b):
    return jnp.dot(a, b, preferred_element_type=F32)


def inner_differences(cur, cm, near, deep):
    size, depth = cur.shape
    half = size // 2
    cm = cm.at[0] if len(cm.shape) == 3 else cm
    own = split(cur[...])
    along = mm(jnp.concatenate(own, axis=1), deep[...])
    blank = jnp.zeros((16, depth), BF16)
    ext = [[jnp.concatenate([blank, part[h * half : h * half + half], blank], axis=0)
            for h in range(2)] for part in own]
    from_c = split(cm[0:half])
    step = GROUP * 4
    for n in range(half // step):
        rhs = [part[h][n * step : n * step + step + 32] for part in ext for h in range(2)]
        rhs += [part[n * step : n * step + step] for part in from_c]
        out = mm(near[...], jnp.concatenate(rhs, axis=0))
        for h in range(2):
            here = slice(h * half + n * step, h * half + n * step + step)
            sums, di, dx = (out[(2 * k + h) * step : (2 * k + h + 1) * step] for k in range(3))
            yield here, sums, along[here, 0:depth], di, dx, along[here, depth:]


def side_differences(zm, side):
    zm = zm.at[0] if len(zm.shape) == 3 else zm
    out = mm(side[...], jnp.concatenate(split(zm[...]), axis=0))
    half = out.shape[0] // 2
    return out[0:half], out[half:]


def edge_differences(flags, size, ym, edge):
    ym = ym.at[0] if len(ym.shape) == 3 else ym
    out = mm(edge[...], jnp.concatenate(split(ym[0:32]), axis=0))
    start = jnp.where(flags[1] == 1, 0, size // 2 - 16)
    for h in range(2):
        at = pl.ds(pl.multiple_of(start + h * (size // 2), 16), 16)
        yield at, out[h * 16 : h * 16 + 16], out[32 + h * 16 : 48 + h * 16]


def to_halves(flags, value):
    rows, depth = value.shape
    pairs = value.reshape(rows // (2 * COLS), 2, COLS, depth)
    a, b = pairs[:, 0], pairs[:, 1]
    low = lax.broadcasted_iota(jnp.int32, a.shape, 1) < 4
    first = jnp.where(low, a, pltpu.roll(b, 4, axis=1)).reshape(rows // 2, depth)
    last = jnp.where(low, pltpu.roll(a, 4, axis=1), b).reshape(rows // 2, depth)
    return jnp.where(flags[0] == 0, first, last), jnp.where(flags[0] == 0, last, first)


def from_halves(flags, value):
    rows, depth = value.shape
    z_side, c_side = value[0 : rows // 2], value[rows // 2 :]
    shape = (rows // (2 * COLS), COLS, depth)
    first = jnp.where(flags[0] == 0, z_side, c_side).reshape(shape)
    last = jnp.where(flags[0] == 0, c_side, z_side).reshape(shape)
    low = lax.broadcasted_iota(jnp.int32, shape, 1) < 4
    a = jnp.where(low, first, pltpu.roll(last, 4, axis=1))
    b = jnp.where(low, pltpu.roll(first, 4, axis=1), last)
    return jnp.stack([a, b], axis=1).reshape(rows, depth)


def place_of(flags, size, i, x):
    near = x - 4 * flags[0]
    return i * 4 + jnp.where((near >= 0) & (near < 4), near, size // 2 + x - 4 * (1 - flags[0]))


def rims(flags, new, zo, co, yo):
    size = new.shape[0]
    half = size // 2
    zo[...] = new[0:half]
    co[...] = new[half:]
    last = jnp.concatenate([new[half - 16 : half], new[size - 16 :]], axis=0)
    first = jnp.concatenate([new[0:16], new[half : half + 16]], axis=0)
    yo[...] = jnp.where(flags[1] == 0, last, first)


def choose(flags, pairs, sems):
    keep = flags[0] == flags[1]

    @pl.when(keep)
    def _():
        copies = [pltpu.make_async_copy(own, out, sems.at[n])
                  for n, (own, recv, out) in enumerate(pairs)]
        for copy in copies:
            copy.start()
        for copy in copies:
            copy.wait()

    @pl.when(jnp.logical_not(keep))
    def _():
        for own, recv, out in pairs:
            out[...] = recv[...]

    for own, recv, out in pairs:
        half = out.shape[0] // 2
        z_side, c_side = to_halves(flags, out[...])
        out[0:half] = z_side
        out[half:] = c_side


def settle_kernel(flags, a, b, recv_a, recv_b, a_out, b_out, zo, co, yo, sems):
    choose(flags, [(a, recv_a, a_out), (b, recv_b, b_out)], sems)
    for n, out in enumerate((a_out, b_out)):
        rims(flags, out, zo.at[n], co.at[n], yo.at[n])


def settle_pair_kernel(flags, a, b, *rest):
    *recv, a_out, b_out, sems = rest
    recv = recv if len(recv) == 2 else (recv[0].at[0], recv[0].at[1])
    choose(flags, [(a, recv[0], a_out), (b, recv[1], b_out)], sems)


def select_kernel(flags, own, recv, *outs):
    keep = flags[0] == flags[1]
    for n, out in enumerate(outs):
        out[...] = jnp.where(keep, own[n], recv[n])


def first_inner_kernel(flags, lr, cur, cm, near, deep, *outs):
    ri, rx, rz, sums_out, di_out, dx_out, dz_out = outs
    for here, spare, spare_z, di, dx, dz in inner_differences(lr, cm.at[0], near, deep):
        ri[here], rx[here], rz[here] = di, dx, dz
    for here, sums, sums_z, di, dx, dz in inner_differences(cur, cm.at[1], near, deep):
        sums_out[here] = sums + sums_z + (3.0 * SECOND[0] * 5040) * cur[here]
        di_out[here], dx_out[here], dz_out[here] = di, dx, dz


def first_outer_kernel(flags, cur, prev, vel, ri, rx, rz, sums, di, dx, dz, inj, zm, ym, side,
                       edge, give, cells, new, zo, co, yo, k0, ki, kx, kz):
    size = cur.shape[0]
    half = size // 2
    kz[...], ki[...], kx[...] = sums[...], di[...], dx[...]
    k0[...], new[...] = ri[...], rx[...]
    more, more_x = side_differences(zm.at[1], side)
    kz[0:half] += more
    kx[0:half] += more_x
    spare, more_x = side_differences(zm.at[0], side)
    new[0:half] += more_x
    for here, more, more_i in edge_differences(flags, size, ym.at[1], edge):
        kz[here] += more
        ki[here] += more_i
    for here, spare, more_i in edge_differences(flags, size, ym.at[0], edge):
        k0[here] += more_i
    for n in range(4):
        here = slice(n * (size // 4), (n + 1) * (size // 4))
        square = vel[here] * vel[here]
        scaled = square * (1.0 / (840 * 840))
        factor = square * (1.0 / 5040)
        along_i, along_x, along_z = scaled * k0[here], scaled * new[here], scaled * rz[here]
        change = factor * kz[here] - (
            along_i * ki[here] + along_x * kx[here] + along_z * dz[here])
        k0[here], ki[here], kx[here], kz[here] = factor, along_i, along_x, along_z
        center = cur[here]
        new[here] = (center - prev[here]) + (center + (change + inj[here]))
    rims(flags, new, zo, co.at[pl.ds(0, half)], yo)
    load(co, half, lambda n: give[n], give.shape[0], [cells[...]])


def inner(cur, prev, k0, ki, kx, kz, cm, near, deep, inj, out):
    for here, sums, sums_z, di, dx, dz in inner_differences(cur, cm, near, deep):
        center = cur[here]
        change = k0[here] * ((sums + sums_z) + (3.0 * SECOND[0] * 5040) * center)
        change = change - (ki[here] * di + kx[here] * dx + kz[here] * dz)
        if inj is not None:
            change = change + inj[here]
        out[here] = (center - prev[here]) + (center + change)


def outer(flags, part, k0, ki, kx, zm, ym, side, edge, new):
    size = part.shape[0]
    half = size // 2
    sums, dx = side_differences(zm, side)
    new[0:half] = part[0:half] + (k0[0:half] * sums - kx[0:half] * dx)
    new[half:] = part[half:]
    for here, sums, di in edge_differences(flags, size, ym, edge):
        new[here] += k0[here] * sums - ki[here] * di


def other_half(stage, flags, count):
    other = 1 - flags[4 + stage]
    for n in range(count // 2):
        high, low = n >> stage, n & ((1 << stage) - 1)
        yield n, (high << (stage + 1)) + (other << stage) + low


def trade(stage, then, flags, mine, got, out, give=None):
    out[...] = mine[...]
    for n, at in other_half(stage, flags, out.shape[0]):
        out[at] = got(n) if callable(got) else got[n]
    if give is not None:
        for n, at in other_half(then, flags, out.shape[0]):
            give[n] = out[at]


def load(message, rim, entry, count, cells):
    for n in range(count):
        message[rim + n // 2 * 8 : rim + n // 2 * 8 + 8, n % 2 * 128 : n % 2 * 128 + 128] = entry(n)
    at = rim + count // 2 * 8
    wide = message.shape[1]
    for k, row in enumerate(cells):
        for m in range(row.shape[1] // 128):
            lane = k * row.shape[1] + m * 128
            message[at + lane // wide : at + lane // wide + 1, lane % wide : lane % wide + 128] = (
                row[:, m * 128 : m * 128 + 128])


def unload(message, rim, count, rows, slots):
    wide = message.shape[1]
    at = rim + count // 2 * 8

    def entry(n):
        return message[rim + n // 2 * 8 : rim + n // 2 * 8 + 8, n % 2 * 128 : n % 2 * 128 + 128]

    cells = []
    for k in range(rows):
        tiles = []
        for m in range(slots // 128):
            lane = k * slots + m * 128
            tiles.append(message[at + lane // wide : at + lane // wide + 1,
                                 lane % wide : lane % wide + 128])
        cells.append(jnp.concatenate(tiles, axis=1) if len(tiles) > 1 else tiles[0])
    return entry, cells


def trade_kernel(stage, then, flags, mine, got, out, give):
    trade(stage, then, flags, mine, got, out, give)


def source_kernel(step, full, flags, src, wave, out):
    size, depth = out.shape
    count = src.shape[0]
    shift = (depth - 1).bit_length()
    plane = shift + (full - 1).bit_length()
    rows = size // COLS
    lane = lax.broadcasted_iota(jnp.int32, (1, count), 1)
    sub = lax.broadcasted_iota(jnp.int32, (count, 1), 0)
    row = jnp.zeros((1, count), jnp.int32)
    deep = jnp.zeros((count, 1), jnp.int32)
    size_of = jnp.zeros((count, 1), F32)
    for n in range(count):
        cell = src[n]
        i = jnp.right_shift(cell, plane) - flags[1] * rows
        x = jnp.bitwise_and(jnp.right_shift(cell, shift), full - 1)
        x = x - (2 * flags[3] + flags[0]) * COLS
        ok = (i >= 0) & (i < rows) & (x >= 0) & (x < COLS)
        row = jnp.where(lane == n, jnp.where(ok, place_of(flags, size, i, x), -1), row)
        deep = jnp.where(sub == n, jnp.bitwise_and(cell, depth - 1), deep)
        size_of = jnp.where(sub == n, wave[step, n], size_of)
    spot = lax.broadcasted_iota(jnp.int32, (size, count), 0) == row
    spot = spot.astype(F32).astype(BF16)
    high, low = split(jnp.where(
        lax.broadcasted_iota(jnp.int32, (count, depth), 1) == deep, size_of, 0.0))
    out[...] = mm(spot, high) + mm(spot, low)


def forward_inner_kernel(step, full, flags, src, wave, cur, prev, k0, ki, kx, kz, cm, near, deep,
                         before, part, change):
    source_kernel(step, full, flags, src, wave, change)
    inner(cur, prev, k0, ki, kx, kz, cm, near, deep, change, part)
    change[...] = (cur[...] - prev[...]) - (prev[...] - before[...])


def outer_kernel(flags, part, k0, ki, kx, zm, ym, side, edge, new, zo, co, yo):
    outer(flags, part, k0, ki, kx, zm, ym, side, edge, new)
    rims(flags, new, zo, co, yo)


def pack_kernel(stage, flags, counts, cells, traces, cells_out, lists, give, counts_v, cells_v, traces_v,
                sems):
    pairs = ((counts, counts_v), (cells, cells_v), (traces, traces_v))
    copies = [pltpu.make_async_copy(a, b, sems.at[n]) for n, (a, b) in enumerate(pairs)]
    for copy in copies:
        copy.start()
    for copy in copies:
        copy.wait()
    subs, n = counts.shape[1], cells.shape[1]
    shape = (subs, n)
    lane = lax.broadcasted_iota(jnp.int32, shape, 1)
    mine = lane // CAP == lax.broadcasted_iota(jnp.int32, shape, 0)
    live = mm(counts_v[...].astype(F32).astype(BF16), mine.astype(F32).astype(BF16))
    slot = jnp.bitwise_and(lane[0:1], CAP - 1)
    cells_out[...] = jnp.where(slot.astype(F32) < live, cells_v[...].astype(F32), -1.0)
    for m in range(subs):
        q, y, c = m >> 2, (m >> 1) & 1, m & 1
        start = ((2 * q + c) * 2 + y) * CAP
        tile = traces_v[:, start // 128 * 128 : start // 128 * 128 + 128]
        lists[m] = pltpu.roll(tile, (128 - start % 128) % 128, axis=1) if start % 128 else tile
    for n, at in other_half(stage, flags, subs):
        give[n] = lists[at]


def core_stage_kernel(flags, part, k0, ki, kx, zm, ym, side, edge, lists, cells, cm, new, zo, co, yo,
                      lists_out, pair):
    outer(flags, part, k0, ki, kx, zm, ym, side, edge, new)
    count, half = lists.shape[0] // 2, new.shape[0] // 2
    entry, (theirs,) = unload(cm, half, count, 1, cells.shape[1])
    trade(0, None, flags, lists, entry, lists_out)
    mine = cells[...]
    pair[0:1] = jnp.where(flags[0] == 0, mine, theirs)
    pair[1:2] = jnp.where(flags[0] == 0, theirs, mine)
    rims(flags, new, zo, co, yo.at[pl.ds(0, 32)])
    at = [k for n, k in other_half(1, flags, lists.shape[0])]
    load(yo, 32, lambda n: lists_out[at[n]], count, [pair[0:1], pair[1:2]])


def y_stage_kernel(flags, part, k0, ki, kx, zm, ym, side, edge, lists, pair, other, new, zo, co, yo,
                   lists_out, cells):
    outer(flags, part, k0, ki, kx, zm, ym, side, edge, new)
    for n, field in enumerate((new, other)):
        rims(flags, field, zo.at[n], co.at[n], yo.at[n])
    entry, theirs = unload(ym, 32, lists.shape[0] // 2, 2, pair.shape[1])
    trade(1, None, flags, lists, entry, lists_out)
    away = flags[0] != flags[1]
    low = jnp.where(away, theirs[0], pair[0:1])
    high = jnp.where(away, theirs[1], pair[1:2])
    cells[...] = jnp.where(flags[1] == 0, low, high)


def lists_kernel(flags, lists, cells, spot, pick, at, obs):
    size, n = spot.shape
    depth = at.shape[1]
    subs, steps = lists.shape[0], obs.shape[1]
    cell = cells[...]
    along = jnp.floor((cell + 0.5) * (1.0 / depth))
    place = along.astype(jnp.int32)
    place = jnp.where(place < 0, -1, place_of(
        flags, size, jnp.right_shift(place, 3), jnp.bitwise_and(place, COLS - 1)))
    same = lax.broadcasted_iota(jnp.int32, (n, n), 0) == lax.broadcasted_iota(jnp.int32, (n, n), 1)

    def column(row):
        return jnp.sum(jnp.where(same, row, 0.0), axis=1, keepdims=True).astype(jnp.int32)

    hot = lax.broadcasted_iota(jnp.int32, (size, n), 0) == place
    spot[...] = hot.astype(F32).astype(BF16)
    hot = lax.broadcasted_iota(jnp.int32, (n, size), 1) == column(place.astype(F32))
    pick[...] = hot.astype(F32).astype(BF16)
    hot = lax.broadcasted_iota(jnp.int32, (n, depth), 1) == column(cell - along * depth)
    at[...] = hot.astype(F32)
    traces = lists[...].reshape(subs * steps, 128).T[0:CAP]
    for s in range(subs):
        obs[s * CAP : s * CAP + CAP, :] = traces[:, s * steps : s * steps + steps]


def injection(t, state, spot, pick, at, obs):
    high, low = split(state[...])
    seen = at[...] * (mm(pick[...], high) + mm(pick[...], low))
    residual = jnp.sum(seen, axis=1, keepdims=True) - obs[:, t : t + 1]
    high, low = split(at[...] * residual)
    return mm(spot[...], high) + mm(spot[...], low)


def adjoint_inner_kernel(t, flags, cur, prev, k0, ki, kx, kz, cm, near, deep, state, spot, pick,
                         at, obs, *rest):
    if len(rest) == 4:
        change, image, part, image_out = rest
        image_out[...] = cur[...] * change[...] + image[...]
    else:
        now, mid, before, part, image_out = rest
        image_out[...] = cur[...] * ((now[...] - mid[...]) - (mid[...] - before[...]))
    inj = injection(t, state, spot, pick, at, obs)
    inner(cur, prev, k0, ki, kx, kz, cm, near, deep, inj, part)


def adjoint_first_kernel(flags, cur, prev, k0, ki, kx, kz, cm, near, deep, part):
    inner(cur, prev, k0, ki, kx, kz, cm.at[1], near, deep, None, part)


def turn_kernel(t, flags, part, k0, ki, kx, zm, ym, side, edge, u_part, u_zm, u_ym, spot, pick, at, obs, new, u_new, zo, co, yo):
    outer(flags, part, k0, ki, kx, zm, ym, side, edge, new)
    outer(flags, u_part, k0, ki, kx, u_zm.at[1], u_ym.at[1], side, edge, u_new)
    u_new[...] += injection(t, new, spot, pick, at, obs)
    rims(flags, u_new, zo, co, yo)


def last_kernel(scale, flags, part, k0, ki, kx, zm, ym, side, edge, image, change, vel,
                prev, states, mine, other):
    new = states.at[1]
    outer(flags, part, k0, ki, kx, zm, ym, side, edge, new)
    raw = from_halves(flags, (image[...] + new[...] * change[...]) * scale / vel[...])
    new[...] = from_halves(flags, new[...])
    states[0] = from_halves(flags, prev[...])
    count, height, lanes = mine.shape
    chunk = raw.shape[1] // (2 * count)
    for n in range(count):
        even, odd = (
            jnp.concatenate(
                [raw[g * height : g * height + height, m * chunk : m * chunk + chunk]
                 for g in range(lanes // chunk)], axis=1)
            for m in (2 * n, 2 * n + 1))
        mine[n] = jnp.where(flags[0] == 0, even, odd)
        other[n] = jnp.where(flags[0] == 0, odd, even)


def join_kernel(flags, mine, got, *outs):
    for s, out in enumerate(outs):
        to = jnp.bitwise_xor(flags[3], s)
        a, b = mine[to], got[to]
        out[0] = jnp.where(flags[0] == 0, a, b)
        out[1] = jnp.where(flags[0] == 0, b, a)


def filter_kernel(flags, *refs):
    *pieces, out = refs
    pieces = pieces[::-1]
    height, lanes = pieces[0].shape[1:]
    chunk, rows, full = out.shape
    groups = lanes // chunk
    q = flags[3]
    shape = (full, full)
    y = lax.broadcasted_iota(jnp.int32, shape, 1)
    at = lax.broadcasted_iota(jnp.int32, shape, 0)
    within = jnp.bitwise_and(at, 2 * COLS - 1)
    place = jnp.bitwise_xor(q * (2 * COLS), at - within) + within
    weights = jnp.exp(jnp.abs(y - place).astype(F32) * (-1.0 / SMOOTH))
    weights = split(weights / jnp.sum(weights, axis=0, keepdims=True))
    ready = []
    for n in range(height // COLS):
        here = slice(n * COLS, n * COLS + COLS)
        lines = jnp.concatenate([piece[b, here, :] for piece in pieces for b in range(2)], axis=0)
        high, low = split(lines.T)
        done = mm(high, weights[0]) + mm(low, weights[0]) + mm(high, weights[1])
        ready.append(done)
    for g in range(groups):
        lines = jnp.stack([done[g * chunk : g * chunk + chunk] for done in ready], axis=0)
        out[:, g * (rows // groups) : (g + 1) * (rows // groups), :] = jnp.swapaxes(lines, 0, 1)


def shaped(*shape):
    return jax.ShapeDtypeStruct(shape, F32)


class Flags:
    def __getitem__(self, n):
        if n == 0:
            return lax.axis_index("inline")
        xline = lax.axis_index("xline")
        if n == 1:
            return jnp.bitwise_and(xline, 1)
        if n == 3:
            return jnp.right_shift(xline, 1)
        place = 2 * xline + lax.axis_index("inline")
        return jnp.bitwise_and(jnp.right_shift(place, n - 4), 1)


def call(kernel, name, outs, *args, weight=0, far=0, scalars=0, scratch=()):
    specs = [pl.BlockSpec(memory_space=pltpu.SMEM)] * scalars
    specs += [pl.BlockSpec(memory_space=pl.ANY)] * far
    specs += [pl.BlockSpec(memory_space=pltpu.VMEM)] * (len(args) - scalars - far)
    return pl.pallas_call(
        functools.partial(kernel, Flags()),
        name=name,
        out_shape=outs,
        in_specs=specs,
        out_specs=[pl.BlockSpec(memory_space=pltpu.VMEM)] * len(outs),
        scratch_shapes=list(scratch) + ([pltpu.SemaphoreType.DMA((far,))] if far else []),
        compiler_params=pltpu.CompilerParams(vmem_limit_bytes=VMEM_BYTES),
        cost_estimate=pl.CostEstimate(
            flops=1000, bytes_accessed=1000 + int(weight * 3_600_000), transcendentals=0),
    )(*args)


def per_device(plan, fwd_now, fwd_before, adj_now, adj_before, velocity, log_density, observed,
               rec_cells, rec_counts, src_cell, wavelet):
    rows, cols, depth = fwd_now.shape
    size = rows * cols
    steps = wavelet.shape[0]
    nx, nq = plan.nx, plan.nq
    subs = 2 * nx
    xline, c = lax.axis_index("xline"), lax.axis_index("inline")
    q, y = xline // 2, xline % 2
    keep = y == c
    z_perm, c_perm, y_perm, swap_perm = plan.z(), plan.core(), plan.y(), plan.swap()
    stages = [(c_perm, c), (y_perm, y)]
    stages += [(plan.flip(1 << b), (q >> b) & 1) for b in range((nq - 1).bit_length())]
    field = shaped(size, depth)
    rim = [shaped(size // 2, depth), shaped(size // 2, depth), shaped(4 * cols, depth)]

    deep = depth_matrix(depth)
    deep = jnp.asarray(np.concatenate([deep, deep]), BF16)
    inside = jnp.where(c == 0, q > 0, q < nq - 1)
    near = [near_matrix(GROUP, cols, k) for k in range(2)]
    wide = (GROUP + 8) * cols
    near = [np.concatenate([m[:, :wide], m[:, :wide], m[:, wide:], m[:, wide:]], axis=1) for m in near]
    near = jnp.where(c == 0, jnp.asarray(near[0], F32), jnp.asarray(near[1], F32)).astype(BF16)
    side = [side_matrix(rows, k) for k in range(2)]
    side = jnp.where(c == 0, jnp.asarray(side[0], BF16), jnp.asarray(side[1], BF16))
    side = jnp.where(inside, side, jnp.zeros_like(side))
    side = jnp.concatenate([side, side], axis=1)
    edge = [edge_matrix(k) for k in range(2)]
    edge = jnp.where(y == 0, jnp.asarray(edge[0], F32), jnp.asarray(edge[1], F32)).astype(BF16)
    edge = jnp.concatenate([edge, edge], axis=1)

    def halo(zo, co, yo):
        return send(zo, z_perm), send(co, c_perm), send(yo, y_perm)

    def after(value, *deps):
        return lax.optimization_barrier((value,) + deps)[0]

    def flat(value):
        return value.reshape(size, depth)

    log_density, fwd_now, velocity = flat(log_density), flat(fwd_now), flat(velocity)
    fwd_before, adj_now, adj_before = flat(fwd_before), flat(adj_now), flat(adj_before)
    got = [send(v, swap_perm) for v in (log_density, fwd_now)]
    stacked = jnp.stack([velocity, fwd_before])
    got_model = send(stacked, swap_perm)
    full = nx * cols
    inj, = call(functools.partial(source_kernel, 0, full), "source", [field], src_cell, wavelet,
                weight=0.7, scalars=2)
    got[0], inj = lax.optimization_barrier((got[0], inj))
    slots = subs * CAP
    entries, half_entries = shaped(subs, steps, 128), shaped(subs // 2, steps, 128)
    order = [*range(2, len(stages)), 0]
    cells, lists, give = call(
        functools.partial(pack_kernel, order[0]), "pack", [shaped(1, slots), entries, half_entries], rec_counts,
        rec_cells, observed, weight=0.2, far=3,
        scratch=[pltpu.VMEM(rec_counts.shape, jnp.int32), pltpu.VMEM(rec_cells.shape, jnp.int32),
                 pltpu.VMEM(observed.shape, F32)])
    for n, bit in enumerate(order[:-1]):
        lists, give = call(
            functools.partial(trade_kernel, bit, order[n + 1]), "trade", [entries, half_entries],
            lists, send(give, stages[bit][0]), weight=0.1)
        if n == len(order) - 2:
            got[0], give = lax.optimization_barrier((got[0], give))

    density, p_now, *out = call(settle_kernel, "settle",
                                [field, field] + [shaped(2, *r.shape) for r in rim],
                                log_density, fwd_now, *got, far=2)
    zm, cm, ym = halo(*out)
    vel, p_before = call(settle_pair_kernel, "settle_model", [field, field],
                         velocity, fwd_before, got_model, weight=0.6, far=2)
    parts = call(first_inner_kernel, "first_inner", [field] * 7, density, p_now, cm,
                 near, deep, weight=1.3)
    got_adjoint = [send(after(v, parts[0]), swap_perm) for v in (adj_now, adj_before)]

    riders = subs // 4 * 8 + 8
    core_rim = shaped(size // 2 + riders, depth)
    y_rim = shaped(4 * cols + riders, depth)

    new, zo, co, yo, k0, ki, kx, kz = call(
        first_outer_kernel, "first_outer", [field, rim[0], core_rim, rim[2]] + [field] * 4,
        p_now, p_before, vel, *parts, inj, zm, ym, side, edge, give, cells)
    model = (k0, ki, kx, kz)
    states = [p_before, p_now, new]
    changes = []
    zm, cm, ym = halo(zo, co, yo)
    for t in range(1, steps):
        cur, prev, before = states[:-4:-1]
        part, change = call(
            functools.partial(forward_inner_kernel, t, full), "forward_inner", [field, field], src_cell, wavelet, cur, prev, *model, cm, near, deep, before, weight=1.2, scalars=2)
        changes.append(change)
        args = [part, k0, ki, kx, zm, ym, side, edge]
        if t == steps - 3:
            u_part, = call(adjoint_first_kernel, "adjoint_first", [field], u_now, u_before,
                           *model, u_cm, near, deep, weight=1.1)
            args[0] = after(part, u_part)
        if t == steps - 2:
            receivers = call(
                lists_kernel, "lists",
                [jax.ShapeDtypeStruct((size, slots), BF16),
                 jax.ShapeDtypeStruct((slots, size), BF16), shaped(slots, depth),
                 shaped(slots, steps)], lists, cells, weight=0.3)
            args[0] = after(part, receivers[0])
        if t == steps - 1:
            new, u_new, *out = call(
                functools.partial(turn_kernel, t), "turn", [field, field] + rim, *args, u_part,
                u_zm, u_ym, *receivers)
            states.append(new)
            break
        if t == 1:
            u_now, u_before = call(settle_pair_kernel, "settle_adjoint", [field, field], adj_now,
                                   adj_before, *got_adjoint, weight=0.6, far=2)
            args[0] = after(part, u_now)
            new, *out, lists, pair = call(
                core_stage_kernel, "forward_outer",
                [field, rim[0], rim[1], y_rim, entries, shaped(2, slots)], *args, lists, cells, cm)
            states.append(new)
            zm, cm, ym = halo(*out)
            continue
        if t == 2:
            new, *out, lists, cells = call(
                y_stage_kernel, "forward_outer",
                [field] + [shaped(2, *r.shape) for r in rim] + [entries, shaped(1, slots)],
                *args, lists, pair, u_now)
            states.append(new)
            zm, cm, ym = halo(*out)
            u_zm, u_cm, u_ym = zm, cm, ym
            continue
        new, *out = call(outer_kernel, "forward_outer", [field] + rim, *args)
        states.append(new)
        zm, cm, ym = halo(*out)

    zm, cm, ym = halo(*out)
    u_before, u_now = u_now, u_new
    image = []
    chunk = depth // nx
    half = shaped(nq, size * chunk // 128, 128)
    for j in range(1, steps):
        t = steps - 1 - j
        terms = [changes[t + 1], *image] if image else states[:-4:-1]
        part, *image = call(
            functools.partial(adjoint_inner_kernel, t), "adjoint_inner", [field, field], u_now, u_before, *model, cm, near, deep, states[t + 2], *receivers, *terms, weight=1.5)
        args = [part, k0, ki, kx, zm, ym, side, edge]
        if j == steps - 1:
            final, mine, other = call(
                functools.partial(last_kernel, 2.0 / steps), "last",
                [shaped(2, *field.shape), half, half], *args, *image, changes[0], vel, u_now)
            break
        u_before = u_now
        u_now, *out = call(outer_kernel, "adjoint_outer", [field] + rim,
                           *args)
        zm, cm, ym = halo(*out)

    got = send(final, swap_perm)
    pieces = call(join_kernel, "join", [shaped(2, *half.shape[1:])] * nq, mine,
                  send(other, c_perm))
    pieces = [send(pieces[s], plan.spread(s)) for s in reversed(range(nq))][::-1]
    adj_prev, adj_out = call(select_kernel, "select", [field, field], final, got, weight=1.2)
    gradient, = call(filter_kernel, "filter", [shaped(chunk, rows, nx * cols)],
                     after(pieces[-1], adj_out), *pieces[-2::-1])
    block = (rows, cols, depth)
    return gradient, adj_out.reshape(block), adj_prev.reshape(block)


def solution(mesh):
    field = P(("shots", "inline"), "xline", None)
    model = P("inline", "xline", None)
    lists = P(("xline", "inline"), None)
    return jax.shard_map(
        functools.partial(per_device, Plan(mesh)),
        mesh=mesh,
        in_specs=(field, field, field, field, model, model, P("shots", ("xline", "inline")),
                  lists, lists, P("shots"), P("shots", None)),
        out_specs=(P(("shots", "xline"), "inline", None), field, field),
        check_vma=False,
    )
```

```python
import functools

import jax
import jax.numpy as jnp
import numpy as np
from jax import lax
from jax.experimental import pallas as pl
from jax.experimental.pallas import tpu as pltpu
from jax.sharding import PartitionSpec as P

CAP = 8
SMOOTH = 16
SECOND = (-205.0 / 72.0, 8.0 / 5.0, -1.0 / 5.0, 8.0 / 315.0, -1.0 / 560.0)
FIRST = (4.0 / 5.0, -1.0 / 5.0, 4.0 / 105.0, -1.0 / 280.0)
ALL = ("shots", "xline", "inline")
COLS = 8
GROUP = 8
VMEM_BYTES = 8 * 1024 * 1024
F32 = jnp.float32
BF16 = jnp.bfloat16


class Plan:
    def __init__(self, mesh):
        self.shots = mesh.shape["shots"]
        self.nx = mesh.shape["xline"]
        self.nq = self.nx // 2

    def index(self, s, q, y, c):
        return (s * self.nx + 2 * q + y) * 2 + c

    def perm(self, partner):
        pairs = []
        for s in range(self.shots):
            for q in range(self.nq):
                for y in range(2):
                    for c in range(2):
                        t = partner(q, y, c)
                        dst = self.index(s ^ 1, q, y, c) if t is None else self.index(s, *t)
                        pairs.append((self.index(s, q, y, c), dst))
        return pairs

    def swap(self):
        return self.perm(lambda q, y, c: None if y == c else (q, c, y))

    def z(self):
        def partner(q, y, c):
            other = q + 1 if c == 1 else q - 1
            return (other, y, 1 - c) if 0 <= other < self.nq else None

        return self.perm(partner)

    def core(self):
        return self.perm(lambda q, y, c: (q, y, 1 - c))

    def y(self):
        return self.perm(lambda q, y, c: (q, 1 - y, c))

    def flip(self, bit):
        return self.perm(lambda q, y, c: (q ^ bit, y, c) if (q ^ bit) < self.nq else None)

    def spread(self, shift):
        return self.perm(lambda q, y, c: (q ^ shift, c, y))


def send(value, pairs):
    return lax.ppermute(value, ALL, pairs)


def depth_matrix(n):
    m = np.zeros((n, 2 * n), np.float32)
    for k in range(1, 5):
        for j in range(n):
            for i, sign in ((j + k, 1.0), (j - k, -1.0)):
                if 0 <= i < n:
                    m[i, j] = round(SECOND[k] * 5040)
                    m[i, n + j] = sign * round(FIRST[k - 1] * 840)
    return m


def stencil_matrix(rows, cols):
    own = (rows + 8) * cols
    m = np.zeros((3, rows, cols, own + rows * 8), np.float32)
    for i in range(rows):
        for x in range(cols):
            for k in range(1, 5):
                total = round(SECOND[k] * 5040)
                slope = round(FIRST[k - 1] * 840)
                for sign in (1, -1):
                    at = (i + 4 + sign * k) * cols + x
                    m[0, i, x, at] += total
                    m[1, i, x, at] += sign * slope
                    to = x + sign * k
                    if to < 0:
                        at = own + i * 4 + to + 4
                    elif to >= cols:
                        at = own + rows * 4 + i * 4 + to - cols
                    else:
                        at = (i + 4) * cols + to
                    m[0, i, x, at] += total
                    m[2, i, x, at] += sign * slope
    return m.reshape(3 * rows * cols, own + rows * 8)


def halved(rows, cols, c):
    at = np.arange(rows)[:, None] * cols
    z_side = (at + 4 * c + np.arange(4)).reshape(-1)
    return np.concatenate([z_side, (at + 4 * (1 - c) + np.arange(4)).reshape(-1)])


def near_matrix(rows, cols, c):
    m = stencil_matrix(rows, cols)
    own = (rows + 8) * cols
    place = halved(rows, cols, c)
    out = np.concatenate([place + k * rows * cols for k in range(3)])
    side = own + (1 - c) * rows * 4 + np.arange(rows * 4)
    return m[out][:, np.concatenate([halved(rows + 8, cols, c), side])]


def side_matrix(rows, c):
    m = np.zeros((2, rows, 4, rows, 4), np.float32)
    for x in range(4):
        for k in range(4):
            d = x + 4 - k if c == 0 else k + 4 - x
            if d <= 4:
                for i in range(rows):
                    m[0, i, x, i, k] = round(SECOND[d] * 5040)
                    m[1, i, x, i, k] = round(FIRST[d - 1] * 840) * (-1 if c == 0 else 1)
    return m.reshape(2 * rows * 4, rows * 4)


def edge_matrix(y):
    m = np.zeros((2, 2, 4, 4, 2, 4, 4), np.float32)
    for i in range(4):
        for k in range(4):
            d = i + 4 - k if y == 1 else k + 4 - i
            if d <= 4:
                for part in range(2):
                    for x in range(4):
                        m[0, part, i, x, part, k, x] = round(SECOND[d] * 5040)
                        m[1, part, i, x, part, k, x] = round(FIRST[d - 1] * 840) * (-1 if y == 1 else 1)
    return m.reshape(64, 32)


def split(value):
    high = value.astype(BF16)
    return high, (value - high.astype(F32)).astype(BF16)


def mm(a, b):
    return jnp.dot(a, b, preferred_element_type=F32)


def inner_differences(cur, cm, near, deep):
    size, depth = cur.shape
    half = size // 2
    cm = cm.at[0] if len(cm.shape) == 3 else cm
    own = split(cur[...])
    along = mm(jnp.concatenate(own, axis=1), deep[...])
    blank = jnp.zeros((16, depth), BF16)
    ext = [[jnp.concatenate([blank, part[h * half : h * half + half], blank], axis=0)
            for h in range(2)] for part in own]
    from_c = split(cm[0:half])
    step = GROUP * 4
    for n in range(half // step):
        rhs = [part[h][n * step : n * step + step + 32] for part in ext for h in range(2)]
        rhs += [part[n * step : n * step + step] for part in from_c]
        out = mm(near[...], jnp.concatenate(rhs, axis=0))
        for h in range(2):
            here = slice(h * half + n * step, h * half + n * step + step)
            sums, di, dx = (out[(2 * k + h) * step : (2 * k + h + 1) * step] for k in range(3))
            yield here, sums, along[here, 0:depth], di, dx, along[here, depth:]


def side_differences(zm, side):
    zm = zm.at[0] if len(zm.shape) == 3 else zm
    out = mm(side[...], jnp.concatenate(split(zm[...]), axis=0))
    half = out.shape[0] // 2
    return out[0:half], out[half:]


def edge_differences(flags, size, ym, edge):
    ym = ym.at[0] if len(ym.shape) == 3 else ym
    out = mm(edge[...], jnp.concatenate(split(ym[0:32]), axis=0))
    start = jnp.where(flags[1] == 1, 0, size // 2 - 16)
    for h in range(2):
        at = pl.ds(pl.multiple_of(start + h * (size // 2), 16), 16)
        yield at, out[h * 16 : h * 16 + 16], out[32 + h * 16 : 48 + h * 16]


def to_halves(flags, value):
    rows, depth = value.shape
    pairs = value.reshape(rows // (2 * COLS), 2, COLS, depth)
    a, b = pairs[:, 0], pairs[:, 1]
    low = lax.broadcasted_iota(jnp.int32, a.shape, 1) < 4
    first = jnp.where(low, a, pltpu.roll(b, 4, axis=1)).reshape(rows // 2, depth)
    last = jnp.where(low, pltpu.roll(a, 4, axis=1), b).reshape(rows // 2, depth)
    return jnp.where(flags[0] == 0, first, last), jnp.where(flags[0] == 0, last, first)


def from_halves(flags, value):
    rows, depth = value.shape
    z_side, c_side = value[0 : rows // 2], value[rows // 2 :]
    shape = (rows // (2 * COLS), COLS, depth)
    first = jnp.where(flags[0] == 0, z_side, c_side).reshape(shape)
    last = jnp.where(flags[0] == 0, c_side, z_side).reshape(shape)
    low = lax.broadcasted_iota(jnp.int32, shape, 1) < 4
    a = jnp.where(low, first, pltpu.roll(last, 4, axis=1))
    b = jnp.where(low, pltpu.roll(first, 4, axis=1), last)
    return jnp.stack([a, b], axis=1).reshape(rows, depth)


def place_of(flags, size, i, x):
    near = x - 4 * flags[0]
    return i * 4 + jnp.where((near >= 0) & (near < 4), near, size // 2 + x - 4 * (1 - flags[0]))


def rims(flags, new, zo, co, yo):
    size = new.shape[0]
    half = size // 2
    zo[...] = new[0:half]
    co[...] = new[half:]
    last = jnp.concatenate([new[half - 16 : half], new[size - 16 :]], axis=0)
    first = jnp.concatenate([new[0:16], new[half : half + 16]], axis=0)
    yo[...] = jnp.where(flags[1] == 0, last, first)


def choose(flags, pairs, sems):
    keep = flags[0] == flags[1]

    @pl.when(keep)
    def _():
        copies = [pltpu.make_async_copy(own, out, sems.at[n])
                  for n, (own, recv, out) in enumerate(pairs)]
        for copy in copies:
            copy.start()
        for copy in copies:
            copy.wait()

    @pl.when(jnp.logical_not(keep))
    def _():
        for own, recv, out in pairs:
            out[...] = recv[...]

    for own, recv, out in pairs:
        half = out.shape[0] // 2
        z_side, c_side = to_halves(flags, out[...])
        out[0:half] = z_side
        out[half:] = c_side


def settle_kernel(flags, a, b, recv_a, recv_b, a_out, b_out, zo, co, yo, sems):
    choose(flags, [(a, recv_a, a_out), (b, recv_b, b_out)], sems)
    for n, out in enumerate((a_out, b_out)):
        rims(flags, out, zo.at[n], co.at[n], yo.at[n])


def settle_pair_kernel(flags, a, b, *rest):
    *recv, a_out, b_out, sems = rest
    recv = recv if len(recv) == 2 else (recv[0].at[0], recv[0].at[1])
    choose(flags, [(a, recv[0], a_out), (b, recv[1], b_out)], sems)


def select_kernel(flags, own, recv, *outs):
    keep = flags[0] == flags[1]
    for n, out in enumerate(outs):
        out[...] = jnp.where(keep, own[n], recv[n])


def first_inner_kernel(flags, lr, cur, cm, near, deep, *outs):
    ri, rx, rz, sums_out, di_out, dx_out, dz_out = outs
    for here, spare, spare_z, di, dx, dz in inner_differences(lr, cm.at[0], near, deep):
        ri[here], rx[here], rz[here] = di, dx, dz
    for here, sums, sums_z, di, dx, dz in inner_differences(cur, cm.at[1], near, deep):
        sums_out[here] = sums + sums_z + (3.0 * SECOND[0] * 5040) * cur[here]
        di_out[here], dx_out[here], dz_out[here] = di, dx, dz


def first_outer_kernel(flags, cur, prev, vel, ri, rx, rz, sums, di, dx, dz, inj, zm, ym, side,
                       edge, give, cells, new, zo, co, yo, k0, ki, kx, kz):
    size = cur.shape[0]
    half = size // 2
    kz[...], ki[...], kx[...] = sums[...], di[...], dx[...]
    k0[...], new[...] = ri[...], rx[...]
    more, more_x = side_differences(zm.at[1], side)
    kz[0:half] += more
    kx[0:half] += more_x
    spare, more_x = side_differences(zm.at[0], side)
    new[0:half] += more_x
    for here, more, more_i in edge_differences(flags, size, ym.at[1], edge):
        kz[here] += more
        ki[here] += more_i
    for here, spare, more_i in edge_differences(flags, size, ym.at[0], edge):
        k0[here] += more_i
    for n in range(4):
        here = slice(n * (size // 4), (n + 1) * (size // 4))
        square = vel[here] * vel[here]
        scaled = square * (1.0 / (840 * 840))
        factor = square * (1.0 / 5040)
        along_i, along_x, along_z = scaled * k0[here], scaled * new[here], scaled * rz[here]
        change = factor * kz[here] - (
            along_i * ki[here] + along_x * kx[here] + along_z * dz[here])
        k0[here], ki[here], kx[here], kz[here] = factor, along_i, along_x, along_z
        center = cur[here]
        new[here] = (center - prev[here]) + (center + (change + inj[here]))
    rims(flags, new, zo, co.at[pl.ds(0, half)], yo)
    load(co, half, lambda n: give[n], give.shape[0], [cells[...]])


def inner(cur, prev, k0, ki, kx, kz, cm, near, deep, inj, out):
    for here, sums, sums_z, di, dx, dz in inner_differences(cur, cm, near, deep):
        center = cur[here]
        change = k0[here] * ((sums + sums_z) + (3.0 * SECOND[0] * 5040) * center)
        change = change - (ki[here] * di + kx[here] * dx + kz[here] * dz)
        if inj is not None:
            change = change + inj[here]
        out[here] = (center - prev[here]) + (center + change)


def outer(flags, part, k0, ki, kx, zm, ym, side, edge, new):
    size = part.shape[0]
    half = size // 2
    sums, dx = side_differences(zm, side)
    new[0:half] = part[0:half] + (k0[0:half] * sums - kx[0:half] * dx)
    new[half:] = part[half:]
    for here, sums, di in edge_differences(flags, size, ym, edge):
        new[here] += k0[here] * sums - ki[here] * di


def other_half(stage, flags, count):
    other = 1 - flags[4 + stage]
    for n in range(count // 2):
        high, low = n >> stage, n & ((1 << stage) - 1)
        yield n, (high << (stage + 1)) + (other << stage) + low


def trade(stage, then, flags, mine, got, out, give=None):
    out[...] = mine[...]
    for n, at in other_half(stage, flags, out.shape[0]):
        out[at] = got(n) if callable(got) else got[n]
    if give is not None:
        for n, at in other_half(then, flags, out.shape[0]):
            give[n] = out[at]


def load(message, rim, entry, count, cells):
    for n in range(count):
        message[rim + n // 2 * 8 : rim + n // 2 * 8 + 8, n % 2 * 128 : n % 2 * 128 + 128] = entry(n)
    at = rim + count // 2 * 8
    wide = message.shape[1]
    for k, row in enumerate(cells):
        for m in range(row.shape[1] // 128):
            lane = k * row.shape[1] + m * 128
            message[at + lane // wide : at + lane // wide + 1, lane % wide : lane % wide + 128] = (
                row[:, m * 128 : m * 128 + 128])


def unload(message, rim, count, rows, slots):
    wide = message.shape[1]
    at = rim + count // 2 * 8

    def entry(n):
        return message[rim + n // 2 * 8 : rim + n // 2 * 8 + 8, n % 2 * 128 : n % 2 * 128 + 128]

    cells = []
    for k in range(rows):
        tiles = []
        for m in range(slots // 128):
            lane = k * slots + m * 128
            tiles.append(message[at + lane // wide : at + lane // wide + 1,
                                 lane % wide : lane % wide + 128])
        cells.append(jnp.concatenate(tiles, axis=1) if len(tiles) > 1 else tiles[0])
    return entry, cells


def trade_kernel(stage, then, flags, mine, got, out, give):
    trade(stage, then, flags, mine, got, out, give)


def source_kernel(step, full, flags, src, wave, out):
    size, depth = out.shape
    count = src.shape[0]
    shift = (depth - 1).bit_length()
    plane = shift + (full - 1).bit_length()
    rows = size // COLS
    lane = lax.broadcasted_iota(jnp.int32, (1, count), 1)
    sub = lax.broadcasted_iota(jnp.int32, (count, 1), 0)
    row = jnp.zeros((1, count), jnp.int32)
    deep = jnp.zeros((count, 1), jnp.int32)
    size_of = jnp.zeros((count, 1), F32)
    for n in range(count):
        cell = src[n]
        i = jnp.right_shift(cell, plane) - flags[1] * rows
        x = jnp.bitwise_and(jnp.right_shift(cell, shift), full - 1)
        x = x - (2 * flags[3] + flags[0]) * COLS
        ok = (i >= 0) & (i < rows) & (x >= 0) & (x < COLS)
        row = jnp.where(lane == n, jnp.where(ok, place_of(flags, size, i, x), -1), row)
        deep = jnp.where(sub == n, jnp.bitwise_and(cell, depth - 1), deep)
        size_of = jnp.where(sub == n, wave[step, n], size_of)
    spot = lax.broadcasted_iota(jnp.int32, (size, count), 0) == row
    spot = spot.astype(F32).astype(BF16)
    high, low = split(jnp.where(
        lax.broadcasted_iota(jnp.int32, (count, depth), 1) == deep, size_of, 0.0))
    out[...] = mm(spot, high) + mm(spot, low)


def forward_inner_kernel(step, full, flags, src, wave, cur, prev, k0, ki, kx, kz, cm, near, deep,
                         before, part, change):
    source_kernel(step, full, flags, src, wave, change)
    inner(cur, prev, k0, ki, kx, kz, cm, near, deep, change, part)
    change[...] = (cur[...] - prev[...]) - (prev[...] - before[...])


def outer_kernel(flags, part, k0, ki, kx, zm, ym, side, edge, new, zo, co, yo):
    outer(flags, part, k0, ki, kx, zm, ym, side, edge, new)
    rims(flags, new, zo, co, yo)


def pack_kernel(stage, flags, counts, cells, traces, cells_out, lists, give, counts_v, cells_v, traces_v,
                sems):
    pairs = ((counts, counts_v), (cells, cells_v), (traces, traces_v))
    copies = [pltpu.make_async_copy(a, b, sems.at[n]) for n, (a, b) in enumerate(pairs)]
    for copy in copies:
        copy.start()
    for copy in copies:
        copy.wait()
    subs, n = counts.shape[1], cells.shape[1]
    shape = (subs, n)
    lane = lax.broadcasted_iota(jnp.int32, shape, 1)
    mine = lane // CAP == lax.broadcasted_iota(jnp.int32, shape, 0)
    live = mm(counts_v[...].astype(F32).astype(BF16), mine.astype(F32).astype(BF16))
    slot = jnp.bitwise_and(lane[0:1], CAP - 1)
    cells_out[...] = jnp.where(slot.astype(F32) < live, cells_v[...].astype(F32), -1.0)
    for m in range(subs):
        q, y, c = m >> 2, (m >> 1) & 1, m & 1
        start = ((2 * q + c) * 2 + y) * CAP
        tile = traces_v[:, start // 128 * 128 : start // 128 * 128 + 128]
        lists[m] = pltpu.roll(tile, (128 - start % 128) % 128, axis=1) if start % 128 else tile
    for n, at in other_half(stage, flags, subs):
        give[n] = lists[at]


def core_stage_kernel(flags, part, k0, ki, kx, zm, ym, side, edge, lists, cells, cm, new, zo, co, yo,
                      lists_out, pair):
    outer(flags, part, k0, ki, kx, zm, ym, side, edge, new)
    count, half = lists.shape[0] // 2, new.shape[0] // 2
    entry, (theirs,) = unload(cm, half, count, 1, cells.shape[1])
    trade(0, None, flags, lists, entry, lists_out)
    mine = cells[...]
    pair[0:1] = jnp.where(flags[0] == 0, mine, theirs)
    pair[1:2] = jnp.where(flags[0] == 0, theirs, mine)
    rims(flags, new, zo, co, yo.at[pl.ds(0, 32)])
    at = [k for n, k in other_half(1, flags, lists.shape[0])]
    load(yo, 32, lambda n: lists_out[at[n]], count, [pair[0:1], pair[1:2]])


def y_stage_kernel(flags, part, k0, ki, kx, zm, ym, side, edge, lists, pair, other, new, zo, co, yo,
                   lists_out, cells):
    outer(flags, part, k0, ki, kx, zm, ym, side, edge, new)
    for n, field in enumerate((new, other)):
        rims(flags, field, zo.at[n], co.at[n], yo.at[n])
    entry, theirs = unload(ym, 32, lists.shape[0] // 2, 2, pair.shape[1])
    trade(1, None, flags, lists, entry, lists_out)
    away = flags[0] != flags[1]
    low = jnp.where(away, theirs[0], pair[0:1])
    high = jnp.where(away, theirs[1], pair[1:2])
    cells[...] = jnp.where(flags[1] == 0, low, high)


def lists_kernel(flags, lists, cells, spot, pick, at, obs):
    size, n = spot.shape
    depth = at.shape[1]
    subs, steps = lists.shape[0], obs.shape[1]
    cell = cells[...]
    along = jnp.floor((cell + 0.5) * (1.0 / depth))
    place = along.astype(jnp.int32)
    place = jnp.where(place < 0, -1, place_of(
        flags, size, jnp.right_shift(place, 3), jnp.bitwise_and(place, COLS - 1)))
    same = lax.broadcasted_iota(jnp.int32, (n, n), 0) == lax.broadcasted_iota(jnp.int32, (n, n), 1)

    def column(row):
        return jnp.sum(jnp.where(same, row, 0.0), axis=1, keepdims=True).astype(jnp.int32)

    hot = lax.broadcasted_iota(jnp.int32, (size, n), 0) == place
    spot[...] = hot.astype(F32).astype(BF16)
    hot = lax.broadcasted_iota(jnp.int32, (n, size), 1) == column(place.astype(F32))
    pick[...] = hot.astype(F32).astype(BF16)
    hot = lax.broadcasted_iota(jnp.int32, (n, depth), 1) == column(cell - along * depth)
    at[...] = hot.astype(F32)
    traces = lists[...].reshape(subs * steps, 128).T[0:CAP]
    for s in range(subs):
        obs[s * CAP : s * CAP + CAP, :] = traces[:, s * steps : s * steps + steps]


def injection(t, state, spot, pick, at, obs):
    high, low = split(state[...])
    seen = at[...] * (mm(pick[...], high) + mm(pick[...], low))
    residual = jnp.sum(seen, axis=1, keepdims=True) - obs[:, t : t + 1]
    high, low = split(at[...] * residual)
    return mm(spot[...], high) + mm(spot[...], low)


def adjoint_inner_kernel(t, flags, cur, prev, k0, ki, kx, kz, cm, near, deep, state, spot, pick,
                         at, obs, *rest):
    if len(rest) == 4:
        change, image, part, image_out = rest
        image_out[...] = cur[...] * change[...] + image[...]
    else:
        now, mid, before, part, image_out = rest
        image_out[...] = cur[...] * ((now[...] - mid[...]) - (mid[...] - before[...]))
    inj = injection(t, state, spot, pick, at, obs)
    inner(cur, prev, k0, ki, kx, kz, cm, near, deep, inj, part)


def adjoint_first_kernel(flags, cur, prev, k0, ki, kx, kz, cm, near, deep, part):
    inner(cur, prev, k0, ki, kx, kz, cm.at[1], near, deep, None, part)


def turn_kernel(t, flags, part, k0, ki, kx, zm, ym, side, edge, u_part, u_zm, u_ym, spot, pick, at, obs, new, u_new, zo, co, yo):
    outer(flags, part, k0, ki, kx, zm, ym, side, edge, new)
    outer(flags, u_part, k0, ki, kx, u_zm.at[1], u_ym.at[1], side, edge, u_new)
    u_new[...] += injection(t, new, spot, pick, at, obs)
    rims(flags, u_new, zo, co, yo)


def last_kernel(scale, flags, part, k0, ki, kx, zm, ym, side, edge, image, change, vel,
                prev, states, mine, other):
    new = states.at[1]
    outer(flags, part, k0, ki, kx, zm, ym, side, edge, new)
    raw = from_halves(flags, (image[...] + new[...] * change[...]) * scale / vel[...])
    new[...] = from_halves(flags, new[...])
    states[0] = from_halves(flags, prev[...])
    count, height, lanes = mine.shape
    chunk = raw.shape[1] // (2 * count)
    for n in range(count):
        even, odd = (
            jnp.concatenate(
                [raw[g * height : g * height + height, m * chunk : m * chunk + chunk]
                 for g in range(lanes // chunk)], axis=1)
            for m in (2 * n, 2 * n + 1))
        mine[n] = jnp.where(flags[0] == 0, even, odd)
        other[n] = jnp.where(flags[0] == 0, odd, even)


def join_kernel(flags, mine, got, *outs):
    for s, out in enumerate(outs):
        to = jnp.bitwise_xor(flags[3], s)
        a, b = mine[to], got[to]
        out[0] = jnp.where(flags[0] == 0, a, b)
        out[1] = jnp.where(flags[0] == 0, b, a)


def filter_kernel(flags, *refs):
    *pieces, out = refs
    pieces = pieces[::-1]
    height, lanes = pieces[0].shape[1:]
    chunk, rows, full = out.shape
    groups = lanes // chunk
    q = flags[3]
    shape = (full, full)
    y = lax.broadcasted_iota(jnp.int32, shape, 1)
    at = lax.broadcasted_iota(jnp.int32, shape, 0)
    within = jnp.bitwise_and(at, 2 * COLS - 1)
    place = jnp.bitwise_xor(q * (2 * COLS), at - within) + within
    weights = jnp.exp(jnp.abs(y - place).astype(F32) * (-1.0 / SMOOTH))
    weights = split(weights / jnp.sum(weights, axis=0, keepdims=True))
    ready = []
    for n in range(height // COLS):
        here = slice(n * COLS, n * COLS + COLS)
        lines = jnp.concatenate([piece[b, here, :] for piece in pieces for b in range(2)], axis=0)
        high, low = split(lines.T)
        done = mm(high, weights[0]) + mm(low, weights[0]) + mm(high, weights[1])
        ready.append(done)
    for g in range(groups):
        lines = jnp.stack([done[g * chunk : g * chunk + chunk] for done in ready], axis=0)
        out[:, g * (rows // groups) : (g + 1) * (rows // groups), :] = jnp.swapaxes(lines, 0, 1)


def shaped(*shape):
    return jax.ShapeDtypeStruct(shape, F32)


class Flags:
    def __getitem__(self, n):
        if n == 0:
            return lax.axis_index("inline")
        xline = lax.axis_index("xline")
        if n == 1:
            return jnp.bitwise_and(xline, 1)
        if n == 3:
            return jnp.right_shift(xline, 1)
        place = 2 * xline + lax.axis_index("inline")
        return jnp.bitwise_and(jnp.right_shift(place, n - 4), 1)


def call(kernel, name, outs, *args, weight=0, far=0, scalars=0, scratch=()):
    specs = [pl.BlockSpec(memory_space=pltpu.SMEM)] * scalars
    specs += [pl.BlockSpec(memory_space=pl.ANY)] * far
    specs += [pl.BlockSpec(memory_space=pltpu.VMEM)] * (len(args) - scalars - far)
    return pl.pallas_call(
        functools.partial(kernel, Flags()),
        name=name,
        out_shape=outs,
        in_specs=specs,
        out_specs=[pl.BlockSpec(memory_space=pltpu.VMEM)] * len(outs),
        scratch_shapes=list(scratch) + ([pltpu.SemaphoreType.DMA((far,))] if far else []),
        compiler_params=pltpu.CompilerParams(vmem_limit_bytes=VMEM_BYTES),
        cost_estimate=pl.CostEstimate(
            flops=1000, bytes_accessed=1000 + int(weight * 3_600_000), transcendentals=0),
    )(*args)


def per_device(plan, fwd_now, fwd_before, adj_now, adj_before, velocity, log_density, observed,
               rec_cells, rec_counts, src_cell, wavelet):
    rows, cols, depth = fwd_now.shape
    size = rows * cols
    steps = wavelet.shape[0]
    nx, nq = plan.nx, plan.nq
    subs = 2 * nx
    xline, c = lax.axis_index("xline"), lax.axis_index("inline")
    q, y = xline // 2, xline % 2
    keep = y == c
    z_perm, c_perm, y_perm, swap_perm = plan.z(), plan.core(), plan.y(), plan.swap()
    stages = [(c_perm, c), (y_perm, y)]
    stages += [(plan.flip(1 << b), (q >> b) & 1) for b in range((nq - 1).bit_length())]
    field = shaped(size, depth)
    rim = [shaped(size // 2, depth), shaped(size // 2, depth), shaped(4 * cols, depth)]

    deep = depth_matrix(depth)
    deep = jnp.asarray(np.concatenate([deep, deep]), BF16)
    inside = jnp.where(c == 0, q > 0, q < nq - 1)
    near = [near_matrix(GROUP, cols, k) for k in range(2)]
    wide = (GROUP + 8) * cols
    near = [np.concatenate([m[:, :wide], m[:, :wide], m[:, wide:], m[:, wide:]], axis=1) for m in near]
    near = jnp.where(c == 0, jnp.asarray(near[0], F32), jnp.asarray(near[1], F32)).astype(BF16)
    side = [side_matrix(rows, k) for k in range(2)]
    side = jnp.where(c == 0, jnp.asarray(side[0], BF16), jnp.asarray(side[1], BF16))
    side = jnp.where(inside, side, jnp.zeros_like(side))
    side = jnp.concatenate([side, side], axis=1)
    edge = [edge_matrix(k) for k in range(2)]
    edge = jnp.where(y == 0, jnp.asarray(edge[0], F32), jnp.asarray(edge[1], F32)).astype(BF16)
    edge = jnp.concatenate([edge, edge], axis=1)

    def halo(zo, co, yo):
        return send(zo, z_perm), send(co, c_perm), send(yo, y_perm)

    def after(value, *deps):
        return lax.optimization_barrier((value,) + deps)[0]

    def flat(value):
        return value.reshape(size, depth)

    log_density, fwd_now, velocity = flat(log_density), flat(fwd_now), flat(velocity)
    fwd_before, adj_now, adj_before = flat(fwd_before), flat(adj_now), flat(adj_before)
    got = [send(v, swap_perm) for v in (log_density, fwd_now)]
    stacked = jnp.stack([velocity, fwd_before])
    got_model = send(stacked, swap_perm)
    full = nx * cols
    inj, = call(functools.partial(source_kernel, 0, full), "source", [field], src_cell, wavelet,
                weight=0.7, scalars=2)
    got[0], inj = lax.optimization_barrier((got[0], inj))
    slots = subs * CAP
    entries, half_entries = shaped(subs, steps, 128), shaped(subs // 2, steps, 128)
    order = [*range(2, len(stages)), 0]
    cells, lists, give = call(
        functools.partial(pack_kernel, order[0]), "pack", [shaped(1, slots), entries, half_entries], after(rec_counts, stacked),
        rec_cells, observed, weight=0.2, far=3,
        scratch=[pltpu.VMEM(rec_counts.shape, jnp.int32), pltpu.VMEM(rec_cells.shape, jnp.int32),
                 pltpu.VMEM(observed.shape, F32)])
    vel, p_before = call(settle_pair_kernel, "settle_model", [field, field],
                         velocity, fwd_before, got_model, weight=0.6, far=2)
    for n, bit in enumerate(order[:-1]):
        lists, give = call(
            functools.partial(trade_kernel, bit, order[n + 1]), "trade", [entries, half_entries],
            after(lists, vel) if n == len(order) - 2 else lists, send(give, stages[bit][0]),
            weight=0.1)
        if n == 0:
            got[0], give = lax.optimization_barrier((got[0], give))

    density, p_now, *out = call(settle_kernel, "settle",
                                [field, field] + [shaped(2, *r.shape) for r in rim],
                                log_density, fwd_now, *got, far=2)
    zm, cm, ym = halo(*out)
    parts = call(first_inner_kernel, "first_inner", [field] * 7, density, p_now, cm,
                 near, deep, weight=1.3)
    got_adjoint = [send(after(v, parts[0]), swap_perm) for v in (adj_now, adj_before)]

    riders = subs // 4 * 8 + 8
    core_rim = shaped(size // 2 + riders, depth)
    y_rim = shaped(4 * cols + riders, depth)

    new, zo, co, yo, k0, ki, kx, kz = call(
        first_outer_kernel, "first_outer", [field, rim[0], core_rim, rim[2]] + [field] * 4,
        p_now, p_before, vel, *parts, inj, zm, ym, side, edge, give, cells)
    model = (k0, ki, kx, kz)
    states = [p_before, p_now, new]
    changes = []
    zm, cm, ym = halo(zo, co, yo)
    for t in range(1, steps):
        cur, prev, before = states[:-4:-1]
        part, change = call(
            functools.partial(forward_inner_kernel, t, full), "forward_inner", [field, field], src_cell, wavelet, cur, prev, *model, cm, near, deep, before, weight=1.2, scalars=2)
        changes.append(change)
        args = [part, k0, ki, kx, zm, ym, side, edge]
        if t == steps - 3:
            u_part, = call(adjoint_first_kernel, "adjoint_first", [field], u_now, u_before,
                           *model, u_cm, near, deep, weight=1.1)
            args[0] = after(part, u_part)
        if t == steps - 2:
            receivers = call(
                lists_kernel, "lists",
                [jax.ShapeDtypeStruct((size, slots), BF16),
                 jax.ShapeDtypeStruct((slots, size), BF16), shaped(slots, depth),
                 shaped(slots, steps)], lists, cells, weight=0.3)
            args[0] = after(part, receivers[0])
        if t == steps - 1:
            new, u_new, *out = call(
                functools.partial(turn_kernel, t), "turn", [field, field] + rim, *args, u_part,
                u_zm, u_ym, *receivers)
            states.append(new)
            break
        if t == 1:
            u_now, u_before = call(settle_pair_kernel, "settle_adjoint", [field, field], adj_now,
                                   adj_before, *got_adjoint, weight=0.6, far=2)
            args[0] = after(part, u_now)
            new, *out, lists, pair = call(
                core_stage_kernel, "forward_outer",
                [field, rim[0], rim[1], y_rim, entries, shaped(2, slots)], *args, lists, cells, cm)
            states.append(new)
            zm, cm, ym = halo(*out)
            continue
        if t == 2:
            new, *out, lists, cells = call(
                y_stage_kernel, "forward_outer",
                [field] + [shaped(2, *r.shape) for r in rim] + [entries, shaped(1, slots)],
                *args, lists, pair, u_now)
            states.append(new)
            zm, cm, ym = halo(*out)
            u_zm, u_cm, u_ym = zm, cm, ym
            continue
        new, *out = call(outer_kernel, "forward_outer", [field] + rim, *args)
        states.append(new)
        zm, cm, ym = halo(*out)

    zm, cm, ym = halo(*out)
    u_before, u_now = u_now, u_new
    image = []
    chunk = depth // nx
    half = shaped(nq, size * chunk // 128, 128)
    for j in range(1, steps):
        t = steps - 1 - j
        terms = [changes[t + 1], *image] if image else states[:-4:-1]
        part, *image = call(
            functools.partial(adjoint_inner_kernel, t), "adjoint_inner", [field, field], u_now, u_before, *model, cm, near, deep, states[t + 2], *receivers, *terms, weight=1.5)
        args = [part, k0, ki, kx, zm, ym, side, edge]
        if j == steps - 1:
            final, mine, other = call(
                functools.partial(last_kernel, 2.0 / steps), "last",
                [shaped(2, *field.shape), half, half], *args, *image, changes[0], vel, u_now)
            break
        u_before = u_now
        u_now, *out = call(outer_kernel, "adjoint_outer", [field] + rim,
                           *args)
        zm, cm, ym = halo(*out)

    got = send(final, swap_perm)
    pieces = call(join_kernel, "join", [shaped(2, *half.shape[1:])] * nq, mine,
                  send(other, c_perm))
    pieces = [send(pieces[s], plan.spread(s)) for s in reversed(range(nq))][::-1]
    adj_prev, adj_out = call(select_kernel, "select", [field, field], final, got, weight=1.2)
    gradient, = call(filter_kernel, "filter", [shaped(chunk, rows, nx * cols)],
                     after(pieces[-1], adj_out), *pieces[-2::-1])
    block = (rows, cols, depth)
    return gradient, adj_out.reshape(block), adj_prev.reshape(block)


def solution(mesh):
    field = P(("shots", "inline"), "xline", None)
    model = P("inline", "xline", None)
    lists = P(("xline", "inline"), None)
    return jax.shard_map(
        functools.partial(per_device, Plan(mesh)),
        mesh=mesh,
        in_specs=(field, field, field, field, model, model, P("shots", ("xline", "inline")),
                  lists, lists, P("shots"), P("shots", None)),
        out_specs=(P(("shots", "xline"), "inline", None), field, field),
        check_vma=False,
    )
```

```python
import functools

import jax
import jax.numpy as jnp
import numpy as np
from jax import lax
from jax.experimental import pallas as pl
from jax.experimental.pallas import tpu as pltpu
from jax.sharding import PartitionSpec as P

CAP = 8
SMOOTH = 16
SECOND = (-205.0 / 72.0, 8.0 / 5.0, -1.0 / 5.0, 8.0 / 315.0, -1.0 / 560.0)
FIRST = (4.0 / 5.0, -1.0 / 5.0, 4.0 / 105.0, -1.0 / 280.0)
ALL = ("shots", "xline", "inline")
COLS = 8
GROUP = 8
VMEM_BYTES = 8 * 1024 * 1024
F32 = jnp.float32
BF16 = jnp.bfloat16


class Plan:
    def __init__(self, mesh):
        self.shots = mesh.shape["shots"]
        self.nx = mesh.shape["xline"]
        self.nq = self.nx // 2

    def index(self, s, q, y, c):
        return (s * self.nx + 2 * q + y) * 2 + c

    def perm(self, partner):
        pairs = []
        for s in range(self.shots):
            for q in range(self.nq):
                for y in range(2):
                    for c in range(2):
                        t = partner(q, y, c)
                        dst = self.index(s ^ 1, q, y, c) if t is None else self.index(s, *t)
                        pairs.append((self.index(s, q, y, c), dst))
        return pairs

    def swap(self):
        return self.perm(lambda q, y, c: None if y == c else (q, c, y))

    def z(self):
        def partner(q, y, c):
            other = q + 1 if c == 1 else q - 1
            return (other, y, 1 - c) if 0 <= other < self.nq else None

        return self.perm(partner)

    def core(self):
        return self.perm(lambda q, y, c: (q, y, 1 - c))

    def y(self):
        return self.perm(lambda q, y, c: (q, 1 - y, c))

    def flip(self, bit):
        return self.perm(lambda q, y, c: (q ^ bit, y, c) if (q ^ bit) < self.nq else None)

    def spread(self, shift):
        return self.perm(lambda q, y, c: (q ^ shift, c, y))


def send(value, pairs):
    return lax.ppermute(value, ALL, pairs)


def depth_matrix(n):
    m = np.zeros((n, 2 * n), np.float32)
    for k in range(1, 5):
        for j in range(n):
            for i, sign in ((j + k, 1.0), (j - k, -1.0)):
                if 0 <= i < n:
                    m[i, j] = round(SECOND[k] * 5040)
                    m[i, n + j] = sign * round(FIRST[k - 1] * 840)
    return m


def stencil_matrix(rows, cols):
    own = (rows + 8) * cols
    m = np.zeros((3, rows, cols, own + rows * 8), np.float32)
    for i in range(rows):
        for x in range(cols):
            for k in range(1, 5):
                total = round(SECOND[k] * 5040)
                slope = round(FIRST[k - 1] * 840)
                for sign in (1, -1):
                    at = (i + 4 + sign * k) * cols + x
                    m[0, i, x, at] += total
                    m[1, i, x, at] += sign * slope
                    to = x + sign * k
                    if to < 0:
                        at = own + i * 4 + to + 4
                    elif to >= cols:
                        at = own + rows * 4 + i * 4 + to - cols
                    else:
                        at = (i + 4) * cols + to
                    m[0, i, x, at] += total
                    m[2, i, x, at] += sign * slope
    return m.reshape(3 * rows * cols, own + rows * 8)


def halved(rows, cols, c):
    at = np.arange(rows)[:, None] * cols
    z_side = (at + 4 * c + np.arange(4)).reshape(-1)
    return np.concatenate([z_side, (at + 4 * (1 - c) + np.arange(4)).reshape(-1)])


def near_matrix(rows, cols, c):
    m = stencil_matrix(rows, cols)
    own = (rows + 8) * cols
    place = halved(rows, cols, c)
    out = np.concatenate([place + k * rows * cols for k in range(3)])
    side = own + (1 - c) * rows * 4 + np.arange(rows * 4)
    return m[out][:, np.concatenate([halved(rows + 8, cols, c), side])]


def side_matrix(rows, c):
    m = np.zeros((2, rows, 4, rows, 4), np.float32)
    for x in range(4):
        for k in range(4):
            d = x + 4 - k if c == 0 else k + 4 - x
            if d <= 4:
                for i in range(rows):
                    m[0, i, x, i, k] = round(SECOND[d] * 5040)
                    m[1, i, x, i, k] = round(FIRST[d - 1] * 840) * (-1 if c == 0 else 1)
    return m.reshape(2 * rows * 4, rows * 4)


def edge_matrix(y):
    m = np.zeros((2, 2, 4, 4, 2, 4, 4), np.float32)
    for i in range(4):
        for k in range(4):
            d = i + 4 - k if y == 1 else k + 4 - i
            if d <= 4:
                for part in range(2):
                    for x in range(4):
                        m[0, part, i, x, part, k, x] = round(SECOND[d] * 5040)
                        m[1, part, i, x, part, k, x] = round(FIRST[d - 1] * 840) * (-1 if y == 1 else 1)
    return m.reshape(64, 32)


def split(value):
    high = value.astype(BF16)
    return high, (value - high.astype(F32)).astype(BF16)


def mm(a, b):
    return jnp.dot(a, b, preferred_element_type=F32)


def inner_differences(cur, cm, near, deep):
    size, depth = cur.shape
    half = size // 2
    cm = cm.at[0] if len(cm.shape) == 3 else cm
    own = split(cur[...])
    along = mm(jnp.concatenate(own, axis=1), deep[...])
    blank = jnp.zeros((16, depth), BF16)
    ext = [[jnp.concatenate([blank, part[h * half : h * half + half], blank], axis=0)
            for h in range(2)] for part in own]
    from_c = split(cm[0:half])
    step = GROUP * 4
    for n in range(half // step):
        rhs = [part[h][n * step : n * step + step + 32] for part in ext for h in range(2)]
        rhs += [part[n * step : n * step + step] for part in from_c]
        out = mm(near[...], jnp.concatenate(rhs, axis=0))
        for h in range(2):
            here = slice(h * half + n * step, h * half + n * step + step)
            sums, di, dx = (out[(2 * k + h) * step : (2 * k + h + 1) * step] for k in range(3))
            yield here, sums, along[here, 0:depth], di, dx, along[here, depth:]


def side_differences(zm, side):
    zm = zm.at[0] if len(zm.shape) == 3 else zm
    out = mm(side[...], jnp.concatenate(split(zm[...]), axis=0))
    half = out.shape[0] // 2
    return out[0:half], out[half:]


def edge_differences(flags, size, ym, edge):
    ym = ym.at[0] if len(ym.shape) == 3 else ym
    out = mm(edge[...], jnp.concatenate(split(ym[0:32]), axis=0))
    start = jnp.where(flags[1] == 1, 0, size // 2 - 16)
    for h in range(2):
        at = pl.ds(pl.multiple_of(start + h * (size // 2), 16), 16)
        yield at, out[h * 16 : h * 16 + 16], out[32 + h * 16 : 48 + h * 16]


def to_halves(flags, value):
    rows, depth = value.shape
    pairs = value.reshape(rows // (2 * COLS), 2, COLS, depth)
    a, b = pairs[:, 0], pairs[:, 1]
    low = lax.broadcasted_iota(jnp.int32, a.shape, 1) < 4
    first = jnp.where(low, a, pltpu.roll(b, 4, axis=1)).reshape(rows // 2, depth)
    last = jnp.where(low, pltpu.roll(a, 4, axis=1), b).reshape(rows // 2, depth)
    return jnp.where(flags[0] == 0, first, last), jnp.where(flags[0] == 0, last, first)


def from_halves(flags, value):
    rows, depth = value.shape
    z_side, c_side = value[0 : rows // 2], value[rows // 2 :]
    shape = (rows // (2 * COLS), COLS, depth)
    first = jnp.where(flags[0] == 0, z_side, c_side).reshape(shape)
    last = jnp.where(flags[0] == 0, c_side, z_side).reshape(shape)
    low = lax.broadcasted_iota(jnp.int32, shape, 1) < 4
    a = jnp.where(low, first, pltpu.roll(last, 4, axis=1))
    b = jnp.where(low, pltpu.roll(first, 4, axis=1), last)
    return jnp.stack([a, b], axis=1).reshape(rows, depth)


def place_of(flags, size, i, x):
    near = x - 4 * flags[0]
    return i * 4 + jnp.where((near >= 0) & (near < 4), near, size // 2 + x - 4 * (1 - flags[0]))


def rims(flags, new, zo, co, yo):
    size = new.shape[0]
    half = size // 2
    zo[...] = new[0:half]
    co[...] = new[half:]
    last = jnp.concatenate([new[half - 16 : half], new[size - 16 :]], axis=0)
    first = jnp.concatenate([new[0:16], new[half : half + 16]], axis=0)
    yo[...] = jnp.where(flags[1] == 0, last, first)


def choose(flags, pairs, sems):
    keep = flags[0] == flags[1]

    @pl.when(keep)
    def _():
        copies = [pltpu.make_async_copy(own, out, sems.at[n])
                  for n, (own, recv, out) in enumerate(pairs)]
        for copy in copies:
            copy.start()
        for copy in copies:
            copy.wait()

    @pl.when(jnp.logical_not(keep))
    def _():
        for own, recv, out in pairs:
            out[...] = recv[...]

    for own, recv, out in pairs:
        half = out.shape[0] // 2
        z_side, c_side = to_halves(flags, out[...])
        out[0:half] = z_side
        out[half:] = c_side


def settle_kernel(flags, a, b, recv_a, recv_b, a_out, b_out, zo, co, yo, sems):
    choose(flags, [(a, recv_a, a_out), (b, recv_b, b_out)], sems)
    for n, out in enumerate((a_out, b_out)):
        rims(flags, out, zo.at[n], co.at[n], yo.at[n])


def settle_pair_kernel(flags, a, b, *rest):
    *recv, a_out, b_out, sems = rest
    recv = recv if len(recv) == 2 else (recv[0].at[0], recv[0].at[1])
    choose(flags, [(a, recv[0], a_out), (b, recv[1], b_out)], sems)


def select_kernel(flags, own, recv, *outs):
    keep = flags[0] == flags[1]
    for n, out in enumerate(outs):
        out[...] = jnp.where(keep, own[n], recv[n])


def first_inner_kernel(flags, lr, cur, cm, near, deep, *outs):
    ri, rx, rz, sums_out, di_out, dx_out, dz_out = outs
    for here, spare, spare_z, di, dx, dz in inner_differences(lr, cm.at[0], near, deep):
        ri[here], rx[here], rz[here] = di, dx, dz
    for here, sums, sums_z, di, dx, dz in inner_differences(cur, cm.at[1], near, deep):
        sums_out[here] = sums + sums_z + (3.0 * SECOND[0] * 5040) * cur[here]
        di_out[here], dx_out[here], dz_out[here] = di, dx, dz


def first_outer_kernel(flags, cur, prev, vel, ri, rx, rz, sums, di, dx, dz, inj, zm, ym, side,
                       edge, give, cells, new, zo, co, yo, k0, ki, kx, kz):
    size = cur.shape[0]
    half = size // 2
    kz[...], ki[...], kx[...] = sums[...], di[...], dx[...]
    k0[...], new[...] = ri[...], rx[...]
    more, more_x = side_differences(zm.at[1], side)
    kz[0:half] += more
    kx[0:half] += more_x
    spare, more_x = side_differences(zm.at[0], side)
    new[0:half] += more_x
    for here, more, more_i in edge_differences(flags, size, ym.at[1], edge):
        kz[here] += more
        ki[here] += more_i
    for here, spare, more_i in edge_differences(flags, size, ym.at[0], edge):
        k0[here] += more_i
    for n in range(4):
        here = slice(n * (size // 4), (n + 1) * (size // 4))
        square = vel[here] * vel[here]
        scaled = square * (1.0 / (840 * 840))
        factor = square * (1.0 / 5040)
        along_i, along_x, along_z = scaled * k0[here], scaled * new[here], scaled * rz[here]
        change = factor * kz[here] - (
            along_i * ki[here] + along_x * kx[here] + along_z * dz[here])
        k0[here], ki[here], kx[here], kz[here] = factor, along_i, along_x, along_z
        center = cur[here]
        new[here] = (center - prev[here]) + (center + (change + inj[here]))
    rims(flags, new, zo, co.at[pl.ds(0, half)], yo)
    load(co, half, lambda n: give[n], give.shape[0], [cells[...]])


def inner(cur, prev, k0, ki, kx, kz, cm, near, deep, inj, out):
    for here, sums, sums_z, di, dx, dz in inner_differences(cur, cm, near, deep):
        center = cur[here]
        change = k0[here] * ((sums + sums_z) + (3.0 * SECOND[0] * 5040) * center)
        change = change - (ki[here] * di + kx[here] * dx + kz[here] * dz)
        if inj is not None:
            change = change + inj[here]
        out[here] = (center - prev[here]) + (center + change)


def outer(flags, part, k0, ki, kx, zm, ym, side, edge, new):
    size = part.shape[0]
    half = size // 2
    sums, dx = side_differences(zm, side)
    new[0:half] = part[0:half] + (k0[0:half] * sums - kx[0:half] * dx)
    new[half:] = part[half:]
    for here, sums, di in edge_differences(flags, size, ym, edge):
        new[here] += k0[here] * sums - ki[here] * di


def other_half(stage, flags, count):
    other = 1 - flags[4 + stage]
    for n in range(count // 2):
        high, low = n >> stage, n & ((1 << stage) - 1)
        yield n, (high << (stage + 1)) + (other << stage) + low


def trade(stage, then, flags, mine, got, out, give=None):
    out[...] = mine[...]
    for n, at in other_half(stage, flags, out.shape[0]):
        out[at] = got(n) if callable(got) else got[n]
    if give is not None:
        for n, at in other_half(then, flags, out.shape[0]):
            give[n] = out[at]


def load(message, rim, entry, count, cells):
    for n in range(count):
        message[rim + n // 2 * 8 : rim + n // 2 * 8 + 8, n % 2 * 128 : n % 2 * 128 + 128] = entry(n)
    at = rim + count // 2 * 8
    wide = message.shape[1]
    for k, row in enumerate(cells):
        for m in range(row.shape[1] // 128):
            lane = k * row.shape[1] + m * 128
            message[at + lane // wide : at + lane // wide + 1, lane % wide : lane % wide + 128] = (
                row[:, m * 128 : m * 128 + 128])


def unload(message, rim, count, rows, slots):
    wide = message.shape[1]
    at = rim + count // 2 * 8

    def entry(n):
        return message[rim + n // 2 * 8 : rim + n // 2 * 8 + 8, n % 2 * 128 : n % 2 * 128 + 128]

    cells = []
    for k in range(rows):
        tiles = []
        for m in range(slots // 128):
            lane = k * slots + m * 128
            tiles.append(message[at + lane // wide : at + lane // wide + 1,
                                 lane % wide : lane % wide + 128])
        cells.append(jnp.concatenate(tiles, axis=1) if len(tiles) > 1 else tiles[0])
    return entry, cells


def trade_kernel(stage, then, flags, mine, got, out, give):
    trade(stage, then, flags, mine, got, out, give)


def source_kernel(step, full, flags, src, wave, out):
    size, depth = out.shape
    count = src.shape[0]
    shift = (depth - 1).bit_length()
    plane = shift + (full - 1).bit_length()
    rows = size // COLS
    lane = lax.broadcasted_iota(jnp.int32, (1, count), 1)
    sub = lax.broadcasted_iota(jnp.int32, (count, 1), 0)
    row = jnp.zeros((1, count), jnp.int32)
    deep = jnp.zeros((count, 1), jnp.int32)
    size_of = jnp.zeros((count, 1), F32)
    for n in range(count):
        cell = src[n]
        i = jnp.right_shift(cell, plane) - flags[1] * rows
        x = jnp.bitwise_and(jnp.right_shift(cell, shift), full - 1)
        x = x - (2 * flags[3] + flags[0]) * COLS
        ok = (i >= 0) & (i < rows) & (x >= 0) & (x < COLS)
        row = jnp.where(lane == n, jnp.where(ok, place_of(flags, size, i, x), -1), row)
        deep = jnp.where(sub == n, jnp.bitwise_and(cell, depth - 1), deep)
        size_of = jnp.where(sub == n, wave[step, n], size_of)
    spot = lax.broadcasted_iota(jnp.int32, (size, count), 0) == row
    spot = spot.astype(F32).astype(BF16)
    high, low = split(jnp.where(
        lax.broadcasted_iota(jnp.int32, (count, depth), 1) == deep, size_of, 0.0))
    out[...] = mm(spot, high) + mm(spot, low)


def forward_inner_kernel(step, full, flags, src, wave, cur, prev, k0, ki, kx, kz, cm, near, deep,
                         before, part, change):
    source_kernel(step, full, flags, src, wave, change)
    inner(cur, prev, k0, ki, kx, kz, cm, near, deep, change, part)
    change[...] = (cur[...] - prev[...]) - (prev[...] - before[...])


def outer_kernel(flags, part, k0, ki, kx, zm, ym, side, edge, new, zo, co, yo):
    outer(flags, part, k0, ki, kx, zm, ym, side, edge, new)
    rims(flags, new, zo, co, yo)


def pack_kernel(stage, flags, counts, cells, traces, cells_out, lists, give, counts_v, cells_v, traces_v,
                sems):
    pairs = ((counts, counts_v), (cells, cells_v), (traces, traces_v))
    copies = [pltpu.make_async_copy(a, b, sems.at[n]) for n, (a, b) in enumerate(pairs)]
    for copy in copies:
        copy.start()
    for copy in copies:
        copy.wait()
    subs, n = counts.shape[1], cells.shape[1]
    shape = (subs, n)
    lane = lax.broadcasted_iota(jnp.int32, shape, 1)
    mine = lane // CAP == lax.broadcasted_iota(jnp.int32, shape, 0)
    live = mm(counts_v[...].astype(F32).astype(BF16), mine.astype(F32).astype(BF16))
    slot = jnp.bitwise_and(lane[0:1], CAP - 1)
    cells_out[...] = jnp.where(slot.astype(F32) < live, cells_v[...].astype(F32), -1.0)
    for m in range(subs):
        q, y, c = m >> 2, (m >> 1) & 1, m & 1
        start = ((2 * q + c) * 2 + y) * CAP
        tile = traces_v[:, start // 128 * 128 : start // 128 * 128 + 128]
        lists[m] = pltpu.roll(tile, (128 - start % 128) % 128, axis=1) if start % 128 else tile
    for n, at in other_half(stage, flags, subs):
        give[n] = lists[at]


def core_stage_kernel(flags, part, k0, ki, kx, zm, ym, side, edge, lists, cells, cm, new, zo, co, yo,
                      lists_out, pair):
    outer(flags, part, k0, ki, kx, zm, ym, side, edge, new)
    count, half = lists.shape[0] // 2, new.shape[0] // 2
    entry, (theirs,) = unload(cm, half, count, 1, cells.shape[1])
    trade(0, None, flags, lists, entry, lists_out)
    mine = cells[...]
    pair[0:1] = jnp.where(flags[0] == 0, mine, theirs)
    pair[1:2] = jnp.where(flags[0] == 0, theirs, mine)
    rims(flags, new, zo, co, yo.at[pl.ds(0, 32)])
    at = [k for n, k in other_half(1, flags, lists.shape[0])]
    load(yo, 32, lambda n: lists_out[at[n]], count, [pair[0:1], pair[1:2]])


def y_stage_kernel(flags, part, k0, ki, kx, zm, ym, side, edge, lists, pair, other, new, zo, co, yo,
                   lists_out, cells):
    outer(flags, part, k0, ki, kx, zm, ym, side, edge, new)
    for n, field in enumerate((new, other)):
        rims(flags, field, zo.at[n], co.at[n], yo.at[n])
    entry, theirs = unload(ym, 32, lists.shape[0] // 2, 2, pair.shape[1])
    trade(1, None, flags, lists, entry, lists_out)
    away = flags[0] != flags[1]
    low = jnp.where(away, theirs[0], pair[0:1])
    high = jnp.where(away, theirs[1], pair[1:2])
    cells[...] = jnp.where(flags[1] == 0, low, high)


def lists_kernel(flags, lists, cells, spot, pick, at, obs):
    size, n = spot.shape
    depth = at.shape[1]
    subs, steps = lists.shape[0], obs.shape[1]
    cell = cells[...]
    along = jnp.floor((cell + 0.5) * (1.0 / depth))
    place = along.astype(jnp.int32)
    place = jnp.where(place < 0, -1, place_of(
        flags, size, jnp.right_shift(place, 3), jnp.bitwise_and(place, COLS - 1)))
    same = lax.broadcasted_iota(jnp.int32, (n, n), 0) == lax.broadcasted_iota(jnp.int32, (n, n), 1)

    def column(row):
        return jnp.sum(jnp.where(same, row, 0.0), axis=1, keepdims=True).astype(jnp.int32)

    hot = lax.broadcasted_iota(jnp.int32, (size, n), 0) == place
    spot[...] = hot.astype(F32).astype(BF16)
    hot = lax.broadcasted_iota(jnp.int32, (n, size), 1) == column(place.astype(F32))
    pick[...] = hot.astype(F32).astype(BF16)
    hot = lax.broadcasted_iota(jnp.int32, (n, depth), 1) == column(cell - along * depth)
    at[...] = hot.astype(F32)
    traces = lists[...].reshape(subs * steps, 128).T[0:CAP]
    for s in range(subs):
        obs[s * CAP : s * CAP + CAP, :] = traces[:, s * steps : s * steps + steps]


def injection(t, state, spot, pick, at, obs):
    high, low = split(state[...])
    seen = at[...] * (mm(pick[...], high) + mm(pick[...], low))
    residual = jnp.sum(seen, axis=1, keepdims=True) - obs[:, t : t + 1]
    high, low = split(at[...] * residual)
    return mm(spot[...], high) + mm(spot[...], low)


def adjoint_inner_kernel(t, flags, cur, prev, k0, ki, kx, kz, cm, near, deep, state, spot, pick,
                         at, obs, *rest):
    if len(rest) == 4:
        change, image, part, image_out = rest
        image_out[...] = cur[...] * change[...] + image[...]
    else:
        now, mid, before, part, image_out = rest
        image_out[...] = cur[...] * ((now[...] - mid[...]) - (mid[...] - before[...]))
    inj = injection(t, state, spot, pick, at, obs)
    inner(cur, prev, k0, ki, kx, kz, cm, near, deep, inj, part)


def adjoint_first_kernel(flags, cur, prev, k0, ki, kx, kz, cm, near, deep, part):
    inner(cur, prev, k0, ki, kx, kz, cm.at[1], near, deep, None, part)


def turn_kernel(t, flags, part, k0, ki, kx, zm, ym, side, edge, u_part, u_zm, u_ym, spot, pick, at, obs, new, u_new, zo, co, yo):
    outer(flags, part, k0, ki, kx, zm, ym, side, edge, new)
    outer(flags, u_part, k0, ki, kx, u_zm.at[1], u_ym.at[1], side, edge, u_new)
    u_new[...] += injection(t, new, spot, pick, at, obs)
    rims(flags, u_new, zo, co, yo)


def last_kernel(scale, flags, part, k0, ki, kx, zm, ym, side, edge, image, change, vel,
                prev, states, mine, other):
    new = states.at[1]
    outer(flags, part, k0, ki, kx, zm, ym, side, edge, new)
    raw = from_halves(flags, (image[...] + new[...] * change[...]) * scale / vel[...])
    new[...] = from_halves(flags, new[...])
    states[0] = from_halves(flags, prev[...])
    count, height, lanes = mine.shape
    chunk = raw.shape[1] // (2 * count)
    for n in range(count):
        even, odd = (
            jnp.concatenate(
                [raw[g * height : g * height + height, m * chunk : m * chunk + chunk]
                 for g in range(lanes // chunk)], axis=1)
            for m in (2 * n, 2 * n + 1))
        mine[n] = jnp.where(flags[0] == 0, even, odd)
        other[n] = jnp.where(flags[0] == 0, odd, even)


def join_kernel(flags, mine, got, *outs):
    for s, out in enumerate(outs):
        to = jnp.bitwise_xor(flags[3], s)
        a, b = mine[to], got[to]
        out[0] = jnp.where(flags[0] == 0, a, b)
        out[1] = jnp.where(flags[0] == 0, b, a)


def filter_kernel(flags, *refs):
    *pieces, out = refs
    pieces = pieces[::-1]
    height, lanes = pieces[0].shape[1:]
    chunk, rows, full = out.shape
    groups = lanes // chunk
    q = flags[3]
    shape = (full, full)
    y = lax.broadcasted_iota(jnp.int32, shape, 1)
    at = lax.broadcasted_iota(jnp.int32, shape, 0)
    within = jnp.bitwise_and(at, 2 * COLS - 1)
    place = jnp.bitwise_xor(q * (2 * COLS), at - within) + within
    weights = jnp.exp(jnp.abs(y - place).astype(F32) * (-1.0 / SMOOTH))
    weights = split(weights / jnp.sum(weights, axis=0, keepdims=True))
    ready = []
    for n in range(height // COLS):
        here = slice(n * COLS, n * COLS + COLS)
        lines = jnp.concatenate([piece[b, here, :] for piece in pieces for b in range(2)], axis=0)
        high, low = split(lines.T)
        done = mm(high, weights[0]) + mm(low, weights[0]) + mm(high, weights[1])
        ready.append(done)
    for g in range(groups):
        lines = jnp.stack([done[g * chunk : g * chunk + chunk] for done in ready], axis=0)
        out[:, g * (rows // groups) : (g + 1) * (rows // groups), :] = jnp.swapaxes(lines, 0, 1)


def shaped(*shape):
    return jax.ShapeDtypeStruct(shape, F32)


class Flags:
    def __getitem__(self, n):
        if n == 0:
            return lax.axis_index("inline")
        xline = lax.axis_index("xline")
        if n == 1:
            return jnp.bitwise_and(xline, 1)
        if n == 3:
            return jnp.right_shift(xline, 1)
        place = 2 * xline + lax.axis_index("inline")
        return jnp.bitwise_and(jnp.right_shift(place, n - 4), 1)


def call(kernel, name, outs, *args, weight=0, far=0, scalars=0, scratch=()):
    specs = [pl.BlockSpec(memory_space=pltpu.SMEM)] * scalars
    specs += [pl.BlockSpec(memory_space=pl.ANY)] * far
    specs += [pl.BlockSpec(memory_space=pltpu.VMEM)] * (len(args) - scalars - far)
    return pl.pallas_call(
        functools.partial(kernel, Flags()),
        name=name,
        out_shape=outs,
        in_specs=specs,
        out_specs=[pl.BlockSpec(memory_space=pltpu.VMEM)] * len(outs),
        scratch_shapes=list(scratch) + ([pltpu.SemaphoreType.DMA((far,))] if far else []),
        compiler_params=pltpu.CompilerParams(vmem_limit_bytes=VMEM_BYTES),
        cost_estimate=pl.CostEstimate(
            flops=1000, bytes_accessed=1000 + int(weight * 3_600_000), transcendentals=0),
    )(*args)


def per_device(plan, fwd_now, fwd_before, adj_now, adj_before, velocity, log_density, observed,
               rec_cells, rec_counts, src_cell, wavelet):
    rows, cols, depth = fwd_now.shape
    size = rows * cols
    steps = wavelet.shape[0]
    nx, nq = plan.nx, plan.nq
    subs = 2 * nx
    xline, c = lax.axis_index("xline"), lax.axis_index("inline")
    q, y = xline // 2, xline % 2
    keep = y == c
    z_perm, c_perm, y_perm, swap_perm = plan.z(), plan.core(), plan.y(), plan.swap()
    stages = [(c_perm, c), (y_perm, y)]
    stages += [(plan.flip(1 << b), (q >> b) & 1) for b in range((nq - 1).bit_length())]
    field = shaped(size, depth)
    rim = [shaped(size // 2, depth), shaped(size // 2, depth), shaped(4 * cols, depth)]

    deep = depth_matrix(depth)
    deep = jnp.asarray(np.concatenate([deep, deep]), BF16)
    inside = jnp.where(c == 0, q > 0, q < nq - 1)
    near = [near_matrix(GROUP, cols, k) for k in range(2)]
    wide = (GROUP + 8) * cols
    near = [np.concatenate([m[:, :wide], m[:, :wide], m[:, wide:], m[:, wide:]], axis=1) for m in near]
    near = jnp.where(c == 0, jnp.asarray(near[0], F32), jnp.asarray(near[1], F32)).astype(BF16)
    side = [side_matrix(rows, k) for k in range(2)]
    side = jnp.where(c == 0, jnp.asarray(side[0], BF16), jnp.asarray(side[1], BF16))
    side = jnp.where(inside, side, jnp.zeros_like(side))
    side = jnp.concatenate([side, side], axis=1)
    edge = [edge_matrix(k) for k in range(2)]
    edge = jnp.where(y == 0, jnp.asarray(edge[0], F32), jnp.asarray(edge[1], F32)).astype(BF16)
    edge = jnp.concatenate([edge, edge], axis=1)

    def halo(zo, co, yo):
        return send(zo, z_perm), send(co, c_perm), send(yo, y_perm)

    def after(value, *deps):
        return lax.optimization_barrier((value,) + deps)[0]

    def flat(value):
        return value.reshape(size, depth)

    log_density, fwd_now, velocity = flat(log_density), flat(fwd_now), flat(velocity)
    fwd_before, adj_now, adj_before = flat(fwd_before), flat(adj_now), flat(adj_before)
    got = [send(v, swap_perm) for v in (log_density, fwd_now)]
    stacked = jnp.stack([velocity, fwd_before])
    got_model = send(stacked, swap_perm)
    full = nx * cols
    slots = subs * CAP
    entries, half_entries = shaped(subs, steps, 128), shaped(subs // 2, steps, 128)
    order = [*range(2, len(stages)), 0]
    cells, lists, give = call(
        functools.partial(pack_kernel, order[0]), "pack", [shaped(1, slots), entries, half_entries], after(rec_counts, stacked),
        rec_cells, observed, weight=0.2, far=3,
        scratch=[pltpu.VMEM(rec_counts.shape, jnp.int32), pltpu.VMEM(rec_cells.shape, jnp.int32),
                 pltpu.VMEM(observed.shape, F32)])
    vel, p_before = call(settle_pair_kernel, "settle_model", [field, field],
                         velocity, fwd_before, got_model, weight=0.6, far=2)
    for n, bit in enumerate(order[:-1]):
        lists, give = call(
            functools.partial(trade_kernel, bit, order[n + 1]), "trade", [entries, half_entries],
            after(lists, vel) if n == len(order) - 2 else lists, send(give, stages[bit][0]),
            weight=0.1)
        if n == 0:
            got[0], give = lax.optimization_barrier((got[0], give))

    density, p_now, *out = call(settle_kernel, "settle",
                                [field, field] + [shaped(2, *r.shape) for r in rim],
                                log_density, fwd_now, *got, far=2)
    zm, cm, ym = halo(*out)
    inj, = call(functools.partial(source_kernel, 0, full), "source", [field], src_cell,
                after(wavelet, density), weight=0.7, scalars=2)
    parts = call(first_inner_kernel, "first_inner", [field] * 7, density, p_now, cm,
                 near, deep, weight=1.3)
    got_adjoint = [send(after(v, parts[0]), swap_perm) for v in (adj_now, adj_before)]

    riders = subs // 4 * 8 + 8
    core_rim = shaped(size // 2 + riders, depth)
    y_rim = shaped(4 * cols + riders, depth)

    new, zo, co, yo, k0, ki, kx, kz = call(
        first_outer_kernel, "first_outer", [field, rim[0], core_rim, rim[2]] + [field] * 4,
        p_now, p_before, vel, *parts, inj, zm, ym, side, edge, give, cells)
    model = (k0, ki, kx, kz)
    states = [p_before, p_now, new]
    changes = []
    zm, cm, ym = halo(zo, co, yo)
    for t in range(1, steps):
        cur, prev, before = states[:-4:-1]
        part, change = call(
            functools.partial(forward_inner_kernel, t, full), "forward_inner", [field, field], src_cell, wavelet, cur, prev, *model, cm, near, deep, before, weight=1.2, scalars=2)
        changes.append(change)
        args = [part, k0, ki, kx, zm, ym, side, edge]
        if t == steps - 3:
            u_part, = call(adjoint_first_kernel, "adjoint_first", [field], u_now, u_before,
                           *model, u_cm, near, deep, weight=1.1)
            args[0] = after(part, u_part)
        if t == steps - 2:
            receivers = call(
                lists_kernel, "lists",
                [jax.ShapeDtypeStruct((size, slots), BF16),
                 jax.ShapeDtypeStruct((slots, size), BF16), shaped(slots, depth),
                 shaped(slots, steps)], lists, cells, weight=0.3)
            args[0] = after(part, receivers[0])
        if t == steps - 1:
            new, u_new, *out = call(
                functools.partial(turn_kernel, t), "turn", [field, field] + rim, *args, u_part,
                u_zm, u_ym, *receivers)
            states.append(new)
            break
        if t == 1:
            u_now, u_before = call(settle_pair_kernel, "settle_adjoint", [field, field], adj_now,
                                   adj_before, *got_adjoint, weight=0.6, far=2)
            args[0] = after(part, u_now)
            new, *out, lists, pair = call(
                core_stage_kernel, "forward_outer",
                [field, rim[0], rim[1], y_rim, entries, shaped(2, slots)], *args, lists, cells, cm)
            states.append(new)
            zm, cm, ym = halo(*out)
            continue
        if t == 2:
            new, *out, lists, cells = call(
                y_stage_kernel, "forward_outer",
                [field] + [shaped(2, *r.shape) for r in rim] + [entries, shaped(1, slots)],
                *args, lists, pair, u_now)
            states.append(new)
            zm, cm, ym = halo(*out)
            u_zm, u_cm, u_ym = zm, cm, ym
            continue
        new, *out = call(outer_kernel, "forward_outer", [field] + rim, *args)
        states.append(new)
        zm, cm, ym = halo(*out)

    zm, cm, ym = halo(*out)
    u_before, u_now = u_now, u_new
    image = []
    chunk = depth // nx
    half = shaped(nq, size * chunk // 128, 128)
    for j in range(1, steps):
        t = steps - 1 - j
        terms = [changes[t + 1], *image] if image else states[:-4:-1]
        part, *image = call(
            functools.partial(adjoint_inner_kernel, t), "adjoint_inner", [field, field], u_now, u_before, *model, cm, near, deep, states[t + 2], *receivers, *terms, weight=1.5)
        args = [part, k0, ki, kx, zm, ym, side, edge]
        if j == steps - 1:
            final, mine, other = call(
                functools.partial(last_kernel, 2.0 / steps), "last",
                [shaped(2, *field.shape), half, half], *args, *image, changes[0], vel, u_now)
            break
        u_before = u_now
        u_now, *out = call(outer_kernel, "adjoint_outer", [field] + rim,
                           *args)
        zm, cm, ym = halo(*out)

    got = send(final, swap_perm)
    pieces = call(join_kernel, "join", [shaped(2, *half.shape[1:])] * nq, mine,
                  send(other, c_perm))
    pieces = [send(pieces[s], plan.spread(s)) for s in reversed(range(nq))][::-1]
    adj_prev, adj_out = call(select_kernel, "select", [field, field], final, got, weight=1.2)
    gradient, = call(filter_kernel, "filter", [shaped(chunk, rows, nx * cols)],
                     after(pieces[-1], adj_out), *pieces[-2::-1])
    block = (rows, cols, depth)
    return gradient, adj_out.reshape(block), adj_prev.reshape(block)


def solution(mesh):
    field = P(("shots", "inline"), "xline", None)
    model = P("inline", "xline", None)
    lists = P(("xline", "inline"), None)
    return jax.shard_map(
        functools.partial(per_device, Plan(mesh)),
        mesh=mesh,
        in_specs=(field, field, field, field, model, model, P("shots", ("xline", "inline")),
                  lists, lists, P("shots"), P("shots", None)),
        out_specs=(P(("shots", "xline"), "inline", None), field, field),
        check_vma=False,
    )
```
